32 devices in a mesh: replica: 8 (over z, core), fsdp: 4 (over y, x).
Axes of the slice: x: 2, y: 2, z: 4, core: 2. Of those that a mesh axis runs over, the one named last changes fastest.
Arguments:
- tokens: bfloat16 [50432, 512], P(('replica', 'fsdp')), may hold values from -8 to 8
- cotangent: bfloat16 [50432, 512], P(('replica', 'fsdp')), may hold values from -6 to 6
- routes: int32 [50432, 2], P(('replica', 'fsdp')), may hold values from 0 to 31, all different within a row
- attn_norm: bfloat16 [2, 512], P(None, 'fsdp'), may hold values from 0.5 to 1.5
- query_w: bfloat16 [2, 512, 512], P(None, 'fsdp'), may hold values from -0.375 to 0.375
- key_w: bfloat16 [2, 512, 512], P(None, 'fsdp'), may hold values from -0.375 to 0.375
- value_w: bfloat16 [2, 512, 512], P(None, 'fsdp'), may hold values from -0.25 to 0.25
- output_w: bfloat16 [2, 512, 512], P(None, 'fsdp'), may hold values from -0.75 to 0.75
- ffn_norm: bfloat16 [2, 512], P(None, 'fsdp'), may hold values from 0.5 to 1.5
- mlp_in: bfloat16 [512, 2048], P('fsdp'), may hold values from -0.25 to 0.25
- mlp_out: bfloat16 [2048, 512], P('fsdp'), may hold values from -0.1875 to 0.1875
- router_w: bfloat16 [512, 32], P('fsdp'), may hold values from -0.1875 to 0.1875
- expert_in: bfloat16 [32, 512, 2048], P('fsdp'), may hold values from -0.25 to 0.25
- expert_out: bfloat16 [32, 2048, 512], P('fsdp'), may hold values from -3 to 3
- updated_query: float32 [2, 512, 512], P(None, 'fsdp'), may hold values from -0.25 to 0.25
- updated_key: float32 [2, 512, 512], P(None, 'fsdp'), may hold values from -0.25 to 0.25
- clip_threshold: float32 [2, 8], replicated, may hold values from 1.5 to 4
Outputs:
- block_output: float32 [50432, 512], P(('replica', 'fsdp'))
- tokens_grad: float32 [50432, 512], P(('replica', 'fsdp'))
- attn_norm_grad: float32 [2, 512], P(None, 'fsdp')
- query_grad: float32 [2, 512, 512], P(None, 'fsdp')
- key_grad: float32 [2, 512, 512], P(None, 'fsdp')
- value_grad: float32 [2, 512, 512], P(None, 'fsdp')
- output_grad: float32 [2, 512, 512], P(None, 'fsdp')
- ffn_norm_grad: float32 [2, 512], P(None, 'fsdp')
- mlp_in_grad: float32 [512, 2048], P('fsdp')
- mlp_out_grad: float32 [2048, 512], P('fsdp')
- router_grad: float32 [512, 32], P('fsdp')
- expert_in_grad: float32 [32, 512, 2048], P('fsdp')
- expert_out_grad: float32 [32, 2048, 512], P('fsdp')
- clipped_query: float32 [2, 512, 512], P(None, 'fsdp')
- clipped_key: float32 [2, 512, 512], P(None, 'fsdp')
The draws below stay inside these ranges and needn't reach their ends.
Inputs may be any that keep to these rules, and one draw needn't show every extreme that they name: `routes`: each token names 2 different experts.
All inputs are finite; a program needn't handle non-finite values.
Results may differ from the reference program's by a relative error of at most 0.025.
Values may be sent and summed in bfloat16 or wider, within the bound.
A program may use at most 448 MiB of HBM per device.

```python
import math
import jax
import jax.numpy as jnp
from jax import lax

D = 512
HEADS = 8
HEAD = 64
FF = 2048
EXPERTS = 32
TOP = 2
SEQ = 197
LAYERS = 2
CAP = 128
TOKENS = 50432
N_REPLICA = 8
N_FSDP = 4


def draw_tokens(key, part):
    key = jax.random.fold_in(key, 7)
    noise_key, common_key = jax.random.split(key)
    images = TOKENS // SEQ
    noise_part = jax.random.normal(noise_key, (images, SEQ, D), jnp.float32)
    common_part = jax.random.normal(common_key, (images, 1, D), jnp.float32)
    amplitude = 1.2 * jnp.arange(images, dtype=jnp.float32) / max(images - 1, 1)
    combined = noise_part + amplitude[:, None, None] * common_part
    return jnp.clip(combined, -8.0, 8.0).reshape(TOKENS, D).astype(jnp.bfloat16)


def steps_of(rng, shape, cuts, least, top_value):
    level = 1.0
    for position, blocks in cuts:
        draws = jax.random.uniform(jax.random.fold_in(jax.random.fold_in(rng, 6), position), (blocks,), jnp.float32, least / len(cuts), top_value / len(cuts))
        level = level * jnp.repeat(jnp.exp(draws), shape[position] // blocks).reshape((-1,) + (1,) * (len(shape) - 1 - position))
    return level


def different_ones(stream_key, rows, amount, top, lift):
    sequence = jax.random.permutation(jax.random.fold_in(stream_key, 1), amount)
    boost = sequence
    for power in range(3):
        boost = boost * boost // amount
    boost = boost * lift // amount
    tickets = jax.random.randint(jax.random.fold_in(stream_key, 2), (rows, amount), 0, 4096) + boost
    holders = jax.random.permutation(jax.random.fold_in(stream_key, 3), rows)[jnp.arange(amount) % rows]
    tickets = jnp.where(jnp.arange(rows)[:, None] == holders[None, :], 1 << 14, tickets)
    score = tickets * amount + jnp.arange(amount)
    return lax.top_k(score.astype(jnp.int32), top)[1].astype(jnp.int32)


def noise(rng, extent, spread, limit, shards=(), kind=jnp.bfloat16):
    level = steps_of(rng, extent, shards, -0.22, 0.18) if shards else 1.0
    values = jax.random.normal(rng, extent, jnp.float32) * spread * level
    return jnp.minimum(jnp.maximum(values, -limit), limit).astype(kind)


def setup_inputs(seed: int = 0) -> dict:
    key_list = jax.random.split(jax.random.key(seed), 18)
    tokens = draw_tokens(jax.random.fold_in(key_list[17], 71), 0)
    cotangent = noise(key_list[1], (TOKENS, D), 1.0, 6.0, ((0, 32),))
    routes = different_ones(key_list[2], TOKENS, EXPERTS, TOP, 512)
    attn_norm = jnp.clip(1.0 + 0.1 * jax.random.normal(key_list[3], (LAYERS, D), jnp.float32), 0.5, 1.5).astype(jnp.bfloat16)
    query_w = noise(key_list[4], (LAYERS, D, D), (D // 2) ** -0.5, 0.375, ((1, 4),))
    key_w = noise(key_list[5], (LAYERS, D, D), (D // 2) ** -0.5, 0.375, ((1, 4),))
    value_w = noise(key_list[6], (LAYERS, D, D), D ** -0.5, 0.25, ((1, 4),))
    output_w = noise(key_list[7], (LAYERS, D, D), (D // 8) ** -0.5, 0.75, ((1, 4),))
    ffn_norm = jnp.clip(1.0 + 0.1 * jax.random.normal(key_list[8], (LAYERS, D), jnp.float32), 0.5, 1.5).astype(jnp.bfloat16)
    mlp_in = noise(key_list[9], (D, FF), D ** -0.5, 0.25, ((0, 4),))
    mlp_out = noise(key_list[10], (FF, D), (FF // 2) ** -0.5, 0.1875, ((0, 4),))
    router_w = noise(key_list[11], (D, EXPERTS), (2 * D) ** -0.5, 0.1875, ((0, 4),))
    expert_in = noise(key_list[12], (EXPERTS, D, FF), D ** -0.5, 0.25, ((0, 4),))
    expert_out = noise(key_list[13], (EXPERTS, FF, D), (max(FF // 512, 1)) ** -0.5, 3.0, ((0, 4),))
    updated_query = noise(key_list[14], (LAYERS, D, D), D ** -0.5, 0.25, ((1, 4),), jnp.float32)
    updated_key = noise(key_list[15], (LAYERS, D, D), D ** -0.5, 0.25, ((1, 4),), jnp.float32)
    clip_threshold = jnp.clip(jnp.exp(jax.random.uniform(key_list[16], (LAYERS, HEADS), jnp.float32, math.log(1.5), math.log(4.0))), 1.5, 4.0)
    return {"tokens": tokens, "cotangent": cotangent, "routes": routes, "attn_norm": attn_norm, "query_w": query_w, "key_w": key_w, "value_w": value_w, "output_w": output_w, "ffn_norm": ffn_norm, "mlp_in": mlp_in, "mlp_out": mlp_out, "router_w": router_w, "expert_in": expert_in, "expert_out": expert_out, "updated_query": updated_query, "updated_key": updated_key, "clip_threshold": clip_threshold}


@jax.custom_vjp
def low(v):
    return lax.optimization_barrier(v.astype(jnp.bfloat16)).astype(jnp.float32)

@jax.custom_vjp
def low_back(v):
    return v

def low_keep(v):
    return (low(v), None)

def low_pass(kept, grad):
    return (grad,)

def back_keep(v):
    return (v, None)

def back_low(kept, grad):
    return (low(grad),)
low.defvjp(low_keep, low_pass)
low_back.defvjp(back_keep, back_low)
EPSILON = 1e-06
HIGHEST = lax.Precision.HIGHEST

def product(former, latter):
    return jnp.matmul(former, latter, precision=HIGHEST)

def layer_norm(values, gain_row):
    centred = values - lax.optimization_barrier(jnp.mean(values, -1, keepdims=True))
    return centred * lax.rsqrt(lax.optimization_barrier(jnp.mean(centred * centred, -1, keepdims=True)) + EPSILON) * gain_row

def softmax_rows(scores):
    shifted = jnp.exp(scores - lax.optimization_barrier(jnp.max(scores, -1, keepdims=True)))
    return shifted / lax.optimization_barrier(jnp.sum(shifted, -1, keepdims=True))

def attention_block(residual, gain_row, query_rows, key_rows, value_rows, output_rows):
    images = residual.shape[0]
    normed = low(layer_norm(residual, gain_row))
    queries = low_back(low(product(normed, query_rows))).reshape(images, SEQ, HEADS, HEAD)
    keys_all = low_back(low(product(normed, key_rows))).reshape(images, SEQ, HEADS, HEAD)
    values_all = low_back(low(product(normed, value_rows))).reshape(images, SEQ, HEADS, HEAD)
    scores = low_back(jnp.einsum('iqhd,ikhd->ihqk', queries, keys_all, precision=HIGHEST) * HEAD ** (-0.5))
    attn_probs = low(softmax_rows(scores))
    mixed_heads = jnp.einsum('ihqk,ikhd->iqhd', attn_probs, values_all, precision=HIGHEST)
    mixed_heads = low_back(low(mixed_heads)).reshape(images, SEQ, D)
    return (residual + low_back(product(mixed_heads, output_rows)), lax.optimization_barrier(jnp.max(scores, axis=(0, 2, 3))))

def dense_layer(residual, attn_gain, query_rows, key_rows, value_rows, output_rows, ffn_gain, inner_w, outer_w):
    after_attn, head_max = attention_block(residual, attn_gain, query_rows, key_rows, value_rows, output_rows)
    normed = low(layer_norm(after_attn, ffn_gain))
    pre_act = low_back(product(normed, inner_w))
    hidden = low(jax.nn.gelu(pre_act, approximate=False))
    return (after_attn + low_back(product(hidden, outer_w)), head_max)

def slot_tables(routes):
    blocks = N_REPLICA * N_FSDP
    per_block = routes.shape[0] // blocks
    top_count = routes.shape[1]
    order = jnp.transpose(routes.reshape(blocks, per_block, top_count), (0, 2, 1)).reshape(blocks, top_count * per_block)
    hits = (order[:, :, None] == jnp.arange(EXPERTS, dtype=jnp.int32)[None, None, :]).astype(jnp.int32)
    place = lax.optimization_barrier(jnp.sum((jnp.cumsum(hits, axis=1, dtype=jnp.int32) - hits) * hits, axis=2, dtype=jnp.int32))
    block_id = jnp.arange(blocks, dtype=jnp.int32)[:, None]
    per_expert = blocks * CAP
    target = jnp.where(place < CAP, order * per_expert + block_id * CAP + place, EXPERTS * per_expert).astype(jnp.int32)
    token_id = block_id * per_block + jnp.arange(top_count * per_block, dtype=jnp.int32)[None, :] % per_block
    source = jnp.full((EXPERTS * per_expert,), routes.shape[0], jnp.int32)
    source = source.at[target.reshape(-1)].set(token_id.reshape(-1).astype(jnp.int32), mode='drop')
    index = jnp.transpose(target.reshape(blocks, top_count, per_block), (0, 2, 1)).reshape(-1, top_count)
    return (index, source)

def expert_layer(residual, gain_row, router_rows, inner_all, outer_all, routes, index, source):
    normed = low(layer_norm(residual, gain_row))
    router_probs = softmax_rows(low_back(product(normed, router_rows)))
    gates = jnp.take_along_axis(router_probs, routes, axis=1)
    padded = jnp.concatenate([normed, jnp.zeros((1, D), jnp.float32)], 0)
    slots = low_back(padded[source]).reshape(EXPERTS, -1, D)

    def one_expert(operands):
        slot_rows, inner_w, outer_w = operands
        pre_act = low_back(product(slot_rows, inner_w))
        hidden = low(jax.nn.gelu(pre_act, approximate=False))
        return low_back(low(product(hidden, outer_w)))
    results = lax.map(jax.checkpoint(one_expert), (slots, inner_all, outer_all)).reshape(-1, D)
    results = jnp.concatenate([results, jnp.zeros((1, D), jnp.float32)], 0)
    return gates[:, 0:1] * results[index[:, 0]] + gates[:, 1:2] * results[index[:, 1]]

def reference(tokens, cotangent, routes, attn_norm, query_w, key_w, value_w, output_w, ffn_norm, mlp_in, mlp_out, router_w, expert_in, expert_out, updated_query, updated_key, clip_threshold):
    index, source = slot_tables(routes)

    def forward(residual, attn_gain, query_all, key_all, value_all, output_all, ffn_gain, inner_w, outer_w, router_rows, expert_inner, expert_outer):
        grouped = residual.reshape(-1, 16, SEQ, D)

        def first_layer(images_block):
            return dense_layer(images_block, attn_gain[0], query_all[0], key_all[0], value_all[0], output_all[0], ffn_gain[0], inner_w, outer_w)

        def second_attention(images_block):
            return attention_block(images_block, attn_gain[1], query_all[1], key_all[1], value_all[1], output_all[1])
        after_first, max_zero = lax.map(jax.checkpoint(first_layer), grouped)
        after_second, max_one = lax.map(jax.checkpoint(second_attention), after_first)
        flattened = after_second.reshape(-1, D)
        output = flattened + expert_layer(flattened, ffn_gain[1], router_rows, expert_inner, expert_outer, routes, index, source)
        return (output, jnp.stack([lax.optimization_barrier(jnp.max(max_zero, 0)), lax.optimization_barrier(jnp.max(max_one, 0))]))
    primals = tuple((argument.astype(jnp.float32) for argument in (tokens, attn_norm, query_w, key_w, value_w, output_w, ffn_norm, mlp_in, mlp_out, router_w, expert_in, expert_out)))
    output, pullback, maxima = jax.vjp(forward, *primals, has_aux=True)
    grads = pullback(cotangent.astype(jnp.float32))
    factor = clip_threshold / jnp.maximum(maxima, clip_threshold)
    column_scale = jnp.repeat(jnp.sqrt(factor), HEAD, axis=1)
    clipped_query = updated_query * column_scale[:, None, :]
    clipped_key = updated_key * column_scale[:, None, :]
    return (output, grads[0], grads[1], grads[2], grads[3], grads[4], grads[5], grads[6], grads[7], grads[8], grads[9], grads[10], grads[11], clipped_query, clipped_key)
```

```python
from functools import partial

import jax
import jax.numpy as jnp
from jax import lax
from jax.experimental import pallas as pl
from jax.experimental.pallas import tpu as pltpu
from jax.sharding import Mesh
from jax.sharding import PartitionSpec as P

D = 512
HEADS = 8
HEAD = 64
FF = 2048
SEQ = 197
SP = 208
CAP = 128
EXPERTS = 32
EPSILON = 1e-06
SCALE = HEAD ** (-0.5)
LOWEST = -1e30
NARROW = jnp.bfloat16
WIDE = jnp.float32
CORES = 2
MIB = 1 << 20


def nn(a, b):
    return lax.dot_general(a, b, (((1,), (0,)), ((), ())), preferred_element_type=WIDE)


def nt(a, b):
    return lax.dot_general(a, b, (((1,), (1,)), ((), ())), preferred_element_type=WIDE)


def tn(a, b):
    return lax.dot_general(a, b, (((0,), (0,)), ((), ())), preferred_element_type=WIDE)


def norm_parts(values):
    centred = values - jnp.mean(values, -1, keepdims=True)
    inverse = lax.rsqrt(jnp.mean(centred * centred, -1, keepdims=True) + EPSILON)
    return centred * inverse, inverse


def norm_backward(incoming, unit, inverse, gain):
    gain_grad = jnp.sum(incoming * unit, 0, keepdims=True)
    scaled = incoming * gain
    centred = (
        scaled
        - jnp.mean(scaled, -1, keepdims=True)
        - unit * jnp.mean(scaled * unit, -1, keepdims=True)
    )
    return inverse * centred, gain_grad


def normal_parts(x):
    z = jnp.abs(x)
    t = 1.0 / (1.0 + (0.3275911 * 0.7071067811865476) * z)
    bell = jnp.exp(-0.5 * (x * x))
    poly = t * (
        0.5 * 0.254829592
        + t
        * (
            0.5 * -0.284496736
            + t * (0.5 * 1.421413741 + t * (0.5 * -1.453152027 + t * (0.5 * 1.061405429)))
        )
    )
    tail = poly * bell
    return jnp.where(x >= 0, 1.0 - tail, tail), bell


INV_ROOT = 0.3989422804014327


def head_masks(dtype):
    lane = lax.broadcasted_iota(jnp.int32, (1, 2 * HEAD), 1)
    low = (lane < HEAD).astype(dtype)
    return (low, (1 - low.astype(WIDE)).astype(dtype))


def attn_fwd_body(x, gain, w_ref, qkv_ref, mixed_ref, peak_ref, ib):
    unit, _ = norm_parts(x)
    normed = (unit * gain).astype(NARROW)
    q = (nn(normed, w_ref[:, 0:D]).astype(NARROW).astype(WIDE) * SCALE).astype(NARROW)
    k = nn(normed, w_ref[:, D : 2 * D]).astype(NARROW)
    v = nn(normed, w_ref[:, 2 * D : 3 * D]).astype(NARROW)
    masks = head_masks(NARROW)
    cols = lax.broadcasted_iota(jnp.int32, (SP, SP), 1)
    rows = lax.broadcasted_iota(jnp.int32, (SP, 1), 0)
    head_row = lax.broadcasted_iota(jnp.int32, (HEADS, 128), 0)
    mixed_all = []
    for i in range(ib):
        peaks = jnp.full((HEADS, 128), LOWEST, WIDE)
        r = slice(i * SP, (i + 1) * SP)
        pairs = []
        for pair in range(HEADS // 2):
            c = slice(pair * 2 * HEAD, (pair + 1) * 2 * HEAD)
            qp, kp, vp = q[r, c], k[r, c], v[r, c]
            acc = None
            for half in range(2):
                s = nt(qp * masks[half], kp)
                s = jnp.where(cols < SEQ, s, LOWEST)
                top = jnp.max(s, -1, keepdims=True)
                e = jnp.exp(s - top)
                p = (e * (1.0 / jnp.sum(e, -1, keepdims=True))).astype(NARROW)
                part = nn(p, vp * masks[half])
                acc = part if acc is None else acc + part
                peak = jnp.max(jnp.where(rows < SEQ, top, LOWEST), 0, keepdims=True)
                peaks = jnp.where(head_row == pair * 2 + half, peak, peaks)
            pairs.append(acc.astype(NARROW))
        mixed_all.append(jnp.concatenate(pairs, 1))
        peak_ref[i] = peaks
    mixed = jnp.concatenate(mixed_all, 0) if ib > 1 else mixed_all[0]
    qkv_ref[...] = jnp.concatenate([q, k, v], 1).reshape(ib, SP, 3 * D)
    mixed_ref[...] = mixed.reshape(ib, SP, D)
    return x + nn(mixed, w_ref[:, 3 * D : 4 * D])


def dense_attn_kernel(ib, x_ref, g_ref, w_ref, y_ref, qkv_ref, mixed_ref, peak_ref):
    x = x_ref[...].astype(WIDE).reshape(ib * SP, D)
    y = attn_fwd_body(x, g_ref[0:1, :], w_ref, qkv_ref, mixed_ref, peak_ref, ib)
    y_ref[...] = y.reshape(ib, SP, D)


def ffn_kernel(ib, x_ref, g_ref, win_ref, wout_ref, y_ref):
    x = x_ref[...].reshape(ib * SP, D)
    unit, _ = norm_parts(x)
    normed = (unit * g_ref[2:3, :]).astype(NARROW)
    acc = x
    for f in range(FF // 512):
        c = slice(f * 512, (f + 1) * 512)
        pre = nn(normed, win_ref[:, c])
        cdf, _ = normal_parts(pre)
        acc = acc + nn((pre * cdf).astype(NARROW), wout_ref[c, :])
    y_ref[...] = acc.reshape(ib, SP, D)


def expert_attn_kernel(
    ib, x_ref, g_ref, w_ref, wr_ref, y_ref, qkv_ref, mixed_ref, peak_ref, moe_ref, prob_ref
):
    x = x_ref[...].reshape(ib * SP, D)
    y = attn_fwd_body(x, g_ref[1:2, :], w_ref, qkv_ref, mixed_ref, peak_ref, ib)
    y_ref[...] = y.reshape(ib, SP, D)
    unit, _ = norm_parts(y)
    moe = (unit * g_ref[3:4, :]).astype(NARROW)
    moe_ref[...] = moe.reshape(ib, SP, D)
    lane = lax.broadcasted_iota(jnp.int32, (1, 128), 1)
    logits = jnp.where(lane < EXPERTS, nn(moe, wr_ref[...]), LOWEST)
    e = jnp.exp(logits - jnp.max(logits, -1, keepdims=True))
    prob_ref[...] = (e / jnp.sum(e, -1, keepdims=True)).reshape(ib, SP, 128)


def whole(shape):
    return pl.BlockSpec(
        shape, lambda *_: (0,) * len(shape), pipeline_mode=pl.Buffered(buffer_count=1)
    )


def per_image(ib, *tail):
    return pl.BlockSpec((ib, *tail), lambda i, *_: (i,) + (0,) * len(tail))


def sds(shape, dtype):
    return jax.ShapeDtypeStruct(shape, dtype)


def cost(flops, moved):
    return pl.CostEstimate(flops=int(flops), bytes_accessed=int(moved), transcendentals=0)


def params(mib):
    return pltpu.CompilerParams(vmem_limit_bytes=mib * MIB)


def dense_attn(x, gains, w0, images, ib):
    return pl.pallas_call(
        partial(dense_attn_kernel, ib),
        grid=(images // ib,),
        in_specs=[per_image(ib, SP, D), whole(gains.shape), whole(w0.shape)],
        out_specs=[
            per_image(ib, SP, D),
            per_image(ib, SP, 3 * D),
            per_image(ib, SP, D),
            per_image(ib, HEADS, 128),
        ],
        out_shape=[
            sds((images, SP, D), WIDE),
            sds((images, SP, 3 * D), NARROW),
            sds((images, SP, D), NARROW),
            sds((images, HEADS, 128), WIDE),
        ],
        compiler_params=params(48),
        name="dense_attention",
    )(x, gains, w0)


def ffn(x, gains, win, wout, images, ib):
    return pl.pallas_call(
        partial(ffn_kernel, ib),
        grid=(images // ib,),
        in_specs=[per_image(ib, SP, D), whole(gains.shape), whole(win.shape), whole(wout.shape)],
        out_specs=per_image(ib, SP, D),
        out_shape=sds((images, SP, D), WIDE),
        compiler_params=params(48),
        name="feed_forward",
    )(x, gains, win, wout)


def expert_attn(x, gains, w1, wr, images, ib):
    return pl.pallas_call(
        partial(expert_attn_kernel, ib),
        grid=(images // ib,),
        in_specs=[per_image(ib, SP, D), whole(gains.shape), whole(w1.shape), whole(wr.shape)],
        out_specs=[
            per_image(ib, SP, D),
            per_image(ib, SP, 3 * D),
            per_image(ib, SP, D),
            per_image(ib, HEADS, 128),
            per_image(ib, SP, D),
            per_image(ib, SP, 128),
        ],
        out_shape=[
            sds((images, SP, D), WIDE),
            sds((images, SP, 3 * D), NARROW),
            sds((images, SP, D), NARROW),
            sds((images, HEADS, 128), WIDE),
            sds((images, SP, D), NARROW),
            sds((images, SP, 128), WIDE),
        ],
        compiler_params=params(48),
        name="expert_attention",
    )(x, gains, w1, wr)


def places_kernel(order_ref, routes_ref, pos_ref, target_ref):
    tokens = routes_ref.shape[1]
    order = order_ref[:, 0:1]
    chunk = 128
    strict = (
        lax.broadcasted_iota(jnp.int32, (chunk, chunk), 0)
        < lax.broadcasted_iota(jnp.int32, (chunk, chunk), 1)
    ).astype(NARROW)
    slot_row = lax.broadcasted_iota(jnp.int32, (EXPERTS, 1), 0).astype(WIDE) * CAP
    base = jnp.zeros((EXPERTS, 1), WIDE)
    for c in range(tokens // chunk):
        pos_ref[:, c * chunk : (c + 1) * chunk] = jnp.full((EXPERTS, chunk), -1.0, WIDE)
    target_ref[...] = jnp.zeros(target_ref.shape, WIDE)
    for k in range(2):
        for c in range(tokens // chunk):
            s = slice(c * chunk, (c + 1) * chunk)
            hit = (order == routes_ref[k : k + 1, s]).astype(WIDE)
            place = base + nn(hit.astype(NARROW), strict)
            base = base + jnp.sum(hit, -1, keepdims=True)
            pos_ref[:, s] = jnp.where(hit > 0, place, pos_ref[:, s])
            slot = jnp.where(place < CAP, slot_row + place, 2.0 * EXPERTS * CAP)
            found = jnp.sum(hit * slot, 0, keepdims=True)
            real = jnp.sum(hit, 0, keepdims=True)
            target_ref[k : k + 1, s] = jnp.where(real > 0, found, 2.0 * EXPERTS * CAP)


def places(order, routes_rows):
    tokens = routes_rows.shape[1]
    return pl.pallas_call(
        places_kernel,
        in_specs=[pl.BlockSpec(memory_space=pltpu.VMEM)] * 2,
        out_specs=[pl.BlockSpec(memory_space=pltpu.VMEM)] * 2,
        out_shape=[sds((EXPERTS, tokens), WIDE), sds((8, tokens), WIDE)],
        name="places",
    )(order, routes_rows)


GROUP = 4


def dispatch_kernel(pos_ref, order_ref, moe_ref, cot_ref, prob_ref, out_ref, parts_ref):
    step = pl.program_id(0)

    @pl.when(step == 0)
    def _():
        prob = prob_ref[...]
        high = prob.astype(NARROW)
        rest = prob - high.astype(WIDE)
        middle = rest.astype(NARROW)
        parts_ref[:, 0:128] = high
        parts_ref[:, 128:256] = middle
        parts_ref[:, 256:384] = (rest - middle.astype(WIDE)).astype(NARROW)

    slot = lax.broadcasted_iota(jnp.int32, (CAP, 1), 0).astype(WIDE)
    lane = lax.broadcasted_iota(jnp.int32, (1, 128), 1)
    hot = jnp.concatenate(
        [(pos_ref[g : g + 1, :] == slot).astype(NARROW) for g in range(GROUP)], 0
    )
    rows = nn(hot, moe_ref[...]).astype(NARROW)
    grads = nn(hot, cot_ref[...])
    parts = nn(hot, parts_ref[...])
    gates = parts[:, 0:128] + parts[:, 128:256] + parts[:, 256:384]
    for g in range(GROUP):
        s = slice(g * CAP, (g + 1) * CAP)
        expert = order_ref[g : g + 1, 0:1]
        gate = jnp.sum(jnp.where(lane == expert, gates[s], 0.0), -1, keepdims=True)
        out_ref[g, 0:CAP, :] = rows[s]
        out_ref[g, CAP : 2 * CAP, :] = (gate * grads[s]).astype(NARROW)


def dispatch(pos, order, moe, cot, prob):
    tokens = moe.shape[0]
    groups = EXPERTS // GROUP
    return pl.pallas_call(
        dispatch_kernel,
        grid=(groups,),
        in_specs=[
            pl.BlockSpec((None, GROUP, tokens), lambda i: (i, 0, 0)),
            pl.BlockSpec((None, GROUP, 128), lambda i: (i, 0, 0)),
            whole(moe.shape),
            whole(cot.shape),
            whole(prob.shape),
        ],
        out_specs=pl.BlockSpec((GROUP, 2 * CAP, D), lambda i: (i, 0, 0)),
        out_shape=sds((EXPERTS, 2 * CAP, D), NARROW),
        scratch_shapes=[pltpu.VMEM((tokens, 384), NARROW)],
        compiler_params=params(48),
        name="dispatch",
    )(pos.reshape(groups, GROUP, tokens), order.reshape(groups, GROUP, 128), moe, cot, prob)


def expert_kernel(pick, rows_ref, win_ref, wout_ref, back_ref, din_ref, dout_ref, res, sgr):
    f = pl.program_id(0)
    senders = rows_ref.shape[0]
    part = min(senders, 8)
    count = part * CAP
    win, wout = win_ref[...], wout_ref[...]
    d_in = d_out = None
    for first in range(0, senders, part):
        slots = rows_ref[first : first + part, 0:CAP, :].reshape(count, D)
        grads = rows_ref[first : first + part, CAP : 2 * CAP, :].reshape(count, D)
        r = slice(first * CAP, (first + part) * CAP)
        pre = nn(slots, win)
        hidden_grad = nt(grads, wout)
        cdf, bell = normal_parts(pre)
        hidden = (pre * cdf).astype(NARROW)
        pre_grad = ((cdf + pre * (bell * INV_ROOT)) * hidden_grad).astype(NARROW)
        result = nn(hidden, wout)
        slot_grad = nt(pre_grad, win)
        in_part, out_part = tn(slots, pre_grad), tn(hidden, grads)
        d_in = in_part if d_in is None else d_in + in_part
        d_out = out_part if d_out is None else d_out + out_part

        @pl.when(f == 0)
        def _(r=r, result=result, slot_grad=slot_grad):
            res[r, :] = result
            sgr[r, :] = slot_grad

        @pl.when(f > 0)
        def _(r=r, result=result, slot_grad=slot_grad):
            res[r, :] += result
            sgr[r, :] += slot_grad

    din_ref[...] = d_in.astype(NARROW)
    dout_ref[...] = d_out.astype(NARROW)

    @pl.when(f == pl.num_programs(0) - 1)
    def _():
        back_ref[:, :, 0:D] = res[...].astype(NARROW).reshape(senders, CAP, D)
        back_ref[:, :, D : 2 * D] = sgr[...].astype(NARROW).reshape(senders, CAP, D)


def expert(pick, rows, win, wout):
    senders = rows.shape[0]
    wide = 512
    return pl.pallas_call(
        expert_kernel,
        grid_spec=pltpu.PrefetchScalarGridSpec(
            num_scalar_prefetch=1,
            grid=(FF // wide,),
            in_specs=[
                whole(rows.shape),
                pl.BlockSpec((None, D, wide), lambda f, p: (p[0], 0, f)),
                pl.BlockSpec((None, wide, D), lambda f, p: (p[0], f, 0)),
            ],
            out_specs=[
                whole((senders, CAP, 2 * D)),
                pl.BlockSpec((None, D, wide), lambda f, p: (f, 0, 0)),
                pl.BlockSpec((None, wide, D), lambda f, p: (f, 0, 0)),
            ],
            scratch_shapes=[
                pltpu.VMEM((senders * CAP, D), WIDE),
                pltpu.VMEM((senders * CAP, D), WIDE),
            ],
        ),
        out_shape=[
            sds((senders, CAP, 2 * D), NARROW),
            sds((FF // wide, D, wide), NARROW),
            sds((FF // wide, wide, D), NARROW),
        ],
        compiler_params=params(56),
        cost_estimate=cost(12 * senders * CAP * D * FF, 8 * D * FF),
        name="one_expert",
    )(pick, rows, win, wout)


def attn_bwd_body(x, incoming, gain, qkv_ref, mixed_ref, w_ref, dw_ref, ib):
    unit, inverse = norm_parts(x)
    normed = (unit * gain).astype(NARROW)
    out_grad = incoming.astype(NARROW)
    mixed = mixed_ref[...].reshape(ib * SP, D)
    dw_ref[:, 3 * D : 4 * D] += tn(mixed, out_grad)
    mixed_grad = nt(out_grad, w_ref[:, 3 * D : 4 * D]).astype(NARROW)
    masks = head_masks(NARROW)
    rows = lax.broadcasted_iota(jnp.int32, (SP, SP), 0)
    dq_all, dk_all, dv_all = [], [], []
    for i in range(ib):
        r = slice(i * SP, (i + 1) * SP)
        dqs, dks, dvs = [], [], []
        for pair in range(HEADS // 2):
            qp = qkv_ref[i, :, pair * 128 : (pair + 1) * 128]
            kp = qkv_ref[i, :, D + pair * 128 : D + (pair + 1) * 128]
            vp = qkv_ref[i, :, 2 * D + pair * 128 : 2 * D + (pair + 1) * 128]
            mp = mixed_grad[r, pair * 128 : (pair + 1) * 128]
            dq = dk = dv = None
            for half in range(2):
                qm, mm, km = qp * masks[half], mp * masks[half], kp * masks[half]
                s = jnp.where(rows < SEQ, nt(kp, qm), LOWEST)
                e = jnp.exp(s - jnp.max(s, 0, keepdims=True))
                soft = e * (1.0 / jnp.sum(e, 0, keepdims=True))
                pg = nt(vp, mm)
                delta = jnp.sum(soft * pg, 0, keepdims=True)
                sg = (soft * (pg - delta)).astype(NARROW)
                v_part = nn(soft.astype(NARROW), mm)
                k_part = nn(sg, qm)
                q_part = tn(sg, km)
                dq = q_part if dq is None else dq + q_part
                dk = k_part if dk is None else dk + k_part
                dv = v_part if dv is None else dv + v_part
            dqs.append((dq * SCALE).astype(NARROW))
            dks.append(dk.astype(NARROW))
            dvs.append(dv.astype(NARROW))
        dq_all.append(jnp.concatenate(dqs, 1))
        dk_all.append(jnp.concatenate(dks, 1))
        dv_all.append(jnp.concatenate(dvs, 1))
    dqkv = jnp.concatenate(
        [
            jnp.concatenate(a, 0) if ib > 1 else a[0]
            for a in (dq_all, dk_all, dv_all)
        ],
        1,
    )
    dw_ref[:, 0 : 3 * D] += tn(normed, dqkv)
    normed_grad = nt(dqkv, w_ref[:, 0 : 3 * D])
    input_grad, gain_grad = norm_backward(normed_grad, unit, inverse, gain)
    return incoming + input_grad, gain_grad


def gain_columns(dg_ref):
    tall = jnp.concatenate(
        [jnp.zeros((EXPERTS, D), WIDE), dg_ref[...], jnp.zeros((128 - EXPERTS - 8, D), WIDE)], 0
    )
    return jnp.transpose(tall)


def put_rows(ref, step, ib, value):
    for image in range(ref.shape[0] // SEQ):

        @pl.when(step == image // ib)
        def _(image=image):
            first = image % ib * SP
            ref[image * SEQ : (image + 1) * SEQ, :] = value[first : first + SEQ]


def moe_bwd_kernel(
    ib,
    tables,
    g_ref,
    w_ref,
    wr_ref,
    mid_ref,
    second_ref,
    cot_ref,
    prob_ref,
    aux_ref,
    qkv_ref,
    mixed_ref,
    *rest,
):
    table_refs = rest[:tables]
    y_ref, grad_ref, dw_out, dr_ref, dg_ref, dw_ref = rest[tables:]
    step = pl.program_id(0)

    @pl.when(step == 0)
    def _():
        dw_ref[...] = jnp.zeros(dw_ref.shape, WIDE)
        dr_ref[...] = jnp.zeros(dr_ref.shape, WIDE)
        dg_ref[...] = jnp.zeros(dg_ref.shape, WIDE)

    second = second_ref[...].reshape(ib * SP, D)
    upstream = cot_ref[...].astype(WIDE).reshape(ib * SP, D)
    prob = prob_ref[...].reshape(ib * SP, 128)
    aux = aux_ref[...].reshape(ib * SP, 128)
    first_pick = second_pick = back = None
    for j, table in enumerate(table_refs):
        owners = table.shape[0]
        count = owners * CAP
        slot = lax.broadcasted_iota(jnp.int32, (1, count), 1) + j * count
        hot_one = (aux[:, 0:1] == slot).astype(NARROW)
        hot_two = (aux[:, 1:2] == slot).astype(NARROW)
        rows = table[...].reshape(count, 2 * D)
        one = nn(hot_one, rows[:, 0:D])
        two = nn(hot_two, rows[:, 0:D])
        both = nn(hot_one + hot_two, rows[:, D : 2 * D])
        first_pick = one if first_pick is None else first_pick + one
        second_pick = two if second_pick is None else second_pick + two
        back = both if back is None else back + both
    lane = lax.broadcasted_iota(jnp.int32, (1, 128), 1)
    first_hit = (aux[:, 2:3] == lane).astype(WIDE)
    second_hit = (aux[:, 3:4] == lane).astype(WIDE)
    gate_one = jnp.sum(prob * first_hit, -1, keepdims=True)
    gate_two = jnp.sum(prob * second_hit, -1, keepdims=True)
    put_rows(y_ref, step, ib, second + (gate_one * first_pick + gate_two * second_pick))
    gate_one_grad = jnp.sum(upstream * first_pick, -1, keepdims=True)
    gate_two_grad = jnp.sum(upstream * second_pick, -1, keepdims=True)
    prob_grad = gate_one_grad * first_hit + gate_two_grad * second_hit
    logit_grad = (prob * (prob_grad - jnp.sum(prob * prob_grad, -1, keepdims=True))).astype(NARROW)
    unit, inverse = norm_parts(second)
    gain = g_ref[3:4, :]
    moe = (unit * gain).astype(NARROW)
    dr_ref[...] += tn(moe, logit_grad)
    normed_grad = back + nt(logit_grad, wr_ref[...])
    moe_grad, gain_grad = norm_backward(normed_grad, unit, inverse, gain)
    dg_ref[3:4, :] += gain_grad
    mid = mid_ref[...].reshape(ib * SP, D)
    grad, gain_grad = attn_bwd_body(
        mid, upstream + moe_grad, g_ref[1:2, :], qkv_ref, mixed_ref, w_ref, dw_ref, ib
    )
    dg_ref[1:2, :] += gain_grad
    grad_ref[...] = grad.reshape(ib, SP, D)

    @pl.when(step == pl.num_programs(0) - 1)
    def _():
        dw_out[:, : 4 * D] = dw_ref[...].astype(NARROW)
        dw_out[:, 4 * D :] = (dr_ref[...] + gain_columns(dg_ref)).astype(NARROW)


def moe_bwd(gains, w1, wr, mid, second, cot, prob, aux, qkv, mixed, tables, images, ib):
    return pl.pallas_call(
        partial(moe_bwd_kernel, ib, len(tables)),
        grid=(images // ib,),
        in_specs=[
            whole(gains.shape),
            whole(w1.shape),
            whole(wr.shape),
            per_image(ib, SP, D),
            per_image(ib, SP, D),
            per_image(ib, SP, D),
            per_image(ib, SP, 128),
            per_image(ib, SP, 128),
            per_image(ib, SP, 3 * D),
            per_image(ib, SP, D),
            *[whole(t.shape) for t in tables],
        ],
        out_specs=[
            whole((images * SEQ, D)),
            per_image(ib, SP, D),
            whole((D, 4 * D + 128)),
        ],
        out_shape=[
            sds((images * SEQ, D), WIDE),
            sds((images, SP, D), WIDE),
            sds((D, 4 * D + 128), NARROW),
        ],
        scratch_shapes=[
            pltpu.VMEM((D, 128), WIDE),
            pltpu.VMEM((8, D), WIDE),
            pltpu.VMEM((D, 4 * D), WIDE),
        ],
        compiler_params=params(56),
        cost_estimate=cost(60e9, 60e6),
        name="expert_block_backward",
    )(gains, w1, wr, mid, second, cot, prob, aux, qkv, mixed, *tables)


def dense_bwd_kernel(
    ib,
    g_ref,
    w_ref,
    win_ref,
    wout_ref,
    x_ref,
    first_ref,
    grad_ref,
    qkv_ref,
    mixed_ref,
    out_ref,
    dw_out,
    dout_out,
    dg_ref,
    dw_ref,
    din_ref,
    dout_ref,
):
    step = pl.program_id(0)

    @pl.when(step == 0)
    def _():
        dw_ref[...] = jnp.zeros(dw_ref.shape, WIDE)
        din_ref[...] = jnp.zeros(din_ref.shape, WIDE)
        dout_ref[...] = jnp.zeros(dout_ref.shape, WIDE)
        dg_ref[...] = jnp.zeros(dg_ref.shape, WIDE)

    incoming = grad_ref[...].reshape(ib * SP, D)
    first = first_ref[...].reshape(ib * SP, D)
    unit, inverse = norm_parts(first)
    gain = g_ref[2:3, :]
    normed = (unit * gain).astype(NARROW)
    out_grad = incoming.astype(NARROW)
    y_grad = None
    for f in range(FF // 512):
        c = slice(f * 512, (f + 1) * 512)
        win, wout = win_ref[:, c], wout_ref[c, :]
        pre = nn(normed, win)
        hidden_grad = nt(out_grad, wout)
        cdf, bell = normal_parts(pre)
        hidden = (pre * cdf).astype(NARROW)
        pre_grad = ((cdf + pre * (bell * INV_ROOT)) * hidden_grad).astype(NARROW)
        dout_ref[c, :] += tn(hidden, out_grad)
        din_ref[:, c] += tn(normed, pre_grad)
        part = nt(pre_grad, win)
        y_grad = part if y_grad is None else y_grad + part
    ffn_grad, gain_grad = norm_backward(y_grad, unit, inverse, gain)
    dg_ref[2:3, :] += gain_grad
    x = x_ref[...].astype(WIDE).reshape(ib * SP, D)
    grad, gain_grad = attn_bwd_body(
        x, incoming + ffn_grad, g_ref[0:1, :], qkv_ref, mixed_ref, w_ref, dw_ref, ib
    )
    dg_ref[0:1, :] += gain_grad
    put_rows(out_ref, step, ib, grad)

    @pl.when(step == pl.num_programs(0) - 1)
    def _():
        dw_out[:, : 4 * D] = dw_ref[...].astype(NARROW)
        dw_out[:, 4 * D : 8 * D] = din_ref[...].astype(NARROW)
        dw_out[:, 8 * D :] = gain_columns(dg_ref).astype(NARROW)
        dout_out[...] = dout_ref[...].astype(NARROW)


def dense_bwd(gains, w0, win, wout, x, first, grad, qkv, mixed, images, ib):
    return pl.pallas_call(
        partial(dense_bwd_kernel, ib),
        grid=(images // ib,),
        in_specs=[
            whole(gains.shape),
            whole(w0.shape),
            whole(win.shape),
            whole(wout.shape),
            per_image(ib, SP, D),
            per_image(ib, SP, D),
            per_image(ib, SP, D),
            per_image(ib, SP, 3 * D),
            per_image(ib, SP, D),
        ],
        out_specs=[
            whole((images * SEQ, D)),
            whole((D, 8 * D + 128)),
            whole((FF, D)),
        ],
        out_shape=[
            sds((images * SEQ, D), WIDE),
            sds((D, 8 * D + 128), NARROW),
            sds((FF, D), NARROW),
        ],
        scratch_shapes=[
            pltpu.VMEM((8, D), WIDE),
            pltpu.VMEM((D, 4 * D), WIDE),
            pltpu.VMEM((D, FF), WIDE),
            pltpu.VMEM((FF, D), WIDE),
        ],
        compiler_params=params(56),
        cost_estimate=cost(60e9, 60e6),
        name="dense_block_backward",
    )(gains, w0, win, wout, x, first, grad, qkv, mixed)


BLOCK = 512
MESH_ID = pl.DeviceIdType.MESH


def add_rows(out, one, two, rows, step):
    @pl.loop(0, rows // step)
    def _(i):
        r = pl.ds(pl.multiple_of(i * step, step), step)
        out[r, :] = (one[r, :].astype(WIDE) + two[r, :].astype(WIDE)).astype(out.dtype)


def sum_kernel(nz, groups, mats, slices, *refs):
    exp_refs, refs = refs[:mats], refs[mats:]
    dense_refs, peak_ref, refs = refs[:3], refs[3], refs[4:]
    exp_out, dense_outs, peak_out, refs = refs[0], refs[1:4], refs[4], refs[5:]
    own, up, down, refs = refs[0], refs[1], refs[2], refs[3:]
    land, refs = refs[:4], refs[4:]
    dense_own, refs = refs[:4], refs[4:]
    dense_up, refs = refs[:4], refs[4:]
    dense_down, refs = refs[:4], refs[4:]
    (own_sem, up_send, up_recv, down_recv, out_send, sib_send, sib_recv, copy_sem, rs_send, rs_recv) = refs

    z, core, f = lax.axis_index("z"), lax.axis_index("core"), lax.axis_index("fsdp")
    half = nz // 2
    left = z < half
    inner = jnp.where(left, z + 1, z - 1)
    outer = jnp.where(left, z - 1, z + 1)
    has_outer = jnp.logical_and(z > 0, z < nz - 1)
    edge = jnp.logical_not(has_outer)
    center = jnp.logical_or(z == half - 1, z == half)
    away = jnp.logical_not(center)
    outer = jnp.where(has_outer, outer, inner)
    sibling = (z, 1 - core, f)
    members = CORES * groups
    me = core * groups + f

    barrier = pltpu.get_barrier_semaphore()
    pl.semaphore_signal(barrier, inc=1, device_id=(inner, core, f), device_id_type=MESH_ID)

    @pl.when(has_outer)
    def _():
        pl.semaphore_signal(barrier, inc=1, device_id=(outer, core, f), device_id_type=MESH_ID)

    for d in range(1, members):
        there = lax.rem(me + d, members)
        pl.semaphore_signal(
            barrier,
            inc=1,
            device_id=(z, there // groups, lax.rem(there, groups)),
            device_id_type=MESH_ID,
        )

    @pl.when(has_outer)
    def _():
        pl.semaphore_wait(barrier, members + 1)

    @pl.when(edge)
    def _():
        pl.semaphore_wait(barrier, members)

    chunks = mats * slices
    items = chunks + 4

    def piece(n, ref, there):
        if n == 3:
            return ref
        rows = ref.shape[0] // members
        place = (lax.rem(there, groups) * CORES + there // groups) * rows
        return ref.at[pl.ds(pl.multiple_of(place, 16), rows), :]

    def scatter(n, d):
        there = lax.rem(me + d, members)
        source = dense_refs[n] if n < 3 else peak_ref
        return pltpu.make_async_remote_copy(
            src_ref=piece(n, source, there),
            dst_ref=land[n].at[d],
            send_sem=rs_send.at[n, d],
            recv_sem=rs_recv.at[n, d],
            device_id=(z, there // groups, lax.rem(there, groups)),
            device_id_type=MESH_ID,
        )

    for n in (3, 1, 0, 2):
        for d in range(1, members):
            scatter(n, d).start()
    keep = [
        pltpu.make_async_copy(
            piece(n, dense_refs[n] if n < 3 else peak_ref, me), land[n].at[0], rs_recv.at[n, 0]
        )
        for n in range(4)
    ]
    for k in keep:
        k.start()

    def load(t):
        return pltpu.make_async_copy(exp_refs[t // slices].at[t % slices], own.at[t], own_sem.at[t])

    @pl.when(has_outer)
    def _():
        for t in range(chunks):
            load(t).start()

    def bufs(t):
        if t < chunks:
            return own.at[t], up.at[t], down.at[t]
        n = t - chunks
        return dense_own[n], dense_up[n], dense_down[n]

    def send_up(t, source, to_center):
        _, u, dn = bufs(t)
        return pltpu.make_async_remote_copy(
            src_ref=source,
            dst_ref=dn if to_center else u,
            send_sem=up_send.at[t],
            recv_sem=(down_recv if to_center else up_recv).at[t],
            device_id=(inner, core, f),
            device_id_type=MESH_ID,
        )

    def source_at_edge(t):
        return exp_refs[t // slices].at[t % slices] if t < chunks else bufs(t)[0]

    def join(t, out, one, two):
        if t == items - 1:
            out[...] = jnp.maximum(one[...], two[...])
        else:
            add_rows(out, one, two, out.shape[0], 16)

    def reduce_own(n):
        for d in range(members):
            if d == 0:
                keep[n].wait()
            else:
                scatter(n, d).wait_recv()
        if n == 3:
            best = land[n][0]
            for d in range(1, members):
                best = jnp.maximum(best, land[n][d])
            dense_own[n][...] = best
            return

        @pl.loop(0, dense_own[n].shape[0] // 16)
        def _(i):
            r = pl.ds(pl.multiple_of(i * 16, 16), 16)
            total = land[n][0, r, :].astype(WIDE)
            for d in range(1, members):
                total = total + land[n][d, r, :].astype(WIDE)
            dense_own[n][r, :] = total.astype(NARROW)

    def up_from_edge(t, before):
        if before is not None:
            send_up(before, source_at_edge(before), half == 1).wait_send()
        if t >= chunks:
            reduce_own(t - chunks)
        send_up(t, source_at_edge(t), half == 1).start()

    def up_from_inside(t):
        o, u, _ = bufs(t)
        if t >= chunks:
            reduce_own(t - chunks)
        else:
            load(t).wait()
        send_up(t, u, False).wait_recv()
        join(t, o, o, u)

        @pl.when(center)
        def _():
            send_up(t, o, True).start()

        if half > 2:

            @pl.when(away)
            def _():
                send_up(t, o, False).start()

    def results(t):
        if t < chunks:
            return exp_out.at[t, core]
        n = t - chunks
        if n == 3:
            return peak_out
        ref = dense_outs[n]
        rows = ref.shape[0] // CORES
        return ref.at[pl.ds(pl.multiple_of(core * rows, 16), rows), :]

    def to_sibling(t):
        return pltpu.make_async_remote_copy(
            src_ref=bufs(t)[2],
            dst_ref=results(t),
            send_sem=sib_send.at[t],
            recv_sem=sib_recv.at[t],
            device_id=sibling,
            device_id_type=MESH_ID,
        )

    def to_outer(t):
        dn = bufs(t)[2]
        return pltpu.make_async_remote_copy(
            src_ref=dn,
            dst_ref=dn,
            send_sem=out_send.at[t],
            recv_sem=down_recv.at[t],
            device_id=(outer, core, f),
            device_id_type=MESH_ID,
        )

    def keep_result(t):
        return pltpu.make_async_copy(bufs(t)[2], results(t), copy_sem.at[t])

    def go_down(t, at_edge):
        o, _, dn = bufs(t)
        to_outer(t).wait_recv()
        if at_edge:
            if half == 1:
                join(t, dn, source_at_edge(t), dn)
        else:

            @pl.when(center)
            def _():
                join(t, dn, o, dn)

            to_outer(t).start()
        keep_result(t).start()
        if t < items - 1:
            to_sibling(t).start()

    early = min(8, chunks)
    sequence = [*range(early), *range(items - 1, chunks - 1, -1), *range(early, chunks)]

    def run(up, at_edge, lag):
        for i in range(items + lag):
            if i < items:
                up(i)
            if i >= lag:
                go_down(sequence[i - lag], at_edge)

    @pl.when(edge)
    def _():
        run(
            lambda i: up_from_edge(sequence[i], sequence[i - 2] if i >= 2 else None),
            True,
            min(7, items),
        )
        for t in sequence[-2:]:
            send_up(t, source_at_edge(t), half == 1).wait_send()

    if half > 1:

        @pl.when(has_outer)
        def _():
            run(lambda i: up_from_inside(sequence[i]), False, 1)
            for t in range(items):
                send_up(t, bufs(t)[0], False).wait_send()
                to_outer(t).wait_send()

    for n in range(4):
        for d in range(1, members):
            scatter(n, d).wait_send()
    for t in range(items):
        keep_result(t).wait()
        if t < items - 1:
            to_sibling(t).wait()


def sum_all(mats, dense, peaks, nz, groups):
    slices = mats[0].shape[0]
    chunks = len(mats) * slices
    members = CORES * groups
    items = chunks + 4
    any_space = pl.BlockSpec(memory_space=pl.ANY)
    vmem = pl.BlockSpec(memory_space=pltpu.VMEM)
    pieces = [(a.shape[0] // members, a.shape[1]) for a in dense]
    block = pltpu.VMEM((chunks, BLOCK, BLOCK), NARROW)

    def four(lead=()):
        return [pltpu.VMEM((*lead, *p), NARROW) for p in pieces] + [
            pltpu.VMEM((*lead, *peaks.shape), WIDE)
        ]

    dma = pltpu.SemaphoreType.DMA
    return pl.pallas_call(
        partial(sum_kernel, nz, groups, len(mats), slices),
        in_specs=[any_space] * (len(mats) + 3) + [vmem],
        out_specs=[any_space] * 4 + [vmem],
        out_shape=[
            sds((chunks, CORES, BLOCK, BLOCK), NARROW),
            *[sds((CORES * r, c), NARROW) for r, c in pieces],
            sds(peaks.shape, WIDE),
        ],
        scratch_shapes=[
            block,
            block,
            block,
            *four((members,)),
            *four(),
            *four(),
            *four(),
            *[dma((items,)) for _ in range(8)],
            dma((4, members)),
            dma((4, members)),
        ],
        compiler_params=pltpu.CompilerParams(
            vmem_limit_bytes=58 * MIB, collective_id=3, has_side_effects=True
        ),
        name="sums",
    )(*mats, *dense, peaks)


def widen_kernel(early, core_ref, *refs):
    own, other, refs = refs[:early], refs[early : 2 * early], refs[2 * early :]
    late, outs = refs[:-2], refs[-2:]
    c, j = pl.program_id(0), pl.program_id(1)

    def put(side, block):
        for f in range(block.shape[0]):
            s = slice(f * BLOCK, (f + 1) * BLOCK)
            if side == 0:
                outs[0][:, s] = block[f].astype(WIDE)
            else:
                outs[1][s, :] = block[f].astype(WIDE)

    for side in range(2):
        for n in range(side, early, 2):
            for source, here in ((own[n], True), (other[n], False)):

                @pl.when(jnp.logical_and(2 * j + side == n, (c == core_ref[0]) == here))
                def _(source=source):
                    put(side, source)

        @pl.when(2 * j + side >= early)
        def _():
            put(side, late[side])


def widen(core, own, other, late, mine, slices):
    early = len(own)
    late = late.reshape(-1, slices, CORES, BLOCK, BLOCK)
    count = late.shape[0]

    def late_spec(side):
        def where_from(c, j, _):
            return (jnp.clip(2 * j + side - early, 0, count - 1), 0, c, 0, 0)

        return pl.BlockSpec((None, slices, None, BLOCK, BLOCK), where_from)

    return pl.pallas_call(
        partial(widen_kernel, early),
        grid_spec=pltpu.PrefetchScalarGridSpec(
            num_scalar_prefetch=1,
            grid=(CORES, mine),
            in_specs=[whole(a.shape) for a in (*own, *other)] + [late_spec(0), late_spec(1)],
            out_specs=[
                pl.BlockSpec((None, D, FF), lambda c, j, _: (c * mine + j, 0, 0)),
                pl.BlockSpec((None, FF, D), lambda c, j, _: (c * mine + j, 0, 0)),
            ],
        ),
        out_shape=[sds((CORES * mine, D, FF), WIDE), sds((CORES * mine, FF, D), WIDE)],
        compiler_params=params(56),
        name="widen",
    )(core, *own, *other, late, late)


def gather(x):
    return lax.all_gather(x, "fsdp", axis=0, tiled=True)


def images_of(x, images):
    return jnp.pad(x.reshape(images, SEQ, x.shape[-1]), ((0, 0), (0, SP - SEQ), (0, 0)))


def local(
    tokens,
    cotangent,
    routes,
    attn_norm,
    query_w,
    key_w,
    value_w,
    output_w,
    ffn_norm,
    mlp_in,
    mlp_out,
    router_w,
    expert_in,
    expert_out,
    updated_query,
    updated_key,
    clip_threshold,
):
    images = tokens.shape[0] // SEQ
    ib = 2
    groups = lax.axis_size("fsdp")
    core = lax.axis_index("core")
    held = expert_in.shape[0]
    mine = held // CORES
    owners = CORES * groups

    small = jnp.concatenate(
        [
            router_w,
            jnp.transpose(attn_norm),
            jnp.transpose(ffn_norm),
            jnp.zeros((router_w.shape[0], 128 - EXPERTS - 4), NARROW),
        ],
        1,
    )
    w0 = gather(jnp.concatenate([query_w[0], key_w[0], value_w[0], output_w[0], small], 1))
    win = gather(mlp_in)
    wout = gather(mlp_out)
    w1 = gather(jnp.concatenate([query_w[1], key_w[1], value_w[1], output_w[1]], 1))
    w_small = w0[:, 4 * D :]
    wr = jnp.where(jnp.arange(128)[None, :] < EXPERTS, w_small, 0)
    gains = jnp.pad(
        jnp.transpose(w_small[:, EXPERTS : EXPERTS + 4]).astype(WIDE), ((0, 4), (0, 0))
    )

    x = images_of(tokens, images)
    cot = images_of(cotangent, images)
    routes_image = jnp.pad(
        routes.reshape(images, SEQ, 2), ((0, 0), (0, SP - SEQ), (0, 0)), constant_values=-1
    )
    routes_rows = jnp.pad(
        jnp.transpose(routes_image.reshape(-1, 2)), ((0, 6), (0, 0)), constant_values=-1
    )
    slot = jnp.arange(EXPERTS, dtype=jnp.int32)
    place_there, owner = slot // owners, slot % owners
    order = (owner % groups) * held + (owner // groups) * mine + place_there
    order = jnp.broadcast_to(order[:, None], (EXPERTS, 128))
    pos, target = places(order, routes_rows)
    aux = jnp.pad(
        jnp.concatenate(
            [
                jnp.transpose(target[0:2]).astype(jnp.int32).reshape(images, SP, 2),
                routes_image,
            ],
            -1,
        ),
        ((0, 0), (0, 0), (0, 124)),
        constant_values=-1,
    )

    first, qkv0, mixed0, peak0 = dense_attn(x, gains, w0, images, ib)
    mid = ffn(first, gains, win, wout, images, ib)
    second, qkv1, mixed1, peak1, moe, prob = expert_attn(mid, gains, w1, wr, images, ib)
    sent = dispatch(
        pos, order, moe.reshape(-1, D), cot.reshape(-1, D), prob.reshape(-1, 128)
    ).reshape(mine, owners, 2 * CAP, D)

    tables, mats, backs = [], [], []
    for j in range(mine):
        chunk = sent[j]
        if j >= 2:
            chunk, _ = lax.optimization_barrier((chunk, backs[j - 2]))
        rows = lax.all_to_all(chunk, ("core", "fsdp"), split_axis=0, concat_axis=0, tiled=True)
        pick = (core * mine + j).astype(jnp.int32).reshape(1)
        back, d_in, d_out = expert(pick, rows, expert_in, expert_out)
        backs.append(back)
        tables.append(
            lax.all_to_all(back, ("core", "fsdp"), split_axis=0, concat_axis=0, tiled=True)
        )
        mats += [d_in, d_out]
    early = len(mats) * 3 // 8
    mats, ready, others = list(mats), [], []
    for n in range(0, early, 2):
        batch = mats[n : min(n + 2, early)]
        if ready:
            batch, _ = lax.optimization_barrier((batch, ready))
        ready += lax.psum(batch, "z")
    others = [lax.ppermute(mat, "core", [(0, 1), (1, 0)]) for mat in ready]

    y, mid_grad, dw1 = moe_bwd(
        gains, w1, wr, mid, second, cot, prob, aux, qkv1, mixed1, tables, images, ib
    )
    x_grad, dw0, d_wout = dense_bwd(
        gains, w0, win, wout, x, first, mid_grad, qkv0, mixed0, images, ib
    )
    lane = jnp.arange(128)[None, :]
    peaks = jnp.where(lane < 64, jnp.max(peak0, 0), jnp.max(peak1, 0))
    late, t1, t0, t_wout, maxima = sum_all(
        mats[early:], [dw1, dw0, d_wout], peaks, lax.axis_size("z"), groups
    )
    expert_in_grad, expert_out_grad = widen(
        core.astype(jnp.int32).reshape(1), ready, others, late, mine, mats[0].shape[0]
    )

    t1, t0 = t1.astype(WIDE), t0.astype(WIDE)
    t_small = t1[:, 4 * D :] + t0[:, 8 * D :]
    norm_rows = jnp.transpose(t_small[:, EXPERTS : EXPERTS + 4])
    maxima = jnp.stack([maxima[:, 0], maxima[:, 64]])
    factor = clip_threshold / jnp.maximum(maxima, clip_threshold)
    column_scale = jnp.repeat(jnp.sqrt(factor), HEAD, axis=1)

    def both(n):
        return jnp.stack([t0[:, n * D : (n + 1) * D], t1[:, n * D : (n + 1) * D]])

    return (
        y,
        x_grad,
        norm_rows[0:2],
        both(0),
        both(1),
        both(2),
        both(3),
        norm_rows[2:4],
        t0[:, 4 * D : 8 * D],
        t_wout.astype(WIDE),
        t_small[:, :EXPERTS],
        expert_in_grad,
        expert_out_grad,
        updated_query * column_scale[:, None, :],
        updated_key * column_scale[:, None, :],
    )


def solution(mesh):
    replicas, groups = mesh.shape["replica"], mesh.shape["fsdp"]
    inner = Mesh(
        mesh.devices.reshape(replicas // CORES, CORES, groups), ("z", "core", "fsdp")
    )
    split = P(("z", "core", "fsdp"), None)
    second = P(None, "fsdp", None)
    in_specs = (
        split,
        split,
        split,
        P(None, "fsdp"),
        second,
        second,
        second,
        second,
        P(None, "fsdp"),
        P("fsdp", None),
        P("fsdp", None),
        P("fsdp", None),
        P("fsdp", None, None),
        P("fsdp", None, None),
        second,
        second,
        P(),
    )
    out_specs = (
        split,
        split,
        P(None, "fsdp"),
        second,
        second,
        second,
        second,
        P(None, "fsdp"),
        P("fsdp", None),
        P("fsdp", None),
        P("fsdp", None),
        P("fsdp", None, None),
        P("fsdp", None, None),
        second,
        second,
    )
    return jax.shard_map(local, mesh=inner, in_specs=in_specs, out_specs=out_specs, check_vma=False)
```

```python
from functools import partial

import jax
import jax.numpy as jnp
from jax import lax
from jax.experimental import pallas as pl
from jax.experimental.pallas import tpu as pltpu
from jax.sharding import Mesh
from jax.sharding import PartitionSpec as P

D = 512
HEADS = 8
HEAD = 64
FF = 2048
SEQ = 197
SP = 208
CAP = 128
EXPERTS = 32
EPSILON = 1e-06
SCALE = HEAD ** (-0.5)
LOWEST = -1e30
NARROW = jnp.bfloat16
WIDE = jnp.float32
CORES = 2
MIB = 1 << 20


def nn(a, b):
    return lax.dot_general(a, b, (((1,), (0,)), ((), ())), preferred_element_type=WIDE)


def nt(a, b):
    return lax.dot_general(a, b, (((1,), (1,)), ((), ())), preferred_element_type=WIDE)


def tn(a, b):
    return lax.dot_general(a, b, (((0,), (0,)), ((), ())), preferred_element_type=WIDE)


def norm_parts(values):
    centred = values - jnp.mean(values, -1, keepdims=True)
    inverse = lax.rsqrt(jnp.mean(centred * centred, -1, keepdims=True) + EPSILON)
    return centred * inverse, inverse


def norm_backward(incoming, unit, inverse, gain):
    gain_grad = jnp.sum(incoming * unit, 0, keepdims=True)
    scaled = incoming * gain
    centred = (
        scaled
        - jnp.mean(scaled, -1, keepdims=True)
        - unit * jnp.mean(scaled * unit, -1, keepdims=True)
    )
    return inverse * centred, gain_grad


def normal_parts(x):
    z = jnp.abs(x)
    t = 1.0 / (1.0 + (0.3275911 * 0.7071067811865476) * z)
    bell = jnp.exp(-0.5 * (x * x))
    poly = t * (
        0.5 * 0.254829592
        + t
        * (
            0.5 * -0.284496736
            + t * (0.5 * 1.421413741 + t * (0.5 * -1.453152027 + t * (0.5 * 1.061405429)))
        )
    )
    tail = poly * bell
    return jnp.where(x >= 0, 1.0 - tail, tail), bell


INV_ROOT = 0.3989422804014327


def head_masks(dtype):
    lane = lax.broadcasted_iota(jnp.int32, (1, 2 * HEAD), 1)
    low = (lane < HEAD).astype(dtype)
    return (low, (1 - low.astype(WIDE)).astype(dtype))


def attn_fwd_body(x, gain, w_ref, qkv_ref, mixed_ref, peak_ref, ib):
    unit, _ = norm_parts(x)
    normed = (unit * gain).astype(NARROW)
    q = (nn(normed, w_ref[:, 0:D]).astype(NARROW).astype(WIDE) * SCALE).astype(NARROW)
    k = nn(normed, w_ref[:, D : 2 * D]).astype(NARROW)
    v = nn(normed, w_ref[:, 2 * D : 3 * D]).astype(NARROW)
    masks = head_masks(NARROW)
    cols = lax.broadcasted_iota(jnp.int32, (SP, SP), 1)
    rows = lax.broadcasted_iota(jnp.int32, (SP, 1), 0)
    head_row = lax.broadcasted_iota(jnp.int32, (HEADS, 128), 0)
    mixed_all = []
    for i in range(ib):
        peaks = jnp.full((HEADS, 128), LOWEST, WIDE)
        r = slice(i * SP, (i + 1) * SP)
        pairs = []
        for pair in range(HEADS // 2):
            c = slice(pair * 2 * HEAD, (pair + 1) * 2 * HEAD)
            qp, kp, vp = q[r, c], k[r, c], v[r, c]
            acc = None
            for half in range(2):
                s = nt(qp * masks[half], kp)
                s = jnp.where(cols < SEQ, s, LOWEST)
                top = jnp.max(s, -1, keepdims=True)
                e = jnp.exp(s - top)
                p = (e * (1.0 / jnp.sum(e, -1, keepdims=True))).astype(NARROW)
                part = nn(p, vp * masks[half])
                acc = part if acc is None else acc + part
                peak = jnp.max(jnp.where(rows < SEQ, top, LOWEST), 0, keepdims=True)
                peaks = jnp.where(head_row == pair * 2 + half, peak, peaks)
            pairs.append(acc.astype(NARROW))
        mixed_all.append(jnp.concatenate(pairs, 1))
        peak_ref[i] = peaks
    mixed = jnp.concatenate(mixed_all, 0) if ib > 1 else mixed_all[0]
    qkv_ref[...] = jnp.concatenate([q, k, v], 1).reshape(ib, SP, 3 * D)
    mixed_ref[...] = mixed.reshape(ib, SP, D)
    return x + nn(mixed, w_ref[:, 3 * D : 4 * D])


def dense_attn_kernel(ib, x_ref, g_ref, w_ref, y_ref, qkv_ref, mixed_ref, peak_ref):
    x = x_ref[...].astype(WIDE).reshape(ib * SP, D)
    y = attn_fwd_body(x, g_ref[0:1, :], w_ref, qkv_ref, mixed_ref, peak_ref, ib)
    y_ref[...] = y.reshape(ib, SP, D)


def ffn_kernel(ib, x_ref, g_ref, win_ref, wout_ref, y_ref):
    x = x_ref[...].reshape(ib * SP, D)
    unit, _ = norm_parts(x)
    normed = (unit * g_ref[2:3, :]).astype(NARROW)
    acc = x
    for f in range(FF // 512):
        c = slice(f * 512, (f + 1) * 512)
        pre = nn(normed, win_ref[:, c])
        cdf, _ = normal_parts(pre)
        acc = acc + nn((pre * cdf).astype(NARROW), wout_ref[c, :])
    y_ref[...] = acc.reshape(ib, SP, D)


def expert_attn_kernel(
    ib, x_ref, g_ref, w_ref, wr_ref, y_ref, qkv_ref, mixed_ref, peak_ref, moe_ref, prob_ref
):
    x = x_ref[...].reshape(ib * SP, D)
    y = attn_fwd_body(x, g_ref[1:2, :], w_ref, qkv_ref, mixed_ref, peak_ref, ib)
    y_ref[...] = y.reshape(ib, SP, D)
    unit, _ = norm_parts(y)
    moe = (unit * g_ref[3:4, :]).astype(NARROW)
    moe_ref[...] = moe.reshape(ib, SP, D)
    lane = lax.broadcasted_iota(jnp.int32, (1, 128), 1)
    logits = jnp.where(lane < EXPERTS, nn(moe, wr_ref[...]), LOWEST)
    e = jnp.exp(logits - jnp.max(logits, -1, keepdims=True))
    prob_ref[...] = (e / jnp.sum(e, -1, keepdims=True)).reshape(ib, SP, 128)


def whole(shape):
    return pl.BlockSpec(
        shape, lambda *_: (0,) * len(shape), pipeline_mode=pl.Buffered(buffer_count=1)
    )


def per_image(ib, *tail):
    return pl.BlockSpec((ib, *tail), lambda i, *_: (i,) + (0,) * len(tail))


def sds(shape, dtype):
    return jax.ShapeDtypeStruct(shape, dtype)


def cost(flops, moved):
    return pl.CostEstimate(flops=int(flops), bytes_accessed=int(moved), transcendentals=0)


def params(mib):
    return pltpu.CompilerParams(vmem_limit_bytes=mib * MIB)


def dense_attn(x, gains, w0, images, ib):
    return pl.pallas_call(
        partial(dense_attn_kernel, ib),
        grid=(images // ib,),
        in_specs=[per_image(ib, SP, D), whole(gains.shape), whole(w0.shape)],
        out_specs=[
            per_image(ib, SP, D),
            per_image(ib, SP, 3 * D),
            per_image(ib, SP, D),
            per_image(ib, HEADS, 128),
        ],
        out_shape=[
            sds((images, SP, D), WIDE),
            sds((images, SP, 3 * D), NARROW),
            sds((images, SP, D), NARROW),
            sds((images, HEADS, 128), WIDE),
        ],
        compiler_params=params(48),
        name="dense_attention",
    )(x, gains, w0)


def ffn(x, gains, win, wout, images, ib):
    return pl.pallas_call(
        partial(ffn_kernel, ib),
        grid=(images // ib,),
        in_specs=[per_image(ib, SP, D), whole(gains.shape), whole(win.shape), whole(wout.shape)],
        out_specs=per_image(ib, SP, D),
        out_shape=sds((images, SP, D), WIDE),
        compiler_params=params(48),
        name="feed_forward",
    )(x, gains, win, wout)


def expert_attn(x, gains, w1, wr, images, ib):
    return pl.pallas_call(
        partial(expert_attn_kernel, ib),
        grid=(images // ib,),
        in_specs=[per_image(ib, SP, D), whole(gains.shape), whole(w1.shape), whole(wr.shape)],
        out_specs=[
            per_image(ib, SP, D),
            per_image(ib, SP, 3 * D),
            per_image(ib, SP, D),
            per_image(ib, HEADS, 128),
            per_image(ib, SP, D),
            per_image(ib, SP, 128),
        ],
        out_shape=[
            sds((images, SP, D), WIDE),
            sds((images, SP, 3 * D), NARROW),
            sds((images, SP, D), NARROW),
            sds((images, HEADS, 128), WIDE),
            sds((images, SP, D), NARROW),
            sds((images, SP, 128), WIDE),
        ],
        compiler_params=params(48),
        name="expert_attention",
    )(x, gains, w1, wr)


def places_kernel(order_ref, routes_ref, pos_ref, target_ref):
    tokens = routes_ref.shape[1]
    order = order_ref[:, 0:1]
    chunk = 128
    strict = (
        lax.broadcasted_iota(jnp.int32, (chunk, chunk), 0)
        < lax.broadcasted_iota(jnp.int32, (chunk, chunk), 1)
    ).astype(NARROW)
    slot_row = lax.broadcasted_iota(jnp.int32, (EXPERTS, 1), 0).astype(WIDE) * CAP
    base = jnp.zeros((EXPERTS, 1), WIDE)
    for c in range(tokens // chunk):
        pos_ref[:, c * chunk : (c + 1) * chunk] = jnp.full((EXPERTS, chunk), -1.0, WIDE)
    target_ref[...] = jnp.zeros(target_ref.shape, WIDE)
    for k in range(2):
        for c in range(tokens // chunk):
            s = slice(c * chunk, (c + 1) * chunk)
            hit = (order == routes_ref[k : k + 1, s]).astype(WIDE)
            place = base + nn(hit.astype(NARROW), strict)
            base = base + jnp.sum(hit, -1, keepdims=True)
            pos_ref[:, s] = jnp.where(hit > 0, place, pos_ref[:, s])
            slot = jnp.where(place < CAP, slot_row + place, 2.0 * EXPERTS * CAP)
            found = jnp.sum(hit * slot, 0, keepdims=True)
            real = jnp.sum(hit, 0, keepdims=True)
            target_ref[k : k + 1, s] = jnp.where(real > 0, found, 2.0 * EXPERTS * CAP)


def places(order, routes_rows):
    tokens = routes_rows.shape[1]
    return pl.pallas_call(
        places_kernel,
        in_specs=[pl.BlockSpec(memory_space=pltpu.VMEM)] * 2,
        out_specs=[pl.BlockSpec(memory_space=pltpu.VMEM)] * 2,
        out_shape=[sds((EXPERTS, tokens), WIDE), sds((8, tokens), WIDE)],
        name="places",
    )(order, routes_rows)


GROUP = 4


def dispatch_kernel(pos_ref, order_ref, moe_ref, cot_ref, prob_ref, out_ref, parts_ref):
    step = pl.program_id(0)

    @pl.when(step == 0)
    def _():
        prob = prob_ref[...]
        high = prob.astype(NARROW)
        rest = prob - high.astype(WIDE)
        middle = rest.astype(NARROW)
        parts_ref[:, 0:128] = high
        parts_ref[:, 128:256] = middle
        parts_ref[:, 256:384] = (rest - middle.astype(WIDE)).astype(NARROW)

    slot = lax.broadcasted_iota(jnp.int32, (CAP, 1), 0).astype(WIDE)
    lane = lax.broadcasted_iota(jnp.int32, (1, 128), 1)
    hot = jnp.concatenate(
        [(pos_ref[g : g + 1, :] == slot).astype(NARROW) for g in range(GROUP)], 0
    )
    rows = nn(hot, moe_ref[...]).astype(NARROW)
    grads = nn(hot, cot_ref[...])
    parts = nn(hot, parts_ref[...])
    gates = parts[:, 0:128] + parts[:, 128:256] + parts[:, 256:384]
    for g in range(GROUP):
        s = slice(g * CAP, (g + 1) * CAP)
        expert = order_ref[g : g + 1, 0:1]
        gate = jnp.sum(jnp.where(lane == expert, gates[s], 0.0), -1, keepdims=True)
        out_ref[g, 0:CAP, :] = rows[s]
        out_ref[g, CAP : 2 * CAP, :] = (gate * grads[s]).astype(NARROW)


def dispatch(pos, order, moe, cot, prob):
    tokens = moe.shape[0]
    groups = EXPERTS // GROUP
    return pl.pallas_call(
        dispatch_kernel,
        grid=(groups,),
        in_specs=[
            pl.BlockSpec((None, GROUP, tokens), lambda i: (i, 0, 0)),
            pl.BlockSpec((None, GROUP, 128), lambda i: (i, 0, 0)),
            whole(moe.shape),
            whole(cot.shape),
            whole(prob.shape),
        ],
        out_specs=pl.BlockSpec((GROUP, 2 * CAP, D), lambda i: (i, 0, 0)),
        out_shape=sds((EXPERTS, 2 * CAP, D), NARROW),
        scratch_shapes=[pltpu.VMEM((tokens, 384), NARROW)],
        compiler_params=params(48),
        name="dispatch",
    )(pos.reshape(groups, GROUP, tokens), order.reshape(groups, GROUP, 128), moe, cot, prob)


def expert_kernel(pick, rows_ref, win_ref, wout_ref, back_ref, din_ref, dout_ref, res, sgr):
    f = pl.program_id(0)
    senders = rows_ref.shape[0]
    part = min(senders, 8)
    count = part * CAP
    win, wout = win_ref[...], wout_ref[...]
    d_in = d_out = None
    for first in range(0, senders, part):
        slots = rows_ref[first : first + part, 0:CAP, :].reshape(count, D)
        grads = rows_ref[first : first + part, CAP : 2 * CAP, :].reshape(count, D)
        r = slice(first * CAP, (first + part) * CAP)
        pre = nn(slots, win)
        hidden_grad = nt(grads, wout)
        cdf, bell = normal_parts(pre)
        hidden = (pre * cdf).astype(NARROW)
        pre_grad = ((cdf + pre * (bell * INV_ROOT)) * hidden_grad).astype(NARROW)
        result = nn(hidden, wout)
        slot_grad = nt(pre_grad, win)
        in_part, out_part = tn(slots, pre_grad), tn(hidden, grads)
        d_in = in_part if d_in is None else d_in + in_part
        d_out = out_part if d_out is None else d_out + out_part

        @pl.when(f == 0)
        def _(r=r, result=result, slot_grad=slot_grad):
            res[r, :] = result
            sgr[r, :] = slot_grad

        @pl.when(f > 0)
        def _(r=r, result=result, slot_grad=slot_grad):
            res[r, :] += result
            sgr[r, :] += slot_grad

    din_ref[...] = d_in.astype(NARROW)
    dout_ref[...] = d_out.astype(NARROW)

    @pl.when(f == pl.num_programs(0) - 1)
    def _():
        back_ref[:, :, 0:D] = res[...].astype(NARROW).reshape(senders, CAP, D)
        back_ref[:, :, D : 2 * D] = sgr[...].astype(NARROW).reshape(senders, CAP, D)


def expert(pick, rows, win, wout):
    senders = rows.shape[0]
    wide = 512
    return pl.pallas_call(
        expert_kernel,
        grid_spec=pltpu.PrefetchScalarGridSpec(
            num_scalar_prefetch=1,
            grid=(FF // wide,),
            in_specs=[
                whole(rows.shape),
                pl.BlockSpec((None, D, wide), lambda f, p: (p[0], 0, f)),
                pl.BlockSpec((None, wide, D), lambda f, p: (p[0], f, 0)),
            ],
            out_specs=[
                whole((senders, CAP, 2 * D)),
                pl.BlockSpec((None, D, wide), lambda f, p: (f, 0, 0)),
                pl.BlockSpec((None, wide, D), lambda f, p: (f, 0, 0)),
            ],
            scratch_shapes=[
                pltpu.VMEM((senders * CAP, D), WIDE),
                pltpu.VMEM((senders * CAP, D), WIDE),
            ],
        ),
        out_shape=[
            sds((senders, CAP, 2 * D), NARROW),
            sds((FF // wide, D, wide), NARROW),
            sds((FF // wide, wide, D), NARROW),
        ],
        compiler_params=params(56),
        cost_estimate=cost(5e9, 1),
        name="one_expert",
    )(pick, rows, win, wout)


def attn_bwd_body(x, incoming, gain, qkv_ref, mixed_ref, w_ref, dw_ref, ib):
    unit, inverse = norm_parts(x)
    normed = (unit * gain).astype(NARROW)
    out_grad = incoming.astype(NARROW)
    mixed = mixed_ref[...].reshape(ib * SP, D)
    dw_ref[:, 3 * D : 4 * D] += tn(mixed, out_grad)
    mixed_grad = nt(out_grad, w_ref[:, 3 * D : 4 * D]).astype(NARROW)
    masks = head_masks(NARROW)
    rows = lax.broadcasted_iota(jnp.int32, (SP, SP), 0)
    dq_all, dk_all, dv_all = [], [], []
    for i in range(ib):
        r = slice(i * SP, (i + 1) * SP)
        dqs, dks, dvs = [], [], []
        for pair in range(HEADS // 2):
            qp = qkv_ref[i, :, pair * 128 : (pair + 1) * 128]
            kp = qkv_ref[i, :, D + pair * 128 : D + (pair + 1) * 128]
            vp = qkv_ref[i, :, 2 * D + pair * 128 : 2 * D + (pair + 1) * 128]
            mp = mixed_grad[r, pair * 128 : (pair + 1) * 128]
            dq = dk = dv = None
            for half in range(2):
                qm, mm, km = qp * masks[half], mp * masks[half], kp * masks[half]
                s = jnp.where(rows < SEQ, nt(kp, qm), LOWEST)
                e = jnp.exp(s - jnp.max(s, 0, keepdims=True))
                soft = e * (1.0 / jnp.sum(e, 0, keepdims=True))
                pg = nt(vp, mm)
                delta = jnp.sum(soft * pg, 0, keepdims=True)
                sg = (soft * (pg - delta)).astype(NARROW)
                v_part = nn(soft.astype(NARROW), mm)
                k_part = nn(sg, qm)
                q_part = tn(sg, km)
                dq = q_part if dq is None else dq + q_part
                dk = k_part if dk is None else dk + k_part
                dv = v_part if dv is None else dv + v_part
            dqs.append((dq * SCALE).astype(NARROW))
            dks.append(dk.astype(NARROW))
            dvs.append(dv.astype(NARROW))
        dq_all.append(jnp.concatenate(dqs, 1))
        dk_all.append(jnp.concatenate(dks, 1))
        dv_all.append(jnp.concatenate(dvs, 1))
    dqkv = jnp.concatenate(
        [
            jnp.concatenate(a, 0) if ib > 1 else a[0]
            for a in (dq_all, dk_all, dv_all)
        ],
        1,
    )
    dw_ref[:, 0 : 3 * D] += tn(normed, dqkv)
    normed_grad = nt(dqkv, w_ref[:, 0 : 3 * D])
    input_grad, gain_grad = norm_backward(normed_grad, unit, inverse, gain)
    return incoming + input_grad, gain_grad


def gain_columns(dg_ref):
    tall = jnp.concatenate(
        [jnp.zeros((EXPERTS, D), WIDE), dg_ref[...], jnp.zeros((128 - EXPERTS - 8, D), WIDE)], 0
    )
    return jnp.transpose(tall)


def put_rows(ref, step, ib, value):
    for image in range(ref.shape[0] // SEQ):

        @pl.when(step == image // ib)
        def _(image=image):
            first = image % ib * SP
            ref[image * SEQ : (image + 1) * SEQ, :] = value[first : first + SEQ]


def moe_bwd_kernel(
    ib,
    tables,
    g_ref,
    w_ref,
    wr_ref,
    mid_ref,
    second_ref,
    cot_ref,
    prob_ref,
    aux_ref,
    qkv_ref,
    mixed_ref,
    *rest,
):
    table_refs = rest[:tables]
    y_ref, grad_ref, dw_out, dr_ref, dg_ref, dw_ref = rest[tables:]
    step = pl.program_id(0)

    @pl.when(step == 0)
    def _():
        dw_ref[...] = jnp.zeros(dw_ref.shape, WIDE)
        dr_ref[...] = jnp.zeros(dr_ref.shape, WIDE)
        dg_ref[...] = jnp.zeros(dg_ref.shape, WIDE)

    second = second_ref[...].reshape(ib * SP, D)
    upstream = cot_ref[...].astype(WIDE).reshape(ib * SP, D)
    prob = prob_ref[...].reshape(ib * SP, 128)
    aux = aux_ref[...].reshape(ib * SP, 128)
    first_pick = second_pick = back = None
    for j, table in enumerate(table_refs):
        owners = table.shape[0]
        count = owners * CAP
        slot = lax.broadcasted_iota(jnp.int32, (1, count), 1) + j * count
        hot_one = (aux[:, 0:1] == slot).astype(NARROW)
        hot_two = (aux[:, 1:2] == slot).astype(NARROW)
        rows = table[...].reshape(count, 2 * D)
        one = nn(hot_one, rows[:, 0:D])
        two = nn(hot_two, rows[:, 0:D])
        both = nn(hot_one + hot_two, rows[:, D : 2 * D])
        first_pick = one if first_pick is None else first_pick + one
        second_pick = two if second_pick is None else second_pick + two
        back = both if back is None else back + both
    lane = lax.broadcasted_iota(jnp.int32, (1, 128), 1)
    first_hit = (aux[:, 2:3] == lane).astype(WIDE)
    second_hit = (aux[:, 3:4] == lane).astype(WIDE)
    gate_one = jnp.sum(prob * first_hit, -1, keepdims=True)
    gate_two = jnp.sum(prob * second_hit, -1, keepdims=True)
    put_rows(y_ref, step, ib, second + (gate_one * first_pick + gate_two * second_pick))
    gate_one_grad = jnp.sum(upstream * first_pick, -1, keepdims=True)
    gate_two_grad = jnp.sum(upstream * second_pick, -1, keepdims=True)
    prob_grad = gate_one_grad * first_hit + gate_two_grad * second_hit
    logit_grad = (prob * (prob_grad - jnp.sum(prob * prob_grad, -1, keepdims=True))).astype(NARROW)
    unit, inverse = norm_parts(second)
    gain = g_ref[3:4, :]
    moe = (unit * gain).astype(NARROW)
    dr_ref[...] += tn(moe, logit_grad)
    normed_grad = back + nt(logit_grad, wr_ref[...])
    moe_grad, gain_grad = norm_backward(normed_grad, unit, inverse, gain)
    dg_ref[3:4, :] += gain_grad
    mid = mid_ref[...].reshape(ib * SP, D)
    grad, gain_grad = attn_bwd_body(
        mid, upstream + moe_grad, g_ref[1:2, :], qkv_ref, mixed_ref, w_ref, dw_ref, ib
    )
    dg_ref[1:2, :] += gain_grad
    grad_ref[...] = grad.reshape(ib, SP, D)

    @pl.when(step == pl.num_programs(0) - 1)
    def _():
        dw_out[:, : 4 * D] = dw_ref[...].astype(NARROW)
        dw_out[:, 4 * D :] = (dr_ref[...] + gain_columns(dg_ref)).astype(NARROW)


def moe_bwd(gains, w1, wr, mid, second, cot, prob, aux, qkv, mixed, tables, images, ib):
    return pl.pallas_call(
        partial(moe_bwd_kernel, ib, len(tables)),
        grid=(images // ib,),
        in_specs=[
            whole(gains.shape),
            whole(w1.shape),
            whole(wr.shape),
            per_image(ib, SP, D),
            per_image(ib, SP, D),
            per_image(ib, SP, D),
            per_image(ib, SP, 128),
            per_image(ib, SP, 128),
            per_image(ib, SP, 3 * D),
            per_image(ib, SP, D),
            *[whole(t.shape) for t in tables],
        ],
        out_specs=[
            whole((images * SEQ, D)),
            per_image(ib, SP, D),
            whole((D, 4 * D + 128)),
        ],
        out_shape=[
            sds((images * SEQ, D), WIDE),
            sds((images, SP, D), WIDE),
            sds((D, 4 * D + 128), NARROW),
        ],
        scratch_shapes=[
            pltpu.VMEM((D, 128), WIDE),
            pltpu.VMEM((8, D), WIDE),
            pltpu.VMEM((D, 4 * D), WIDE),
        ],
        compiler_params=params(56),
        cost_estimate=cost(1e6, 1),
        name="expert_block_backward",
    )(gains, w1, wr, mid, second, cot, prob, aux, qkv, mixed, *tables)


def dense_bwd_kernel(
    ib,
    g_ref,
    w_ref,
    win_ref,
    wout_ref,
    x_ref,
    first_ref,
    grad_ref,
    qkv_ref,
    mixed_ref,
    out_ref,
    dw_out,
    dout_out,
    dg_ref,
    dw_ref,
    din_ref,
    dout_ref,
):
    step = pl.program_id(0)

    @pl.when(step == 0)
    def _():
        dw_ref[...] = jnp.zeros(dw_ref.shape, WIDE)
        din_ref[...] = jnp.zeros(din_ref.shape, WIDE)
        dout_ref[...] = jnp.zeros(dout_ref.shape, WIDE)
        dg_ref[...] = jnp.zeros(dg_ref.shape, WIDE)

    incoming = grad_ref[...].reshape(ib * SP, D)
    first = first_ref[...].reshape(ib * SP, D)
    unit, inverse = norm_parts(first)
    gain = g_ref[2:3, :]
    normed = (unit * gain).astype(NARROW)
    out_grad = incoming.astype(NARROW)
    y_grad = None
    for f in range(FF // 512):
        c = slice(f * 512, (f + 1) * 512)
        win, wout = win_ref[:, c], wout_ref[c, :]
        pre = nn(normed, win)
        hidden_grad = nt(out_grad, wout)
        cdf, bell = normal_parts(pre)
        hidden = (pre * cdf).astype(NARROW)
        pre_grad = ((cdf + pre * (bell * INV_ROOT)) * hidden_grad).astype(NARROW)
        dout_ref[c, :] += tn(hidden, out_grad)
        din_ref[:, c] += tn(normed, pre_grad)
        part = nt(pre_grad, win)
        y_grad = part if y_grad is None else y_grad + part
    ffn_grad, gain_grad = norm_backward(y_grad, unit, inverse, gain)
    dg_ref[2:3, :] += gain_grad
    x = x_ref[...].astype(WIDE).reshape(ib * SP, D)
    grad, gain_grad = attn_bwd_body(
        x, incoming + ffn_grad, g_ref[0:1, :], qkv_ref, mixed_ref, w_ref, dw_ref, ib
    )
    dg_ref[0:1, :] += gain_grad
    put_rows(out_ref, step, ib, grad)

    @pl.when(step == pl.num_programs(0) - 1)
    def _():
        dw_out[:, : 4 * D] = dw_ref[...].astype(NARROW)
        dw_out[:, 4 * D : 8 * D] = din_ref[...].astype(NARROW)
        dw_out[:, 8 * D :] = gain_columns(dg_ref).astype(NARROW)
        dout_out[...] = dout_ref[...].astype(NARROW)


def dense_bwd(gains, w0, win, wout, x, first, grad, qkv, mixed, images, ib):
    return pl.pallas_call(
        partial(dense_bwd_kernel, ib),
        grid=(images // ib,),
        in_specs=[
            whole(gains.shape),
            whole(w0.shape),
            whole(win.shape),
            whole(wout.shape),
            per_image(ib, SP, D),
            per_image(ib, SP, D),
            per_image(ib, SP, D),
            per_image(ib, SP, 3 * D),
            per_image(ib, SP, D),
        ],
        out_specs=[
            whole((images * SEQ, D)),
            whole((D, 8 * D + 128)),
            whole((FF, D)),
        ],
        out_shape=[
            sds((images * SEQ, D), WIDE),
            sds((D, 8 * D + 128), NARROW),
            sds((FF, D), NARROW),
        ],
        scratch_shapes=[
            pltpu.VMEM((8, D), WIDE),
            pltpu.VMEM((D, 4 * D), WIDE),
            pltpu.VMEM((D, FF), WIDE),
            pltpu.VMEM((FF, D), WIDE),
        ],
        compiler_params=params(56),
        cost_estimate=cost(1e6, 1),
        name="dense_block_backward",
    )(gains, w0, win, wout, x, first, grad, qkv, mixed)


BLOCK = 512
MESH_ID = pl.DeviceIdType.MESH


def add_rows(out, one, two, rows, step):
    @pl.loop(0, rows // step)
    def _(i):
        r = pl.ds(pl.multiple_of(i * step, step), step)
        out[r, :] = (one[r, :].astype(WIDE) + two[r, :].astype(WIDE)).astype(out.dtype)


def sum_kernel(nz, groups, mats, slices, *refs):
    exp_refs, refs = refs[:mats], refs[mats:]
    dense_refs, peak_ref, refs = refs[:3], refs[3], refs[4:]
    exp_out, dense_outs, peak_out, refs = refs[0], refs[1:4], refs[4], refs[5:]
    own, up, down, refs = refs[0], refs[1], refs[2], refs[3:]
    land, refs = refs[:4], refs[4:]
    dense_own, refs = refs[:4], refs[4:]
    dense_up, refs = refs[:4], refs[4:]
    dense_down, refs = refs[:4], refs[4:]
    (own_sem, up_send, up_recv, down_recv, out_send, sib_send, sib_recv, copy_sem, rs_send, rs_recv) = refs

    z, core, f = lax.axis_index("z"), lax.axis_index("core"), lax.axis_index("fsdp")
    half = nz // 2
    left = z < half
    inner = jnp.where(left, z + 1, z - 1)
    outer = jnp.where(left, z - 1, z + 1)
    has_outer = jnp.logical_and(z > 0, z < nz - 1)
    edge = jnp.logical_not(has_outer)
    center = jnp.logical_or(z == half - 1, z == half)
    away = jnp.logical_not(center)
    outer = jnp.where(has_outer, outer, inner)
    sibling = (z, 1 - core, f)
    members = CORES * groups
    me = core * groups + f

    barrier = pltpu.get_barrier_semaphore()
    pl.semaphore_signal(barrier, inc=1, device_id=(inner, core, f), device_id_type=MESH_ID)

    @pl.when(has_outer)
    def _():
        pl.semaphore_signal(barrier, inc=1, device_id=(outer, core, f), device_id_type=MESH_ID)

    for d in range(1, members):
        there = lax.rem(me + d, members)
        pl.semaphore_signal(
            barrier,
            inc=1,
            device_id=(z, there // groups, lax.rem(there, groups)),
            device_id_type=MESH_ID,
        )

    @pl.when(has_outer)
    def _():
        pl.semaphore_wait(barrier, members + 1)

    @pl.when(edge)
    def _():
        pl.semaphore_wait(barrier, members)

    chunks = mats * slices
    items = chunks + 4

    def piece(n, ref, there):
        if n == 3:
            return ref
        rows = ref.shape[0] // members
        place = (lax.rem(there, groups) * CORES + there // groups) * rows
        return ref.at[pl.ds(pl.multiple_of(place, 16), rows), :]

    def scatter(n, d):
        there = lax.rem(me + d, members)
        source = dense_refs[n] if n < 3 else peak_ref
        return pltpu.make_async_remote_copy(
            src_ref=piece(n, source, there),
            dst_ref=land[n].at[d],
            send_sem=rs_send.at[n, d],
            recv_sem=rs_recv.at[n, d],
            device_id=(z, there // groups, lax.rem(there, groups)),
            device_id_type=MESH_ID,
        )

    for n in (3, 1, 0, 2):
        for d in range(1, members):
            scatter(n, d).start()
    keep = [
        pltpu.make_async_copy(
            piece(n, dense_refs[n] if n < 3 else peak_ref, me), land[n].at[0], rs_recv.at[n, 0]
        )
        for n in range(4)
    ]
    for k in keep:
        k.start()

    def load(t):
        return pltpu.make_async_copy(exp_refs[t // slices].at[t % slices], own.at[t], own_sem.at[t])

    @pl.when(has_outer)
    def _():
        for t in range(chunks):
            load(t).start()

    def bufs(t):
        if t < chunks:
            return own.at[t], up.at[t], down.at[t]
        n = t - chunks
        return dense_own[n], dense_up[n], dense_down[n]

    def send_up(t, source, to_center):
        _, u, dn = bufs(t)
        return pltpu.make_async_remote_copy(
            src_ref=source,
            dst_ref=dn if to_center else u,
            send_sem=up_send.at[t],
            recv_sem=(down_recv if to_center else up_recv).at[t],
            device_id=(inner, core, f),
            device_id_type=MESH_ID,
        )

    def source_at_edge(t):
        return exp_refs[t // slices].at[t % slices] if t < chunks else bufs(t)[0]

    def join(t, out, one, two):
        if t == items - 1:
            out[...] = jnp.maximum(one[...], two[...])
        else:
            add_rows(out, one, two, out.shape[0], 16)

    def reduce_own(n):
        for d in range(members):
            if d == 0:
                keep[n].wait()
            else:
                scatter(n, d).wait_recv()
        if n == 3:
            best = land[n][0]
            for d in range(1, members):
                best = jnp.maximum(best, land[n][d])
            dense_own[n][...] = best
            return

        @pl.loop(0, dense_own[n].shape[0] // 16)
        def _(i):
            r = pl.ds(pl.multiple_of(i * 16, 16), 16)
            total = land[n][0, r, :].astype(WIDE)
            for d in range(1, members):
                total = total + land[n][d, r, :].astype(WIDE)
            dense_own[n][r, :] = total.astype(NARROW)

    def up_from_edge(t, before):
        if before is not None:
            send_up(before, source_at_edge(before), half == 1).wait_send()
        if t >= chunks:
            reduce_own(t - chunks)
        send_up(t, source_at_edge(t), half == 1).start()

    def up_from_inside(t):
        o, u, _ = bufs(t)
        if t >= chunks:
            reduce_own(t - chunks)
        else:
            load(t).wait()
        send_up(t, u, False).wait_recv()
        join(t, o, o, u)

        @pl.when(center)
        def _():
            send_up(t, o, True).start()

        if half > 2:

            @pl.when(away)
            def _():
                send_up(t, o, False).start()

    def results(t):
        if t < chunks:
            return exp_out.at[t, core]
        n = t - chunks
        if n == 3:
            return peak_out
        ref = dense_outs[n]
        rows = ref.shape[0] // CORES
        return ref.at[pl.ds(pl.multiple_of(core * rows, 16), rows), :]

    def to_sibling(t):
        return pltpu.make_async_remote_copy(
            src_ref=bufs(t)[2],
            dst_ref=results(t),
            send_sem=sib_send.at[t],
            recv_sem=sib_recv.at[t],
            device_id=sibling,
            device_id_type=MESH_ID,
        )

    def to_outer(t):
        dn = bufs(t)[2]
        return pltpu.make_async_remote_copy(
            src_ref=dn,
            dst_ref=dn,
            send_sem=out_send.at[t],
            recv_sem=down_recv.at[t],
            device_id=(outer, core, f),
            device_id_type=MESH_ID,
        )

    def keep_result(t):
        return pltpu.make_async_copy(bufs(t)[2], results(t), copy_sem.at[t])

    def go_down(t, at_edge):
        o, _, dn = bufs(t)
        to_outer(t).wait_recv()
        if at_edge:
            if half == 1:
                join(t, dn, source_at_edge(t), dn)
        else:

            @pl.when(center)
            def _():
                join(t, dn, o, dn)

            to_outer(t).start()
        keep_result(t).start()
        if t < items - 1:
            to_sibling(t).start()

    early = min(8, chunks)
    sequence = [*range(early), *range(items - 1, chunks - 1, -1), *range(early, chunks)]

    def run(up, at_edge, lag):
        for i in range(items + lag):
            if i < items:
                up(i)
            if i >= lag:
                go_down(sequence[i - lag], at_edge)

    @pl.when(edge)
    def _():
        run(
            lambda i: up_from_edge(sequence[i], sequence[i - 2] if i >= 2 else None),
            True,
            min(7, items),
        )
        for t in sequence[-2:]:
            send_up(t, source_at_edge(t), half == 1).wait_send()

    if half > 1:

        @pl.when(has_outer)
        def _():
            run(lambda i: up_from_inside(sequence[i]), False, 1)
            for t in range(items):
                send_up(t, bufs(t)[0], False).wait_send()
                to_outer(t).wait_send()

    for n in range(4):
        for d in range(1, members):
            scatter(n, d).wait_send()
    for t in range(items):
        keep_result(t).wait()
        if t < items - 1:
            to_sibling(t).wait()


def sum_all(mats, dense, peaks, nz, groups):
    slices = mats[0].shape[0]
    chunks = len(mats) * slices
    members = CORES * groups
    items = chunks + 4
    any_space = pl.BlockSpec(memory_space=pl.ANY)
    vmem = pl.BlockSpec(memory_space=pltpu.VMEM)
    pieces = [(a.shape[0] // members, a.shape[1]) for a in dense]
    block = pltpu.VMEM((chunks, BLOCK, BLOCK), NARROW)

    def four(lead=()):
        return [pltpu.VMEM((*lead, *p), NARROW) for p in pieces] + [
            pltpu.VMEM((*lead, *peaks.shape), WIDE)
        ]

    dma = pltpu.SemaphoreType.DMA
    return pl.pallas_call(
        partial(sum_kernel, nz, groups, len(mats), slices),
        in_specs=[any_space] * (len(mats) + 3) + [vmem],
        out_specs=[any_space] * 4 + [vmem],
        out_shape=[
            sds((chunks, CORES, BLOCK, BLOCK), NARROW),
            *[sds((CORES * r, c), NARROW) for r, c in pieces],
            sds(peaks.shape, WIDE),
        ],
        scratch_shapes=[
            block,
            block,
            block,
            *four((members,)),
            *four(),
            *four(),
            *four(),
            *[dma((items,)) for _ in range(8)],
            dma((4, members)),
            dma((4, members)),
        ],
        compiler_params=pltpu.CompilerParams(
            vmem_limit_bytes=58 * MIB, collective_id=3, has_side_effects=True
        ),
        name="sums",
    )(*mats, *dense, peaks)


def widen_kernel(early, core_ref, *refs):
    own, other, refs = refs[:early], refs[early : 2 * early], refs[2 * early :]
    late, outs = refs[:-2], refs[-2:]
    c, j = pl.program_id(0), pl.program_id(1)

    def put(side, block):
        for f in range(block.shape[0]):
            s = slice(f * BLOCK, (f + 1) * BLOCK)
            if side == 0:
                outs[0][:, s] = block[f].astype(WIDE)
            else:
                outs[1][s, :] = block[f].astype(WIDE)

    for side in range(2):
        for n in range(side, early, 2):
            for source, here in ((own[n], True), (other[n], False)):

                @pl.when(jnp.logical_and(2 * j + side == n, (c == core_ref[0]) == here))
                def _(source=source):
                    put(side, source)

        @pl.when(2 * j + side >= early)
        def _():
            put(side, late[side])


def widen(core, own, other, late, mine, slices):
    early = len(own)
    late = late.reshape(-1, slices, CORES, BLOCK, BLOCK)
    count = late.shape[0]

    def late_spec(side):
        def where_from(c, j, _):
            return (jnp.clip(2 * j + side - early, 0, count - 1), 0, c, 0, 0)

        return pl.BlockSpec((None, slices, None, BLOCK, BLOCK), where_from)

    return pl.pallas_call(
        partial(widen_kernel, early),
        grid_spec=pltpu.PrefetchScalarGridSpec(
            num_scalar_prefetch=1,
            grid=(CORES, mine),
            in_specs=[whole(a.shape) for a in (*own, *other)] + [late_spec(0), late_spec(1)],
            out_specs=[
                pl.BlockSpec((None, D, FF), lambda c, j, _: (c * mine + j, 0, 0)),
                pl.BlockSpec((None, FF, D), lambda c, j, _: (c * mine + j, 0, 0)),
            ],
        ),
        out_shape=[sds((CORES * mine, D, FF), WIDE), sds((CORES * mine, FF, D), WIDE)],
        compiler_params=params(56),
        name="widen",
    )(core, *own, *other, late, late)


def gather_kernel(groups, q_ref, k_ref, v_ref, o_ref, small_ref, in_ref, out_ref, *refs):
    w_all, small_all, in_all, out_all, send, recv, pass_send, pass_recv, copy = refs
    z, core, f = lax.axis_index("z"), lax.axis_index("core"), lax.axis_index("fsdp")
    barrier = pltpu.get_barrier_semaphore()
    for d in range(1, groups):
        pl.semaphore_signal(
            barrier, inc=1, device_id=(z, core, lax.rem(f + d, groups)), device_id_type=MESH_ID
        )
    pl.semaphore_signal(barrier, inc=1, device_id=(z, 1 - core, f), device_id_type=MESH_ID)
    pl.semaphore_wait(barrier, groups)

    def rows(count, owner, side):
        half = count // CORES
        return pl.ds(pl.multiple_of(owner * count + side * half, 16), half)

    def item(n):
        if n < 4:
            ref = (q_ref, k_ref, v_ref, o_ref)[n]
            count = ref.shape[1]
            cols = pl.ds(n * D, D)
            return (
                lambda side: ref.at[0, rows(count, 0, side), :],
                lambda owner, side: w_all.at[rows(count, owner, side), cols],
            )
        ref, full = ((small_ref, small_all), (in_ref, in_all), (out_ref, out_all))[n - 4]
        count = ref.shape[0]
        return (
            lambda side: ref.at[rows(count, 0, side), :],
            lambda owner, side: full.at[rows(count, owner, side), :],
        )

    def fetch(n, d):
        source, place = item(n)
        return pltpu.make_async_remote_copy(
            src_ref=source(core),
            dst_ref=place(f, core),
            send_sem=send.at[n, d],
            recv_sem=recv.at[n, d],
            device_id=(z, core, lax.rem(f + d, groups)),
            device_id_type=MESH_ID,
        )

    def hand_on(n, d):
        _, place = item(n)
        there = place(lax.rem(f + groups - d, groups), core)
        return pltpu.make_async_remote_copy(
            src_ref=there,
            dst_ref=there,
            send_sem=pass_send.at[n, d],
            recv_sem=pass_recv.at[n, d],
            device_id=(z, 1 - core, f),
            device_id_type=MESH_ID,
        )

    def keep(n, side):
        source, place = item(n)
        return pltpu.make_async_copy(source(side), place(f, side), copy.at[n, side])

    count = 7
    for n in range(count):
        for d in range(1, groups):
            fetch(n, d).start()
    for n in range(count):
        for side in range(CORES):
            keep(n, side).start()
    for n in range(count):
        for d in range(1, groups):
            fetch(n, d).wait_recv()
            hand_on(n, d).start()
    for n in range(count):
        for side in range(CORES):
            keep(n, side).wait()
        for d in range(1, groups):
            fetch(n, d).wait_send()
            hand_on(n, d).wait()


def gather_dense(query_w, key_w, value_w, output_w, small, mlp_in, mlp_out, groups):
    any_space = pl.BlockSpec(memory_space=pl.ANY)
    dma = pltpu.SemaphoreType.DMA
    return pl.pallas_call(
        partial(gather_kernel, groups),
        in_specs=[any_space] * 7,
        out_specs=[any_space] * 4,
        out_shape=[
            sds((D, 4 * D), NARROW),
            sds((D, 128), NARROW),
            sds((D, FF), NARROW),
            sds((FF, D), NARROW),
        ],
        scratch_shapes=[
            *[dma((7, groups)) for _ in range(4)],
            dma((7, CORES)),
        ],
        compiler_params=pltpu.CompilerParams(
            vmem_limit_bytes=8 * MIB, collective_id=5, has_side_effects=True
        ),
        name="gather_weights",
    )(query_w, key_w, value_w, output_w, small, mlp_in, mlp_out)


def gather(x):
    return lax.all_gather(x, "fsdp", axis=0, tiled=True)


def images_of(x, images):
    return jnp.pad(x.reshape(images, SEQ, x.shape[-1]), ((0, 0), (0, SP - SEQ), (0, 0)))


def local(
    tokens,
    cotangent,
    routes,
    attn_norm,
    query_w,
    key_w,
    value_w,
    output_w,
    ffn_norm,
    mlp_in,
    mlp_out,
    router_w,
    expert_in,
    expert_out,
    updated_query,
    updated_key,
    clip_threshold,
):
    images = tokens.shape[0] // SEQ
    ib = 2
    groups = lax.axis_size("fsdp")
    core = lax.axis_index("core")
    held = expert_in.shape[0]
    mine = held // CORES
    owners = CORES * groups

    small = jnp.concatenate(
        [
            router_w,
            jnp.transpose(attn_norm),
            jnp.transpose(ffn_norm),
            jnp.zeros((router_w.shape[0], 128 - EXPERTS - 4), NARROW),
        ],
        1,
    )
    w0, w_small, win, wout = gather_dense(
        query_w, key_w, value_w, output_w, small, mlp_in, mlp_out, groups
    )
    w1 = gather(jnp.concatenate([query_w[1], key_w[1], value_w[1], output_w[1]], 1))
    wr = jnp.where(jnp.arange(128)[None, :] < EXPERTS, w_small, 0)
    gains = jnp.pad(
        jnp.transpose(w_small[:, EXPERTS : EXPERTS + 4]).astype(WIDE), ((0, 4), (0, 0))
    )

    x = images_of(tokens, images)
    cot = images_of(cotangent, images)
    routes_image = jnp.pad(
        routes.reshape(images, SEQ, 2), ((0, 0), (0, SP - SEQ), (0, 0)), constant_values=-1
    )
    routes_rows = jnp.pad(
        jnp.transpose(routes_image.reshape(-1, 2)), ((0, 6), (0, 0)), constant_values=-1
    )
    slot = jnp.arange(EXPERTS, dtype=jnp.int32)
    place_there, owner = slot // owners, slot % owners
    order = (owner % groups) * held + (owner // groups) * mine + place_there
    order = jnp.broadcast_to(order[:, None], (EXPERTS, 128))
    pos, target = places(order, routes_rows)
    aux = jnp.pad(
        jnp.concatenate(
            [
                jnp.transpose(target[0:2]).astype(jnp.int32).reshape(images, SP, 2),
                routes_image,
            ],
            -1,
        ),
        ((0, 0), (0, 0), (0, 124)),
        constant_values=-1,
    )

    first, qkv0, mixed0, peak0 = dense_attn(x, gains, w0, images, ib)
    mid = ffn(first, gains, win, wout, images, ib)
    second, qkv1, mixed1, peak1, moe, prob = expert_attn(mid, gains, w1, wr, images, ib)
    sent = dispatch(
        pos, order, moe.reshape(-1, D), cot.reshape(-1, D), prob.reshape(-1, 128)
    ).reshape(mine, owners, 2 * CAP, D)

    tables, mats, backs = [], [], []
    for j in range(mine):
        chunk = sent[j]
        if j >= 2:
            chunk, _ = lax.optimization_barrier((chunk, backs[j - 2]))
        rows = lax.all_to_all(chunk, ("core", "fsdp"), split_axis=0, concat_axis=0, tiled=True)
        pick = (core * mine + j).astype(jnp.int32).reshape(1)
        back, d_in, d_out = expert(pick, rows, expert_in, expert_out)
        backs.append(back)
        tables.append(
            lax.all_to_all(back, ("core", "fsdp"), split_axis=0, concat_axis=0, tiled=True)
        )
        mats += [d_in, d_out]
    early = len(mats) // 2
    ready = lax.psum(mats[:early], "z")
    others = [lax.ppermute(mat, "core", [(0, 1), (1, 0)]) for mat in ready]

    y, mid_grad, dw1 = moe_bwd(
        gains, w1, wr, mid, second, cot, prob, aux, qkv1, mixed1, tables, images, ib
    )
    x_grad, dw0, d_wout = dense_bwd(
        gains, w0, win, wout, x, first, mid_grad, qkv0, mixed0, images, ib
    )
    lane = jnp.arange(128)[None, :]
    peaks = jnp.where(lane < 64, jnp.max(peak0, 0), jnp.max(peak1, 0))
    late, t1, t0, t_wout, maxima = sum_all(
        mats[early:], [dw1, dw0, d_wout], peaks, lax.axis_size("z"), groups
    )
    expert_in_grad, expert_out_grad = widen(
        core.astype(jnp.int32).reshape(1), ready, others, late, mine, mats[0].shape[0]
    )

    t1, t0 = t1.astype(WIDE), t0.astype(WIDE)
    t_small = t1[:, 4 * D :] + t0[:, 8 * D :]
    norm_rows = jnp.transpose(t_small[:, EXPERTS : EXPERTS + 4])
    maxima = jnp.stack([maxima[:, 0], maxima[:, 64]])
    factor = clip_threshold / jnp.maximum(maxima, clip_threshold)
    column_scale = jnp.repeat(jnp.sqrt(factor), HEAD, axis=1)

    def both(n):
        return jnp.stack([t0[:, n * D : (n + 1) * D], t1[:, n * D : (n + 1) * D]])

    return (
        y,
        x_grad,
        norm_rows[0:2],
        both(0),
        both(1),
        both(2),
        both(3),
        norm_rows[2:4],
        t0[:, 4 * D : 8 * D],
        t_wout.astype(WIDE),
        t_small[:, :EXPERTS],
        expert_in_grad,
        expert_out_grad,
        updated_query * column_scale[:, None, :],
        updated_key * column_scale[:, None, :],
    )


def solution(mesh):
    replicas, groups = mesh.shape["replica"], mesh.shape["fsdp"]
    inner = Mesh(
        mesh.devices.reshape(replicas // CORES, CORES, groups), ("z", "core", "fsdp")
    )
    split = P(("z", "core", "fsdp"), None)
    second = P(None, "fsdp", None)
    in_specs = (
        split,
        split,
        split,
        P(None, "fsdp"),
        second,
        second,
        second,
        second,
        P(None, "fsdp"),
        P("fsdp", None),
        P("fsdp", None),
        P("fsdp", None),
        P("fsdp", None, None),
        P("fsdp", None, None),
        second,
        second,
        P(),
    )
    out_specs = (
        split,
        split,
        P(None, "fsdp"),
        second,
        second,
        second,
        second,
        P(None, "fsdp"),
        P("fsdp", None),
        P("fsdp", None),
        P("fsdp", None),
        P("fsdp", None, None),
        P("fsdp", None, None),
        second,
        second,
    )
    return jax.shard_map(local, mesh=inner, in_specs=in_specs, out_specs=out_specs, check_vma=False)
```

```python
from functools import partial

import jax
import jax.numpy as jnp
from jax import lax
from jax.experimental import pallas as pl
from jax.experimental.pallas import tpu as pltpu
from jax.sharding import Mesh
from jax.sharding import PartitionSpec as P

D = 512
HEADS = 8
HEAD = 64
FF = 2048
SEQ = 197
SP = 208
CAP = 128
EXPERTS = 32
EPSILON = 1e-06
SCALE = HEAD ** (-0.5)
LOWEST = -1e30
NARROW = jnp.bfloat16
WIDE = jnp.float32
CORES = 2
MIB = 1 << 20


def nn(a, b):
    return lax.dot_general(a, b, (((1,), (0,)), ((), ())), preferred_element_type=WIDE)


def nt(a, b):
    return lax.dot_general(a, b, (((1,), (1,)), ((), ())), preferred_element_type=WIDE)


def tn(a, b):
    return lax.dot_general(a, b, (((0,), (0,)), ((), ())), preferred_element_type=WIDE)


def norm_parts(values):
    centred = values - jnp.mean(values, -1, keepdims=True)
    inverse = lax.rsqrt(jnp.mean(centred * centred, -1, keepdims=True) + EPSILON)
    return centred * inverse, inverse


def norm_backward(incoming, unit, inverse, gain):
    gain_grad = jnp.sum(incoming * unit, 0, keepdims=True)
    scaled = incoming * gain
    centred = (
        scaled
        - jnp.mean(scaled, -1, keepdims=True)
        - unit * jnp.mean(scaled * unit, -1, keepdims=True)
    )
    return inverse * centred, gain_grad


def normal_parts(x):
    z = jnp.abs(x)
    t = 1.0 / (1.0 + (0.3275911 * 0.7071067811865476) * z)
    bell = jnp.exp(-0.5 * (x * x))
    poly = t * (
        0.5 * 0.254829592
        + t
        * (
            0.5 * -0.284496736
            + t * (0.5 * 1.421413741 + t * (0.5 * -1.453152027 + t * (0.5 * 1.061405429)))
        )
    )
    tail = poly * bell
    return jnp.where(x >= 0, 1.0 - tail, tail), bell


INV_ROOT = 0.3989422804014327


def head_masks(dtype):
    lane = lax.broadcasted_iota(jnp.int32, (1, 2 * HEAD), 1)
    low = (lane < HEAD).astype(dtype)
    return (low, (1 - low.astype(WIDE)).astype(dtype))


def attn_fwd_body(x, gain, w_ref, qkv_ref, mixed_ref, peak_ref, ib):
    unit, _ = norm_parts(x)
    normed = (unit * gain).astype(NARROW)
    q = (nn(normed, w_ref[:, 0:D]).astype(NARROW).astype(WIDE) * SCALE).astype(NARROW)
    k = nn(normed, w_ref[:, D : 2 * D]).astype(NARROW)
    v = nn(normed, w_ref[:, 2 * D : 3 * D]).astype(NARROW)
    masks = head_masks(NARROW)
    cols = lax.broadcasted_iota(jnp.int32, (SP, SP), 1)
    rows = lax.broadcasted_iota(jnp.int32, (SP, 1), 0)
    head_row = lax.broadcasted_iota(jnp.int32, (HEADS, 128), 0)
    mixed_all = []
    for i in range(ib):
        peaks = jnp.full((HEADS, 128), LOWEST, WIDE)
        r = slice(i * SP, (i + 1) * SP)
        pairs = []
        for pair in range(HEADS // 2):
            c = slice(pair * 2 * HEAD, (pair + 1) * 2 * HEAD)
            qp, kp, vp = q[r, c], k[r, c], v[r, c]
            acc = None
            for half in range(2):
                s = nt(qp * masks[half], kp)
                s = jnp.where(cols < SEQ, s, LOWEST)
                top = jnp.max(s, -1, keepdims=True)
                e = jnp.exp(s - top)
                p = (e * (1.0 / jnp.sum(e, -1, keepdims=True))).astype(NARROW)
                part = nn(p, vp * masks[half])
                acc = part if acc is None else acc + part
                peak = jnp.max(jnp.where(rows < SEQ, top, LOWEST), 0, keepdims=True)
                peaks = jnp.where(head_row == pair * 2 + half, peak, peaks)
            pairs.append(acc.astype(NARROW))
        mixed_all.append(jnp.concatenate(pairs, 1))
        peak_ref[i] = peaks
    mixed = jnp.concatenate(mixed_all, 0) if ib > 1 else mixed_all[0]
    qkv_ref[...] = jnp.concatenate([q, k, v], 1).reshape(ib, SP, 3 * D)
    mixed_ref[...] = mixed.reshape(ib, SP, D)
    return x + nn(mixed, w_ref[:, 3 * D : 4 * D])


def dense_attn_kernel(ib, x_ref, g_ref, w_ref, y_ref, qkv_ref, mixed_ref, peak_ref):
    x = x_ref[...].astype(WIDE).reshape(ib * SP, D)
    y = attn_fwd_body(x, g_ref[0:1, :], w_ref, qkv_ref, mixed_ref, peak_ref, ib)
    y_ref[...] = y.reshape(ib, SP, D)


def ffn_kernel(ib, x_ref, g_ref, win_ref, wout_ref, y_ref):
    x = x_ref[...].reshape(ib * SP, D)
    unit, _ = norm_parts(x)
    normed = (unit * g_ref[2:3, :]).astype(NARROW)
    acc = x
    for f in range(FF // 512):
        c = slice(f * 512, (f + 1) * 512)
        pre = nn(normed, win_ref[:, c])
        cdf, _ = normal_parts(pre)
        acc = acc + nn((pre * cdf).astype(NARROW), wout_ref[c, :])
    y_ref[...] = acc.reshape(ib, SP, D)


def expert_attn_kernel(
    ib, x_ref, g_ref, w_ref, wr_ref, y_ref, qkv_ref, mixed_ref, peak_ref, moe_ref, prob_ref
):
    x = x_ref[...].reshape(ib * SP, D)
    y = attn_fwd_body(x, g_ref[1:2, :], w_ref, qkv_ref, mixed_ref, peak_ref, ib)
    y_ref[...] = y.reshape(ib, SP, D)
    unit, _ = norm_parts(y)
    moe = (unit * g_ref[3:4, :]).astype(NARROW)
    moe_ref[...] = moe.reshape(ib, SP, D)
    lane = lax.broadcasted_iota(jnp.int32, (1, 128), 1)
    logits = jnp.where(lane < EXPERTS, nn(moe, wr_ref[...]), LOWEST)
    e = jnp.exp(logits - jnp.max(logits, -1, keepdims=True))
    prob_ref[...] = (e / jnp.sum(e, -1, keepdims=True)).reshape(ib, SP, 128)


def whole(shape):
    return pl.BlockSpec(
        shape, lambda *_: (0,) * len(shape), pipeline_mode=pl.Buffered(buffer_count=1)
    )


def per_image(ib, *tail):
    return pl.BlockSpec((ib, *tail), lambda i, *_: (i,) + (0,) * len(tail))


def sds(shape, dtype):
    return jax.ShapeDtypeStruct(shape, dtype)


def cost(flops, moved):
    return pl.CostEstimate(flops=int(flops), bytes_accessed=int(moved), transcendentals=0)


def params(mib):
    return pltpu.CompilerParams(vmem_limit_bytes=mib * MIB)


def dense_attn(x, gains, w0, images, ib):
    return pl.pallas_call(
        partial(dense_attn_kernel, ib),
        grid=(images // ib,),
        in_specs=[per_image(ib, SP, D), whole(gains.shape), whole(w0.shape)],
        out_specs=[
            per_image(ib, SP, D),
            per_image(ib, SP, 3 * D),
            per_image(ib, SP, D),
            per_image(ib, HEADS, 128),
        ],
        out_shape=[
            sds((images, SP, D), WIDE),
            sds((images, SP, 3 * D), NARROW),
            sds((images, SP, D), NARROW),
            sds((images, HEADS, 128), WIDE),
        ],
        compiler_params=params(48),
        name="dense_attention",
    )(x, gains, w0)


def ffn(x, gains, win, wout, images, ib):
    return pl.pallas_call(
        partial(ffn_kernel, ib),
        grid=(images // ib,),
        in_specs=[per_image(ib, SP, D), whole(gains.shape), whole(win.shape), whole(wout.shape)],
        out_specs=per_image(ib, SP, D),
        out_shape=sds((images, SP, D), WIDE),
        compiler_params=params(48),
        name="feed_forward",
    )(x, gains, win, wout)


def expert_attn(x, gains, w1, wr, images, ib):
    return pl.pallas_call(
        partial(expert_attn_kernel, ib),
        grid=(images // ib,),
        in_specs=[per_image(ib, SP, D), whole(gains.shape), whole(w1.shape), whole(wr.shape)],
        out_specs=[
            per_image(ib, SP, D),
            per_image(ib, SP, 3 * D),
            per_image(ib, SP, D),
            per_image(ib, HEADS, 128),
            per_image(ib, SP, D),
            per_image(ib, SP, 128),
        ],
        out_shape=[
            sds((images, SP, D), WIDE),
            sds((images, SP, 3 * D), NARROW),
            sds((images, SP, D), NARROW),
            sds((images, HEADS, 128), WIDE),
            sds((images, SP, D), NARROW),
            sds((images, SP, 128), WIDE),
        ],
        compiler_params=params(48),
        name="expert_attention",
    )(x, gains, w1, wr)


def places_kernel(order_ref, routes_ref, pos_ref, target_ref):
    tokens = routes_ref.shape[1]
    order = order_ref[:, 0:1]
    chunk = 128
    strict = (
        lax.broadcasted_iota(jnp.int32, (chunk, chunk), 0)
        < lax.broadcasted_iota(jnp.int32, (chunk, chunk), 1)
    ).astype(NARROW)
    slot_row = lax.broadcasted_iota(jnp.int32, (EXPERTS, 1), 0).astype(WIDE) * CAP
    base = jnp.zeros((EXPERTS, 1), WIDE)
    for c in range(tokens // chunk):
        pos_ref[:, c * chunk : (c + 1) * chunk] = jnp.full((EXPERTS, chunk), -1.0, WIDE)
    target_ref[...] = jnp.zeros(target_ref.shape, WIDE)
    for k in range(2):
        for c in range(tokens // chunk):
            s = slice(c * chunk, (c + 1) * chunk)
            hit = (order == routes_ref[k : k + 1, s]).astype(WIDE)
            place = base + nn(hit.astype(NARROW), strict)
            base = base + jnp.sum(hit, -1, keepdims=True)
            pos_ref[:, s] = jnp.where(hit > 0, place, pos_ref[:, s])
            slot = jnp.where(place < CAP, slot_row + place, 2.0 * EXPERTS * CAP)
            found = jnp.sum(hit * slot, 0, keepdims=True)
            real = jnp.sum(hit, 0, keepdims=True)
            target_ref[k : k + 1, s] = jnp.where(real > 0, found, 2.0 * EXPERTS * CAP)


def places(order, routes_rows):
    tokens = routes_rows.shape[1]
    return pl.pallas_call(
        places_kernel,
        in_specs=[pl.BlockSpec(memory_space=pltpu.VMEM)] * 2,
        out_specs=[pl.BlockSpec(memory_space=pltpu.VMEM)] * 2,
        out_shape=[sds((EXPERTS, tokens), WIDE), sds((8, tokens), WIDE)],
        name="places",
    )(order, routes_rows)


GROUP = 4


def dispatch_kernel(pos_ref, order_ref, moe_ref, cot_ref, prob_ref, out_ref, parts_ref):
    step = pl.program_id(0)

    @pl.when(step == 0)
    def _():
        prob = prob_ref[...]
        high = prob.astype(NARROW)
        rest = prob - high.astype(WIDE)
        middle = rest.astype(NARROW)
        parts_ref[:, 0:128] = high
        parts_ref[:, 128:256] = middle
        parts_ref[:, 256:384] = (rest - middle.astype(WIDE)).astype(NARROW)

    slot = lax.broadcasted_iota(jnp.int32, (CAP, 1), 0).astype(WIDE)
    lane = lax.broadcasted_iota(jnp.int32, (1, 128), 1)
    hot = jnp.concatenate(
        [(pos_ref[g : g + 1, :] == slot).astype(NARROW) for g in range(GROUP)], 0
    )
    rows = nn(hot, moe_ref[...]).astype(NARROW)
    grads = nn(hot, cot_ref[...])
    parts = nn(hot, parts_ref[...])
    gates = parts[:, 0:128] + parts[:, 128:256] + parts[:, 256:384]
    for g in range(GROUP):
        s = slice(g * CAP, (g + 1) * CAP)
        expert = order_ref[g : g + 1, 0:1]
        gate = jnp.sum(jnp.where(lane == expert, gates[s], 0.0), -1, keepdims=True)
        out_ref[g, 0:CAP, :] = rows[s]
        out_ref[g, CAP : 2 * CAP, :] = (gate * grads[s]).astype(NARROW)


def dispatch(pos, order, moe, cot, prob):
    tokens = moe.shape[0]
    groups = EXPERTS // GROUP
    return pl.pallas_call(
        dispatch_kernel,
        grid=(groups,),
        in_specs=[
            pl.BlockSpec((None, GROUP, tokens), lambda i: (i, 0, 0)),
            pl.BlockSpec((None, GROUP, 128), lambda i: (i, 0, 0)),
            whole(moe.shape),
            whole(cot.shape),
            whole(prob.shape),
        ],
        out_specs=pl.BlockSpec((GROUP, 2 * CAP, D), lambda i: (i, 0, 0)),
        out_shape=sds((EXPERTS, 2 * CAP, D), NARROW),
        scratch_shapes=[pltpu.VMEM((tokens, 384), NARROW)],
        compiler_params=params(48),
        name="dispatch",
    )(pos.reshape(groups, GROUP, tokens), order.reshape(groups, GROUP, 128), moe, cot, prob)


def expert_math(slots, grads, win, wout):
    pre = nn(slots, win)
    hidden_grad = nt(grads, wout)
    cdf, bell = normal_parts(pre)
    hidden = (pre * cdf).astype(NARROW)
    pre_grad = ((cdf + pre * (bell * INV_ROOT)) * hidden_grad).astype(NARROW)
    return nn(hidden, wout), nt(pre_grad, win), tn(slots, pre_grad), tn(hidden, grads)


def expert_kernel(pick, rows_ref, win_ref, wout_ref, back_ref, din_ref, dout_ref, res, sgr):
    f = pl.program_id(0)
    senders = rows_ref.shape[0]
    part = min(senders, 8)
    count = part * CAP
    win, wout = win_ref[...], wout_ref[...]
    d_in = d_out = None
    for first in range(0, senders, part):
        slots = rows_ref[first : first + part, 0:CAP, :].reshape(count, D)
        grads = rows_ref[first : first + part, CAP : 2 * CAP, :].reshape(count, D)
        r = slice(first * CAP, (first + part) * CAP)
        result, slot_grad, in_part, out_part = expert_math(slots, grads, win, wout)
        d_in = in_part if d_in is None else d_in + in_part
        d_out = out_part if d_out is None else d_out + out_part

        @pl.when(f == 0)
        def _(r=r, result=result, slot_grad=slot_grad):
            res[r, :] = result
            sgr[r, :] = slot_grad

        @pl.when(f > 0)
        def _(r=r, result=result, slot_grad=slot_grad):
            res[r, :] += result
            sgr[r, :] += slot_grad

    din_ref[...] = d_in.astype(NARROW)
    dout_ref[...] = d_out.astype(NARROW)

    @pl.when(f == pl.num_programs(0) - 1)
    def _():
        back_ref[:, :, 0:D] = res[...].astype(NARROW).reshape(senders, CAP, D)
        back_ref[:, :, D : 2 * D] = sgr[...].astype(NARROW).reshape(senders, CAP, D)


def expert(pick, rows, win, wout):
    senders = rows.shape[0]
    wide = 512
    return pl.pallas_call(
        expert_kernel,
        grid_spec=pltpu.PrefetchScalarGridSpec(
            num_scalar_prefetch=1,
            grid=(FF // wide,),
            in_specs=[
                whole(rows.shape),
                pl.BlockSpec((None, D, wide), lambda f, p: (p[0], 0, f)),
                pl.BlockSpec((None, wide, D), lambda f, p: (p[0], f, 0)),
            ],
            out_specs=[
                whole((senders, CAP, 2 * D)),
                pl.BlockSpec((None, D, wide), lambda f, p: (f, 0, 0)),
                pl.BlockSpec((None, wide, D), lambda f, p: (f, 0, 0)),
            ],
            scratch_shapes=[
                pltpu.VMEM((senders * CAP, D), WIDE),
                pltpu.VMEM((senders * CAP, D), WIDE),
            ],
        ),
        out_shape=[
            sds((senders, CAP, 2 * D), NARROW),
            sds((FF // wide, D, wide), NARROW),
            sds((FF // wide, wide, D), NARROW),
        ],
        compiler_params=params(56),
        cost_estimate=cost(5e9, 1),
        name="one_expert",
    )(pick, rows, win, wout)


def attn_bwd_body(x, incoming, gain, qkv_ref, mixed_ref, w_ref, dw_ref, ib):
    unit, inverse = norm_parts(x)
    normed = (unit * gain).astype(NARROW)
    out_grad = incoming.astype(NARROW)
    mixed = mixed_ref[...].reshape(ib * SP, D)
    dw_ref[:, 3 * D : 4 * D] += tn(mixed, out_grad)
    mixed_grad = nt(out_grad, w_ref[:, 3 * D : 4 * D]).astype(NARROW)
    masks = head_masks(NARROW)
    rows = lax.broadcasted_iota(jnp.int32, (SP, SP), 0)
    dq_all, dk_all, dv_all = [], [], []
    for i in range(ib):
        r = slice(i * SP, (i + 1) * SP)
        dqs, dks, dvs = [], [], []
        for pair in range(HEADS // 2):
            qp = qkv_ref[i, :, pair * 128 : (pair + 1) * 128]
            kp = qkv_ref[i, :, D + pair * 128 : D + (pair + 1) * 128]
            vp = qkv_ref[i, :, 2 * D + pair * 128 : 2 * D + (pair + 1) * 128]
            mp = mixed_grad[r, pair * 128 : (pair + 1) * 128]
            dq = dk = dv = None
            for half in range(2):
                qm, mm, km = qp * masks[half], mp * masks[half], kp * masks[half]
                s = jnp.where(rows < SEQ, nt(kp, qm), LOWEST)
                e = jnp.exp(s - jnp.max(s, 0, keepdims=True))
                soft = e * (1.0 / jnp.sum(e, 0, keepdims=True))
                pg = nt(vp, mm)
                delta = jnp.sum(soft * pg, 0, keepdims=True)
                sg = (soft * (pg - delta)).astype(NARROW)
                v_part = nn(soft.astype(NARROW), mm)
                k_part = nn(sg, qm)
                q_part = tn(sg, km)
                dq = q_part if dq is None else dq + q_part
                dk = k_part if dk is None else dk + k_part
                dv = v_part if dv is None else dv + v_part
            dqs.append((dq * SCALE).astype(NARROW))
            dks.append(dk.astype(NARROW))
            dvs.append(dv.astype(NARROW))
        dq_all.append(jnp.concatenate(dqs, 1))
        dk_all.append(jnp.concatenate(dks, 1))
        dv_all.append(jnp.concatenate(dvs, 1))
    dqkv = jnp.concatenate(
        [
            jnp.concatenate(a, 0) if ib > 1 else a[0]
            for a in (dq_all, dk_all, dv_all)
        ],
        1,
    )
    dw_ref[:, 0 : 3 * D] += tn(normed, dqkv)
    normed_grad = nt(dqkv, w_ref[:, 0 : 3 * D])
    input_grad, gain_grad = norm_backward(normed_grad, unit, inverse, gain)
    return incoming + input_grad, gain_grad


def gain_columns(dg_ref):
    tall = jnp.concatenate(
        [jnp.zeros((EXPERTS, D), WIDE), dg_ref[...], jnp.zeros((128 - EXPERTS - 8, D), WIDE)], 0
    )
    return jnp.transpose(tall)


def put_rows(ref, step, ib, value):
    for image in range(ref.shape[0] // SEQ):

        @pl.when(step == image // ib)
        def _(image=image):
            first = image % ib * SP
            ref[image * SEQ : (image + 1) * SEQ, :] = value[first : first + SEQ]


def moe_bwd_kernel(
    ib,
    g_ref,
    w_ref,
    wr_ref,
    mid_ref,
    second_ref,
    cot_ref,
    prob_ref,
    aux_ref,
    qkv_ref,
    mixed_ref,
    table_ref,
    y_ref,
    grad_ref,
    dw_out,
    dr_ref,
    dg_ref,
    dw_ref,
):
    step = pl.program_id(0)

    @pl.when(step == 0)
    def _():
        dw_ref[...] = jnp.zeros(dw_ref.shape, WIDE)
        dr_ref[...] = jnp.zeros(dr_ref.shape, WIDE)
        dg_ref[...] = jnp.zeros(dg_ref.shape, WIDE)

    second = second_ref[...].reshape(ib * SP, D)
    upstream = cot_ref[...].astype(WIDE).reshape(ib * SP, D)
    prob = prob_ref[...].reshape(ib * SP, 128)
    aux = aux_ref[...].reshape(ib * SP, 128)
    first_pick = second_pick = back = None
    for j in range(table_ref.shape[0]):
        count = table_ref.shape[1] * CAP
        slot = lax.broadcasted_iota(jnp.int32, (1, count), 1) + j * count
        hot_one = (aux[:, 0:1] == slot).astype(NARROW)
        hot_two = (aux[:, 1:2] == slot).astype(NARROW)
        rows = table_ref[j].reshape(count, 2 * D)
        one = nn(hot_one, rows[:, 0:D])
        two = nn(hot_two, rows[:, 0:D])
        both = nn(hot_one + hot_two, rows[:, D : 2 * D])
        first_pick = one if first_pick is None else first_pick + one
        second_pick = two if second_pick is None else second_pick + two
        back = both if back is None else back + both
    lane = lax.broadcasted_iota(jnp.int32, (1, 128), 1)
    first_hit = (aux[:, 2:3] == lane).astype(WIDE)
    second_hit = (aux[:, 3:4] == lane).astype(WIDE)
    gate_one = jnp.sum(prob * first_hit, -1, keepdims=True)
    gate_two = jnp.sum(prob * second_hit, -1, keepdims=True)
    put_rows(y_ref, step, ib, second + (gate_one * first_pick + gate_two * second_pick))
    gate_one_grad = jnp.sum(upstream * first_pick, -1, keepdims=True)
    gate_two_grad = jnp.sum(upstream * second_pick, -1, keepdims=True)
    prob_grad = gate_one_grad * first_hit + gate_two_grad * second_hit
    logit_grad = (prob * (prob_grad - jnp.sum(prob * prob_grad, -1, keepdims=True))).astype(NARROW)
    unit, inverse = norm_parts(second)
    gain = g_ref[3:4, :]
    moe = (unit * gain).astype(NARROW)
    dr_ref[...] += tn(moe, logit_grad)
    normed_grad = back + nt(logit_grad, wr_ref[...])
    moe_grad, gain_grad = norm_backward(normed_grad, unit, inverse, gain)
    dg_ref[3:4, :] += gain_grad
    mid = mid_ref[...].reshape(ib * SP, D)
    grad, gain_grad = attn_bwd_body(
        mid, upstream + moe_grad, g_ref[1:2, :], qkv_ref, mixed_ref, w_ref, dw_ref, ib
    )
    dg_ref[1:2, :] += gain_grad
    grad_ref[...] = grad.reshape(ib, SP, D)

    @pl.when(step == pl.num_programs(0) - 1)
    def _():
        dw_out[:, : 4 * D] = dw_ref[...].astype(NARROW)
        dw_out[:, 4 * D :] = (dr_ref[...] + gain_columns(dg_ref)).astype(NARROW)


def moe_bwd(gains, w1, wr, mid, second, cot, prob, aux, qkv, mixed, tables, images, ib):
    return pl.pallas_call(
        partial(moe_bwd_kernel, ib),
        grid=(images // ib,),
        in_specs=[
            whole(gains.shape),
            whole(w1.shape),
            whole(wr.shape),
            per_image(ib, SP, D),
            per_image(ib, SP, D),
            per_image(ib, SP, D),
            per_image(ib, SP, 128),
            per_image(ib, SP, 128),
            per_image(ib, SP, 3 * D),
            per_image(ib, SP, D),
            whole(tables.shape),
        ],
        out_specs=[
            whole((images * SEQ, D)),
            per_image(ib, SP, D),
            whole((D, 4 * D + 128)),
        ],
        out_shape=[
            sds((images * SEQ, D), WIDE),
            sds((images, SP, D), WIDE),
            sds((D, 4 * D + 128), NARROW),
        ],
        scratch_shapes=[
            pltpu.VMEM((D, 128), WIDE),
            pltpu.VMEM((8, D), WIDE),
            pltpu.VMEM((D, 4 * D), WIDE),
        ],
        compiler_params=params(56),
        cost_estimate=cost(1e6, 1),
        name="expert_block_backward",
    )(gains, w1, wr, mid, second, cot, prob, aux, qkv, mixed, tables)


def dense_bwd_kernel(
    ib,
    g_ref,
    w_ref,
    win_ref,
    wout_ref,
    x_ref,
    first_ref,
    grad_ref,
    qkv_ref,
    mixed_ref,
    out_ref,
    dw_out,
    dout_out,
    dg_ref,
    dw_ref,
    din_ref,
    dout_ref,
):
    step = pl.program_id(0)

    @pl.when(step == 0)
    def _():
        dw_ref[...] = jnp.zeros(dw_ref.shape, WIDE)
        din_ref[...] = jnp.zeros(din_ref.shape, WIDE)
        dout_ref[...] = jnp.zeros(dout_ref.shape, WIDE)
        dg_ref[...] = jnp.zeros(dg_ref.shape, WIDE)

    incoming = grad_ref[...].reshape(ib * SP, D)
    first = first_ref[...].reshape(ib * SP, D)
    unit, inverse = norm_parts(first)
    gain = g_ref[2:3, :]
    normed = (unit * gain).astype(NARROW)
    out_grad = incoming.astype(NARROW)
    y_grad = None
    for f in range(FF // 512):
        c = slice(f * 512, (f + 1) * 512)
        win, wout = win_ref[:, c], wout_ref[c, :]
        pre = nn(normed, win)
        hidden_grad = nt(out_grad, wout)
        cdf, bell = normal_parts(pre)
        hidden = (pre * cdf).astype(NARROW)
        pre_grad = ((cdf + pre * (bell * INV_ROOT)) * hidden_grad).astype(NARROW)
        dout_ref[c, :] += tn(hidden, out_grad)
        din_ref[:, c] += tn(normed, pre_grad)
        part = nt(pre_grad, win)
        y_grad = part if y_grad is None else y_grad + part
    ffn_grad, gain_grad = norm_backward(y_grad, unit, inverse, gain)
    dg_ref[2:3, :] += gain_grad
    x = x_ref[...].astype(WIDE).reshape(ib * SP, D)
    grad, gain_grad = attn_bwd_body(
        x, incoming + ffn_grad, g_ref[0:1, :], qkv_ref, mixed_ref, w_ref, dw_ref, ib
    )
    dg_ref[0:1, :] += gain_grad
    put_rows(out_ref, step, ib, grad)

    @pl.when(step == pl.num_programs(0) - 1)
    def _():
        dw_out[:, : 4 * D] = dw_ref[...].astype(NARROW)
        dw_out[:, 4 * D : 8 * D] = din_ref[...].astype(NARROW)
        dw_out[:, 8 * D :] = gain_columns(dg_ref).astype(NARROW)
        dout_out[...] = dout_ref[...].astype(NARROW)


def dense_bwd(gains, w0, win, wout, x, first, grad, qkv, mixed, images, ib):
    return pl.pallas_call(
        partial(dense_bwd_kernel, ib),
        grid=(images // ib,),
        in_specs=[
            whole(gains.shape),
            whole(w0.shape),
            whole(win.shape),
            whole(wout.shape),
            per_image(ib, SP, D),
            per_image(ib, SP, D),
            per_image(ib, SP, D),
            per_image(ib, SP, 3 * D),
            per_image(ib, SP, D),
        ],
        out_specs=[
            whole((images * SEQ, D)),
            whole((D, 8 * D + 128)),
            whole((FF, D)),
        ],
        out_shape=[
            sds((images * SEQ, D), WIDE),
            sds((D, 8 * D + 128), NARROW),
            sds((FF, D), NARROW),
        ],
        scratch_shapes=[
            pltpu.VMEM((8, D), WIDE),
            pltpu.VMEM((D, 4 * D), WIDE),
            pltpu.VMEM((D, FF), WIDE),
            pltpu.VMEM((FF, D), WIDE),
        ],
        compiler_params=params(56),
        cost_estimate=cost(1e6, 1),
        name="dense_block_backward",
    )(gains, w0, win, wout, x, first, grad, qkv, mixed)


BLOCK = 512
MESH_ID = pl.DeviceIdType.MESH


def add_rows(out, one, two, rows, step):
    @pl.loop(0, rows // step)
    def _(i):
        r = pl.ds(pl.multiple_of(i * step, step), step)
        out[r, :] = (one[r, :].astype(WIDE) + two[r, :].astype(WIDE)).astype(out.dtype)


def sum_kernel(nz, groups, mats, slices, *refs):
    exp_refs, refs = refs[:mats], refs[mats:]
    dense_refs, peak_ref, refs = refs[:3], refs[3], refs[4:]
    exp_out, dense_outs, peak_out, refs = refs[0], refs[1:4], refs[4], refs[5:]
    own, up, down, refs = refs[0], refs[1], refs[2], refs[3:]
    land, refs = refs[:4], refs[4:]
    dense_own, refs = refs[:4], refs[4:]
    dense_up, refs = refs[:4], refs[4:]
    dense_down, refs = refs[:4], refs[4:]
    (own_sem, up_send, up_recv, down_recv, out_send, sib_send, sib_recv, copy_sem, rs_send, rs_recv) = refs

    z, core, f = lax.axis_index("z"), lax.axis_index("core"), lax.axis_index("fsdp")
    half = nz // 2
    left = z < half
    inner = jnp.where(left, z + 1, z - 1)
    outer = jnp.where(left, z - 1, z + 1)
    has_outer = jnp.logical_and(z > 0, z < nz - 1)
    edge = jnp.logical_not(has_outer)
    center = jnp.logical_or(z == half - 1, z == half)
    away = jnp.logical_not(center)
    outer = jnp.where(has_outer, outer, inner)
    sibling = (z, 1 - core, f)
    members = CORES * groups
    me = core * groups + f

    barrier = pltpu.get_barrier_semaphore()
    pl.semaphore_signal(barrier, inc=1, device_id=(inner, core, f), device_id_type=MESH_ID)

    @pl.when(has_outer)
    def _():
        pl.semaphore_signal(barrier, inc=1, device_id=(outer, core, f), device_id_type=MESH_ID)

    for d in range(1, members):
        there = lax.rem(me + d, members)
        pl.semaphore_signal(
            barrier,
            inc=1,
            device_id=(z, there // groups, lax.rem(there, groups)),
            device_id_type=MESH_ID,
        )

    @pl.when(has_outer)
    def _():
        pl.semaphore_wait(barrier, members + 1)

    @pl.when(edge)
    def _():
        pl.semaphore_wait(barrier, members)

    chunks = mats * slices
    items = chunks + 4

    def piece(n, ref, there):
        if n == 3:
            return ref
        rows = ref.shape[0] // members
        place = (lax.rem(there, groups) * CORES + there // groups) * rows
        return ref.at[pl.ds(pl.multiple_of(place, 16), rows), :]

    def scatter(n, d):
        there = lax.rem(me + d, members)
        source = dense_refs[n] if n < 3 else peak_ref
        return pltpu.make_async_remote_copy(
            src_ref=piece(n, source, there),
            dst_ref=land[n].at[d],
            send_sem=rs_send.at[n, d],
            recv_sem=rs_recv.at[n, d],
            device_id=(z, there // groups, lax.rem(there, groups)),
            device_id_type=MESH_ID,
        )

    for n in (3, 1, 0, 2):
        for d in range(1, members):
            scatter(n, d).start()
    keep = [
        pltpu.make_async_copy(
            piece(n, dense_refs[n] if n < 3 else peak_ref, me), land[n].at[0], rs_recv.at[n, 0]
        )
        for n in range(4)
    ]
    for k in keep:
        k.start()

    def load(t):
        return pltpu.make_async_copy(exp_refs[t // slices].at[t % slices], own.at[t], own_sem.at[t])

    @pl.when(has_outer)
    def _():
        for t in range(chunks):
            load(t).start()

    def bufs(t):
        if t < chunks:
            return own.at[t], up.at[t], down.at[t]
        n = t - chunks
        return dense_own[n], dense_up[n], dense_down[n]

    def send_up(t, source, to_center):
        _, u, dn = bufs(t)
        return pltpu.make_async_remote_copy(
            src_ref=source,
            dst_ref=dn if to_center else u,
            send_sem=up_send.at[t],
            recv_sem=(down_recv if to_center else up_recv).at[t],
            device_id=(inner, core, f),
            device_id_type=MESH_ID,
        )

    def source_at_edge(t):
        return exp_refs[t // slices].at[t % slices] if t < chunks else bufs(t)[0]

    def join(t, out, one, two):
        if t == items - 1:
            out[...] = jnp.maximum(one[...], two[...])
        else:
            add_rows(out, one, two, out.shape[0], 16)

    def reduce_own(n):
        for d in range(members):
            if d == 0:
                keep[n].wait()
            else:
                scatter(n, d).wait_recv()
        if n == 3:
            best = land[n][0]
            for d in range(1, members):
                best = jnp.maximum(best, land[n][d])
            dense_own[n][...] = best
            return

        @pl.loop(0, dense_own[n].shape[0] // 16)
        def _(i):
            r = pl.ds(pl.multiple_of(i * 16, 16), 16)
            total = land[n][0, r, :].astype(WIDE)
            for d in range(1, members):
                total = total + land[n][d, r, :].astype(WIDE)
            dense_own[n][r, :] = total.astype(NARROW)

    def up_from_edge(t, before):
        if before is not None:
            send_up(before, source_at_edge(before), half == 1).wait_send()
        if t >= chunks:
            reduce_own(t - chunks)
        send_up(t, source_at_edge(t), half == 1).start()

    def up_from_inside(t):
        o, u, _ = bufs(t)
        if t >= chunks:
            reduce_own(t - chunks)
        else:
            load(t).wait()
        send_up(t, u, False).wait_recv()
        join(t, o, o, u)

        @pl.when(center)
        def _():
            send_up(t, o, True).start()

        if half > 2:

            @pl.when(away)
            def _():
                send_up(t, o, False).start()

    def results(t):
        if t < chunks:
            return exp_out.at[t, core]
        n = t - chunks
        if n == 3:
            return peak_out
        ref = dense_outs[n]
        rows = ref.shape[0] // CORES
        return ref.at[pl.ds(pl.multiple_of(core * rows, 16), rows), :]

    def to_sibling(t):
        return pltpu.make_async_remote_copy(
            src_ref=bufs(t)[2],
            dst_ref=results(t),
            send_sem=sib_send.at[t],
            recv_sem=sib_recv.at[t],
            device_id=sibling,
            device_id_type=MESH_ID,
        )

    def to_outer(t):
        dn = bufs(t)[2]
        return pltpu.make_async_remote_copy(
            src_ref=dn,
            dst_ref=dn,
            send_sem=out_send.at[t],
            recv_sem=down_recv.at[t],
            device_id=(outer, core, f),
            device_id_type=MESH_ID,
        )

    def keep_result(t):
        return pltpu.make_async_copy(bufs(t)[2], results(t), copy_sem.at[t])

    def go_down(t, at_edge):
        o, _, dn = bufs(t)
        to_outer(t).wait_recv()
        if at_edge:
            if half == 1:
                join(t, dn, source_at_edge(t), dn)
        else:

            @pl.when(center)
            def _():
                join(t, dn, o, dn)

            to_outer(t).start()
        keep_result(t).start()
        if t < items - 1:
            to_sibling(t).start()

    early = min(8, chunks)
    sequence = [*range(early), *range(items - 1, chunks - 1, -1), *range(early, chunks)]

    def run(up, at_edge, lag):
        for i in range(items + lag):
            if i < items:
                up(i)
            if i >= lag:
                go_down(sequence[i - lag], at_edge)

    @pl.when(edge)
    def _():
        run(
            lambda i: up_from_edge(sequence[i], sequence[i - 2] if i >= 2 else None),
            True,
            min(7, items),
        )
        for t in sequence[-2:]:
            send_up(t, source_at_edge(t), half == 1).wait_send()

    if half > 1:

        @pl.when(has_outer)
        def _():
            run(lambda i: up_from_inside(sequence[i]), False, 1)
            for t in range(items):
                send_up(t, bufs(t)[0], False).wait_send()
                to_outer(t).wait_send()

    for n in range(4):
        for d in range(1, members):
            scatter(n, d).wait_send()
    for t in range(items):
        keep_result(t).wait()
        if t < items - 1:
            to_sibling(t).wait()


def sum_all(mats, dense, peaks, nz, groups):
    slices = mats[0].shape[0]
    chunks = len(mats) * slices
    members = CORES * groups
    items = chunks + 4
    any_space = pl.BlockSpec(memory_space=pl.ANY)
    vmem = pl.BlockSpec(memory_space=pltpu.VMEM)
    pieces = [(a.shape[0] // members, a.shape[1]) for a in dense]
    block = pltpu.VMEM((chunks, BLOCK, BLOCK), NARROW)

    def four(lead=()):
        return [pltpu.VMEM((*lead, *p), NARROW) for p in pieces] + [
            pltpu.VMEM((*lead, *peaks.shape), WIDE)
        ]

    dma = pltpu.SemaphoreType.DMA
    return pl.pallas_call(
        partial(sum_kernel, nz, groups, len(mats), slices),
        in_specs=[any_space] * (len(mats) + 3) + [vmem],
        out_specs=[any_space] * 4 + [vmem],
        out_shape=[
            sds((chunks, CORES, BLOCK, BLOCK), NARROW),
            *[sds((CORES * r, c), NARROW) for r, c in pieces],
            sds(peaks.shape, WIDE),
        ],
        scratch_shapes=[
            block,
            block,
            block,
            *four((members,)),
            *four(),
            *four(),
            *four(),
            *[dma((items,)) for _ in range(8)],
            dma((4, members)),
            dma((4, members)),
        ],
        compiler_params=pltpu.CompilerParams(
            vmem_limit_bytes=58 * MIB, collective_id=3, has_side_effects=True
        ),
        name="sums",
    )(*mats, *dense, peaks)


SUMMED = 12
BESIDE = 8


def exchange_kernel(nz, groups, mine, *refs):
    (sent_ref, win_hbm, wout_hbm, table_out, sum_out, beside_out, rest_out) = refs[:7]
    (rows, back, res, sgr, w_in, w_out, own, up, down, made) = refs[7:17]
    (d_send, d_recv, r_send, r_recv, w_sem, made_sem, up_send, up_recv, down_recv) = refs[17:26]
    (out_send, sib_send, sib_recv, keep_sem) = refs[26:]
    s = pl.program_id(0)
    z, core, f = lax.axis_index("z"), lax.axis_index("core"), lax.axis_index("fsdp")
    members = CORES * groups
    me = core * groups + f
    parts = FF // BLOCK
    steps = mine * parts
    last = pl.num_programs(0) - 1
    left = z < nz // 2
    inner = jnp.where(left, z + 1, z - 1)
    has_outer = jnp.logical_and(z > 0, z < nz - 1)
    edge = jnp.logical_not(has_outer)
    outer = jnp.where(has_outer, jnp.where(left, z - 1, z + 1), inner)

    def member(d):
        there = lax.rem(me + d, members)
        return there, (z, there // groups, lax.rem(there, groups))

    def rows_to(j, d):
        there, device = member(d)
        return pltpu.make_async_remote_copy(
            src_ref=sent_ref.at[j, there],
            dst_ref=rows.at[j, me],
            send_sem=d_send.at[j, d],
            recv_sem=d_recv.at[j, d],
            device_id=device,
            device_id_type=MESH_ID,
        )

    def rows_here(j):
        return pltpu.make_async_copy(sent_ref.at[j, me], rows.at[j, me], d_recv.at[j, 0])

    def send_rows(j):
        for d in range(1, members):
            rows_to(j, d).start()
        rows_here(j).start()

    def results_to(j, d):
        there, device = member(d)
        return pltpu.make_async_remote_copy(
            src_ref=back.at[j % 2, there],
            dst_ref=table_out.at[j, me],
            send_sem=r_send.at[j, d],
            recv_sem=r_recv.at[j, d],
            device_id=device,
            device_id_type=MESH_ID,
        )

    def results_here(j):
        return pltpu.make_async_copy(back.at[j % 2, me], table_out.at[j, me], r_recv.at[j, 0])

    def weights(step):
        e = core * mine + step // parts
        c = pl.ds(pl.multiple_of(lax.rem(step, parts) * BLOCK, BLOCK), BLOCK)
        slot = lax.rem(step, 2)
        return (
            pltpu.make_async_copy(win_hbm.at[e, :, c], w_in.at[slot], w_sem.at[0, slot]),
            pltpu.make_async_copy(wout_hbm.at[e, c, :], w_out.at[slot], w_sem.at[1, slot]),
        )

    @pl.when(s == 0)
    def _():
        barrier = pltpu.get_barrier_semaphore()
        pl.semaphore_signal(barrier, inc=1, device_id=(inner, core, f), device_id_type=MESH_ID)

        @pl.when(has_outer)
        def _():
            pl.semaphore_signal(barrier, inc=1, device_id=(outer, core, f), device_id_type=MESH_ID)

        for d in range(1, members):
            pl.semaphore_signal(barrier, inc=1, device_id=member(d)[1], device_id_type=MESH_ID)

        @pl.when(has_outer)
        def _():
            pl.semaphore_wait(barrier, members + 1)

        @pl.when(edge)
        def _():
            pl.semaphore_wait(barrier, members)

        send_rows(0)
        for w in weights(s):
            w.start()

    for j in range(mine):

        @pl.when(s == j * parts)
        def _(j=j):
            for d in range(1, members):
                rows_to(j, d).wait_recv()
            rows_here(j).wait()
            if j == 0:
                send_rows(1)
            if j == 1:
                send_rows(3)

    slot = lax.rem(s, 2)

    def made_to(step, side, near):
        place = 2 * step + side - SUMMED - (0 if near else BESIDE)
        there = lax.rem(step, 2)
        out = beside_out if near else rest_out
        return pltpu.make_async_copy(
            made.at[there, side],
            out.at[jnp.clip(place, 0, out.shape[0] - 1)],
            made_sem.at[there, side],
        )

    def each_made(step, act):
        near = step < (SUMMED + BESIDE) // 2

        @pl.when(near)
        def _():
            for side in range(2):
                act(made_to(step, side, True))

        @pl.when(jnp.logical_not(near))
        def _():
            for side in range(2):
                act(made_to(step, side, False))

    @pl.when(s < steps)
    def _():
        for w in weights(s):
            w.wait()

        @pl.when(s + 1 < steps)
        def _():
            for w in weights(s + 1):
                w.start()

        @pl.when(jnp.logical_and(s >= SUMMED // 2 + 2, s < steps))
        def _():
            each_made(s - 2, lambda copy: copy.wait())

        j = s // parts
        part = lax.rem(s, parts)
        count = members * CAP
        slots = rows[j, :, 0:CAP, :].reshape(count, D)
        grads = rows[j, :, CAP : 2 * CAP, :].reshape(count, D)
        result, slot_grad, d_in, d_out = expert_math(slots, grads, w_in[slot], w_out[slot])

        @pl.when(part == 0)
        def _():
            res[...] = result
            sgr[...] = slot_grad

        @pl.when(part > 0)
        def _():
            res[...] += result
            sgr[...] += slot_grad

        @pl.when(s < SUMMED // 2)
        def _():
            own[2 * s] = d_in.astype(NARROW)
            own[2 * s + 1] = d_out.astype(NARROW)

        @pl.when(s >= SUMMED // 2)
        def _():
            made[slot, 0] = d_in.astype(NARROW)
            made[slot, 1] = d_out.astype(NARROW)

            each_made(s, lambda copy: copy.start())

    @pl.when(s == 1)
    def _():
        send_rows(2)

    for j in range(mine):

        @pl.when(s == (j + 1) * parts - 1)
        def _(j=j):
            if j >= 2:
                for d in range(1, members):
                    results_to(j - 2, d).wait_send()
                results_here(j - 2).wait()
            back[j % 2, :, :, 0:D] = res[...].astype(NARROW).reshape(members, CAP, D)
            back[j % 2, :, :, D : 2 * D] = sgr[...].astype(NARROW).reshape(members, CAP, D)
            for d in range(1, members):
                results_to(j, d).start()
            results_here(j).start()

    def send_up(t, to_center):
        return pltpu.make_async_remote_copy(
            src_ref=own.at[t],
            dst_ref=(down if to_center else up).at[t],
            send_sem=up_send.at[t],
            recv_sem=(down_recv if to_center else up_recv).at[t],
            device_id=(inner, core, f),
            device_id_type=MESH_ID,
        )

    def send_out(t):
        return pltpu.make_async_remote_copy(
            src_ref=down.at[t],
            dst_ref=down.at[t],
            send_sem=out_send.at[t],
            recv_sem=down_recv.at[t],
            device_id=(outer, core, f),
            device_id_type=MESH_ID,
        )

    def to_sibling(t):
        return pltpu.make_async_remote_copy(
            src_ref=down.at[t],
            dst_ref=sum_out.at[t, core],
            send_sem=sib_send.at[t],
            recv_sem=sib_recv.at[t],
            device_id=(z, 1 - core, f),
            device_id_type=MESH_ID,
        )

    def keep_sum(t):
        return pltpu.make_async_copy(down.at[t], sum_out.at[t, core], keep_sem.at[t])

    def at(lag, role):
        t = s - lag
        return pl.when(jnp.logical_and(role, jnp.logical_and(t >= 0, t < SUMMED)))

    def tick(t):
        return jnp.clip(t, 0, SUMMED - 1)

    @at(0, edge)
    def _():
        send_up(tick(s), False).start()

    @at(2, has_outer)
    def _():
        t = tick(s - 2)
        send_up(t, False).wait_recv()
        add_rows(own.at[t], own.at[t], up.at[t], BLOCK, 16)
        send_up(t, True).start()

    @at(4, has_outer)
    def _():
        t = tick(s - 4)
        send_out(t).wait_recv()
        add_rows(down.at[t], own.at[t], down.at[t], BLOCK, 16)
        send_out(t).start()
        keep_sum(t).start()
        to_sibling(t).start()

    @at(6, edge)
    def _():
        t = tick(s - 6)
        send_out(t).wait_recv()
        keep_sum(t).start()
        to_sibling(t).start()

    @pl.when(s == last)
    def _():
        for step in (steps - 2, steps - 1):
            for side in range(2):
                made_to(step, side, False).wait()
        for j in range(mine):
            for d in range(1, members):
                rows_to(j, d).wait_send()
                results_to(j, d).wait_recv()
                if j >= mine - 2:
                    results_to(j, d).wait_send()
            if j >= mine - 2:
                results_here(j).wait()

        for t in range(SUMMED):
            send_up(t, False).wait_send()
            keep_sum(t).wait()
            to_sibling(t).wait()

        @pl.when(has_outer)
        def _():
            for t in range(SUMMED):
                send_out(t).wait_send()


def exchange(sent, win, wout, nz, groups):
    mine, members = sent.shape[0], sent.shape[1]
    steps = mine * (FF // BLOCK)
    rest = 2 * steps - SUMMED - BESIDE
    any_space = pl.BlockSpec(memory_space=pl.ANY)
    dma = pltpu.SemaphoreType.DMA
    block = pltpu.VMEM((SUMMED, BLOCK, BLOCK), NARROW)
    return pl.pallas_call(
        partial(exchange_kernel, nz, groups, mine),
        grid=(steps + 2,),
        in_specs=[any_space] * 3,
        out_specs=[any_space] * 4,
        out_shape=[
            sds((mine, members, CAP, 2 * D), NARROW),
            sds((SUMMED, CORES, BLOCK, BLOCK), NARROW),
            sds((BESIDE, BLOCK, BLOCK), NARROW),
            sds((rest, BLOCK, BLOCK), NARROW),
        ],
        scratch_shapes=[
            pltpu.VMEM((mine, members, 2 * CAP, D), NARROW),
            pltpu.VMEM((2, members, CAP, 2 * D), NARROW),
            pltpu.VMEM((members * CAP, D), WIDE),
            pltpu.VMEM((members * CAP, D), WIDE),
            pltpu.VMEM((2, D, BLOCK), NARROW),
            pltpu.VMEM((2, BLOCK, D), NARROW),
            block,
            block,
            block,
            pltpu.VMEM((2, 2, BLOCK, BLOCK), NARROW),
            *[dma((mine, members)) for _ in range(4)],
            dma((2, 2)),
            dma((2, 2)),
            *[dma((SUMMED,)) for _ in range(7)],
        ],
        compiler_params=pltpu.CompilerParams(
            vmem_limit_bytes=58 * MIB, collective_id=7, has_side_effects=True
        ),
        name="experts",
    )(sent, win, wout)


def widen_kernel(counts, core_ref, *refs):
    in_ref, out_ref = refs[-2:]
    c, s = pl.program_id(0), pl.program_id(1)

    def put(ref):
        in_ref[...] = ref[0].astype(WIDE)
        out_ref[...] = ref[1].astype(WIDE)

    first, at = 0, 0
    for kind, count in enumerate(counts):
        if count:
            here = jnp.logical_and(s >= first, s < first + count)
            if kind == 1:
                for ref, mine in ((refs[at], True), (refs[at + 1], False)):
                    pl.when(jnp.logical_and(here, (c == core_ref[0]) == mine))(partial(put, ref))
                at += 2
            else:
                pl.when(here)(partial(put, refs[at]))
                at += 1
        first += count


def widen(core, early, own, other, late, mine):
    block = (None, 2, None, BLOCK, BLOCK)
    arrays, specs, counts, first = [], [], [], 0
    for kind, group in enumerate(((early,), (own, other), (late,))):
        count = 0 if group[0] is None else group[0].shape[0] // 2
        counts.append(count)
        if count:

            def pair(s, first=first, count=count):
                return jnp.clip(s - first, 0, count - 1)

            for a in group:
                if kind == 1:
                    arrays.append(a.reshape(count, 2, BLOCK, BLOCK))
                    specs.append(
                        pl.BlockSpec(
                            (None, 2, BLOCK, BLOCK),
                            lambda c, s, _, pair=pair: (pair(s), 0, 0, 0),
                        )
                    )
                else:
                    arrays.append(a.reshape(count, 2, CORES, BLOCK, BLOCK))
                    specs.append(
                        pl.BlockSpec(block, lambda c, s, _, pair=pair: (pair(s), 0, c, 0, 0))
                    )
        first += count
    parts = FF // BLOCK
    return pl.pallas_call(
        partial(widen_kernel, counts),
        grid_spec=pltpu.PrefetchScalarGridSpec(
            num_scalar_prefetch=1,
            grid=(CORES, mine * parts),
            in_specs=specs,
            out_specs=[
                pl.BlockSpec(
                    (None, D, BLOCK), lambda c, s, _: (c * mine + s // parts, 0, s % parts)
                ),
                pl.BlockSpec(
                    (None, BLOCK, D), lambda c, s, _: (c * mine + s // parts, s % parts, 0)
                ),
            ],
        ),
        out_shape=[sds((CORES * mine, D, FF), WIDE), sds((CORES * mine, FF, D), WIDE)],
        compiler_params=params(56),
        name="widen",
    )(core, *arrays)


def gather_kernel(groups, q_ref, k_ref, v_ref, o_ref, small_ref, in_ref, out_ref, *refs):
    w_all, small_all, in_all, out_all, send, recv, pass_send, pass_recv, copy = refs
    z, core, f = lax.axis_index("z"), lax.axis_index("core"), lax.axis_index("fsdp")
    barrier = pltpu.get_barrier_semaphore()
    for d in range(1, groups):
        pl.semaphore_signal(
            barrier, inc=1, device_id=(z, core, lax.rem(f + d, groups)), device_id_type=MESH_ID
        )
    pl.semaphore_signal(barrier, inc=1, device_id=(z, 1 - core, f), device_id_type=MESH_ID)
    pl.semaphore_wait(barrier, groups)

    def rows(count, owner, side):
        half = count // CORES
        return pl.ds(pl.multiple_of(owner * count + side * half, 16), half)

    def item(n):
        if n < 4:
            ref = (q_ref, k_ref, v_ref, o_ref)[n]
            count = ref.shape[1]
            cols = pl.ds(n * D, D)
            return (
                lambda side: ref.at[0, rows(count, 0, side), :],
                lambda owner, side: w_all.at[rows(count, owner, side), cols],
            )
        ref, full = ((small_ref, small_all), (in_ref, in_all), (out_ref, out_all))[n - 4]
        count = ref.shape[0]
        return (
            lambda side: ref.at[rows(count, 0, side), :],
            lambda owner, side: full.at[rows(count, owner, side), :],
        )

    def fetch(n, d):
        source, place = item(n)
        return pltpu.make_async_remote_copy(
            src_ref=source(core),
            dst_ref=place(f, core),
            send_sem=send.at[n, d],
            recv_sem=recv.at[n, d],
            device_id=(z, core, lax.rem(f + d, groups)),
            device_id_type=MESH_ID,
        )

    def hand_on(n, d):
        _, place = item(n)
        there = place(lax.rem(f + groups - d, groups), core)
        return pltpu.make_async_remote_copy(
            src_ref=there,
            dst_ref=there,
            send_sem=pass_send.at[n, d],
            recv_sem=pass_recv.at[n, d],
            device_id=(z, 1 - core, f),
            device_id_type=MESH_ID,
        )

    def keep(n, side):
        source, place = item(n)
        return pltpu.make_async_copy(source(side), place(f, side), copy.at[n, side])

    count = 7
    for n in range(count):
        for d in range(1, groups):
            fetch(n, d).start()
    for n in range(count):
        for side in range(CORES):
            keep(n, side).start()
    for n in range(count):
        for d in range(1, groups):
            fetch(n, d).wait_recv()
            hand_on(n, d).start()
    for n in range(count):
        for side in range(CORES):
            keep(n, side).wait()
        for d in range(1, groups):
            fetch(n, d).wait_send()
            hand_on(n, d).wait()


def gather_dense(query_w, key_w, value_w, output_w, small, mlp_in, mlp_out, groups):
    any_space = pl.BlockSpec(memory_space=pl.ANY)
    dma = pltpu.SemaphoreType.DMA
    return pl.pallas_call(
        partial(gather_kernel, groups),
        in_specs=[any_space] * 7,
        out_specs=[any_space] * 4,
        out_shape=[
            sds((D, 4 * D), NARROW),
            sds((D, 128), NARROW),
            sds((D, FF), NARROW),
            sds((FF, D), NARROW),
        ],
        scratch_shapes=[
            *[dma((7, groups)) for _ in range(4)],
            dma((7, CORES)),
        ],
        compiler_params=pltpu.CompilerParams(
            vmem_limit_bytes=8 * MIB, collective_id=5, has_side_effects=True
        ),
        name="gather_weights",
    )(query_w, key_w, value_w, output_w, small, mlp_in, mlp_out)


def gather(x):
    return lax.all_gather(x, "fsdp", axis=0, tiled=True)


def images_of(x, images):
    return jnp.pad(x.reshape(images, SEQ, x.shape[-1]), ((0, 0), (0, SP - SEQ), (0, 0)))


def local(
    tokens,
    cotangent,
    routes,
    attn_norm,
    query_w,
    key_w,
    value_w,
    output_w,
    ffn_norm,
    mlp_in,
    mlp_out,
    router_w,
    expert_in,
    expert_out,
    updated_query,
    updated_key,
    clip_threshold,
):
    images = tokens.shape[0] // SEQ
    ib = 2
    groups = lax.axis_size("fsdp")
    core = lax.axis_index("core")
    held = expert_in.shape[0]
    mine = held // CORES
    owners = CORES * groups

    small = jnp.concatenate(
        [
            router_w,
            jnp.transpose(attn_norm),
            jnp.transpose(ffn_norm),
            jnp.zeros((router_w.shape[0], 128 - EXPERTS - 4), NARROW),
        ],
        1,
    )
    w0, w_small, win, wout = gather_dense(
        query_w, key_w, value_w, output_w, small, mlp_in, mlp_out, groups
    )
    w1 = gather(jnp.concatenate([query_w[1], key_w[1], value_w[1], output_w[1]], 1))
    wr = jnp.where(jnp.arange(128)[None, :] < EXPERTS, w_small, 0)
    gains = jnp.pad(
        jnp.transpose(w_small[:, EXPERTS : EXPERTS + 4]).astype(WIDE), ((0, 4), (0, 0))
    )

    x = images_of(tokens, images)
    cot = images_of(cotangent, images)
    routes_image = jnp.pad(
        routes.reshape(images, SEQ, 2), ((0, 0), (0, SP - SEQ), (0, 0)), constant_values=-1
    )
    routes_rows = jnp.pad(
        jnp.transpose(routes_image.reshape(-1, 2)), ((0, 6), (0, 0)), constant_values=-1
    )
    slot = jnp.arange(EXPERTS, dtype=jnp.int32)
    place_there, owner = slot // owners, slot % owners
    order = (owner % groups) * held + (owner // groups) * mine + place_there
    order = jnp.broadcast_to(order[:, None], (EXPERTS, 128))
    pos, target = places(order, routes_rows)
    aux = jnp.pad(
        jnp.concatenate(
            [
                jnp.transpose(target[0:2]).astype(jnp.int32).reshape(images, SP, 2),
                routes_image,
            ],
            -1,
        ),
        ((0, 0), (0, 0), (0, 124)),
        constant_values=-1,
    )

    first, qkv0, mixed0, peak0 = dense_attn(x, gains, w0, images, ib)
    mid = ffn(first, gains, win, wout, images, ib)
    second, qkv1, mixed1, peak1, moe, prob = expert_attn(mid, gains, w1, wr, images, ib)
    sent = dispatch(
        pos, order, moe.reshape(-1, D), cot.reshape(-1, D), prob.reshape(-1, 128)
    ).reshape(mine, owners, 2 * CAP, D)

    nz = lax.axis_size("z")
    early = own = other = None
    if nz == 4 and owners == 8 and mine == 4:
        tables, early, own, late = exchange(sent, expert_in, expert_out, nz, groups)
        own = lax.psum(own, "z")
    else:
        tables, blocks = [], []
        for j in range(mine):
            rows = lax.all_to_all(
                sent[j], ("core", "fsdp"), split_axis=0, concat_axis=0, tiled=True
            )
            pick = (core * mine + j).astype(jnp.int32).reshape(1)
            back, d_in, d_out = expert(pick, rows, expert_in, expert_out)
            tables.append(
                lax.all_to_all(back, ("core", "fsdp"), split_axis=0, concat_axis=0, tiled=True)
            )
            blocks.append(jnp.stack([d_in, d_out], 1).reshape(-1, BLOCK, BLOCK))
        tables = jnp.stack(tables)
        late = jnp.concatenate(blocks)

    y, mid_grad, dw1 = moe_bwd(
        gains, w1, wr, mid, second, cot, prob, aux, qkv1, mixed1, tables, images, ib
    )
    x_grad, dw0, d_wout = dense_bwd(
        gains, w0, win, wout, x, first, mid_grad, qkv0, mixed0, images, ib
    )
    lane = jnp.arange(128)[None, :]
    peaks = jnp.where(lane < 64, jnp.max(peak0, 0), jnp.max(peak1, 0))
    late, t1, t0, t_wout, maxima = sum_all([late], [dw1, dw0, d_wout], peaks, nz, groups)
    if own is not None:
        own, late = lax.optimization_barrier((own, late))
        other = lax.ppermute(own, "core", [(0, 1), (1, 0)])
    expert_in_grad, expert_out_grad = widen(
        core.astype(jnp.int32).reshape(1), early, own, other, late, mine
    )

    t1, t0 = t1.astype(WIDE), t0.astype(WIDE)
    t_small = t1[:, 4 * D :] + t0[:, 8 * D :]
    norm_rows = jnp.transpose(t_small[:, EXPERTS : EXPERTS + 4])
    maxima = jnp.stack([maxima[:, 0], maxima[:, 64]])
    factor = clip_threshold / jnp.maximum(maxima, clip_threshold)
    column_scale = jnp.repeat(jnp.sqrt(factor), HEAD, axis=1)

    def both(n):
        return jnp.stack([t0[:, n * D : (n + 1) * D], t1[:, n * D : (n + 1) * D]])

    return (
        y,
        x_grad,
        norm_rows[0:2],
        both(0),
        both(1),
        both(2),
        both(3),
        norm_rows[2:4],
        t0[:, 4 * D : 8 * D],
        t_wout.astype(WIDE),
        t_small[:, :EXPERTS],
        expert_in_grad,
        expert_out_grad,
        updated_query * column_scale[:, None, :],
        updated_key * column_scale[:, None, :],
    )


def solution(mesh):
    replicas, groups = mesh.shape["replica"], mesh.shape["fsdp"]
    inner = Mesh(
        mesh.devices.reshape(replicas // CORES, CORES, groups), ("z", "core", "fsdp")
    )
    split = P(("z", "core", "fsdp"), None)
    second = P(None, "fsdp", None)
    in_specs = (
        split,
        split,
        split,
        P(None, "fsdp"),
        second,
        second,
        second,
        second,
        P(None, "fsdp"),
        P("fsdp", None),
        P("fsdp", None),
        P("fsdp", None),
        P("fsdp", None, None),
        P("fsdp", None, None),
        second,
        second,
        P(),
    )
    out_specs = (
        split,
        split,
        P(None, "fsdp"),
        second,
        second,
        second,
        second,
        P(None, "fsdp"),
        P("fsdp", None),
        P("fsdp", None),
        P("fsdp", None),
        P("fsdp", None, None),
        P("fsdp", None, None),
        second,
        second,
    )
    return jax.shard_map(local, mesh=inner, in_specs=in_specs, out_specs=out_specs, check_vma=False)
```

```python
from functools import partial

import jax
import jax.numpy as jnp
import numpy as np
from jax import lax
from jax.experimental import pallas as pl
from jax.experimental.pallas import tpu as pltpu
from jax.sharding import Mesh
from jax.sharding import PartitionSpec as P

D = 512
HEADS = 8
HEAD = 64
FF = 2048
SEQ = 197
SP = 208
CAP = 128
EXPERTS = 32
EPSILON = 1e-06
SCALE = HEAD ** (-0.5)
LOWEST = -1e30
NARROW = jnp.bfloat16
WIDE = jnp.float32
CORES = 2
MIB = 1 << 20


def nn(a, b):
    return lax.dot_general(a, b, (((1,), (0,)), ((), ())), preferred_element_type=WIDE)


def nt(a, b):
    return lax.dot_general(a, b, (((1,), (1,)), ((), ())), preferred_element_type=WIDE)


def tn(a, b):
    return lax.dot_general(a, b, (((0,), (0,)), ((), ())), preferred_element_type=WIDE)


def norm_parts(values):
    centred = values - jnp.mean(values, -1, keepdims=True)
    inverse = lax.rsqrt(jnp.mean(centred * centred, -1, keepdims=True) + EPSILON)
    return centred * inverse, inverse


def norm_backward(incoming, unit, inverse, gain):
    gain_grad = jnp.sum(incoming * unit, 0, keepdims=True)
    scaled = incoming * gain
    centred = (
        scaled
        - jnp.mean(scaled, -1, keepdims=True)
        - unit * jnp.mean(scaled * unit, -1, keepdims=True)
    )
    return inverse * centred, gain_grad


def normal_parts(x):
    z = jnp.abs(x)
    t = 1.0 / (1.0 + (0.3275911 * 0.7071067811865476) * z)
    bell = jnp.exp(-0.5 * (x * x))
    poly = t * (
        0.5 * 0.254829592
        + t
        * (
            0.5 * -0.284496736
            + t * (0.5 * 1.421413741 + t * (0.5 * -1.453152027 + t * (0.5 * 1.061405429)))
        )
    )
    tail = poly * bell
    return jnp.where(x >= 0, 1.0 - tail, tail), bell


INV_ROOT = 0.3989422804014327


def head_masks(dtype):
    lane = lax.broadcasted_iota(jnp.int32, (1, 2 * HEAD), 1)
    low = (lane < HEAD).astype(dtype)
    return (low, (1 - low.astype(WIDE)).astype(dtype))


def attn_fwd_body(x, gain, w_ref, qkv_ref, mixed_ref, peak_ref, ib):
    unit, _ = norm_parts(x)
    normed = (unit * gain).astype(NARROW)
    q = (nn(normed, w_ref[:, 0:D]).astype(NARROW).astype(WIDE) * SCALE).astype(NARROW)
    k = nn(normed, w_ref[:, D : 2 * D]).astype(NARROW)
    v = nn(normed, w_ref[:, 2 * D : 3 * D]).astype(NARROW)
    masks = head_masks(NARROW)
    cols = lax.broadcasted_iota(jnp.int32, (SP, SP), 1)
    rows = lax.broadcasted_iota(jnp.int32, (SP, 1), 0)
    head_row = lax.broadcasted_iota(jnp.int32, (HEADS, 128), 0)
    mixed_all = []
    for i in range(ib):
        peaks = jnp.full((HEADS, 128), LOWEST, WIDE)
        r = slice(i * SP, (i + 1) * SP)
        pairs = []
        for pair in range(HEADS // 2):
            c = slice(pair * 2 * HEAD, (pair + 1) * 2 * HEAD)
            qp, kp, vp = q[r, c], k[r, c], v[r, c]
            acc = None
            for half in range(2):
                s = nt(qp * masks[half], kp)
                s = jnp.where(cols < SEQ, s, LOWEST)
                top = jnp.max(s, -1, keepdims=True)
                e = jnp.exp(s - top)
                p = (e * (1.0 / jnp.sum(e, -1, keepdims=True))).astype(NARROW)
                part = nn(p, vp * masks[half])
                acc = part if acc is None else acc + part
                peak = jnp.max(jnp.where(rows < SEQ, top, LOWEST), 0, keepdims=True)
                peaks = jnp.where(head_row == pair * 2 + half, peak, peaks)
            pairs.append(acc.astype(NARROW))
        mixed_all.append(jnp.concatenate(pairs, 1))
        peak_ref[i] = peaks
    mixed = jnp.concatenate(mixed_all, 0) if ib > 1 else mixed_all[0]
    qkv_ref[...] = jnp.concatenate([q, k, v], 1).reshape(ib, SP, 3 * D)
    mixed_ref[...] = mixed.reshape(ib, SP, D)
    return x + nn(mixed, w_ref[:, 3 * D : 4 * D])


def whole(shape):
    return pl.BlockSpec(
        shape, lambda *_: (0,) * len(shape), pipeline_mode=pl.Buffered(buffer_count=1)
    )


def per_image(ib, *tail):
    return pl.BlockSpec((ib, *tail), lambda i, *_: (i,) + (0,) * len(tail))


def sds(shape, dtype):
    return jax.ShapeDtypeStruct(shape, dtype)


def cost(flops, moved):
    return pl.CostEstimate(flops=int(flops), bytes_accessed=int(moved), transcendentals=0)


def params(mib):
    return pltpu.CompilerParams(vmem_limit_bytes=mib * MIB)


def find_places(order_ref, routes_ref, pos_ref, aux_ref, line_ref):
    tokens = routes_ref.shape[1]
    order = order_ref[:, 0:1]
    chunk = 128
    strict = (
        lax.broadcasted_iota(jnp.int32, (chunk, chunk), 0)
        < lax.broadcasted_iota(jnp.int32, (chunk, chunk), 1)
    ).astype(NARROW)
    slot_row = lax.broadcasted_iota(jnp.int32, (EXPERTS, 1), 0).astype(WIDE) * CAP
    base = jnp.zeros((EXPERTS, 1), WIDE)
    pos_ref[...] = jnp.full(pos_ref.shape, -1.0, WIDE)
    line_ref[...] = jnp.zeros(line_ref.shape, WIDE)
    for k in range(2):
        for c in range(tokens // chunk):
            s = slice(c * chunk, (c + 1) * chunk)
            hit = (order == routes_ref[k : k + 1, s]).astype(WIDE)
            place = base + nn(hit.astype(NARROW), strict)
            base = base + jnp.sum(hit, -1, keepdims=True)
            pos_ref[:, s] = jnp.where(hit > 0, place, pos_ref[:, s])
            slot = jnp.where(place < CAP, slot_row + place, 2.0 * EXPERTS * CAP)
            found = jnp.sum(hit * slot, 0, keepdims=True)
            real = jnp.sum(hit, 0, keepdims=True)
            line_ref[k : k + 1, s] = jnp.where(real > 0, found, 2.0 * EXPERTS * CAP)
            line_ref[2 + k : 3 + k, s] = routes_ref[k : k + 1, s].astype(WIDE)
    for c in range(tokens // chunk):
        s = slice(c * chunk, (c + 1) * chunk)
        aux_ref[s, :] = jnp.transpose(line_ref[:, s])


def pad_images(ref, wide_ref, out_ref):
    tokens = ref.shape[0]
    wide_ref[0:tokens, :] = ref[...].astype(WIDE)
    rows = lax.broadcasted_iota(jnp.int32, (SP, 1), 0)
    for i in range(tokens // SEQ):
        image = wide_ref[i * SEQ : i * SEQ + SP, :]
        out_ref[i] = jnp.where(rows < SEQ, image, 0.0).astype(NARROW)


GROUP = 8


def slot_expert(index, groups, held):
    owners, mine = CORES * groups, held // CORES
    owner = index % owners
    return (owner % groups) * held + (owner // groups) * mine + index // owners


def dispatch_kernel(groups, held, pos_ref, moe_ref, cot_ref, prob_ref, out_ref, line_ref):
    step = pl.program_id(0)

    @pl.when(step == 0)
    def _():
        for c in range(prob_ref.shape[0] // 128):
            s = slice(c * 128, (c + 1) * 128)
            line_ref[:, s] = jnp.transpose(prob_ref[s, :])

    slot = lax.broadcasted_iota(jnp.int32, (CAP, 1), 0).astype(WIDE)
    hot, gates = [], []
    for g in range(GROUP):
        mine = pos_ref[g : g + 1, :] == slot
        hot.append(mine.astype(WIDE).astype(NARROW))
        gate_row = line_ref[pl.ds(slot_expert(step * GROUP + g, groups, held), 1), :]
        gates.append(jnp.sum(jnp.where(mine, gate_row, 0.0), -1, keepdims=True))
    hot = jnp.concatenate(hot, 0)
    rows = nn(hot, moe_ref[...]).astype(NARROW)
    grads = nn(hot, cot_ref[...])
    for g in range(GROUP):
        s = slice(g * CAP, (g + 1) * CAP)
        out_ref[g, 0:CAP, :] = rows[s]
        out_ref[g, CAP : 2 * CAP, :] = (gates[g] * grads[s]).astype(NARROW)


def dispatch(pos, moe, cot, prob, groups, held):
    tokens = moe.shape[0]
    return pl.pallas_call(
        partial(dispatch_kernel, groups, held),
        grid=(EXPERTS // GROUP,),
        in_specs=[
            pl.BlockSpec((GROUP, tokens), lambda i: (i, 0)),
            whole(moe.shape),
            whole(cot.shape),
            whole(prob.shape),
        ],
        out_specs=pl.BlockSpec((GROUP, 2 * CAP, D), lambda i: (i, 0, 0)),
        out_shape=sds((EXPERTS, 2 * CAP, D), NARROW),
        scratch_shapes=[pltpu.VMEM((128, tokens), WIDE)],
        compiler_params=params(60),
        name="dispatch",
    )(pos, moe, cot, prob)


def expert_math(slots, grads, win, wout):
    pre = nn(slots, win)
    hidden_grad = nt(grads, wout)
    cdf, bell = normal_parts(pre)
    hidden = (pre * cdf).astype(NARROW)
    pre_grad = ((cdf + pre * (bell * INV_ROOT)) * hidden_grad).astype(NARROW)
    return nn(hidden, wout), nt(pre_grad, win), tn(slots, pre_grad), tn(hidden, grads)


def expert_kernel(pick, rows_ref, win_ref, wout_ref, back_ref, din_ref, dout_ref, res, sgr):
    f = pl.program_id(0)
    senders = rows_ref.shape[0]
    part = min(senders, 8)
    count = part * CAP
    win, wout = win_ref[...], wout_ref[...]
    d_in = d_out = None
    for first in range(0, senders, part):
        slots = rows_ref[first : first + part, 0:CAP, :].reshape(count, D)
        grads = rows_ref[first : first + part, CAP : 2 * CAP, :].reshape(count, D)
        r = slice(first * CAP, (first + part) * CAP)
        result, slot_grad, in_part, out_part = expert_math(slots, grads, win, wout)
        d_in = in_part if d_in is None else d_in + in_part
        d_out = out_part if d_out is None else d_out + out_part

        @pl.when(f == 0)
        def _(r=r, result=result, slot_grad=slot_grad):
            res[r, :] = result
            sgr[r, :] = slot_grad

        @pl.when(f > 0)
        def _(r=r, result=result, slot_grad=slot_grad):
            res[r, :] += result
            sgr[r, :] += slot_grad

    din_ref[...] = d_in.astype(NARROW)
    dout_ref[...] = d_out.astype(NARROW)

    @pl.when(f == pl.num_programs(0) - 1)
    def _():
        back_ref[:, :, 0:D] = res[...].astype(NARROW).reshape(senders, CAP, D)
        back_ref[:, :, D : 2 * D] = sgr[...].astype(NARROW).reshape(senders, CAP, D)


def expert(pick, rows, win, wout):
    senders = rows.shape[0]
    wide = 512
    return pl.pallas_call(
        expert_kernel,
        grid_spec=pltpu.PrefetchScalarGridSpec(
            num_scalar_prefetch=1,
            grid=(FF // wide,),
            in_specs=[
                whole(rows.shape),
                pl.BlockSpec((None, D, wide), lambda f, p: (p[0], 0, f)),
                pl.BlockSpec((None, wide, D), lambda f, p: (p[0], f, 0)),
            ],
            out_specs=[
                whole((senders, CAP, 2 * D)),
                pl.BlockSpec((None, D, wide), lambda f, p: (f, 0, 0)),
                pl.BlockSpec((None, wide, D), lambda f, p: (f, 0, 0)),
            ],
            scratch_shapes=[
                pltpu.VMEM((senders * CAP, D), WIDE),
                pltpu.VMEM((senders * CAP, D), WIDE),
            ],
        ),
        out_shape=[
            sds((senders, CAP, 2 * D), NARROW),
            sds((FF // wide, D, wide), NARROW),
            sds((FF // wide, wide, D), NARROW),
        ],
        compiler_params=params(60),
        cost_estimate=cost(5e9, 1),
        name="one_expert",
    )(pick, rows, win, wout)


def attn_bwd_body(x, incoming, gain, qkv_ref, mixed_ref, w_ref, dw_ref, ib):
    unit, inverse = norm_parts(x)
    normed = (unit * gain).astype(NARROW)
    out_grad = incoming.astype(NARROW)
    mixed = mixed_ref[...].reshape(ib * SP, D)
    dw_ref[:, 3 * D : 4 * D] += tn(mixed, out_grad)
    mixed_grad = nt(out_grad, w_ref[:, 3 * D : 4 * D]).astype(NARROW)
    masks = head_masks(NARROW)
    rows = lax.broadcasted_iota(jnp.int32, (SP, SP), 0)
    dq_all, dk_all, dv_all = [], [], []
    for i in range(ib):
        r = slice(i * SP, (i + 1) * SP)
        dqs, dks, dvs = [], [], []
        for pair in range(HEADS // 2):
            qp = qkv_ref[i, :, pair * 128 : (pair + 1) * 128]
            kp = qkv_ref[i, :, D + pair * 128 : D + (pair + 1) * 128]
            vp = qkv_ref[i, :, 2 * D + pair * 128 : 2 * D + (pair + 1) * 128]
            mp = mixed_grad[r, pair * 128 : (pair + 1) * 128]
            dq = dk = dv = None
            for half in range(2):
                qm, mm, km = qp * masks[half], mp * masks[half], kp * masks[half]
                s = jnp.where(rows < SEQ, nt(kp, qm), LOWEST)
                e = jnp.exp(s - jnp.max(s, 0, keepdims=True))
                soft = e * (1.0 / jnp.sum(e, 0, keepdims=True))
                pg = nt(vp, mm)
                delta = jnp.sum(soft * pg, 0, keepdims=True)
                sg = (soft * (pg - delta)).astype(NARROW)
                v_part = nn(soft.astype(NARROW), mm)
                k_part = nn(sg, qm)
                q_part = tn(sg, km)
                dq = q_part if dq is None else dq + q_part
                dk = k_part if dk is None else dk + k_part
                dv = v_part if dv is None else dv + v_part
            dqs.append((dq * SCALE).astype(NARROW))
            dks.append(dk.astype(NARROW))
            dvs.append(dv.astype(NARROW))
        dq_all.append(jnp.concatenate(dqs, 1))
        dk_all.append(jnp.concatenate(dks, 1))
        dv_all.append(jnp.concatenate(dvs, 1))
    dqkv = jnp.concatenate(
        [
            jnp.concatenate(a, 0) if ib > 1 else a[0]
            for a in (dq_all, dk_all, dv_all)
        ],
        1,
    )
    dw_ref[:, 0 : 3 * D] += tn(normed, dqkv)
    normed_grad = nt(dqkv, w_ref[:, 0 : 3 * D])
    input_grad, gain_grad = norm_backward(normed_grad, unit, inverse, gain)
    return incoming + input_grad, gain_grad


def gain_columns(dg_ref):
    tall = jnp.concatenate(
        [jnp.zeros((EXPERTS, D), WIDE), dg_ref[...], jnp.zeros((128 - EXPERTS - 8, D), WIDE)], 0
    )
    return jnp.transpose(tall)


def put_rows(ref, step, ib, value):
    for image in range(ref.shape[0] // SEQ):

        @pl.when(step == image // ib)
        def _(image=image):
            first = image % ib * SP
            ref[image * SEQ : (image + 1) * SEQ, :] = value[first : first + SEQ]


def moe_bwd_kernel(
    ib,
    g_ref,
    w_ref,
    wr_ref,
    mid_ref,
    second_ref,
    cot_ref,
    prob_ref,
    aux_ref,
    qkv_ref,
    mixed_ref,
    table_ref,
    y_ref,
    grad_ref,
    dw_out,
    dr_ref,
    dg_ref,
    dw_ref,
):
    step = pl.program_id(0)

    @pl.when(step == 0)
    def _():
        dw_ref[...] = jnp.zeros(dw_ref.shape, WIDE)
        dr_ref[...] = jnp.zeros(dr_ref.shape, WIDE)
        dg_ref[...] = jnp.zeros(dg_ref.shape, WIDE)

    second = second_ref[...].reshape(ib * SP, D)
    upstream = cot_ref[...].astype(WIDE).reshape(ib * SP, D)
    prob = prob_ref[...].reshape(ib * SP, 128)
    aux = aux_ref[...].reshape(ib * SP, 128)
    first_pick = second_pick = back = None
    for j in range(table_ref.shape[0]):
        count = table_ref.shape[1] * CAP
        slot = lax.broadcasted_iota(jnp.int32, (1, count), 1).astype(WIDE) + float(j * count)
        hot_one = (aux[:, 0:1] == slot).astype(WIDE).astype(NARROW)
        hot_two = (aux[:, 1:2] == slot).astype(WIDE).astype(NARROW)
        rows = table_ref[j].reshape(count, 2 * D)
        one = nn(hot_one, rows[:, 0:D])
        two = nn(hot_two, rows[:, 0:D])
        both = nn(hot_one + hot_two, rows[:, D : 2 * D])
        first_pick = one if first_pick is None else first_pick + one
        second_pick = two if second_pick is None else second_pick + two
        back = both if back is None else back + both
    lane = lax.broadcasted_iota(jnp.int32, (1, 128), 1)
    first_hit = (aux[:, 2:3] == lane.astype(WIDE)).astype(WIDE)
    second_hit = (aux[:, 3:4] == lane.astype(WIDE)).astype(WIDE)
    gate_one = jnp.sum(prob * first_hit, -1, keepdims=True)
    gate_two = jnp.sum(prob * second_hit, -1, keepdims=True)
    put_rows(y_ref, step, ib, second + (gate_one * first_pick + gate_two * second_pick))
    gate_one_grad = jnp.sum(upstream * first_pick, -1, keepdims=True)
    gate_two_grad = jnp.sum(upstream * second_pick, -1, keepdims=True)
    prob_grad = gate_one_grad * first_hit + gate_two_grad * second_hit
    logit_grad = (prob * (prob_grad - jnp.sum(prob * prob_grad, -1, keepdims=True))).astype(NARROW)
    unit, inverse = norm_parts(second)
    gain = g_ref[3:4, :]
    moe = (unit * gain).astype(NARROW)
    dr_ref[...] += tn(moe, logit_grad)
    normed_grad = back + nt(logit_grad, wr_ref[...])
    moe_grad, gain_grad = norm_backward(normed_grad, unit, inverse, gain)
    dg_ref[3:4, :] += gain_grad
    mid = mid_ref[...].reshape(ib * SP, D)
    grad, gain_grad = attn_bwd_body(
        mid, upstream + moe_grad, g_ref[1:2, :], qkv_ref, mixed_ref, w_ref, dw_ref, ib
    )
    dg_ref[1:2, :] += gain_grad
    grad_ref[...] = grad.reshape(ib, SP, D)

    @pl.when(step == pl.num_programs(0) - 1)
    def _():
        dw_out[:, : 4 * D] = dw_ref[...].astype(NARROW)
        dw_out[:, 4 * D :] = (dr_ref[...] + gain_columns(dg_ref)).astype(NARROW)


def moe_bwd(gains, w1, wr, mid, second, cot, prob, aux, qkv, mixed, tables, images, ib):
    return pl.pallas_call(
        partial(moe_bwd_kernel, ib),
        grid=(images // ib,),
        in_specs=[
            whole(gains.shape),
            whole(w1.shape),
            whole(wr.shape),
            per_image(ib, SP, D),
            per_image(ib, SP, D),
            per_image(ib, SP, D),
            per_image(ib, SP, 128),
            per_image(ib, SP, 128),
            per_image(ib, SP, 3 * D),
            per_image(ib, SP, D),
            whole(tables.shape),
        ],
        out_specs=[
            whole((images * SEQ, D)),
            per_image(ib, SP, D),
            whole((D, 4 * D + 128)),
        ],
        out_shape=[
            sds((images * SEQ, D), WIDE),
            sds((images, SP, D), WIDE),
            sds((D, 4 * D + 128), NARROW),
        ],
        scratch_shapes=[
            pltpu.VMEM((D, 128), WIDE),
            pltpu.VMEM((8, D), WIDE),
            pltpu.VMEM((D, 4 * D), WIDE),
        ],
        compiler_params=params(60),
        cost_estimate=cost(1e6, 1),
        name="expert_block_backward",
    )(gains, w1, wr, mid, second, cot, prob, aux, qkv, mixed, tables)


def dense_bwd_kernel(
    ib,
    g_ref,
    w_ref,
    win_ref,
    wout_ref,
    x_ref,
    first_ref,
    grad_ref,
    qkv_ref,
    mixed_ref,
    out_ref,
    dw_out,
    dout_out,
    dg_ref,
    dw_ref,
    din_ref,
    dout_ref,
):
    step = pl.program_id(0)

    @pl.when(step == 0)
    def _():
        dw_ref[...] = jnp.zeros(dw_ref.shape, WIDE)
        din_ref[...] = jnp.zeros(din_ref.shape, WIDE)
        dout_ref[...] = jnp.zeros(dout_ref.shape, WIDE)
        dg_ref[...] = jnp.zeros(dg_ref.shape, WIDE)

    incoming = grad_ref[...].reshape(ib * SP, D)
    first = first_ref[...].reshape(ib * SP, D)
    unit, inverse = norm_parts(first)
    gain = g_ref[2:3, :]
    normed = (unit * gain).astype(NARROW)
    out_grad = incoming.astype(NARROW)
    y_grad = None
    for f in range(FF // 512):
        c = slice(f * 512, (f + 1) * 512)
        win, wout = win_ref[:, c], wout_ref[c, :]
        pre = nn(normed, win)
        hidden_grad = nt(out_grad, wout)
        cdf, bell = normal_parts(pre)
        hidden = (pre * cdf).astype(NARROW)
        pre_grad = ((cdf + pre * (bell * INV_ROOT)) * hidden_grad).astype(NARROW)
        dout_ref[c, :] += tn(hidden, out_grad)
        din_ref[:, c] += tn(normed, pre_grad)
        part = nt(pre_grad, win)
        y_grad = part if y_grad is None else y_grad + part
    ffn_grad, gain_grad = norm_backward(y_grad, unit, inverse, gain)
    dg_ref[2:3, :] += gain_grad
    x = x_ref[...].astype(WIDE).reshape(ib * SP, D)
    grad, gain_grad = attn_bwd_body(
        x, incoming + ffn_grad, g_ref[0:1, :], qkv_ref, mixed_ref, w_ref, dw_ref, ib
    )
    dg_ref[0:1, :] += gain_grad
    put_rows(out_ref, step, ib, grad)

    @pl.when(step == pl.num_programs(0) - 1)
    def _():
        dw_out[:, : 4 * D] = dw_ref[...].astype(NARROW)
        dw_out[:, 4 * D : 8 * D] = din_ref[...].astype(NARROW)
        dw_out[:, 8 * D :] = gain_columns(dg_ref).astype(NARROW)
        dout_out[...] = dout_ref[...].astype(NARROW)


def dense_bwd(gains, w0, win, wout, x, first, grad, qkv, mixed, images, ib):
    return pl.pallas_call(
        partial(dense_bwd_kernel, ib),
        grid=(images // ib,),
        in_specs=[
            whole(gains.shape),
            whole(w0.shape),
            whole(win.shape),
            whole(wout.shape),
            per_image(ib, SP, D),
            per_image(ib, SP, D),
            per_image(ib, SP, D),
            per_image(ib, SP, 3 * D),
            per_image(ib, SP, D),
        ],
        out_specs=[
            whole((images * SEQ, D)),
            whole((D, 8 * D + 128)),
            whole((FF, D)),
        ],
        out_shape=[
            sds((images * SEQ, D), WIDE),
            sds((D, 8 * D + 128), NARROW),
            sds((FF, D), NARROW),
        ],
        scratch_shapes=[
            pltpu.VMEM((8, D), WIDE),
            pltpu.VMEM((D, 4 * D), WIDE),
            pltpu.VMEM((D, FF), WIDE),
            pltpu.VMEM((FF, D), WIDE),
        ],
        compiler_params=params(60),
        cost_estimate=cost(1e6, 1),
        name="dense_block_backward",
    )(gains, w0, win, wout, x, first, grad, qkv, mixed)


BLOCK = 512
MESH_ID = pl.DeviceIdType.MESH


def add_rows(out, one, two, rows, step):
    @pl.loop(0, rows // step)
    def _(i):
        r = pl.ds(pl.multiple_of(i * step, step), step)
        out[r, :] = (one[r, :].astype(WIDE) + two[r, :].astype(WIDE)).astype(out.dtype)


def sum_kernel(nz, groups, mats, slices, first, handed, *refs):
    exp_refs, refs = refs[:mats], refs[mats:]
    dense_refs, peak_ref, refs = refs[:3], refs[3], refs[4:]
    if handed:
        _, hand_ref, refs = refs[0], refs[1], refs[2:]
    exp_out, dense_outs, peak_out, refs = refs[0], refs[1:4], refs[4], refs[5:]
    if handed:
        hand_buf, hand_sem, refs = refs[-2], refs[-1], refs[:-2]
    own, up, down, refs = refs[0], refs[1], refs[2], refs[3:]
    land, refs = refs[:4], refs[4:]
    dense_own, refs = refs[:4], refs[4:]
    dense_up, refs = refs[:4], refs[4:]
    dense_down, refs = refs[:4], refs[4:]
    (own_sem, up_send, up_recv, down_recv, out_send, sib_send, sib_recv, copy_sem, rs_send, rs_recv) = refs

    z, core, f = lax.axis_index("z"), lax.axis_index("core"), lax.axis_index("fsdp")
    half = nz // 2
    left = z < half
    inner = jnp.where(left, z + 1, z - 1)
    outer = jnp.where(left, z - 1, z + 1)
    has_outer = jnp.logical_and(z > 0, z < nz - 1)
    edge = jnp.logical_not(has_outer)
    center = jnp.logical_or(z == half - 1, z == half)
    away = jnp.logical_not(center)
    outer = jnp.where(has_outer, outer, inner)
    sibling = (z, 1 - core, f)
    members = CORES * groups
    me = core * groups + f

    barrier = pltpu.get_barrier_semaphore()
    pl.semaphore_signal(barrier, inc=1, device_id=(inner, core, f), device_id_type=MESH_ID)

    @pl.when(has_outer)
    def _():
        pl.semaphore_signal(barrier, inc=1, device_id=(outer, core, f), device_id_type=MESH_ID)

    for d in range(1, members):
        there = lax.rem(me + d, members)
        pl.semaphore_signal(
            barrier,
            inc=1,
            device_id=(z, there // groups, lax.rem(there, groups)),
            device_id_type=MESH_ID,
        )

    @pl.when(has_outer)
    def _():
        pl.semaphore_wait(barrier, members + 1)

    @pl.when(edge)
    def _():
        pl.semaphore_wait(barrier, members)

    chunks = mats * slices
    items = chunks + 4

    def piece(n, ref, there):
        if n == 3:
            return ref
        rows = ref.shape[0] // members
        place = (lax.rem(there, groups) * CORES + there // groups) * rows
        return ref.at[pl.ds(pl.multiple_of(place, 16), rows), :]

    def scatter(n, d):
        there = lax.rem(me + d, members)
        source = dense_refs[n] if n < 3 else peak_ref
        return pltpu.make_async_remote_copy(
            src_ref=piece(n, source, there),
            dst_ref=land[n].at[d],
            send_sem=rs_send.at[n, d],
            recv_sem=rs_recv.at[n, d],
            device_id=(z, there // groups, lax.rem(there, groups)),
            device_id_type=MESH_ID,
        )

    def hand():
        return pltpu.make_async_remote_copy(
            src_ref=hand_buf,
            dst_ref=exp_out.at[pl.ds(first - handed, handed), core],
            send_sem=hand_sem.at[0],
            recv_sem=hand_sem.at[1],
            device_id=sibling,
            device_id_type=MESH_ID,
        )

    if handed:
        arrived = pltpu.make_async_copy(hand_ref, hand_buf, hand_sem.at[2])
        arrived.start()
        arrived.wait()
        handed_here = pltpu.make_async_copy(
            hand_buf, exp_out.at[pl.ds(first - handed, handed), core], hand_sem.at[2]
        )
        handed_here.start()
        hand().start()
    for n in (3, 1, 0, 2):
        for d in range(1, members):
            scatter(n, d).start()
    keep = [
        pltpu.make_async_copy(
            piece(n, dense_refs[n] if n < 3 else peak_ref, me), land[n].at[0], rs_recv.at[n, 0]
        )
        for n in range(4)
    ]
    for k in keep:
        k.start()

    def load(t):
        return pltpu.make_async_copy(exp_refs[t // slices].at[t % slices], own.at[t], own_sem.at[t])

    @pl.when(has_outer)
    def _():
        for t in range(chunks):
            load(t).start()

    def bufs(t):
        if t < chunks:
            return own.at[t], up.at[t], down.at[t]
        n = t - chunks
        return dense_own[n], dense_up[n], dense_down[n]

    def send_up(t, source, to_center):
        _, u, dn = bufs(t)
        return pltpu.make_async_remote_copy(
            src_ref=source,
            dst_ref=dn if to_center else u,
            send_sem=up_send.at[t],
            recv_sem=(down_recv if to_center else up_recv).at[t],
            device_id=(inner, core, f),
            device_id_type=MESH_ID,
        )

    def source_at_edge(t):
        return exp_refs[t // slices].at[t % slices] if t < chunks else bufs(t)[0]

    def join(t, out, one, two):
        if t == items - 1:
            out[...] = jnp.maximum(one[...], two[...])
        else:
            add_rows(out, one, two, out.shape[0], 16)

    def reduce_own(n):
        for d in range(members):
            if d == 0:
                keep[n].wait()
            else:
                scatter(n, d).wait_recv()
        if n == 3:
            best = land[n][0]
            for d in range(1, members):
                best = jnp.maximum(best, land[n][d])
            dense_own[n][...] = best
            return

        @pl.loop(0, dense_own[n].shape[0] // 16)
        def _(i):
            r = pl.ds(pl.multiple_of(i * 16, 16), 16)
            total = land[n][0, r, :].astype(WIDE)
            for d in range(1, members):
                total = total + land[n][d, r, :].astype(WIDE)
            dense_own[n][r, :] = total.astype(NARROW)

    def up_from_edge(t, before):
        if before is not None:
            send_up(before, source_at_edge(before), half == 1).wait_send()
        if t >= chunks:
            reduce_own(t - chunks)
        send_up(t, source_at_edge(t), half == 1).start()

    def up_from_inside(t):
        o, u, _ = bufs(t)
        if t >= chunks:
            reduce_own(t - chunks)
        else:
            load(t).wait()
        send_up(t, u, False).wait_recv()
        join(t, o, o, u)

        @pl.when(center)
        def _():
            send_up(t, o, True).start()

        if half > 2:

            @pl.when(away)
            def _():
                send_up(t, o, False).start()

    def results(t):
        if t < chunks:
            return exp_out.at[first + t, core]
        n = t - chunks
        if n == 3:
            return peak_out
        ref = dense_outs[n]
        rows = ref.shape[0] // CORES
        return ref.at[pl.ds(pl.multiple_of(core * rows, 16), rows), :]

    def to_sibling(t):
        return pltpu.make_async_remote_copy(
            src_ref=bufs(t)[2],
            dst_ref=results(t),
            send_sem=sib_send.at[t],
            recv_sem=sib_recv.at[t],
            device_id=sibling,
            device_id_type=MESH_ID,
        )

    def to_outer(t):
        dn = bufs(t)[2]
        return pltpu.make_async_remote_copy(
            src_ref=dn,
            dst_ref=dn,
            send_sem=out_send.at[t],
            recv_sem=down_recv.at[t],
            device_id=(outer, core, f),
            device_id_type=MESH_ID,
        )

    def keep_result(t):
        return pltpu.make_async_copy(bufs(t)[2], results(t), copy_sem.at[t])

    def go_down(t, at_edge):
        o, _, dn = bufs(t)
        to_outer(t).wait_recv()
        if at_edge:
            if half == 1:
                join(t, dn, source_at_edge(t), dn)
        else:

            @pl.when(center)
            def _():
                join(t, dn, o, dn)

            to_outer(t).start()
        keep_result(t).start()
        if t < items - 1:
            to_sibling(t).start()

    early = min(8, chunks)
    sequence = [*range(early), *range(items - 1, chunks - 1, -1), *range(early, chunks)]

    def run(up, at_edge, lag):
        for i in range(items + lag):
            if i < items:
                up(i)
            if i >= lag:
                go_down(sequence[i - lag], at_edge)

    @pl.when(edge)
    def _():
        run(
            lambda i: up_from_edge(sequence[i], sequence[i - 2] if i >= 2 else None),
            True,
            min(7, items),
        )
        for t in sequence[-2:]:
            send_up(t, source_at_edge(t), half == 1).wait_send()

    if half > 1:

        @pl.when(has_outer)
        def _():
            run(lambda i: up_from_inside(sequence[i]), False, 1)
            for t in range(items):
                send_up(t, bufs(t)[0], False).wait_send()
                to_outer(t).wait_send()

    for n in range(4):
        for d in range(1, members):
            scatter(n, d).wait_send()
    if handed:
        hand().wait()
        handed_here.wait()
    for t in range(items):
        keep_result(t).wait()
        if t < items - 1:
            to_sibling(t).wait()


def sum_all(mats, dense, peaks, early, handed, nz, groups):
    slices = mats[0].shape[0]
    chunks = len(mats) * slices
    members = CORES * groups
    items = chunks + 4
    any_space = pl.BlockSpec(memory_space=pl.ANY)
    vmem = pl.BlockSpec(memory_space=pltpu.VMEM)
    pieces = [(a.shape[0] // members, a.shape[1]) for a in dense]
    block = pltpu.VMEM((chunks, BLOCK, BLOCK), NARROW)

    def four(lead=()):
        return [pltpu.VMEM((*lead, *p), NARROW) for p in pieces] + [
            pltpu.VMEM((*lead, *peaks.shape), WIDE)
        ]

    dma = pltpu.SemaphoreType.DMA
    extra = [] if handed is None else [early, handed]
    count = handed.shape[0] if extra else 0
    first = early.shape[0] - chunks if extra else 0
    return pl.pallas_call(
        partial(sum_kernel, nz, groups, len(mats), slices, first, count),
        in_specs=[any_space] * (len(mats) + 3) + [vmem] + [any_space] * len(extra),
        out_specs=[any_space] * 4 + [vmem],
        out_shape=[
            sds((first + chunks, CORES, BLOCK, BLOCK), NARROW),
            *[sds((CORES * r, c), NARROW) for r, c in pieces],
            sds(peaks.shape, WIDE),
        ],
        scratch_shapes=[
            block,
            block,
            block,
            *four((members,)),
            *four(),
            *four(),
            *four(),
            *[dma((items,)) for _ in range(8)],
            dma((4, members)),
            dma((4, members)),
            *([pltpu.VMEM(handed.shape, NARROW), dma((3,))] if extra else []),
        ],
        compiler_params=pltpu.CompilerParams(
            vmem_limit_bytes=58 * MIB, collective_id=3, has_side_effects=True
        ),
        input_output_aliases={len(mats) + 4: 0} if extra else {},
        name="sums",
    )(*mats, *dense, peaks, *extra)


SUMMED = 12
LAGS = (2, 4, 6)
BESIDE = 8


def exchange_kernel(nz, groups, mine, *refs):
    (sent_ref, win_hbm, wout_hbm, table_out, sum_out, beside_out, rest_out) = refs[:7]
    (rows, back, res, sgr, w_in, w_out, own, up, down, made) = refs[7:17]
    (d_send, d_recv, r_send, r_recv, w_sem, made_sem, up_send, up_recv, down_recv) = refs[17:26]
    (out_send, sib_send, sib_recv, keep_sem) = refs[26:]
    s = pl.program_id(0)
    z, core, f = lax.axis_index("z"), lax.axis_index("core"), lax.axis_index("fsdp")
    members = CORES * groups
    me = core * groups + f
    parts = FF // BLOCK
    steps = mine * parts
    last = pl.num_programs(0) - 1
    left = z < nz // 2
    inner = jnp.where(left, z + 1, z - 1)
    has_outer = jnp.logical_and(z > 0, z < nz - 1)
    edge = jnp.logical_not(has_outer)
    outer = jnp.where(has_outer, jnp.where(left, z - 1, z + 1), inner)

    def member(d):
        there = lax.rem(me + d, members)
        return there, (z, there // groups, lax.rem(there, groups))

    def rows_to(j, d):
        there, device = member(d)
        return pltpu.make_async_remote_copy(
            src_ref=sent_ref.at[j, there],
            dst_ref=rows.at[j, me],
            send_sem=d_send.at[j, d],
            recv_sem=d_recv.at[j, d],
            device_id=device,
            device_id_type=MESH_ID,
        )

    def rows_here(j):
        return pltpu.make_async_copy(sent_ref.at[j, me], rows.at[j, me], d_recv.at[j, 0])

    def send_rows(j):
        for d in range(1, members):
            rows_to(j, d).start()
        rows_here(j).start()

    def results_to(j, d):
        there, device = member(d)
        return pltpu.make_async_remote_copy(
            src_ref=back.at[j % 2, there],
            dst_ref=table_out.at[j, me],
            send_sem=r_send.at[j, d],
            recv_sem=r_recv.at[j, d],
            device_id=device,
            device_id_type=MESH_ID,
        )

    def results_here(j):
        return pltpu.make_async_copy(back.at[j % 2, me], table_out.at[j, me], r_recv.at[j, 0])

    def weights(step):
        e = core * mine + step // parts
        c = pl.ds(pl.multiple_of(lax.rem(step, parts) * BLOCK, BLOCK), BLOCK)
        slot = lax.rem(step, 2)
        return (
            pltpu.make_async_copy(win_hbm.at[e, :, c], w_in.at[slot], w_sem.at[0, slot]),
            pltpu.make_async_copy(wout_hbm.at[e, c, :], w_out.at[slot], w_sem.at[1, slot]),
        )

    @pl.when(s == 0)
    def _():
        barrier = pltpu.get_barrier_semaphore()
        pl.semaphore_signal(barrier, inc=1, device_id=(inner, core, f), device_id_type=MESH_ID)

        @pl.when(has_outer)
        def _():
            pl.semaphore_signal(barrier, inc=1, device_id=(outer, core, f), device_id_type=MESH_ID)

        for d in range(1, members):
            pl.semaphore_signal(barrier, inc=1, device_id=member(d)[1], device_id_type=MESH_ID)

        @pl.when(has_outer)
        def _():
            pl.semaphore_wait(barrier, members + 1)

        @pl.when(edge)
        def _():
            pl.semaphore_wait(barrier, members)

        send_rows(0)
        for w in weights(s):
            w.start()

    for j in range(mine):

        @pl.when(s == j * parts)
        def _(j=j):
            for d in range(1, members):
                rows_to(j, d).wait_recv()
            rows_here(j).wait()
            if j == 0:
                send_rows(1)
            if j == 1:
                send_rows(3)

    slot = lax.rem(s, 2)

    def made_to(step, side, near):
        place = 2 * step + side - SUMMED - (0 if near else BESIDE)
        there = lax.rem(step, 2)
        out = beside_out if near else rest_out
        return pltpu.make_async_copy(
            made.at[there, side],
            out.at[jnp.clip(place, 0, out.shape[0] - 1)],
            made_sem.at[there, side],
        )

    def each_made(step, act):
        near = step < (SUMMED + BESIDE) // 2

        @pl.when(near)
        def _():
            for side in range(2):
                act(made_to(step, side, True))

        @pl.when(jnp.logical_not(near))
        def _():
            for side in range(2):
                act(made_to(step, side, False))

    @pl.when(s < steps)
    def _():
        for w in weights(s):
            w.wait()

        @pl.when(s + 1 < steps)
        def _():
            for w in weights(s + 1):
                w.start()

        @pl.when(jnp.logical_and(s >= SUMMED // 2 + 2, s < steps))
        def _():
            each_made(s - 2, lambda copy: copy.wait())

        j = s // parts
        part = lax.rem(s, parts)
        count = members * CAP
        slots = rows[j, :, 0:CAP, :].reshape(count, D)
        grads = rows[j, :, CAP : 2 * CAP, :].reshape(count, D)
        result, slot_grad, d_in, d_out = expert_math(slots, grads, w_in[slot], w_out[slot])

        @pl.when(part == 0)
        def _():
            res[...] = result
            sgr[...] = slot_grad

        @pl.when(part > 0)
        def _():
            res[...] += result
            sgr[...] += slot_grad

        @pl.when(s < SUMMED // 2)
        def _():
            own[2 * s] = d_in.astype(NARROW)
            own[2 * s + 1] = d_out.astype(NARROW)

        @pl.when(s >= SUMMED // 2)
        def _():
            made[slot, 0] = d_in.astype(NARROW)
            made[slot, 1] = d_out.astype(NARROW)

            each_made(s, lambda copy: copy.start())

    @pl.when(s == 1)
    def _():
        send_rows(2)

    for j in range(mine):

        @pl.when(s == (j + 1) * parts - 1)
        def _(j=j):
            if j >= 2:
                for d in range(1, members):
                    results_to(j - 2, d).wait_send()
                results_here(j - 2).wait()
            back[j % 2, :, :, 0:D] = res[...].astype(NARROW).reshape(members, CAP, D)
            back[j % 2, :, :, D : 2 * D] = sgr[...].astype(NARROW).reshape(members, CAP, D)
            for d in range(1, members):
                results_to(j, d).start()
            results_here(j).start()

    def send_up(t, to_center):
        return pltpu.make_async_remote_copy(
            src_ref=own.at[t],
            dst_ref=(down if to_center else up).at[t],
            send_sem=up_send.at[t],
            recv_sem=(down_recv if to_center else up_recv).at[t],
            device_id=(inner, core, f),
            device_id_type=MESH_ID,
        )

    def send_out(t):
        return pltpu.make_async_remote_copy(
            src_ref=down.at[t],
            dst_ref=down.at[t],
            send_sem=out_send.at[t],
            recv_sem=down_recv.at[t],
            device_id=(outer, core, f),
            device_id_type=MESH_ID,
        )

    def to_sibling(t):
        return pltpu.make_async_remote_copy(
            src_ref=down.at[t],
            dst_ref=sum_out.at[t, core],
            send_sem=sib_send.at[t],
            recv_sem=sib_recv.at[t],
            device_id=(z, 1 - core, f),
            device_id_type=MESH_ID,
        )

    def keep_sum(t):
        return pltpu.make_async_copy(down.at[t], sum_out.at[t, core], keep_sem.at[t])

    def at(lag, role):
        t = s - lag
        return pl.when(jnp.logical_and(role, jnp.logical_and(t >= 0, t < SUMMED)))

    def tick(t):
        return jnp.clip(t, 0, SUMMED - 1)

    @at(0, edge)
    def _():
        send_up(tick(s), False).start()

    @at(LAGS[0], has_outer)
    def _():
        t = tick(s - LAGS[0])
        send_up(t, False).wait_recv()
        add_rows(own.at[t], own.at[t], up.at[t], BLOCK, 16)
        send_up(t, True).start()

    @at(LAGS[1], has_outer)
    def _():
        t = tick(s - LAGS[1])
        send_out(t).wait_recv()
        add_rows(down.at[t], own.at[t], down.at[t], BLOCK, 16)
        send_out(t).start()
        keep_sum(t).start()
        to_sibling(t).start()

    @at(LAGS[2], edge)
    def _():
        t = tick(s - LAGS[2])
        send_out(t).wait_recv()
        keep_sum(t).start()
        to_sibling(t).start()

    @pl.when(s == last)
    def _():
        for step in (steps - 2, steps - 1):
            for side in range(2):
                made_to(step, side, False).wait()
        for j in range(mine):
            for d in range(1, members):
                rows_to(j, d).wait_send()
                results_to(j, d).wait_recv()
                if j >= mine - 2:
                    results_to(j, d).wait_send()
            if j >= mine - 2:
                results_here(j).wait()

        for t in range(SUMMED):
            send_up(t, False).wait_send()
            keep_sum(t).wait()
            to_sibling(t).wait()

        @pl.when(has_outer)
        def _():
            for t in range(SUMMED):
                send_out(t).wait_send()


def exchange(sent, win, wout, nz, groups):
    mine, members = sent.shape[0], sent.shape[1]
    steps = mine * (FF // BLOCK)
    rest = 2 * steps - SUMMED - BESIDE
    any_space = pl.BlockSpec(memory_space=pl.ANY)
    dma = pltpu.SemaphoreType.DMA
    block = pltpu.VMEM((SUMMED, BLOCK, BLOCK), NARROW)
    return pl.pallas_call(
        partial(exchange_kernel, nz, groups, mine),
        grid=(max(steps, SUMMED + LAGS[2]),),
        in_specs=[any_space] * 3,
        out_specs=[any_space] * 4,
        out_shape=[
            sds((mine, members, CAP, 2 * D), NARROW),
            sds((2 * steps, CORES, BLOCK, BLOCK), NARROW),
            sds((BESIDE, BLOCK, BLOCK), NARROW),
            sds((rest, BLOCK, BLOCK), NARROW),
        ],
        scratch_shapes=[
            pltpu.VMEM((mine, members, 2 * CAP, D), NARROW),
            pltpu.VMEM((2, members, CAP, 2 * D), NARROW),
            pltpu.VMEM((members * CAP, D), WIDE),
            pltpu.VMEM((members * CAP, D), WIDE),
            pltpu.VMEM((2, D, BLOCK), NARROW),
            pltpu.VMEM((2, BLOCK, D), NARROW),
            block,
            block,
            block,
            pltpu.VMEM((2, 2, BLOCK, BLOCK), NARROW),
            *[dma((mine, members)) for _ in range(4)],
            dma((2, 2)),
            dma((2, 2)),
            *[dma((SUMMED,)) for _ in range(7)],
        ],
        compiler_params=pltpu.CompilerParams(
            vmem_limit_bytes=58 * MIB, collective_id=7, has_side_effects=True
        ),
        name="experts",
    )(sent, win, wout)


def finish_small(refs):
    (wide_ref, deep_ref, out_ref, peak_ref, limit_ref, query_ref, key_ref) = refs[:7]
    (gain_out, q_out, k_out, v_out, o_out, ffn_out, in_out, mlp_out, router_out, cq_out, ck_out) = refs[7:]
    for n, ref in enumerate((q_out, k_out, v_out, o_out)):
        c = slice(n * D, (n + 1) * D)
        ref[0] = wide_ref[:, c].astype(WIDE)
        ref[1] = deep_ref[:, c].astype(WIDE)
    in_out[...] = wide_ref[:, 4 * D : 8 * D].astype(WIDE)
    mlp_out[...] = out_ref[...].astype(WIDE)
    small = deep_ref[:, 4 * D :].astype(WIDE) + wide_ref[:, 8 * D :].astype(WIDE)
    router_out[...] = small[:, :EXPERTS]
    count = small.shape[0]
    if count < 128:
        small = jnp.concatenate([small, jnp.zeros((128 - count, 128), WIDE)], 0)
    turned = jnp.transpose(small)
    gain_out[...] = turned[EXPERTS : EXPERTS + 2, :count]
    ffn_out[...] = turned[EXPERTS + 2 : EXPERTS + 4, :count]
    head = lax.broadcasted_iota(jnp.int32, (HEADS, D), 0)
    feature = lax.broadcasted_iota(jnp.int32, (HEADS, D), 1)
    owns = jnp.logical_and(feature >= head * HEAD, feature < (head + 1) * HEAD)
    for layer in range(2):
        limit = limit_ref[:, layer : layer + 1]
        top = peak_ref[:, layer * 64 : layer * 64 + 1]
        scale = jnp.sqrt(limit / jnp.maximum(top, limit))
        row = jnp.sum(jnp.where(owns, scale, 0.0), 0, keepdims=True)
        cq_out[layer] = query_ref[layer] * row
        ck_out[layer] = key_ref[layer] * row


def finish_kernel(blocks_ref, *refs):
    small, (in_ref, out_ref) = refs[:-2], refs[-2:]

    @pl.when(jnp.logical_and(pl.program_id(0) == 0, pl.program_id(1) == 0))
    def _():
        finish_small(small)

    for n in range(FF // BLOCK):
        r = slice(n * BLOCK, (n + 1) * BLOCK)
        in_ref[:, r] = blocks_ref[n, 0].astype(WIDE)
        out_ref[r, :] = blocks_ref[n, 1].astype(WIDE)


def finish(blocks, mine, small, outs):
    parts = FF // BLOCK
    return pl.pallas_call(
        finish_kernel,
        grid=(CORES, mine),
        in_specs=[
            pl.BlockSpec((parts, 2, None, BLOCK, BLOCK), lambda c, j: (j, 0, c, 0, 0)),
            *[whole(a.shape) for a in small],
        ],
        out_specs=[whole(o.shape) for o in outs]
        + [
            pl.BlockSpec((None, D, FF), lambda c, j: (c * mine + j, 0, 0)),
            pl.BlockSpec((None, FF, D), lambda c, j: (c * mine + j, 0, 0)),
        ],
        out_shape=[*outs, sds((CORES * mine, D, FF), WIDE), sds((CORES * mine, FF, D), WIDE)],
        compiler_params=params(60),
        name="finish",
    )(blocks.reshape(mine * parts, 2, CORES, BLOCK, BLOCK), *small)


def forward_kernel(groups, ib, *refs):
    q_ref, k_ref, v_ref, o_ref, small_ref, in_ref, out_ref, refs = *refs[:7], refs[7:]
    token_ref, cot_ref, order_ref, routes_ref, refs = *refs[:4], refs[4:]
    kept, refs = refs[:4], refs[4:]
    gain_ref, router_ref, x_out, cot_out, pos_ref, aux_ref, refs = *refs[:6], refs[6:]
    first_ref, qkv0_ref, mixed0_ref, peak0_ref, mid_ref, refs = *refs[:5], refs[5:]
    second_ref, qkv1_ref, mixed1_ref, peak1_ref, moe_ref, prob_ref, refs = *refs[:6], refs[6:]
    w0, win, wout, w1, small_all, state, wide_ref, line_ref, rows_ref, refs = *refs[:9], refs[9:]
    send, recv, pass_send, pass_recv, copy, rows_sem, kept_sem = refs
    phase, i = pl.program_id(0), pl.program_id(1)
    z, core, f = lax.axis_index("z"), lax.axis_index("core"), lax.axis_index("fsdp")

    def rows(count, owner, side):
        half = count // CORES
        return pl.ds(pl.multiple_of(owner * count + side * half, 16), half)

    def item(n):
        if n < 4 or n >= 7:
            ref = (q_ref, k_ref, v_ref, o_ref)[n % 7]
            full, layer = (w0, 0) if n < 4 else (w1, 1)
            count = ref.shape[1]
            cols = pl.ds(n % 7 * D, D)
            return (
                lambda side: ref.at[layer, rows(count, 0, side), :],
                lambda owner, side: full.at[rows(count, owner, side), cols],
            )
        ref, full = ((small_ref, small_all), (in_ref, win), (out_ref, wout))[n - 4]
        count = ref.shape[0]
        return (
            lambda side: ref.at[rows(count, 0, side), :],
            lambda owner, side: full.at[rows(count, owner, side), :],
        )

    def fetch(n, d):
        source, place = item(n)
        return pltpu.make_async_remote_copy(
            src_ref=source(core),
            dst_ref=place(f, core),
            send_sem=send.at[n, d],
            recv_sem=recv.at[n, d],
            device_id=(z, core, lax.rem(f + d, groups)),
            device_id_type=MESH_ID,
        )

    def hand_on(n, d):
        _, place = item(n)
        there = place(lax.rem(f + groups - d, groups), core)
        return pltpu.make_async_remote_copy(
            src_ref=there,
            dst_ref=there,
            send_sem=pass_send.at[n, d],
            recv_sem=pass_recv.at[n, d],
            device_id=(z, 1 - core, f),
            device_id_type=MESH_ID,
        )

    def keep(n, side):
        source, place = item(n)
        return pltpu.make_async_copy(source(side), place(f, side), copy.at[n, side])

    sets = ((0, 1, 2, 3, 4), (5, 6), (7, 8, 9, 10))

    def begin(stage):
        for n in sets[stage]:
            for d in range(1, groups):
                fetch(n, d).start()
            for side in range(CORES):
                keep(n, side).start()

    def arrive(stage):
        for n in sets[stage]:
            for d in range(1, groups):
                fetch(n, d).wait_recv()
                hand_on(n, d).start()

    def complete(stage):
        for n in sets[stage]:
            for side in range(CORES):
                keep(n, side).wait()
            for d in range(1, groups):
                fetch(n, d).wait_send()
                hand_on(n, d).wait()

    def keepers():
        return [
            pltpu.make_async_copy(ref, out, kept_sem.at[n])
            for n, (ref, out) in enumerate(zip((w0, win, wout, w1), kept))
        ]

    start = i == 0

    @pl.when(jnp.logical_and(phase == 0, start))
    def _():
        barrier = pltpu.get_barrier_semaphore()
        for d in range(1, groups):
            there = (z, core, lax.rem(f + d, groups))
            pl.semaphore_signal(barrier, inc=1, device_id=there, device_id_type=MESH_ID)
        pl.semaphore_signal(barrier, inc=1, device_id=(z, 1 - core, f), device_id_type=MESH_ID)
        pl.semaphore_wait(barrier, groups)
        begin(0)
        loads = [
            pltpu.make_async_copy(ref, rows_ref.at[n], rows_sem.at[n])
            for n, ref in enumerate((token_ref, cot_ref))
        ]
        for load in loads:
            load.start()
        for n, out in enumerate((x_out, cot_out)):
            loads[n].wait()
            pad_images(rows_ref.at[n], wide_ref, out)
        arrive(0)
        begin(1)
        find_places(order_ref, routes_ref, pos_ref, aux_ref, line_ref)
        complete(0)
        lane = lax.broadcasted_iota(jnp.int32, (1, 128), 1)
        small = small_all[...].astype(WIDE)
        router_ref[...] = jnp.where(lane < EXPERTS, small, 0.0).astype(NARROW)
        gain_ref[...] = jnp.transpose(small)[EXPERTS : EXPERTS + 8, :]

    @pl.when(jnp.logical_and(phase == 1, start))
    def _():
        arrive(1)
        begin(2)
        complete(1)

    @pl.when(jnp.logical_and(phase == 2, start))
    def _():
        arrive(2)
        complete(2)
        for k in keepers():
            k.start()

    images = pl.ds(i * ib, ib)

    @pl.when(phase == 0)
    def _():
        x = x_out[images].astype(WIDE).reshape(ib * SP, D)
        y = attn_fwd_body(x, gain_ref[0:1, :], w0, qkv0_ref, mixed0_ref, peak0_ref, ib)
        y = y.reshape(ib, SP, D)
        first_ref[...] = y
        state[images] = y

    @pl.when(phase == 1)
    def _():
        x = state[images].reshape(ib * SP, D)
        unit, _ = norm_parts(x)
        normed = (unit * gain_ref[2:3, :]).astype(NARROW)
        acc = x
        for n in range(FF // 512):
            c = slice(n * 512, (n + 1) * 512)
            pre = nn(normed, win[:, c])
            cdf, _ = normal_parts(pre)
            acc = acc + nn((pre * cdf).astype(NARROW), wout[c, :])
        y = acc.reshape(ib, SP, D)
        mid_ref[...] = y
        state[images] = y

    @pl.when(phase == 2)
    def _():
        x = state[images].reshape(ib * SP, D)
        y = attn_fwd_body(x, gain_ref[1:2, :], w1, qkv1_ref, mixed1_ref, peak1_ref, ib)
        second_ref[...] = y.reshape(ib, SP, D)
        unit, _ = norm_parts(y)
        moe = (unit * gain_ref[3:4, :]).astype(NARROW)
        moe_ref[...] = moe.reshape(ib, SP, D)
        lane = lax.broadcasted_iota(jnp.int32, (1, 128), 1)
        logits = jnp.where(lane < EXPERTS, nn(moe, router_ref[...]), LOWEST)
        e = jnp.exp(logits - jnp.max(logits, -1, keepdims=True))
        prob_ref[...] = (e / jnp.sum(e, -1, keepdims=True)).reshape(ib, SP, 128)

    @pl.when(jnp.logical_and(phase == 2, i == pl.num_programs(1) - 1))
    def _():
        for k in keepers():
            k.wait()


def forward(weights, tokens, cotangent, routes_rows, groups, held, ib):
    any_space = pl.BlockSpec(memory_space=pl.ANY)
    vmem = pl.BlockSpec(memory_space=pltpu.VMEM)
    dma = pltpu.SemaphoreType.DMA
    images = tokens.shape[0] // SEQ
    padded, pairs = images * SP, images // ib
    slots = np.arange(EXPERTS, dtype=np.int32)[:, None]
    order = np.broadcast_to(slot_expert(slots, groups, held), (EXPERTS, 128)).astype(np.int32)

    def of_phase(n, *tail):
        def place(phase, i):
            return (jnp.where(phase == n, i, jnp.where(phase < n, 0, pairs - 1)), *[0] * len(tail))

        return pl.BlockSpec((ib, *tail), place)

    tails = (
        (0, WIDE, SP, D),
        (0, NARROW, SP, 3 * D),
        (0, NARROW, SP, D),
        (0, WIDE, HEADS, 128),
        (1, WIDE, SP, D),
        (2, WIDE, SP, D),
        (2, NARROW, SP, 3 * D),
        (2, NARROW, SP, D),
        (2, WIDE, HEADS, 128),
        (2, NARROW, SP, D),
        (2, WIDE, SP, 128),
    )
    matrices = [(D, 4 * D), (D, FF), (FF, D), (D, 4 * D)]
    return pl.pallas_call(
        partial(forward_kernel, groups, ib),
        grid=(3, pairs),
        in_specs=[any_space] * 9 + [vmem] * 2,
        out_specs=[any_space] * 4
        + [vmem] * 6
        + [of_phase(n, *tail) for n, _, *tail in tails],
        out_shape=[
            *[sds(m, NARROW) for m in matrices],
            sds((8, D), WIDE),
            sds((D, 128), NARROW),
            sds((images, SP, D), NARROW),
            sds((images, SP, D), NARROW),
            sds((EXPERTS, padded), WIDE),
            sds((padded, 128), WIDE),
            *[sds((images, *tail), dtype) for _, dtype, *tail in tails],
        ],
        scratch_shapes=[
            *[pltpu.VMEM(m, NARROW) for m in matrices],
            pltpu.VMEM((D, 128), NARROW),
            pltpu.VMEM((images, SP, D), WIDE),
            pltpu.VMEM((-(-(tokens.shape[0] + SP) // 16) * 16, D), WIDE),
            pltpu.VMEM((128, padded), WIDE),
            pltpu.VMEM((2, *tokens.shape), NARROW),
            *[dma((11, groups)) for _ in range(4)],
            dma((11, CORES)),
            dma((2,)),
            dma((4,)),
        ],
        compiler_params=pltpu.CompilerParams(
            vmem_limit_bytes=60 * MIB, collective_id=5, has_side_effects=True
        ),
        name="forward",
    )(*weights, tokens, cotangent, jnp.asarray(order), routes_rows)


def local(
    tokens,
    cotangent,
    routes,
    attn_norm,
    query_w,
    key_w,
    value_w,
    output_w,
    ffn_norm,
    mlp_in,
    mlp_out,
    router_w,
    expert_in,
    expert_out,
    updated_query,
    updated_key,
    clip_threshold,
):
    images = tokens.shape[0] // SEQ
    ib = 2
    groups = lax.axis_size("fsdp")
    core = lax.axis_index("core")
    held = expert_in.shape[0]
    mine = held // CORES
    owners = CORES * groups

    small = jnp.concatenate(
        [
            router_w,
            jnp.transpose(attn_norm),
            jnp.transpose(ffn_norm),
            jnp.zeros((router_w.shape[0], 128 - EXPERTS - 4), NARROW),
        ],
        1,
    )
    routes_rows = jnp.pad(
        jnp.transpose(routes).reshape(2, images, SEQ),
        ((0, 6), (0, 0), (0, SP - SEQ)),
        constant_values=-1,
    ).reshape(8, -1)
    w0, win, wout, w1, gains, wr, x, cot, pos, aux, *states = forward(
        (query_w, key_w, value_w, output_w, small, mlp_in, mlp_out),
        tokens,
        cotangent,
        routes_rows,
        groups,
        held,
        ib,
    )
    first, qkv0, mixed0, peak0, mid, second, qkv1, mixed1, peak1, moe, prob = states
    aux = aux.reshape(images, SP, 128)

    sent = dispatch(
        pos, moe.reshape(-1, D), cot.reshape(-1, D), prob.reshape(-1, 128), groups, held
    ).reshape(mine, owners, 2 * CAP, D)

    nz = lax.axis_size("z")
    early = own = None
    if nz == 4 and owners == 8 and mine == 4:
        tables, early, own, late = exchange(sent, expert_in, expert_out, nz, groups)
        own = lax.psum(own, "z")
    else:
        tables, blocks = [], []
        for j in range(mine):
            rows = lax.all_to_all(
                sent[j], ("core", "fsdp"), split_axis=0, concat_axis=0, tiled=True
            )
            pick = (core * mine + j).astype(jnp.int32).reshape(1)
            back, d_in, d_out = expert(pick, rows, expert_in, expert_out)
            tables.append(
                lax.all_to_all(back, ("core", "fsdp"), split_axis=0, concat_axis=0, tiled=True)
            )
            blocks.append(jnp.stack([d_in, d_out], 1).reshape(-1, BLOCK, BLOCK))
        tables = jnp.stack(tables)
        late = jnp.concatenate(blocks)

    y, mid_grad, dw1 = moe_bwd(
        gains, w1, wr, mid, second, cot, prob, aux, qkv1, mixed1, tables, images, ib
    )
    x_grad, dw0, d_wout = dense_bwd(
        gains, w0, win, wout, x, first, mid_grad, qkv0, mixed0, images, ib
    )
    lane = jnp.arange(128)[None, :]
    peaks = jnp.where(lane < 64, jnp.max(peak0, 0), jnp.max(peak1, 0))
    blocks, t1, t0, t_wout, maxima = sum_all(
        [late], [dw1, dw0, d_wout], peaks, early, own, nz, groups
    )
    small_outs = [
        sds(attn_norm.shape, WIDE),
        *[sds(query_w.shape, WIDE)] * 4,
        sds(ffn_norm.shape, WIDE),
        sds(mlp_in.shape, WIDE),
        sds(mlp_out.shape, WIDE),
        sds(router_w.shape, WIDE),
        sds(updated_query.shape, WIDE),
        sds(updated_key.shape, WIDE),
    ]
    *grads, clipped_query, clipped_key, expert_in_grad, expert_out_grad = finish(
        blocks,
        mine,
        [t0, t1, t_wout, maxima, jnp.transpose(clip_threshold), updated_query, updated_key],
        small_outs,
    )
    return (y, x_grad, *grads, expert_in_grad, expert_out_grad, clipped_query, clipped_key)


def solution(mesh):
    replicas, groups = mesh.shape["replica"], mesh.shape["fsdp"]
    inner = Mesh(
        mesh.devices.reshape(replicas // CORES, CORES, groups), ("z", "core", "fsdp")
    )
    split = P(("z", "core", "fsdp"), None)
    second = P(None, "fsdp", None)
    in_specs = (
        split,
        split,
        split,
        P(None, "fsdp"),
        second,
        second,
        second,
        second,
        P(None, "fsdp"),
        P("fsdp", None),
        P("fsdp", None),
        P("fsdp", None),
        P("fsdp", None, None),
        P("fsdp", None, None),
        second,
        second,
        P(),
    )
    out_specs = (
        split,
        split,
        P(None, "fsdp"),
        second,
        second,
        second,
        second,
        P(None, "fsdp"),
        P("fsdp", None),
        P("fsdp", None),
        P("fsdp", None),
        P("fsdp", None, None),
        P("fsdp", None, None),
        second,
        second,
    )
    return jax.shard_map(local, mesh=inner, in_specs=in_specs, out_specs=out_specs, check_vma=False)
```

```python
from functools import partial

import jax
import jax.numpy as jnp
import numpy as np
from jax import lax
from jax.experimental import pallas as pl
from jax.experimental.pallas import tpu as pltpu
from jax.sharding import Mesh
from jax.sharding import PartitionSpec as P

D = 512
HEADS = 8
HEAD = 64
FF = 2048
SEQ = 197
SP = 208
CAP = 128
EXPERTS = 32
EPSILON = 1e-06
SCALE = HEAD ** (-0.5)
LOWEST = -1e30
NARROW = jnp.bfloat16
WIDE = jnp.float32
CORES = 2
MIB = 1 << 20


def nn(a, b):
    return lax.dot_general(a, b, (((1,), (0,)), ((), ())), preferred_element_type=WIDE)


def nt(a, b):
    return lax.dot_general(a, b, (((1,), (1,)), ((), ())), preferred_element_type=WIDE)


def tn(a, b):
    return lax.dot_general(a, b, (((0,), (0,)), ((), ())), preferred_element_type=WIDE)


def norm_parts(values):
    centred = values - jnp.mean(values, -1, keepdims=True)
    inverse = lax.rsqrt(jnp.mean(centred * centred, -1, keepdims=True) + EPSILON)
    return centred * inverse, inverse


def norm_backward(incoming, unit, inverse, gain):
    gain_grad = jnp.sum(incoming * unit, 0, keepdims=True)
    scaled = incoming * gain
    centred = (
        scaled
        - jnp.mean(scaled, -1, keepdims=True)
        - unit * jnp.mean(scaled * unit, -1, keepdims=True)
    )
    return inverse * centred, gain_grad


def normal_parts(x):
    z = jnp.abs(x)
    t = 1.0 / (1.0 + (0.3275911 * 0.7071067811865476) * z)
    bell = jnp.exp(-0.5 * (x * x))
    poly = t * (
        0.5 * 0.254829592
        + t
        * (
            0.5 * -0.284496736
            + t * (0.5 * 1.421413741 + t * (0.5 * -1.453152027 + t * (0.5 * 1.061405429)))
        )
    )
    tail = poly * bell
    return jnp.where(x >= 0, 1.0 - tail, tail), bell


INV_ROOT = 0.3989422804014327


def head_masks(dtype):
    lane = lax.broadcasted_iota(jnp.int32, (1, 2 * HEAD), 1)
    low = (lane < HEAD).astype(dtype)
    return (low, (1 - low.astype(WIDE)).astype(dtype))


def attn_fwd_body(x, gain, w_ref, qkv_ref, mixed_ref, peak_ref, ib):
    unit, _ = norm_parts(x)
    normed = (unit * gain).astype(NARROW)
    q = (nn(normed, w_ref[:, 0:D]).astype(NARROW).astype(WIDE) * SCALE).astype(NARROW)
    k = nn(normed, w_ref[:, D : 2 * D]).astype(NARROW)
    v = nn(normed, w_ref[:, 2 * D : 3 * D]).astype(NARROW)
    masks = head_masks(NARROW)
    cols = lax.broadcasted_iota(jnp.int32, (SP, SP), 1)
    rows = lax.broadcasted_iota(jnp.int32, (SP, 1), 0)
    head_row = lax.broadcasted_iota(jnp.int32, (HEADS, 128), 0)
    mixed_all = []
    for i in range(ib):
        peaks = jnp.full((HEADS, 128), LOWEST, WIDE)
        r = slice(i * SP, (i + 1) * SP)
        pairs = []
        for pair in range(HEADS // 2):
            c = slice(pair * 2 * HEAD, (pair + 1) * 2 * HEAD)
            qp, kp, vp = q[r, c], k[r, c], v[r, c]
            acc = None
            for half in range(2):
                s = nt(qp * masks[half], kp)
                s = jnp.where(cols < SEQ, s, LOWEST)
                top = jnp.max(s, -1, keepdims=True)
                e = jnp.exp(s - top)
                p = (e * (1.0 / jnp.sum(e, -1, keepdims=True))).astype(NARROW)
                part = nn(p, vp * masks[half])
                acc = part if acc is None else acc + part
                peak = jnp.max(jnp.where(rows < SEQ, top, LOWEST), 0, keepdims=True)
                peaks = jnp.where(head_row == pair * 2 + half, peak, peaks)
            pairs.append(acc.astype(NARROW))
        mixed_all.append(jnp.concatenate(pairs, 1))
        peak_ref[i] = peaks
    mixed = jnp.concatenate(mixed_all, 0) if ib > 1 else mixed_all[0]
    qkv_ref[...] = jnp.concatenate([q, k, v], 1).reshape(ib, SP, 3 * D)
    mixed_ref[...] = mixed.reshape(ib, SP, D)
    return x + nn(mixed, w_ref[:, 3 * D : 4 * D])


def whole(shape):
    return pl.BlockSpec(
        shape, lambda *_: (0,) * len(shape), pipeline_mode=pl.Buffered(buffer_count=1)
    )


def per_image(ib, *tail):
    return pl.BlockSpec((ib, *tail), lambda i, *_: (i,) + (0,) * len(tail))


def sds(shape, dtype):
    return jax.ShapeDtypeStruct(shape, dtype)


def cost(flops, moved):
    return pl.CostEstimate(flops=int(flops), bytes_accessed=int(moved), transcendentals=0)


def params(mib):
    return pltpu.CompilerParams(vmem_limit_bytes=mib * MIB)


def find_places(order_ref, routes_ref, pos_ref, aux_ref, line_ref):
    tokens = routes_ref.shape[1]
    order = order_ref[:, 0:1]
    chunk = 128
    strict = (
        lax.broadcasted_iota(jnp.int32, (chunk, chunk), 0)
        < lax.broadcasted_iota(jnp.int32, (chunk, chunk), 1)
    ).astype(NARROW)
    slot_row = lax.broadcasted_iota(jnp.int32, (EXPERTS, 1), 0).astype(WIDE) * CAP
    base = jnp.zeros((EXPERTS, 1), WIDE)
    pos_ref[...] = jnp.full(pos_ref.shape, -1.0, WIDE)
    line_ref[...] = jnp.zeros(line_ref.shape, WIDE)
    for k in range(2):
        for c in range(tokens // chunk):
            s = slice(c * chunk, (c + 1) * chunk)
            hit = (order == routes_ref[k : k + 1, s]).astype(WIDE)
            place = base + nn(hit.astype(NARROW), strict)
            base = base + jnp.sum(hit, -1, keepdims=True)
            pos_ref[:, s] = jnp.where(hit > 0, place, pos_ref[:, s])
            slot = jnp.where(place < CAP, slot_row + place, 2.0 * EXPERTS * CAP)
            found = jnp.sum(hit * slot, 0, keepdims=True)
            real = jnp.sum(hit, 0, keepdims=True)
            line_ref[k : k + 1, s] = jnp.where(real > 0, found, 2.0 * EXPERTS * CAP)
            line_ref[2 + k : 3 + k, s] = routes_ref[k : k + 1, s].astype(WIDE)
    for c in range(tokens // chunk):
        s = slice(c * chunk, (c + 1) * chunk)
        aux_ref[s, :] = jnp.transpose(line_ref[:, s])


def pad_images(ref, wide_ref, out_ref):
    tokens = ref.shape[0]
    wide_ref[0:tokens, :] = ref[...].astype(WIDE)
    rows = lax.broadcasted_iota(jnp.int32, (SP, 1), 0)
    for i in range(tokens // SEQ):
        image = wide_ref[i * SEQ : i * SEQ + SP, :]
        out_ref[i] = jnp.where(rows < SEQ, image, 0.0).astype(NARROW)


GROUP = 8


def slot_expert(index, groups, held):
    owners, mine = CORES * groups, held // CORES
    owner = index % owners
    return (owner % groups) * held + (owner // groups) * mine + index // owners


def dispatch_kernel(groups, held, pos_ref, moe_ref, cot_ref, prob_ref, out_ref, line_ref):
    step = pl.program_id(0)

    @pl.when(step == 0)
    def _():
        for c in range(prob_ref.shape[0] // 128):
            s = slice(c * 128, (c + 1) * 128)
            line_ref[:, s] = jnp.transpose(prob_ref[s, :])

    slot = lax.broadcasted_iota(jnp.int32, (CAP, 1), 0).astype(WIDE)
    hot, gates = [], []
    for g in range(GROUP):
        mine = pos_ref[g : g + 1, :] == slot
        hot.append(mine.astype(WIDE).astype(NARROW))
        gate_row = line_ref[pl.ds(slot_expert(step * GROUP + g, groups, held), 1), :]
        gates.append(jnp.sum(jnp.where(mine, gate_row, 0.0), -1, keepdims=True))
    hot = jnp.concatenate(hot, 0)
    rows = nn(hot, moe_ref[...]).astype(NARROW)
    grads = nn(hot, cot_ref[...])
    for g in range(GROUP):
        s = slice(g * CAP, (g + 1) * CAP)
        out_ref[g, 0:CAP, :] = rows[s]
        out_ref[g, CAP : 2 * CAP, :] = (gates[g] * grads[s]).astype(NARROW)


def dispatch(pos, moe, cot, prob, groups, held):
    tokens = moe.shape[0]
    return pl.pallas_call(
        partial(dispatch_kernel, groups, held),
        grid=(EXPERTS // GROUP,),
        in_specs=[
            pl.BlockSpec((GROUP, tokens), lambda i: (i, 0)),
            whole(moe.shape),
            whole(cot.shape),
            whole(prob.shape),
        ],
        out_specs=pl.BlockSpec((GROUP, 2 * CAP, D), lambda i: (i, 0, 0)),
        out_shape=sds((EXPERTS, 2 * CAP, D), NARROW),
        scratch_shapes=[pltpu.VMEM((128, tokens), WIDE)],
        compiler_params=params(60),
        name="dispatch",
    )(pos, moe, cot, prob)


def expert_math(slots, grads, win, wout):
    pre = nn(slots, win)
    hidden_grad = nt(grads, wout)
    cdf, bell = normal_parts(pre)
    hidden = (pre * cdf).astype(NARROW)
    pre_grad = ((cdf + pre * (bell * INV_ROOT)) * hidden_grad).astype(NARROW)
    return nn(hidden, wout), nt(pre_grad, win), tn(slots, pre_grad), tn(hidden, grads)


def expert_kernel(pick, rows_ref, win_ref, wout_ref, back_ref, din_ref, dout_ref, res, sgr):
    f = pl.program_id(0)
    senders = rows_ref.shape[0]
    part = min(senders, 8)
    count = part * CAP
    win, wout = win_ref[...], wout_ref[...]
    d_in = d_out = None
    for first in range(0, senders, part):
        slots = rows_ref[first : first + part, 0:CAP, :].reshape(count, D)
        grads = rows_ref[first : first + part, CAP : 2 * CAP, :].reshape(count, D)
        r = slice(first * CAP, (first + part) * CAP)
        result, slot_grad, in_part, out_part = expert_math(slots, grads, win, wout)
        d_in = in_part if d_in is None else d_in + in_part
        d_out = out_part if d_out is None else d_out + out_part

        @pl.when(f == 0)
        def _(r=r, result=result, slot_grad=slot_grad):
            res[r, :] = result
            sgr[r, :] = slot_grad

        @pl.when(f > 0)
        def _(r=r, result=result, slot_grad=slot_grad):
            res[r, :] += result
            sgr[r, :] += slot_grad

    din_ref[...] = d_in.astype(NARROW)
    dout_ref[...] = d_out.astype(NARROW)

    @pl.when(f == pl.num_programs(0) - 1)
    def _():
        back_ref[:, :, 0:D] = res[...].astype(NARROW).reshape(senders, CAP, D)
        back_ref[:, :, D : 2 * D] = sgr[...].astype(NARROW).reshape(senders, CAP, D)


def expert(pick, rows, win, wout):
    senders = rows.shape[0]
    wide = 512
    return pl.pallas_call(
        expert_kernel,
        grid_spec=pltpu.PrefetchScalarGridSpec(
            num_scalar_prefetch=1,
            grid=(FF // wide,),
            in_specs=[
                whole(rows.shape),
                pl.BlockSpec((None, D, wide), lambda f, p: (p[0], 0, f)),
                pl.BlockSpec((None, wide, D), lambda f, p: (p[0], f, 0)),
            ],
            out_specs=[
                whole((senders, CAP, 2 * D)),
                pl.BlockSpec((None, D, wide), lambda f, p: (f, 0, 0)),
                pl.BlockSpec((None, wide, D), lambda f, p: (f, 0, 0)),
            ],
            scratch_shapes=[
                pltpu.VMEM((senders * CAP, D), WIDE),
                pltpu.VMEM((senders * CAP, D), WIDE),
            ],
        ),
        out_shape=[
            sds((senders, CAP, 2 * D), NARROW),
            sds((FF // wide, D, wide), NARROW),
            sds((FF // wide, wide, D), NARROW),
        ],
        compiler_params=params(60),
        cost_estimate=cost(5e9, 1),
        name="one_expert",
    )(pick, rows, win, wout)


def attn_bwd_body(x, incoming, gain, qkv_ref, mixed_ref, w_ref, dw_ref, ib):
    unit, inverse = norm_parts(x)
    normed = (unit * gain).astype(NARROW)
    out_grad = incoming.astype(NARROW)
    mixed = mixed_ref[...].reshape(ib * SP, D)
    dw_ref[:, 3 * D : 4 * D] += tn(mixed, out_grad)
    mixed_grad = nt(out_grad, w_ref[:, 3 * D : 4 * D]).astype(NARROW)
    masks = head_masks(NARROW)
    rows = lax.broadcasted_iota(jnp.int32, (SP, SP), 0)
    dq_all, dk_all, dv_all = [], [], []
    for i in range(ib):
        r = slice(i * SP, (i + 1) * SP)
        dqs, dks, dvs = [], [], []
        for pair in range(HEADS // 2):
            qp = qkv_ref[i, :, pair * 128 : (pair + 1) * 128]
            kp = qkv_ref[i, :, D + pair * 128 : D + (pair + 1) * 128]
            vp = qkv_ref[i, :, 2 * D + pair * 128 : 2 * D + (pair + 1) * 128]
            mp = mixed_grad[r, pair * 128 : (pair + 1) * 128]
            dq = dk = dv = None
            for half in range(2):
                qm, mm, km = qp * masks[half], mp * masks[half], kp * masks[half]
                s = jnp.where(rows < SEQ, nt(kp, qm), LOWEST)
                e = jnp.exp(s - jnp.max(s, 0, keepdims=True))
                soft = e * (1.0 / jnp.sum(e, 0, keepdims=True))
                pg = nt(vp, mm)
                delta = jnp.sum(soft * pg, 0, keepdims=True)
                sg = (soft * (pg - delta)).astype(NARROW)
                v_part = nn(soft.astype(NARROW), mm)
                k_part = nn(sg, qm)
                q_part = tn(sg, km)
                dq = q_part if dq is None else dq + q_part
                dk = k_part if dk is None else dk + k_part
                dv = v_part if dv is None else dv + v_part
            dqs.append((dq * SCALE).astype(NARROW))
            dks.append(dk.astype(NARROW))
            dvs.append(dv.astype(NARROW))
        dq_all.append(jnp.concatenate(dqs, 1))
        dk_all.append(jnp.concatenate(dks, 1))
        dv_all.append(jnp.concatenate(dvs, 1))
    dqkv = jnp.concatenate(
        [
            jnp.concatenate(a, 0) if ib > 1 else a[0]
            for a in (dq_all, dk_all, dv_all)
        ],
        1,
    )
    dw_ref[:, 0 : 3 * D] += tn(normed, dqkv)
    normed_grad = nt(dqkv, w_ref[:, 0 : 3 * D])
    input_grad, gain_grad = norm_backward(normed_grad, unit, inverse, gain)
    return incoming + input_grad, gain_grad


def gain_columns(dg_ref):
    tall = jnp.concatenate(
        [jnp.zeros((EXPERTS, D), WIDE), dg_ref[...], jnp.zeros((128 - EXPERTS - 8, D), WIDE)], 0
    )
    return jnp.transpose(tall)


def put_rows(ref, step, ib, value):
    for image in range(ref.shape[0] // SEQ):

        @pl.when(step == image // ib)
        def _(image=image):
            first = image % ib * SP
            ref[image * SEQ : (image + 1) * SEQ, :] = value[first : first + SEQ]


def moe_bwd_kernel(
    ib,
    g_ref,
    w_ref,
    wr_ref,
    mid_ref,
    second_ref,
    cot_ref,
    prob_ref,
    aux_ref,
    qkv_ref,
    mixed_ref,
    table_ref,
    y_ref,
    grad_ref,
    dw_out,
    dr_ref,
    dg_ref,
    dw_ref,
):
    step = pl.program_id(0)

    @pl.when(step == 0)
    def _():
        dw_ref[...] = jnp.zeros(dw_ref.shape, WIDE)
        dr_ref[...] = jnp.zeros(dr_ref.shape, WIDE)
        dg_ref[...] = jnp.zeros(dg_ref.shape, WIDE)

    second = second_ref[...].reshape(ib * SP, D)
    upstream = cot_ref[...].astype(WIDE).reshape(ib * SP, D)
    prob = prob_ref[...].reshape(ib * SP, 128)
    aux = aux_ref[...].reshape(ib * SP, 128)
    first_pick = second_pick = back = None
    for j in range(table_ref.shape[0]):
        count = table_ref.shape[1] * CAP
        slot = lax.broadcasted_iota(jnp.int32, (1, count), 1).astype(WIDE) + float(j * count)
        hot_one = (aux[:, 0:1] == slot).astype(WIDE).astype(NARROW)
        hot_two = (aux[:, 1:2] == slot).astype(WIDE).astype(NARROW)
        rows = table_ref[j].reshape(count, 2 * D)
        one = nn(hot_one, rows[:, 0:D])
        two = nn(hot_two, rows[:, 0:D])
        both = nn(hot_one + hot_two, rows[:, D : 2 * D])
        first_pick = one if first_pick is None else first_pick + one
        second_pick = two if second_pick is None else second_pick + two
        back = both if back is None else back + both
    lane = lax.broadcasted_iota(jnp.int32, (1, 128), 1)
    first_hit = (aux[:, 2:3] == lane.astype(WIDE)).astype(WIDE)
    second_hit = (aux[:, 3:4] == lane.astype(WIDE)).astype(WIDE)
    gate_one = jnp.sum(prob * first_hit, -1, keepdims=True)
    gate_two = jnp.sum(prob * second_hit, -1, keepdims=True)
    put_rows(y_ref, step, ib, second + (gate_one * first_pick + gate_two * second_pick))
    gate_one_grad = jnp.sum(upstream * first_pick, -1, keepdims=True)
    gate_two_grad = jnp.sum(upstream * second_pick, -1, keepdims=True)
    prob_grad = gate_one_grad * first_hit + gate_two_grad * second_hit
    logit_grad = (prob * (prob_grad - jnp.sum(prob * prob_grad, -1, keepdims=True))).astype(NARROW)
    unit, inverse = norm_parts(second)
    gain = g_ref[3:4, :]
    moe = (unit * gain).astype(NARROW)
    dr_ref[...] += tn(moe, logit_grad)
    normed_grad = back + nt(logit_grad, wr_ref[...])
    moe_grad, gain_grad = norm_backward(normed_grad, unit, inverse, gain)
    dg_ref[3:4, :] += gain_grad
    mid = mid_ref[...].reshape(ib * SP, D)
    grad, gain_grad = attn_bwd_body(
        mid, upstream + moe_grad, g_ref[1:2, :], qkv_ref, mixed_ref, w_ref, dw_ref, ib
    )
    dg_ref[1:2, :] += gain_grad
    grad_ref[...] = grad.reshape(ib, SP, D)

    @pl.when(step == pl.num_programs(0) - 1)
    def _():
        dw_out[:, : 4 * D] = dw_ref[...].astype(NARROW)
        dw_out[:, 4 * D :] = (dr_ref[...] + gain_columns(dg_ref)).astype(NARROW)


def moe_bwd(gains, w1, wr, mid, second, cot, prob, aux, qkv, mixed, tables, images, ib):
    return pl.pallas_call(
        partial(moe_bwd_kernel, ib),
        grid=(images // ib,),
        in_specs=[
            whole(gains.shape),
            whole(w1.shape),
            whole(wr.shape),
            per_image(ib, SP, D),
            per_image(ib, SP, D),
            per_image(ib, SP, D),
            per_image(ib, SP, 128),
            per_image(ib, SP, 128),
            per_image(ib, SP, 3 * D),
            per_image(ib, SP, D),
            whole(tables.shape),
        ],
        out_specs=[
            whole((images * SEQ, D)),
            per_image(ib, SP, D),
            whole((D, 4 * D + 128)),
        ],
        out_shape=[
            sds((images * SEQ, D), WIDE),
            sds((images, SP, D), WIDE),
            sds((D, 4 * D + 128), NARROW),
        ],
        scratch_shapes=[
            pltpu.VMEM((D, 128), WIDE),
            pltpu.VMEM((8, D), WIDE),
            pltpu.VMEM((D, 4 * D), WIDE),
        ],
        compiler_params=params(60),
        cost_estimate=cost(1e6, 1),
        name="expert_block_backward",
    )(gains, w1, wr, mid, second, cot, prob, aux, qkv, mixed, tables)


def dense_bwd_kernel(
    ib,
    g_ref,
    w_ref,
    win_ref,
    wout_ref,
    x_ref,
    first_ref,
    grad_ref,
    qkv_ref,
    mixed_ref,
    out_ref,
    dw_out,
    dout_out,
    dg_ref,
    dw_ref,
    din_ref,
    dout_ref,
):
    step = pl.program_id(0)

    @pl.when(step == 0)
    def _():
        dw_ref[...] = jnp.zeros(dw_ref.shape, WIDE)
        din_ref[...] = jnp.zeros(din_ref.shape, WIDE)
        dout_ref[...] = jnp.zeros(dout_ref.shape, WIDE)
        dg_ref[...] = jnp.zeros(dg_ref.shape, WIDE)

    incoming = grad_ref[...].reshape(ib * SP, D)
    first = first_ref[...].reshape(ib * SP, D)
    unit, inverse = norm_parts(first)
    gain = g_ref[2:3, :]
    normed = (unit * gain).astype(NARROW)
    out_grad = incoming.astype(NARROW)
    y_grad = None
    for f in range(FF // 512):
        c = slice(f * 512, (f + 1) * 512)
        win, wout = win_ref[:, c], wout_ref[c, :]
        pre = nn(normed, win)
        hidden_grad = nt(out_grad, wout)
        cdf, bell = normal_parts(pre)
        hidden = (pre * cdf).astype(NARROW)
        pre_grad = ((cdf + pre * (bell * INV_ROOT)) * hidden_grad).astype(NARROW)
        dout_ref[c, :] += tn(hidden, out_grad)
        din_ref[:, c] += tn(normed, pre_grad)
        part = nt(pre_grad, win)
        y_grad = part if y_grad is None else y_grad + part
    ffn_grad, gain_grad = norm_backward(y_grad, unit, inverse, gain)
    dg_ref[2:3, :] += gain_grad
    x = x_ref[...].astype(WIDE).reshape(ib * SP, D)
    grad, gain_grad = attn_bwd_body(
        x, incoming + ffn_grad, g_ref[0:1, :], qkv_ref, mixed_ref, w_ref, dw_ref, ib
    )
    dg_ref[0:1, :] += gain_grad
    put_rows(out_ref, step, ib, grad)

    @pl.when(step == pl.num_programs(0) - 1)
    def _():
        dw_out[:, : 4 * D] = dw_ref[...].astype(NARROW)
        dw_out[:, 4 * D : 8 * D] = din_ref[...].astype(NARROW)
        dw_out[:, 8 * D :] = gain_columns(dg_ref).astype(NARROW)
        dout_out[...] = dout_ref[...].astype(NARROW)


def dense_bwd(gains, w0, win, wout, x, first, grad, qkv, mixed, images, ib):
    return pl.pallas_call(
        partial(dense_bwd_kernel, ib),
        grid=(images // ib,),
        in_specs=[
            whole(gains.shape),
            whole(w0.shape),
            whole(win.shape),
            whole(wout.shape),
            per_image(ib, SP, D),
            per_image(ib, SP, D),
            per_image(ib, SP, D),
            per_image(ib, SP, 3 * D),
            per_image(ib, SP, D),
        ],
        out_specs=[
            whole((images * SEQ, D)),
            whole((D, 8 * D + 128)),
            whole((FF, D)),
        ],
        out_shape=[
            sds((images * SEQ, D), WIDE),
            sds((D, 8 * D + 128), NARROW),
            sds((FF, D), NARROW),
        ],
        scratch_shapes=[
            pltpu.VMEM((8, D), WIDE),
            pltpu.VMEM((D, 4 * D), WIDE),
            pltpu.VMEM((D, FF), WIDE),
            pltpu.VMEM((FF, D), WIDE),
        ],
        compiler_params=params(60),
        cost_estimate=cost(1e6, 1),
        name="dense_block_backward",
    )(gains, w0, win, wout, x, first, grad, qkv, mixed)


BLOCK = 512
CUTS = 2
AHEAD = 3
MESH_ID = pl.DeviceIdType.MESH


def add_rows(out, one, two, rows, step):
    @pl.loop(0, rows // step)
    def _(i):
        r = pl.ds(pl.multiple_of(i * step, step), step)
        out[r, :] = (one[r, :].astype(WIDE) + two[r, :].astype(WIDE)).astype(out.dtype)


def sum_kernel(nz, groups, mats, slices, first, handed, *refs):
    exp_refs, refs = refs[:mats], refs[mats:]
    dense_refs, peak_ref, refs = refs[:3], refs[3], refs[4:]
    if handed:
        _, hand_ref, refs = refs[0], refs[1], refs[2:]
    exp_out, dense_outs, peak_out, refs = refs[0], refs[1:4], refs[4], refs[5:]
    if handed:
        hand_buf, hand_sem, refs = refs[-2], refs[-1], refs[:-2]
    own, up, down, refs = refs[0], refs[1], refs[2], refs[3:]
    land, refs = refs[:4], refs[4:]
    dense_own, refs = refs[:4], refs[4:]
    dense_up, refs = refs[:4], refs[4:]
    dense_down, refs = refs[:4], refs[4:]
    (own_sem, up_send, up_recv, down_recv, out_send, sib_send, sib_recv, copy_sem, rs_send, rs_recv) = refs

    z, core, f = lax.axis_index("z"), lax.axis_index("core"), lax.axis_index("fsdp")
    half = nz // 2
    left = z < half
    inner = jnp.where(left, z + 1, z - 1)
    outer = jnp.where(left, z - 1, z + 1)
    has_outer = jnp.logical_and(z > 0, z < nz - 1)
    edge = jnp.logical_not(has_outer)
    center = jnp.logical_or(z == half - 1, z == half)
    away = jnp.logical_not(center)
    outer = jnp.where(has_outer, outer, inner)
    sibling = (z, 1 - core, f)
    members = CORES * groups
    me = core * groups + f

    barrier = pltpu.get_barrier_semaphore()
    pl.semaphore_signal(barrier, inc=1, device_id=(inner, core, f), device_id_type=MESH_ID)

    @pl.when(has_outer)
    def _():
        pl.semaphore_signal(barrier, inc=1, device_id=(outer, core, f), device_id_type=MESH_ID)

    for d in range(1, members):
        there = lax.rem(me + d, members)
        pl.semaphore_signal(
            barrier,
            inc=1,
            device_id=(z, there // groups, lax.rem(there, groups)),
            device_id_type=MESH_ID,
        )

    @pl.when(has_outer)
    def _():
        pl.semaphore_wait(barrier, members + 1)

    @pl.when(edge)
    def _():
        pl.semaphore_wait(barrier, members)

    chunks = mats * slices * CUTS
    items = chunks + 4

    def cut_rows(t):
        return pl.ds(t % CUTS * (BLOCK // CUTS), BLOCK // CUTS)

    def piece(n, ref, there):
        if n == 3:
            return ref
        rows = ref.shape[0] // members
        place = (lax.rem(there, groups) * CORES + there // groups) * rows
        return ref.at[pl.ds(pl.multiple_of(place, 16), rows), :]

    def scatter(n, d):
        there = lax.rem(me + d, members)
        source = dense_refs[n] if n < 3 else peak_ref
        return pltpu.make_async_remote_copy(
            src_ref=piece(n, source, there),
            dst_ref=land[n].at[d],
            send_sem=rs_send.at[n, d],
            recv_sem=rs_recv.at[n, d],
            device_id=(z, there // groups, lax.rem(there, groups)),
            device_id_type=MESH_ID,
        )

    def hand():
        return pltpu.make_async_remote_copy(
            src_ref=hand_buf,
            dst_ref=exp_out.at[pl.ds(first - handed, handed), core],
            send_sem=hand_sem.at[0],
            recv_sem=hand_sem.at[1],
            device_id=sibling,
            device_id_type=MESH_ID,
        )

    if handed:
        arrived = pltpu.make_async_copy(hand_ref, hand_buf, hand_sem.at[2])
        arrived.start()
        arrived.wait()
        handed_here = pltpu.make_async_copy(
            hand_buf, exp_out.at[pl.ds(first - handed, handed), core], hand_sem.at[2]
        )
        handed_here.start()
        hand().start()
    for n in (3, 1, 0, 2):
        for d in range(1, members):
            scatter(n, d).start()
    keep = [
        pltpu.make_async_copy(
            piece(n, dense_refs[n] if n < 3 else peak_ref, me), land[n].at[0], rs_recv.at[n, 0]
        )
        for n in range(4)
    ]
    for k in keep:
        k.start()

    def source_at_edge(t):
        if t >= chunks:
            return dense_own[t - chunks]
        return exp_refs[t // CUTS // slices].at[t // CUTS % slices, cut_rows(t), :]

    def load(t):
        return pltpu.make_async_copy(source_at_edge(t), own.at[t], own_sem.at[t])

    @pl.when(has_outer)
    def _():
        for t in range(chunks):
            load(t).start()

    def bufs(t):
        if t < chunks:
            return own.at[t], up.at[t], down.at[t]
        n = t - chunks
        return dense_own[n], dense_up[n], dense_down[n]

    def send_up(t, source, to_center):
        _, u, dn = bufs(t)
        return pltpu.make_async_remote_copy(
            src_ref=source,
            dst_ref=dn if to_center else u,
            send_sem=up_send.at[t],
            recv_sem=(down_recv if to_center else up_recv).at[t],
            device_id=(inner, core, f),
            device_id_type=MESH_ID,
        )

    def join(t, out, one, two):
        if t == items - 1:
            out[...] = jnp.maximum(one[...], two[...])
        else:
            add_rows(out, one, two, out.shape[0], 16)

    def reduce_own(n):
        for d in range(members):
            if d == 0:
                keep[n].wait()
            else:
                scatter(n, d).wait_recv()
        if n == 3:
            best = land[n][0]
            for d in range(1, members):
                best = jnp.maximum(best, land[n][d])
            dense_own[n][...] = best
            return

        @pl.loop(0, dense_own[n].shape[0] // 16)
        def _(i):
            r = pl.ds(pl.multiple_of(i * 16, 16), 16)
            total = land[n][0, r, :].astype(WIDE)
            for d in range(1, members):
                total = total + land[n][d, r, :].astype(WIDE)
            dense_own[n][r, :] = total.astype(NARROW)

    def up_from_edge(t, before):
        if before is not None:
            send_up(before, source_at_edge(before), half == 1).wait_send()
        if t >= chunks:
            reduce_own(t - chunks)
        send_up(t, source_at_edge(t), half == 1).start()

    def up_from_inside(t):
        o, u, _ = bufs(t)
        if t >= chunks:
            reduce_own(t - chunks)
        else:
            load(t).wait()
        send_up(t, u, False).wait_recv()
        join(t, o, o, u)

        @pl.when(center)
        def _():
            send_up(t, o, True).start()

        if half > 2:

            @pl.when(away)
            def _():
                send_up(t, o, False).start()

    def results(t):
        if t < chunks:
            return exp_out.at[first + t // CUTS, core, cut_rows(t), :]
        n = t - chunks
        if n == 3:
            return peak_out
        ref = dense_outs[n]
        rows = ref.shape[0] // CORES
        return ref.at[pl.ds(pl.multiple_of(core * rows, 16), rows), :]

    def to_sibling(t):
        return pltpu.make_async_remote_copy(
            src_ref=bufs(t)[2],
            dst_ref=results(t),
            send_sem=sib_send.at[t],
            recv_sem=sib_recv.at[t],
            device_id=sibling,
            device_id_type=MESH_ID,
        )

    def to_outer(t):
        dn = bufs(t)[2]
        return pltpu.make_async_remote_copy(
            src_ref=dn,
            dst_ref=dn,
            send_sem=out_send.at[t],
            recv_sem=down_recv.at[t],
            device_id=(outer, core, f),
            device_id_type=MESH_ID,
        )

    def keep_result(t):
        return pltpu.make_async_copy(bufs(t)[2], results(t), copy_sem.at[t])

    def go_down(t, at_edge):
        o, _, dn = bufs(t)
        to_outer(t).wait_recv()
        if at_edge:
            if half == 1:
                join(t, dn, source_at_edge(t), dn)
        else:

            @pl.when(center)
            def _():
                join(t, dn, o, dn)

            to_outer(t).start()
        keep_result(t).start()
        if t < items - 1:
            to_sibling(t).start()

    early = min(11 * CUTS, chunks)
    sequence = [*range(early), *range(items - 1, chunks - 1, -1), *range(early, chunks)]

    def run(up, at_edge, lag):
        for i in range(items + lag):
            if i < items:
                up(i)
            if i >= lag:
                go_down(sequence[i - lag], at_edge)

    @pl.when(edge)
    def _():
        run(
            lambda i: up_from_edge(sequence[i], sequence[i - AHEAD] if i >= AHEAD else None),
            True,
            min(7 * CUTS, items),
        )
        for t in sequence[-AHEAD:]:
            send_up(t, source_at_edge(t), half == 1).wait_send()

    if half > 1:

        @pl.when(has_outer)
        def _():
            run(lambda i: up_from_inside(sequence[i]), False, 1)
            for t in range(items):
                send_up(t, bufs(t)[0], False).wait_send()
                to_outer(t).wait_send()

    for n in range(4):
        for d in range(1, members):
            scatter(n, d).wait_send()
    if handed:
        hand().wait()
        handed_here.wait()
    for t in range(items):
        keep_result(t).wait()
        if t < items - 1:
            to_sibling(t).wait()


def sum_all(mats, dense, peaks, early, handed, nz, groups):
    slices = mats[0].shape[0]
    blocks = len(mats) * slices
    chunks = blocks * CUTS
    members = CORES * groups
    items = chunks + 4
    any_space = pl.BlockSpec(memory_space=pl.ANY)
    vmem = pl.BlockSpec(memory_space=pltpu.VMEM)
    pieces = [(a.shape[0] // members, a.shape[1]) for a in dense]
    block = pltpu.VMEM((chunks, BLOCK // CUTS, BLOCK), NARROW)

    def four(lead=()):
        return [pltpu.VMEM((*lead, *p), NARROW) for p in pieces] + [
            pltpu.VMEM((*lead, *peaks.shape), WIDE)
        ]

    dma = pltpu.SemaphoreType.DMA
    extra = [] if handed is None else [early, handed]
    count = handed.shape[0] if extra else 0
    first = early.shape[0] - blocks if extra else 0
    return pl.pallas_call(
        partial(sum_kernel, nz, groups, len(mats), slices, first, count),
        in_specs=[any_space] * (len(mats) + 3) + [vmem] + [any_space] * len(extra),
        out_specs=[any_space] * 4 + [vmem],
        out_shape=[
            sds((first + blocks, CORES, BLOCK, BLOCK), NARROW),
            *[sds((CORES * r, c), NARROW) for r, c in pieces],
            sds(peaks.shape, WIDE),
        ],
        scratch_shapes=[
            block,
            block,
            block,
            *four((members,)),
            *four(),
            *four(),
            *four(),
            *[dma((items,)) for _ in range(8)],
            dma((4, members)),
            dma((4, members)),
            *([pltpu.VMEM(handed.shape, NARROW), dma((3,))] if extra else []),
        ],
        compiler_params=pltpu.CompilerParams(
            vmem_limit_bytes=58 * MIB, collective_id=3, has_side_effects=True
        ),
        input_output_aliases={len(mats) + 4: 0} if extra else {},
        name="sums",
    )(*mats, *dense, peaks, *extra)


SUMMED = 12
LAGS = (2, 4, 6)
BESIDE = 8


def exchange_kernel(nz, groups, mine, *refs):
    (sent_ref, win_hbm, wout_hbm, table_out, sum_out, beside_out, rest_out) = refs[:7]
    (rows, back, res, sgr, w_in, w_out, own, up, down, made) = refs[7:17]
    (d_send, d_recv, r_send, r_recv, w_sem, made_sem, up_send, up_recv, down_recv) = refs[17:26]
    (out_send, sib_send, sib_recv, keep_sem) = refs[26:]
    s = pl.program_id(0)
    z, core, f = lax.axis_index("z"), lax.axis_index("core"), lax.axis_index("fsdp")
    members = CORES * groups
    me = core * groups + f
    parts = FF // BLOCK
    steps = mine * parts
    last = pl.num_programs(0) - 1
    left = z < nz // 2
    inner = jnp.where(left, z + 1, z - 1)
    has_outer = jnp.logical_and(z > 0, z < nz - 1)
    edge = jnp.logical_not(has_outer)
    outer = jnp.where(has_outer, jnp.where(left, z - 1, z + 1), inner)

    def member(d):
        there = lax.rem(me + d, members)
        return there, (z, there // groups, lax.rem(there, groups))

    def rows_to(j, d):
        there, device = member(d)
        return pltpu.make_async_remote_copy(
            src_ref=sent_ref.at[j, there],
            dst_ref=rows.at[j, me],
            send_sem=d_send.at[j, d],
            recv_sem=d_recv.at[j, d],
            device_id=device,
            device_id_type=MESH_ID,
        )

    def rows_here(j):
        return pltpu.make_async_copy(sent_ref.at[j, me], rows.at[j, me], d_recv.at[j, 0])

    def send_rows(j):
        for d in range(1, members):
            rows_to(j, d).start()
        rows_here(j).start()

    def results_to(j, d):
        there, device = member(d)
        return pltpu.make_async_remote_copy(
            src_ref=back.at[j % 2, there],
            dst_ref=table_out.at[j, me],
            send_sem=r_send.at[j, d],
            recv_sem=r_recv.at[j, d],
            device_id=device,
            device_id_type=MESH_ID,
        )

    def results_here(j):
        return pltpu.make_async_copy(back.at[j % 2, me], table_out.at[j, me], r_recv.at[j, 0])

    def weights(step):
        e = core * mine + step // parts
        c = pl.ds(pl.multiple_of(lax.rem(step, parts) * BLOCK, BLOCK), BLOCK)
        slot = lax.rem(step, 2)
        return (
            pltpu.make_async_copy(win_hbm.at[e, :, c], w_in.at[slot], w_sem.at[0, slot]),
            pltpu.make_async_copy(wout_hbm.at[e, c, :], w_out.at[slot], w_sem.at[1, slot]),
        )

    @pl.when(s == 0)
    def _():
        barrier = pltpu.get_barrier_semaphore()
        pl.semaphore_signal(barrier, inc=1, device_id=(inner, core, f), device_id_type=MESH_ID)

        @pl.when(has_outer)
        def _():
            pl.semaphore_signal(barrier, inc=1, device_id=(outer, core, f), device_id_type=MESH_ID)

        for d in range(1, members):
            pl.semaphore_signal(barrier, inc=1, device_id=member(d)[1], device_id_type=MESH_ID)

        @pl.when(has_outer)
        def _():
            pl.semaphore_wait(barrier, members + 1)

        @pl.when(edge)
        def _():
            pl.semaphore_wait(barrier, members)

        send_rows(0)
        for w in weights(s):
            w.start()

    for j in range(mine):

        @pl.when(s == j * parts)
        def _(j=j):
            for d in range(1, members):
                rows_to(j, d).wait_recv()
            rows_here(j).wait()
            if j == 0:
                send_rows(1)
            if j == 1:
                send_rows(3)

    slot = lax.rem(s, 2)

    def made_to(step, side, near):
        place = 2 * step + side - SUMMED - (0 if near else BESIDE)
        there = lax.rem(step, 2)
        out = beside_out if near else rest_out
        return pltpu.make_async_copy(
            made.at[there, side],
            out.at[jnp.clip(place, 0, out.shape[0] - 1)],
            made_sem.at[there, side],
        )

    def each_made(step, act):
        near = step < (SUMMED + BESIDE) // 2

        @pl.when(near)
        def _():
            for side in range(2):
                act(made_to(step, side, True))

        @pl.when(jnp.logical_not(near))
        def _():
            for side in range(2):
                act(made_to(step, side, False))

    @pl.when(s < steps)
    def _():
        for w in weights(s):
            w.wait()

        @pl.when(s + 1 < steps)
        def _():
            for w in weights(s + 1):
                w.start()

        @pl.when(jnp.logical_and(s >= SUMMED // 2 + 2, s < steps))
        def _():
            each_made(s - 2, lambda copy: copy.wait())

        j = s // parts
        part = lax.rem(s, parts)
        count = members * CAP
        slots = rows[j, :, 0:CAP, :].reshape(count, D)
        grads = rows[j, :, CAP : 2 * CAP, :].reshape(count, D)
        result, slot_grad, d_in, d_out = expert_math(slots, grads, w_in[slot], w_out[slot])

        @pl.when(part == 0)
        def _():
            res[...] = result
            sgr[...] = slot_grad

        @pl.when(part > 0)
        def _():
            res[...] += result
            sgr[...] += slot_grad

        @pl.when(s < SUMMED // 2)
        def _():
            own[2 * s] = d_in.astype(NARROW)
            own[2 * s + 1] = d_out.astype(NARROW)

        @pl.when(s >= SUMMED // 2)
        def _():
            made[slot, 0] = d_in.astype(NARROW)
            made[slot, 1] = d_out.astype(NARROW)

            each_made(s, lambda copy: copy.start())

    @pl.when(s == 1)
    def _():
        send_rows(2)

    for j in range(mine):

        @pl.when(s == (j + 1) * parts - 1)
        def _(j=j):
            if j >= 2:
                for d in range(1, members):
                    results_to(j - 2, d).wait_send()
                results_here(j - 2).wait()
            back[j % 2, :, :, 0:D] = res[...].astype(NARROW).reshape(members, CAP, D)
            back[j % 2, :, :, D : 2 * D] = sgr[...].astype(NARROW).reshape(members, CAP, D)
            for d in range(1, members):
                results_to(j, d).start()
            results_here(j).start()

    def send_up(t, to_center):
        return pltpu.make_async_remote_copy(
            src_ref=own.at[t],
            dst_ref=(down if to_center else up).at[t],
            send_sem=up_send.at[t],
            recv_sem=(down_recv if to_center else up_recv).at[t],
            device_id=(inner, core, f),
            device_id_type=MESH_ID,
        )

    def send_out(t):
        return pltpu.make_async_remote_copy(
            src_ref=down.at[t],
            dst_ref=down.at[t],
            send_sem=out_send.at[t],
            recv_sem=down_recv.at[t],
            device_id=(outer, core, f),
            device_id_type=MESH_ID,
        )

    def to_sibling(t):
        return pltpu.make_async_remote_copy(
            src_ref=down.at[t],
            dst_ref=sum_out.at[t, core],
            send_sem=sib_send.at[t],
            recv_sem=sib_recv.at[t],
            device_id=(z, 1 - core, f),
            device_id_type=MESH_ID,
        )

    def keep_sum(t):
        return pltpu.make_async_copy(down.at[t], sum_out.at[t, core], keep_sem.at[t])

    def at(lag, role):
        t = s - lag
        return pl.when(jnp.logical_and(role, jnp.logical_and(t >= 0, t < SUMMED)))

    def tick(t):
        return jnp.clip(t, 0, SUMMED - 1)

    @at(0, edge)
    def _():
        send_up(tick(s), False).start()

    @at(LAGS[0], has_outer)
    def _():
        t = tick(s - LAGS[0])
        send_up(t, False).wait_recv()
        add_rows(own.at[t], own.at[t], up.at[t], BLOCK, 16)
        send_up(t, True).start()

    @at(LAGS[1], has_outer)
    def _():
        t = tick(s - LAGS[1])
        send_out(t).wait_recv()
        add_rows(down.at[t], own.at[t], down.at[t], BLOCK, 16)
        send_out(t).start()
        keep_sum(t).start()
        to_sibling(t).start()

    @at(LAGS[2], edge)
    def _():
        t = tick(s - LAGS[2])
        send_out(t).wait_recv()
        keep_sum(t).start()
        to_sibling(t).start()

    @pl.when(s == last)
    def _():
        for step in (steps - 2, steps - 1):
            for side in range(2):
                made_to(step, side, False).wait()
        for j in range(mine):
            for d in range(1, members):
                rows_to(j, d).wait_send()
                results_to(j, d).wait_recv()
                if j >= mine - 2:
                    results_to(j, d).wait_send()
            if j >= mine - 2:
                results_here(j).wait()

        for t in range(SUMMED):
            send_up(t, False).wait_send()
            keep_sum(t).wait()
            to_sibling(t).wait()

        @pl.when(has_outer)
        def _():
            for t in range(SUMMED):
                send_out(t).wait_send()


def exchange(sent, win, wout, nz, groups):
    mine, members = sent.shape[0], sent.shape[1]
    steps = mine * (FF // BLOCK)
    rest = 2 * steps - SUMMED - BESIDE
    any_space = pl.BlockSpec(memory_space=pl.ANY)
    dma = pltpu.SemaphoreType.DMA
    block = pltpu.VMEM((SUMMED, BLOCK, BLOCK), NARROW)
    return pl.pallas_call(
        partial(exchange_kernel, nz, groups, mine),
        grid=(max(steps, SUMMED + LAGS[2]),),
        in_specs=[any_space] * 3,
        out_specs=[any_space] * 4,
        out_shape=[
            sds((mine, members, CAP, 2 * D), NARROW),
            sds((2 * steps, CORES, BLOCK, BLOCK), NARROW),
            sds((BESIDE, BLOCK, BLOCK), NARROW),
            sds((rest, BLOCK, BLOCK), NARROW),
        ],
        scratch_shapes=[
            pltpu.VMEM((mine, members, 2 * CAP, D), NARROW),
            pltpu.VMEM((2, members, CAP, 2 * D), NARROW),
            pltpu.VMEM((members * CAP, D), WIDE),
            pltpu.VMEM((members * CAP, D), WIDE),
            pltpu.VMEM((2, D, BLOCK), NARROW),
            pltpu.VMEM((2, BLOCK, D), NARROW),
            block,
            block,
            block,
            pltpu.VMEM((2, 2, BLOCK, BLOCK), NARROW),
            *[dma((mine, members)) for _ in range(4)],
            dma((2, 2)),
            dma((2, 2)),
            *[dma((SUMMED,)) for _ in range(7)],
        ],
        compiler_params=pltpu.CompilerParams(
            vmem_limit_bytes=58 * MIB, collective_id=7, has_side_effects=True
        ),
        name="experts",
    )(sent, win, wout)


def finish_small(refs):
    (wide_ref, deep_ref, out_ref, peak_ref, limit_ref, query_ref, key_ref) = refs[:7]
    (gain_out, q_out, k_out, v_out, o_out, ffn_out, in_out, mlp_out, router_out, cq_out, ck_out) = refs[7:]
    for n, ref in enumerate((q_out, k_out, v_out, o_out)):
        c = slice(n * D, (n + 1) * D)
        ref[0] = wide_ref[:, c].astype(WIDE)
        ref[1] = deep_ref[:, c].astype(WIDE)
    in_out[...] = wide_ref[:, 4 * D : 8 * D].astype(WIDE)
    mlp_out[...] = out_ref[...].astype(WIDE)
    small = deep_ref[:, 4 * D :].astype(WIDE) + wide_ref[:, 8 * D :].astype(WIDE)
    router_out[...] = small[:, :EXPERTS]
    count = small.shape[0]
    if count < 128:
        small = jnp.concatenate([small, jnp.zeros((128 - count, 128), WIDE)], 0)
    turned = jnp.transpose(small)
    gain_out[...] = turned[EXPERTS : EXPERTS + 2, :count]
    ffn_out[...] = turned[EXPERTS + 2 : EXPERTS + 4, :count]
    head = lax.broadcasted_iota(jnp.int32, (HEADS, D), 0)
    feature = lax.broadcasted_iota(jnp.int32, (HEADS, D), 1)
    owns = jnp.logical_and(feature >= head * HEAD, feature < (head + 1) * HEAD)
    for layer in range(2):
        limit = limit_ref[:, layer : layer + 1]
        top = peak_ref[:, layer * 64 : layer * 64 + 1]
        scale = jnp.sqrt(limit / jnp.maximum(top, limit))
        row = jnp.sum(jnp.where(owns, scale, 0.0), 0, keepdims=True)
        cq_out[layer] = query_ref[layer] * row
        ck_out[layer] = key_ref[layer] * row


PAIRS = 2


def widen_blocks(blocks_ref, in_ref, out_ref):
    for n in range(PAIRS):
        r = slice(n * BLOCK, (n + 1) * BLOCK)
        in_ref[:, r] = blocks_ref[n, 0].astype(WIDE)
        out_ref[r, :] = blocks_ref[n, 1].astype(WIDE)


def block_specs(mine, first):
    parts = FF // BLOCK // PAIRS
    wide = PAIRS * BLOCK

    def place(c, s):
        return c * mine + (s + first) // parts, (s + first) % parts

    return (
        pl.BlockSpec((PAIRS, 2, None, BLOCK, BLOCK), lambda c, s: (s + first, 0, c, 0, 0)),
        [
            pl.BlockSpec((None, D, wide), lambda c, s: (place(c, s)[0], 0, place(c, s)[1])),
            pl.BlockSpec((None, wide, D), lambda c, s: (*place(c, s), 0)),
        ],
    )


def gradient_shapes(mine):
    return [sds((CORES * mine, D, FF), WIDE), sds((CORES * mine, FF, D), WIDE)]


def widen_early(blocks, count, mine):
    source, places = block_specs(mine, 0)
    return pl.pallas_call(
        widen_blocks,
        grid=(CORES, count // 2 // PAIRS),
        in_specs=[source],
        out_specs=places,
        out_shape=gradient_shapes(mine),
        compiler_params=params(60),
        name="widen_early",
    )(blocks.reshape(-1, 2, CORES, BLOCK, BLOCK))


def finish_kernel(given, blocks_ref, *refs):
    small, (in_ref, out_ref) = refs[given:-2], refs[-2:]

    @pl.when(jnp.logical_and(pl.program_id(0) == 0, pl.program_id(1) == 0))
    def _():
        finish_small(small)

    widen_blocks(blocks_ref, in_ref, out_ref)


def finish(blocks, done, given, mine, small, outs):
    first = done // 2 // PAIRS
    source, places = block_specs(mine, first)
    steps = blocks.shape[0] // 2 // PAIRS - first
    return pl.pallas_call(
        partial(finish_kernel, len(given)),
        grid=(CORES, steps),
        in_specs=[
            source,
            *[pl.BlockSpec(memory_space=pl.ANY)] * len(given),
            *[whole(a.shape) for a in small],
        ],
        out_specs=[whole(o.shape) for o in outs] + places,
        out_shape=[*outs, *gradient_shapes(mine)],
        input_output_aliases={1 + n: len(outs) + n for n in range(len(given))},
        compiler_params=params(60),
        name="finish",
    )(blocks.reshape(-1, 2, CORES, BLOCK, BLOCK), *given, *small)


def forward_kernel(groups, ib, *refs):
    q_ref, k_ref, v_ref, o_ref, small_ref, in_ref, out_ref, refs = *refs[:7], refs[7:]
    token_ref, cot_ref, order_ref, routes_ref, refs = *refs[:4], refs[4:]
    kept, refs = refs[:4], refs[4:]
    gain_ref, router_ref, x_out, cot_out, pos_ref, aux_ref, refs = *refs[:6], refs[6:]
    first_ref, qkv0_ref, mixed0_ref, peak0_ref, mid_ref, refs = *refs[:5], refs[5:]
    second_ref, qkv1_ref, mixed1_ref, peak1_ref, moe_ref, prob_ref, refs = *refs[:6], refs[6:]
    w0, win, wout, w1, small_all, state, wide_ref, line_ref, rows_ref, refs = *refs[:9], refs[9:]
    send, recv, pass_send, pass_recv, copy, rows_sem, kept_sem = refs
    phase, i = pl.program_id(0), pl.program_id(1)
    z, core, f = lax.axis_index("z"), lax.axis_index("core"), lax.axis_index("fsdp")

    def rows(count, owner, side):
        half = count // CORES
        return pl.ds(pl.multiple_of(owner * count + side * half, 16), half)

    def item(n):
        if n < 4 or n >= 7:
            ref = (q_ref, k_ref, v_ref, o_ref)[n % 7]
            full, layer = (w0, 0) if n < 4 else (w1, 1)
            count = ref.shape[1]
            cols = pl.ds(n % 7 * D, D)
            return (
                lambda side: ref.at[layer, rows(count, 0, side), :],
                lambda owner, side: full.at[rows(count, owner, side), cols],
            )
        ref, full = ((small_ref, small_all), (in_ref, win), (out_ref, wout))[n - 4]
        count = ref.shape[0]
        return (
            lambda side: ref.at[rows(count, 0, side), :],
            lambda owner, side: full.at[rows(count, owner, side), :],
        )

    def fetch(n, d):
        source, place = item(n)
        return pltpu.make_async_remote_copy(
            src_ref=source(core),
            dst_ref=place(f, core),
            send_sem=send.at[n, d],
            recv_sem=recv.at[n, d],
            device_id=(z, core, lax.rem(f + d, groups)),
            device_id_type=MESH_ID,
        )

    def hand_on(n, d):
        _, place = item(n)
        there = place(lax.rem(f + groups - d, groups), core)
        return pltpu.make_async_remote_copy(
            src_ref=there,
            dst_ref=there,
            send_sem=pass_send.at[n, d],
            recv_sem=pass_recv.at[n, d],
            device_id=(z, 1 - core, f),
            device_id_type=MESH_ID,
        )

    def keep(n, side):
        source, place = item(n)
        return pltpu.make_async_copy(source(side), place(f, side), copy.at[n, side])

    sets = ((0, 1, 2, 3, 4), (5, 6), (7, 8, 9, 10))

    def begin(stage):
        for n in sets[stage]:
            for d in range(1, groups):
                fetch(n, d).start()
            for side in range(CORES):
                keep(n, side).start()

    def arrive(stage):
        for n in sets[stage]:
            for d in range(1, groups):
                fetch(n, d).wait_recv()
                hand_on(n, d).start()

    def complete(stage):
        for n in sets[stage]:
            for side in range(CORES):
                keep(n, side).wait()
            for d in range(1, groups):
                fetch(n, d).wait_send()
                hand_on(n, d).wait()

    def keepers():
        return [
            pltpu.make_async_copy(ref, out, kept_sem.at[n])
            for n, (ref, out) in enumerate(zip((w0, win, wout, w1), kept))
        ]

    start = i == 0

    @pl.when(jnp.logical_and(phase == 0, start))
    def _():
        barrier = pltpu.get_barrier_semaphore()
        for d in range(1, groups):
            there = (z, core, lax.rem(f + d, groups))
            pl.semaphore_signal(barrier, inc=1, device_id=there, device_id_type=MESH_ID)
        pl.semaphore_signal(barrier, inc=1, device_id=(z, 1 - core, f), device_id_type=MESH_ID)
        pl.semaphore_wait(barrier, groups)
        begin(0)
        begin(1)
        loads = [
            pltpu.make_async_copy(ref, rows_ref.at[n], rows_sem.at[n])
            for n, ref in enumerate((token_ref, cot_ref))
        ]
        for load in loads:
            load.start()
        for n, out in enumerate((x_out, cot_out)):
            loads[n].wait()
            pad_images(rows_ref.at[n], wide_ref, out)
        arrive(0)
        find_places(order_ref, routes_ref, pos_ref, aux_ref, line_ref)
        complete(0)
        lane = lax.broadcasted_iota(jnp.int32, (1, 128), 1)
        small = small_all[...].astype(WIDE)
        router_ref[...] = jnp.where(lane < EXPERTS, small, 0.0).astype(NARROW)
        gain_ref[...] = jnp.transpose(small)[EXPERTS : EXPERTS + 8, :]

    @pl.when(jnp.logical_and(phase == 1, start))
    def _():
        arrive(1)
        begin(2)
        complete(1)

    @pl.when(jnp.logical_and(phase == 2, start))
    def _():
        arrive(2)
        complete(2)
        for k in keepers():
            k.start()

    images = pl.ds(i * ib, ib)

    @pl.when(phase == 0)
    def _():
        x = x_out[images].astype(WIDE).reshape(ib * SP, D)
        y = attn_fwd_body(x, gain_ref[0:1, :], w0, qkv0_ref, mixed0_ref, peak0_ref, ib)
        y = y.reshape(ib, SP, D)
        first_ref[...] = y
        state[images] = y

    @pl.when(phase == 1)
    def _():
        x = state[images].reshape(ib * SP, D)
        unit, _ = norm_parts(x)
        normed = (unit * gain_ref[2:3, :]).astype(NARROW)
        acc = x
        for n in range(FF // 512):
            c = slice(n * 512, (n + 1) * 512)
            pre = nn(normed, win[:, c])
            cdf, _ = normal_parts(pre)
            acc = acc + nn((pre * cdf).astype(NARROW), wout[c, :])
        y = acc.reshape(ib, SP, D)
        mid_ref[...] = y
        state[images] = y

    @pl.when(phase == 2)
    def _():
        x = state[images].reshape(ib * SP, D)
        y = attn_fwd_body(x, gain_ref[1:2, :], w1, qkv1_ref, mixed1_ref, peak1_ref, ib)
        second_ref[...] = y.reshape(ib, SP, D)
        unit, _ = norm_parts(y)
        moe = (unit * gain_ref[3:4, :]).astype(NARROW)
        moe_ref[...] = moe.reshape(ib, SP, D)
        lane = lax.broadcasted_iota(jnp.int32, (1, 128), 1)
        logits = jnp.where(lane < EXPERTS, nn(moe, router_ref[...]), LOWEST)
        e = jnp.exp(logits - jnp.max(logits, -1, keepdims=True))
        prob_ref[...] = (e / jnp.sum(e, -1, keepdims=True)).reshape(ib, SP, 128)

    @pl.when(jnp.logical_and(phase == 2, i == pl.num_programs(1) - 1))
    def _():
        for k in keepers():
            k.wait()


def forward(weights, tokens, cotangent, routes_rows, groups, held, ib):
    any_space = pl.BlockSpec(memory_space=pl.ANY)
    vmem = pl.BlockSpec(memory_space=pltpu.VMEM)
    dma = pltpu.SemaphoreType.DMA
    images = tokens.shape[0] // SEQ
    padded, pairs = images * SP, images // ib
    slots = np.arange(EXPERTS, dtype=np.int32)[:, None]
    order = np.broadcast_to(slot_expert(slots, groups, held), (EXPERTS, 128)).astype(np.int32)

    def of_phase(n, *tail):
        def place(phase, i):
            return (jnp.where(phase == n, i, jnp.where(phase < n, 0, pairs - 1)), *[0] * len(tail))

        return pl.BlockSpec((ib, *tail), place)

    tails = (
        (0, WIDE, SP, D),
        (0, NARROW, SP, 3 * D),
        (0, NARROW, SP, D),
        (0, WIDE, HEADS, 128),
        (1, WIDE, SP, D),
        (2, WIDE, SP, D),
        (2, NARROW, SP, 3 * D),
        (2, NARROW, SP, D),
        (2, WIDE, HEADS, 128),
        (2, NARROW, SP, D),
        (2, WIDE, SP, 128),
    )
    matrices = [(D, 4 * D), (D, FF), (FF, D), (D, 4 * D)]
    return pl.pallas_call(
        partial(forward_kernel, groups, ib),
        grid=(3, pairs),
        in_specs=[any_space] * 9 + [vmem] * 2,
        out_specs=[any_space] * 4
        + [vmem] * 6
        + [of_phase(n, *tail) for n, _, *tail in tails],
        out_shape=[
            *[sds(m, NARROW) for m in matrices],
            sds((8, D), WIDE),
            sds((D, 128), NARROW),
            sds((images, SP, D), NARROW),
            sds((images, SP, D), NARROW),
            sds((EXPERTS, padded), WIDE),
            sds((padded, 128), WIDE),
            *[sds((images, *tail), dtype) for _, dtype, *tail in tails],
        ],
        scratch_shapes=[
            *[pltpu.VMEM(m, NARROW) for m in matrices],
            pltpu.VMEM((D, 128), NARROW),
            pltpu.VMEM((images, SP, D), WIDE),
            pltpu.VMEM((-(-(tokens.shape[0] + SP) // 16) * 16, D), WIDE),
            pltpu.VMEM((128, padded), WIDE),
            pltpu.VMEM((2, *tokens.shape), NARROW),
            *[dma((11, groups)) for _ in range(4)],
            dma((11, CORES)),
            dma((2,)),
            dma((4,)),
        ],
        compiler_params=pltpu.CompilerParams(
            vmem_limit_bytes=60 * MIB, collective_id=5, has_side_effects=True
        ),
        name="forward",
    )(*weights, tokens, cotangent, jnp.asarray(order), routes_rows)


def local(
    tokens,
    cotangent,
    routes,
    attn_norm,
    query_w,
    key_w,
    value_w,
    output_w,
    ffn_norm,
    mlp_in,
    mlp_out,
    router_w,
    expert_in,
    expert_out,
    updated_query,
    updated_key,
    clip_threshold,
):
    images = tokens.shape[0] // SEQ
    ib = 2
    groups = lax.axis_size("fsdp")
    core = lax.axis_index("core")
    held = expert_in.shape[0]
    mine = held // CORES
    owners = CORES * groups

    small = jnp.concatenate(
        [
            router_w,
            jnp.transpose(attn_norm),
            jnp.transpose(ffn_norm),
            jnp.zeros((router_w.shape[0], 128 - EXPERTS - 4), NARROW),
        ],
        1,
    )
    routes_rows = jnp.pad(
        jnp.transpose(routes).reshape(2, images, SEQ),
        ((0, 6), (0, 0), (0, SP - SEQ)),
        constant_values=-1,
    ).reshape(8, -1)
    w0, win, wout, w1, gains, wr, x, cot, pos, aux, *states = forward(
        (query_w, key_w, value_w, output_w, small, mlp_in, mlp_out),
        tokens,
        cotangent,
        routes_rows,
        groups,
        held,
        ib,
    )
    first, qkv0, mixed0, peak0, mid, second, qkv1, mixed1, peak1, moe, prob = states
    aux = aux.reshape(images, SP, 128)

    sent = dispatch(
        pos, moe.reshape(-1, D), cot.reshape(-1, D), prob.reshape(-1, 128), groups, held
    ).reshape(mine, owners, 2 * CAP, D)

    nz = lax.axis_size("z")
    early = own = None
    if nz == 4 and owners == 8 and mine == 4:
        tables, early, own, late = exchange(sent, expert_in, expert_out, nz, groups)
        own = lax.psum(own, "z")
    else:
        tables, blocks = [], []
        for j in range(mine):
            rows = lax.all_to_all(
                sent[j], ("core", "fsdp"), split_axis=0, concat_axis=0, tiled=True
            )
            pick = (core * mine + j).astype(jnp.int32).reshape(1)
            back, d_in, d_out = expert(pick, rows, expert_in, expert_out)
            tables.append(
                lax.all_to_all(back, ("core", "fsdp"), split_axis=0, concat_axis=0, tiled=True)
            )
            blocks.append(jnp.stack([d_in, d_out], 1).reshape(-1, BLOCK, BLOCK))
        tables = jnp.stack(tables)
        late = jnp.concatenate(blocks)

    y, mid_grad, dw1 = moe_bwd(
        gains, w1, wr, mid, second, cot, prob, aux, qkv1, mixed1, tables, images, ib
    )
    x_grad, dw0, d_wout = dense_bwd(
        gains, w0, win, wout, x, first, mid_grad, qkv0, mixed0, images, ib
    )
    lane = jnp.arange(128)[None, :]
    peaks = jnp.where(lane < 64, jnp.max(peak0, 0), jnp.max(peak1, 0))
    given = []
    if early is not None:
        (early, _, _) = lax.optimization_barrier((early, dw0, d_wout))
        given = widen_early(early, SUMMED, mine)
        (late, *given) = lax.optimization_barrier((late, *given))
    blocks, t1, t0, t_wout, maxima = sum_all(
        [late], [dw1, dw0, d_wout], peaks, early, own, nz, groups
    )
    small_outs = [
        sds(attn_norm.shape, WIDE),
        *[sds(query_w.shape, WIDE)] * 4,
        sds(ffn_norm.shape, WIDE),
        sds(mlp_in.shape, WIDE),
        sds(mlp_out.shape, WIDE),
        sds(router_w.shape, WIDE),
        sds(updated_query.shape, WIDE),
        sds(updated_key.shape, WIDE),
    ]
    *grads, clipped_query, clipped_key, expert_in_grad, expert_out_grad = finish(
        blocks,
        SUMMED if given else 0,
        given,
        mine,
        [t0, t1, t_wout, maxima, jnp.transpose(clip_threshold), updated_query, updated_key],
        small_outs,
    )
    return (y, x_grad, *grads, expert_in_grad, expert_out_grad, clipped_query, clipped_key)


def solution(mesh):
    replicas, groups = mesh.shape["replica"], mesh.shape["fsdp"]
    inner = Mesh(
        mesh.devices.reshape(replicas // CORES, CORES, groups), ("z", "core", "fsdp")
    )
    split = P(("z", "core", "fsdp"), None)
    second = P(None, "fsdp", None)
    in_specs = (
        split,
        split,
        split,
        P(None, "fsdp"),
        second,
        second,
        second,
        second,
        P(None, "fsdp"),
        P("fsdp", None),
        P("fsdp", None),
        P("fsdp", None),
        P("fsdp", None, None),
        P("fsdp", None, None),
        second,
        second,
        P(),
    )
    out_specs = (
        split,
        split,
        P(None, "fsdp"),
        second,
        second,
        second,
        second,
        P(None, "fsdp"),
        P("fsdp", None),
        P("fsdp", None),
        P("fsdp", None),
        P("fsdp", None, None),
        P("fsdp", None, None),
        second,
        second,
    )
    return jax.shard_map(local, mesh=inner, in_specs=in_specs, out_specs=out_specs, check_vma=False)
```

```python
from functools import partial

import jax
import jax.numpy as jnp
import numpy as np
from jax import lax
from jax.experimental import pallas as pl
from jax.experimental.pallas import tpu as pltpu
from jax.sharding import Mesh
from jax.sharding import PartitionSpec as P

D = 512
HEADS = 8
HEAD = 64
FF = 2048
SEQ = 197
SP = 208
CAP = 128
EXPERTS = 32
EPSILON = 1e-06
SCALE = HEAD ** (-0.5)
LOWEST = -1e30
NARROW = jnp.bfloat16
WIDE = jnp.float32
CORES = 2
MIB = 1 << 20


def nn(a, b):
    return lax.dot_general(a, b, (((1,), (0,)), ((), ())), preferred_element_type=WIDE)


def nt(a, b):
    return lax.dot_general(a, b, (((1,), (1,)), ((), ())), preferred_element_type=WIDE)


def tn(a, b):
    return lax.dot_general(a, b, (((0,), (0,)), ((), ())), preferred_element_type=WIDE)


def norm_parts(values):
    centred = values - jnp.mean(values, -1, keepdims=True)
    inverse = lax.rsqrt(jnp.mean(centred * centred, -1, keepdims=True) + EPSILON)
    return centred * inverse, inverse


def norm_backward(incoming, unit, inverse, gain):
    gain_grad = jnp.sum(incoming * unit, 0, keepdims=True)
    scaled = incoming * gain
    centred = (
        scaled
        - jnp.mean(scaled, -1, keepdims=True)
        - unit * jnp.mean(scaled * unit, -1, keepdims=True)
    )
    return inverse * centred, gain_grad


def normal_parts(x):
    z = jnp.abs(x)
    t = 1.0 / (1.0 + (0.3275911 * 0.7071067811865476) * z)
    bell = jnp.exp(-0.5 * (x * x))
    poly = t * (
        0.5 * 0.254829592
        + t
        * (
            0.5 * -0.284496736
            + t * (0.5 * 1.421413741 + t * (0.5 * -1.453152027 + t * (0.5 * 1.061405429)))
        )
    )
    tail = poly * bell
    return jnp.where(x >= 0, 1.0 - tail, tail), bell


INV_ROOT = 0.3989422804014327


def head_masks(dtype):
    lane = lax.broadcasted_iota(jnp.int32, (1, 2 * HEAD), 1)
    low = (lane < HEAD).astype(dtype)
    return (low, (1 - low.astype(WIDE)).astype(dtype))


def attn_fwd_body(x, gain, w_ref, qkv_ref, mixed_ref, peak_ref, ib):
    unit, _ = norm_parts(x)
    normed = (unit * gain).astype(NARROW)
    q = (nn(normed, w_ref[:, 0:D]).astype(NARROW).astype(WIDE) * SCALE).astype(NARROW)
    k = nn(normed, w_ref[:, D : 2 * D]).astype(NARROW)
    v = nn(normed, w_ref[:, 2 * D : 3 * D]).astype(NARROW)
    masks = head_masks(NARROW)
    cols = lax.broadcasted_iota(jnp.int32, (SP, SP), 1)
    rows = lax.broadcasted_iota(jnp.int32, (SP, 1), 0)
    head_row = lax.broadcasted_iota(jnp.int32, (HEADS, 128), 0)
    mixed_all = []
    for i in range(ib):
        peaks = jnp.full((HEADS, 128), LOWEST, WIDE)
        r = slice(i * SP, (i + 1) * SP)
        pairs = []
        for pair in range(HEADS // 2):
            c = slice(pair * 2 * HEAD, (pair + 1) * 2 * HEAD)
            qp, kp, vp = q[r, c], k[r, c], v[r, c]
            acc = None
            for half in range(2):
                s = nt(qp * masks[half], kp)
                s = jnp.where(cols < SEQ, s, LOWEST)
                top = jnp.max(s, -1, keepdims=True)
                e = jnp.exp(s - top)
                p = (e * (1.0 / jnp.sum(e, -1, keepdims=True))).astype(NARROW)
                part = nn(p, vp * masks[half])
                acc = part if acc is None else acc + part
                peak = jnp.max(jnp.where(rows < SEQ, top, LOWEST), 0, keepdims=True)
                peaks = jnp.where(head_row == pair * 2 + half, peak, peaks)
            pairs.append(acc.astype(NARROW))
        mixed_all.append(jnp.concatenate(pairs, 1))
        peak_ref[i] = peaks
    mixed = jnp.concatenate(mixed_all, 0) if ib > 1 else mixed_all[0]
    qkv_ref[...] = jnp.concatenate([q, k, v], 1).reshape(ib, SP, 3 * D)
    mixed_ref[...] = mixed.reshape(ib, SP, D)
    return x + nn(mixed, w_ref[:, 3 * D : 4 * D])


def whole(shape):
    return pl.BlockSpec(
        shape, lambda *_: (0,) * len(shape), pipeline_mode=pl.Buffered(buffer_count=1)
    )


def per_image(ib, *tail):
    return pl.BlockSpec((ib, *tail), lambda i, *_: (i,) + (0,) * len(tail))


def sds(shape, dtype):
    return jax.ShapeDtypeStruct(shape, dtype)


def cost(flops, moved):
    return pl.CostEstimate(flops=int(flops), bytes_accessed=int(moved), transcendentals=0)


def params(mib):
    return pltpu.CompilerParams(vmem_limit_bytes=mib * MIB)


def find_places(order_ref, routes_ref, pos_ref, aux_ref, line_ref):
    tokens = routes_ref.shape[1]
    order = order_ref[:, 0:1]
    chunk = 128
    strict = (
        lax.broadcasted_iota(jnp.int32, (chunk, chunk), 0)
        < lax.broadcasted_iota(jnp.int32, (chunk, chunk), 1)
    ).astype(NARROW)
    slot_row = lax.broadcasted_iota(jnp.int32, (EXPERTS, 1), 0).astype(WIDE) * CAP
    base = jnp.zeros((EXPERTS, 1), WIDE)
    pos_ref[...] = jnp.full(pos_ref.shape, -1.0, WIDE)
    line_ref[...] = jnp.zeros(line_ref.shape, WIDE)
    for k in range(2):
        for c in range(tokens // chunk):
            s = slice(c * chunk, (c + 1) * chunk)
            hit = (order == routes_ref[k : k + 1, s]).astype(WIDE)
            place = base + nn(hit.astype(NARROW), strict)
            base = base + jnp.sum(hit, -1, keepdims=True)
            pos_ref[:, s] = jnp.where(hit > 0, place, pos_ref[:, s])
            slot = jnp.where(place < CAP, slot_row + place, 2.0 * EXPERTS * CAP)
            found = jnp.sum(hit * slot, 0, keepdims=True)
            real = jnp.sum(hit, 0, keepdims=True)
            line_ref[k : k + 1, s] = jnp.where(real > 0, found, 2.0 * EXPERTS * CAP)
            line_ref[2 + k : 3 + k, s] = routes_ref[k : k + 1, s].astype(WIDE)
    for c in range(tokens // chunk):
        s = slice(c * chunk, (c + 1) * chunk)
        aux_ref[s, :] = jnp.transpose(line_ref[:, s])


def pad_images(ref, wide_ref, out_ref):
    tokens = ref.shape[0]
    wide_ref[0:tokens, :] = ref[...].astype(WIDE)
    rows = lax.broadcasted_iota(jnp.int32, (SP, 1), 0)
    for i in range(tokens // SEQ):
        image = wide_ref[i * SEQ : i * SEQ + SP, :]
        out_ref[i] = jnp.where(rows < SEQ, image, 0.0).astype(NARROW)


GROUP = 8


def slot_expert(index, groups, held):
    owners, mine = CORES * groups, held // CORES
    owner = index % owners
    return (owner % groups) * held + (owner // groups) * mine + index // owners


def turn_probs(prob_ref, line_ref):
    for c in range(prob_ref.shape[0] // 128):
        s = slice(c * 128, (c + 1) * 128)
        line_ref[:, s] = jnp.transpose(prob_ref[s, :])


def make_rows(experts, places, moe, cot, line_ref, outs):
    slot = lax.broadcasted_iota(jnp.int32, (CAP, 1), 0).astype(WIDE)
    hot, gates = [], []
    for expert, place in zip(experts, places):
        mine = place == slot
        hot.append(mine.astype(WIDE).astype(NARROW))
        gate_row = line_ref[pl.ds(expert, 1), :]
        gates.append(jnp.sum(jnp.where(mine, gate_row, 0.0), -1, keepdims=True))
    hot = jnp.concatenate(hot, 0)
    rows = nn(hot, moe).astype(NARROW)
    grads = nn(hot, cot)
    for g, (gate, out) in enumerate(zip(gates, outs)):
        s = slice(g * CAP, (g + 1) * CAP)
        out[0:CAP, :] = rows[s]
        out[CAP : 2 * CAP, :] = (gate * grads[s]).astype(NARROW)


def dispatch_kernel(groups, held, pos_ref, moe_ref, cot_ref, prob_ref, out_ref, line_ref):
    step = pl.program_id(0)

    @pl.when(step == 0)
    def _():
        turn_probs(prob_ref, line_ref)

    make_rows(
        [slot_expert(step * GROUP + g, groups, held) for g in range(GROUP)],
        [pos_ref[g : g + 1, :] for g in range(GROUP)],
        moe_ref[...],
        cot_ref[...],
        line_ref,
        [out_ref.at[g] for g in range(GROUP)],
    )


def dispatch(pos, moe, cot, prob, groups, held):
    tokens = moe.shape[0]
    return pl.pallas_call(
        partial(dispatch_kernel, groups, held),
        grid=(EXPERTS // GROUP,),
        in_specs=[
            pl.BlockSpec((GROUP, tokens), lambda i: (i, 0)),
            whole(moe.shape),
            whole(cot.shape),
            whole(prob.shape),
        ],
        out_specs=pl.BlockSpec((GROUP, 2 * CAP, D), lambda i: (i, 0, 0)),
        out_shape=sds((EXPERTS, 2 * CAP, D), NARROW),
        scratch_shapes=[pltpu.VMEM((128, tokens), WIDE)],
        compiler_params=params(60),
        name="dispatch",
    )(pos, moe, cot, prob)


def expert_math(slots, grads, win, wout):
    pre = nn(slots, win)
    hidden_grad = nt(grads, wout)
    cdf, bell = normal_parts(pre)
    hidden = (pre * cdf).astype(NARROW)
    pre_grad = ((cdf + pre * (bell * INV_ROOT)) * hidden_grad).astype(NARROW)
    return nn(hidden, wout), nt(pre_grad, win), tn(slots, pre_grad), tn(hidden, grads)


def expert_kernel(pick, rows_ref, win_ref, wout_ref, back_ref, din_ref, dout_ref, res, sgr):
    f = pl.program_id(0)
    senders = rows_ref.shape[0]
    part = min(senders, 8)
    count = part * CAP
    win, wout = win_ref[...], wout_ref[...]
    d_in = d_out = None
    for first in range(0, senders, part):
        slots = rows_ref[first : first + part, 0:CAP, :].reshape(count, D)
        grads = rows_ref[first : first + part, CAP : 2 * CAP, :].reshape(count, D)
        r = slice(first * CAP, (first + part) * CAP)
        result, slot_grad, in_part, out_part = expert_math(slots, grads, win, wout)
        d_in = in_part if d_in is None else d_in + in_part
        d_out = out_part if d_out is None else d_out + out_part

        @pl.when(f == 0)
        def _(r=r, result=result, slot_grad=slot_grad):
            res[r, :] = result
            sgr[r, :] = slot_grad

        @pl.when(f > 0)
        def _(r=r, result=result, slot_grad=slot_grad):
            res[r, :] += result
            sgr[r, :] += slot_grad

    din_ref[...] = d_in.astype(NARROW)
    dout_ref[...] = d_out.astype(NARROW)

    @pl.when(f == pl.num_programs(0) - 1)
    def _():
        back_ref[:, :, 0:D] = res[...].astype(NARROW).reshape(senders, CAP, D)
        back_ref[:, :, D : 2 * D] = sgr[...].astype(NARROW).reshape(senders, CAP, D)


def expert(pick, rows, win, wout):
    senders = rows.shape[0]
    wide = 512
    return pl.pallas_call(
        expert_kernel,
        grid_spec=pltpu.PrefetchScalarGridSpec(
            num_scalar_prefetch=1,
            grid=(FF // wide,),
            in_specs=[
                whole(rows.shape),
                pl.BlockSpec((None, D, wide), lambda f, p: (p[0], 0, f)),
                pl.BlockSpec((None, wide, D), lambda f, p: (p[0], f, 0)),
            ],
            out_specs=[
                whole((senders, CAP, 2 * D)),
                pl.BlockSpec((None, D, wide), lambda f, p: (f, 0, 0)),
                pl.BlockSpec((None, wide, D), lambda f, p: (f, 0, 0)),
            ],
            scratch_shapes=[
                pltpu.VMEM((senders * CAP, D), WIDE),
                pltpu.VMEM((senders * CAP, D), WIDE),
            ],
        ),
        out_shape=[
            sds((senders, CAP, 2 * D), NARROW),
            sds((FF // wide, D, wide), NARROW),
            sds((FF // wide, wide, D), NARROW),
        ],
        compiler_params=params(60),
        cost_estimate=cost(5e9, 1),
        name="one_expert",
    )(pick, rows, win, wout)


def attn_bwd_body(x, incoming, gain, qkv_ref, mixed_ref, w_ref, dw_ref, ib):
    unit, inverse = norm_parts(x)
    normed = (unit * gain).astype(NARROW)
    out_grad = incoming.astype(NARROW)
    mixed = mixed_ref[...].reshape(ib * SP, D)
    dw_ref[:, 3 * D : 4 * D] += tn(mixed, out_grad)
    mixed_grad = nt(out_grad, w_ref[:, 3 * D : 4 * D]).astype(NARROW)
    masks = head_masks(NARROW)
    rows = lax.broadcasted_iota(jnp.int32, (SP, SP), 0)
    dq_all, dk_all, dv_all = [], [], []
    for i in range(ib):
        r = slice(i * SP, (i + 1) * SP)
        dqs, dks, dvs = [], [], []
        for pair in range(HEADS // 2):
            qp = qkv_ref[i, :, pair * 128 : (pair + 1) * 128]
            kp = qkv_ref[i, :, D + pair * 128 : D + (pair + 1) * 128]
            vp = qkv_ref[i, :, 2 * D + pair * 128 : 2 * D + (pair + 1) * 128]
            mp = mixed_grad[r, pair * 128 : (pair + 1) * 128]
            dq = dk = dv = None
            for half in range(2):
                qm, mm, km = qp * masks[half], mp * masks[half], kp * masks[half]
                s = jnp.where(rows < SEQ, nt(kp, qm), LOWEST)
                e = jnp.exp(s - jnp.max(s, 0, keepdims=True))
                soft = e * (1.0 / jnp.sum(e, 0, keepdims=True))
                pg = nt(vp, mm)
                delta = jnp.sum(soft * pg, 0, keepdims=True)
                sg = (soft * (pg - delta)).astype(NARROW)
                v_part = nn(soft.astype(NARROW), mm)
                k_part = nn(sg, qm)
                q_part = tn(sg, km)
                dq = q_part if dq is None else dq + q_part
                dk = k_part if dk is None else dk + k_part
                dv = v_part if dv is None else dv + v_part
            dqs.append((dq * SCALE).astype(NARROW))
            dks.append(dk.astype(NARROW))
            dvs.append(dv.astype(NARROW))
        dq_all.append(jnp.concatenate(dqs, 1))
        dk_all.append(jnp.concatenate(dks, 1))
        dv_all.append(jnp.concatenate(dvs, 1))
    dqkv = jnp.concatenate(
        [
            jnp.concatenate(a, 0) if ib > 1 else a[0]
            for a in (dq_all, dk_all, dv_all)
        ],
        1,
    )
    dw_ref[:, 0 : 3 * D] += tn(normed, dqkv)
    normed_grad = nt(dqkv, w_ref[:, 0 : 3 * D])
    input_grad, gain_grad = norm_backward(normed_grad, unit, inverse, gain)
    return incoming + input_grad, gain_grad


def gain_columns(dg_ref):
    tall = jnp.concatenate(
        [jnp.zeros((EXPERTS, D), WIDE), dg_ref[...], jnp.zeros((128 - EXPERTS - 8, D), WIDE)], 0
    )
    return jnp.transpose(tall)


def put_rows(ref, step, ib, value):
    for image in range(ref.shape[0] // SEQ):

        @pl.when(step == image // ib)
        def _(image=image):
            first = image % ib * SP
            ref[image * SEQ : (image + 1) * SEQ, :] = value[first : first + SEQ]


def moe_bwd_kernel(
    ib,
    g_ref,
    w_ref,
    wr_ref,
    mid_ref,
    second_ref,
    cot_ref,
    prob_ref,
    aux_ref,
    qkv_ref,
    mixed_ref,
    table_ref,
    y_ref,
    grad_ref,
    dw_out,
    dr_ref,
    dg_ref,
    dw_ref,
):
    step = pl.program_id(0)

    @pl.when(step == 0)
    def _():
        dw_ref[...] = jnp.zeros(dw_ref.shape, WIDE)
        dr_ref[...] = jnp.zeros(dr_ref.shape, WIDE)
        dg_ref[...] = jnp.zeros(dg_ref.shape, WIDE)

    second = second_ref[...].reshape(ib * SP, D)
    upstream = cot_ref[...].astype(WIDE).reshape(ib * SP, D)
    prob = prob_ref[...].reshape(ib * SP, 128)
    aux = aux_ref[...].reshape(ib * SP, 128)
    first_pick = second_pick = back = None
    for j in range(table_ref.shape[0]):
        count = table_ref.shape[1] * CAP
        slot = lax.broadcasted_iota(jnp.int32, (1, count), 1).astype(WIDE) + float(j * count)
        hot_one = (aux[:, 0:1] == slot).astype(WIDE).astype(NARROW)
        hot_two = (aux[:, 1:2] == slot).astype(WIDE).astype(NARROW)
        rows = table_ref[j].reshape(count, 2 * D)
        one = nn(hot_one, rows[:, 0:D])
        two = nn(hot_two, rows[:, 0:D])
        both = nn(hot_one + hot_two, rows[:, D : 2 * D])
        first_pick = one if first_pick is None else first_pick + one
        second_pick = two if second_pick is None else second_pick + two
        back = both if back is None else back + both
    lane = lax.broadcasted_iota(jnp.int32, (1, 128), 1)
    first_hit = (aux[:, 2:3] == lane.astype(WIDE)).astype(WIDE)
    second_hit = (aux[:, 3:4] == lane.astype(WIDE)).astype(WIDE)
    gate_one = jnp.sum(prob * first_hit, -1, keepdims=True)
    gate_two = jnp.sum(prob * second_hit, -1, keepdims=True)
    put_rows(y_ref, step, ib, second + (gate_one * first_pick + gate_two * second_pick))
    gate_one_grad = jnp.sum(upstream * first_pick, -1, keepdims=True)
    gate_two_grad = jnp.sum(upstream * second_pick, -1, keepdims=True)
    prob_grad = gate_one_grad * first_hit + gate_two_grad * second_hit
    logit_grad = (prob * (prob_grad - jnp.sum(prob * prob_grad, -1, keepdims=True))).astype(NARROW)
    unit, inverse = norm_parts(second)
    gain = g_ref[3:4, :]
    moe = (unit * gain).astype(NARROW)
    dr_ref[...] += tn(moe, logit_grad)
    normed_grad = back + nt(logit_grad, wr_ref[...])
    moe_grad, gain_grad = norm_backward(normed_grad, unit, inverse, gain)
    dg_ref[3:4, :] += gain_grad
    mid = mid_ref[...].reshape(ib * SP, D)
    grad, gain_grad = attn_bwd_body(
        mid, upstream + moe_grad, g_ref[1:2, :], qkv_ref, mixed_ref, w_ref, dw_ref, ib
    )
    dg_ref[1:2, :] += gain_grad
    grad_ref[...] = grad.reshape(ib, SP, D)

    @pl.when(step == pl.num_programs(0) - 1)
    def _():
        dw_out[:, : 4 * D] = dw_ref[...].astype(NARROW)
        dw_out[:, 4 * D :] = (dr_ref[...] + gain_columns(dg_ref)).astype(NARROW)


def moe_bwd(gains, w1, wr, mid, second, cot, prob, aux, qkv, mixed, tables, images, ib):
    return pl.pallas_call(
        partial(moe_bwd_kernel, ib),
        grid=(images // ib,),
        in_specs=[
            whole(gains.shape),
            whole(w1.shape),
            whole(wr.shape),
            per_image(ib, SP, D),
            per_image(ib, SP, D),
            per_image(ib, SP, D),
            per_image(ib, SP, 128),
            per_image(ib, SP, 128),
            per_image(ib, SP, 3 * D),
            per_image(ib, SP, D),
            whole(tables.shape),
        ],
        out_specs=[
            whole((images * SEQ, D)),
            per_image(ib, SP, D),
            whole((D, 4 * D + 128)),
        ],
        out_shape=[
            sds((images * SEQ, D), WIDE),
            sds((images, SP, D), WIDE),
            sds((D, 4 * D + 128), NARROW),
        ],
        scratch_shapes=[
            pltpu.VMEM((D, 128), WIDE),
            pltpu.VMEM((8, D), WIDE),
            pltpu.VMEM((D, 4 * D), WIDE),
        ],
        compiler_params=params(60),
        cost_estimate=cost(1e6, 1),
        name="expert_block_backward",
    )(gains, w1, wr, mid, second, cot, prob, aux, qkv, mixed, tables)


def dense_bwd_kernel(
    ib,
    g_ref,
    w_ref,
    win_ref,
    wout_ref,
    x_ref,
    first_ref,
    grad_ref,
    qkv_ref,
    mixed_ref,
    out_ref,
    dw_out,
    dout_out,
    dg_ref,
    dw_ref,
    din_ref,
    dout_ref,
):
    step = pl.program_id(0)

    @pl.when(step == 0)
    def _():
        dw_ref[...] = jnp.zeros(dw_ref.shape, WIDE)
        din_ref[...] = jnp.zeros(din_ref.shape, WIDE)
        dout_ref[...] = jnp.zeros(dout_ref.shape, WIDE)
        dg_ref[...] = jnp.zeros(dg_ref.shape, WIDE)

    incoming = grad_ref[...].reshape(ib * SP, D)
    first = first_ref[...].reshape(ib * SP, D)
    unit, inverse = norm_parts(first)
    gain = g_ref[2:3, :]
    normed = (unit * gain).astype(NARROW)
    out_grad = incoming.astype(NARROW)
    y_grad = None
    for f in range(FF // 512):
        c = slice(f * 512, (f + 1) * 512)
        win, wout = win_ref[:, c], wout_ref[c, :]
        pre = nn(normed, win)
        hidden_grad = nt(out_grad, wout)
        cdf, bell = normal_parts(pre)
        hidden = (pre * cdf).astype(NARROW)
        pre_grad = ((cdf + pre * (bell * INV_ROOT)) * hidden_grad).astype(NARROW)
        dout_ref[c, :] += tn(hidden, out_grad)
        din_ref[:, c] += tn(normed, pre_grad)
        part = nt(pre_grad, win)
        y_grad = part if y_grad is None else y_grad + part
    ffn_grad, gain_grad = norm_backward(y_grad, unit, inverse, gain)
    dg_ref[2:3, :] += gain_grad
    x = x_ref[...].astype(WIDE).reshape(ib * SP, D)
    grad, gain_grad = attn_bwd_body(
        x, incoming + ffn_grad, g_ref[0:1, :], qkv_ref, mixed_ref, w_ref, dw_ref, ib
    )
    dg_ref[0:1, :] += gain_grad
    put_rows(out_ref, step, ib, grad)

    @pl.when(step == pl.num_programs(0) - 1)
    def _():
        dw_out[:, : 4 * D] = dw_ref[...].astype(NARROW)
        dw_out[:, 4 * D : 8 * D] = din_ref[...].astype(NARROW)
        dw_out[:, 8 * D :] = gain_columns(dg_ref).astype(NARROW)
        dout_out[...] = dout_ref[...].astype(NARROW)


def dense_bwd(gains, w0, win, wout, x, first, grad, qkv, mixed, images, ib):
    return pl.pallas_call(
        partial(dense_bwd_kernel, ib),
        grid=(images // ib,),
        in_specs=[
            whole(gains.shape),
            whole(w0.shape),
            whole(win.shape),
            whole(wout.shape),
            per_image(ib, SP, D),
            per_image(ib, SP, D),
            per_image(ib, SP, D),
            per_image(ib, SP, 3 * D),
            per_image(ib, SP, D),
        ],
        out_specs=[
            whole((images * SEQ, D)),
            whole((D, 8 * D + 128)),
            whole((FF, D)),
        ],
        out_shape=[
            sds((images * SEQ, D), WIDE),
            sds((D, 8 * D + 128), NARROW),
            sds((FF, D), NARROW),
        ],
        scratch_shapes=[
            pltpu.VMEM((8, D), WIDE),
            pltpu.VMEM((D, 4 * D), WIDE),
            pltpu.VMEM((D, FF), WIDE),
            pltpu.VMEM((FF, D), WIDE),
        ],
        compiler_params=params(60),
        cost_estimate=cost(1e6, 1),
        name="dense_block_backward",
    )(gains, w0, win, wout, x, first, grad, qkv, mixed)


BLOCK = 512
CUTS = 2
AHEAD = 3
MESH_ID = pl.DeviceIdType.MESH


def add_rows(out, one, two, rows, step):
    @pl.loop(0, rows // step)
    def _(i):
        r = pl.ds(pl.multiple_of(i * step, step), step)
        out[r, :] = (one[r, :].astype(WIDE) + two[r, :].astype(WIDE)).astype(out.dtype)


def sum_kernel(nz, groups, mats, slices, first, handed, *refs):
    exp_refs, refs = refs[:mats], refs[mats:]
    dense_refs, peak_ref, refs = refs[:3], refs[3], refs[4:]
    if handed:
        _, hand_ref, refs = refs[0], refs[1], refs[2:]
    exp_out, dense_outs, peak_out, refs = refs[0], refs[1:4], refs[4], refs[5:]
    if handed:
        hand_buf, hand_sem, refs = refs[-2], refs[-1], refs[:-2]
    own, up, down, refs = refs[0], refs[1], refs[2], refs[3:]
    land, refs = refs[:4], refs[4:]
    dense_own, refs = refs[:4], refs[4:]
    dense_up, refs = refs[:4], refs[4:]
    dense_down, refs = refs[:4], refs[4:]
    (own_sem, up_send, up_recv, down_recv, out_send, sib_send, sib_recv, copy_sem, rs_send, rs_recv) = refs

    z, core, f = lax.axis_index("z"), lax.axis_index("core"), lax.axis_index("fsdp")
    half = nz // 2
    left = z < half
    inner = jnp.where(left, z + 1, z - 1)
    outer = jnp.where(left, z - 1, z + 1)
    has_outer = jnp.logical_and(z > 0, z < nz - 1)
    edge = jnp.logical_not(has_outer)
    center = jnp.logical_or(z == half - 1, z == half)
    away = jnp.logical_not(center)
    outer = jnp.where(has_outer, outer, inner)
    sibling = (z, 1 - core, f)
    members = CORES * groups
    me = core * groups + f

    barrier = pltpu.get_barrier_semaphore()
    pl.semaphore_signal(barrier, inc=1, device_id=(inner, core, f), device_id_type=MESH_ID)

    @pl.when(has_outer)
    def _():
        pl.semaphore_signal(barrier, inc=1, device_id=(outer, core, f), device_id_type=MESH_ID)

    for d in range(1, members):
        there = lax.rem(me + d, members)
        pl.semaphore_signal(
            barrier,
            inc=1,
            device_id=(z, there // groups, lax.rem(there, groups)),
            device_id_type=MESH_ID,
        )

    @pl.when(has_outer)
    def _():
        pl.semaphore_wait(barrier, members + 1)

    @pl.when(edge)
    def _():
        pl.semaphore_wait(barrier, members)

    chunks = mats * slices * CUTS
    items = chunks + 4

    def cut_rows(t):
        return pl.ds(t % CUTS * (BLOCK // CUTS), BLOCK // CUTS)

    def piece(n, ref, there):
        if n == 3:
            return ref
        rows = ref.shape[0] // members
        place = (lax.rem(there, groups) * CORES + there // groups) * rows
        return ref.at[pl.ds(pl.multiple_of(place, 16), rows), :]

    def scatter(n, d):
        there = lax.rem(me + d, members)
        source = dense_refs[n] if n < 3 else peak_ref
        return pltpu.make_async_remote_copy(
            src_ref=piece(n, source, there),
            dst_ref=land[n].at[d],
            send_sem=rs_send.at[n, d],
            recv_sem=rs_recv.at[n, d],
            device_id=(z, there // groups, lax.rem(there, groups)),
            device_id_type=MESH_ID,
        )

    def hand():
        return pltpu.make_async_remote_copy(
            src_ref=hand_buf,
            dst_ref=exp_out.at[pl.ds(first - handed, handed), core],
            send_sem=hand_sem.at[0],
            recv_sem=hand_sem.at[1],
            device_id=sibling,
            device_id_type=MESH_ID,
        )

    if handed:
        arrived = pltpu.make_async_copy(hand_ref, hand_buf, hand_sem.at[2])
        arrived.start()
        arrived.wait()
        handed_here = pltpu.make_async_copy(
            hand_buf, exp_out.at[pl.ds(first - handed, handed), core], hand_sem.at[2]
        )
        handed_here.start()
        hand().start()
    for n in (3, 1, 0, 2):
        for d in range(1, members):
            scatter(n, d).start()
    keep = [
        pltpu.make_async_copy(
            piece(n, dense_refs[n] if n < 3 else peak_ref, me), land[n].at[0], rs_recv.at[n, 0]
        )
        for n in range(4)
    ]
    for k in keep:
        k.start()

    def source_at_edge(t):
        if t >= chunks:
            return dense_own[t - chunks]
        return exp_refs[t // CUTS // slices].at[t // CUTS % slices, cut_rows(t), :]

    def load(t):
        return pltpu.make_async_copy(source_at_edge(t), own.at[t], own_sem.at[t])

    @pl.when(has_outer)
    def _():
        for t in range(chunks):
            load(t).start()

    def bufs(t):
        if t < chunks:
            return own.at[t], up.at[t], down.at[t]
        n = t - chunks
        return dense_own[n], dense_up[n], dense_down[n]

    def send_up(t, source, to_center):
        _, u, dn = bufs(t)
        return pltpu.make_async_remote_copy(
            src_ref=source,
            dst_ref=dn if to_center else u,
            send_sem=up_send.at[t],
            recv_sem=(down_recv if to_center else up_recv).at[t],
            device_id=(inner, core, f),
            device_id_type=MESH_ID,
        )

    def join(t, out, one, two):
        if t == items - 1:
            out[...] = jnp.maximum(one[...], two[...])
        else:
            add_rows(out, one, two, out.shape[0], 16)

    def reduce_own(n):
        for d in range(members):
            if d == 0:
                keep[n].wait()
            else:
                scatter(n, d).wait_recv()
        if n == 3:
            best = land[n][0]
            for d in range(1, members):
                best = jnp.maximum(best, land[n][d])
            dense_own[n][...] = best
            return

        @pl.loop(0, dense_own[n].shape[0] // 16)
        def _(i):
            r = pl.ds(pl.multiple_of(i * 16, 16), 16)
            total = land[n][0, r, :].astype(WIDE)
            for d in range(1, members):
                total = total + land[n][d, r, :].astype(WIDE)
            dense_own[n][r, :] = total.astype(NARROW)

    def up_from_edge(t, before):
        if before is not None:
            send_up(before, source_at_edge(before), half == 1).wait_send()
        if t >= chunks:
            reduce_own(t - chunks)
        send_up(t, source_at_edge(t), half == 1).start()

    def up_from_inside(t):
        o, u, _ = bufs(t)
        if t >= chunks:
            reduce_own(t - chunks)
        else:
            load(t).wait()
        send_up(t, u, False).wait_recv()
        join(t, o, o, u)

        @pl.when(center)
        def _():
            send_up(t, o, True).start()

        if half > 2:

            @pl.when(away)
            def _():
                send_up(t, o, False).start()

    def results(t):
        if t < chunks:
            return exp_out.at[first + t // CUTS, core, cut_rows(t), :]
        n = t - chunks
        if n == 3:
            return peak_out
        ref = dense_outs[n]
        rows = ref.shape[0] // CORES
        return ref.at[pl.ds(pl.multiple_of(core * rows, 16), rows), :]

    def to_sibling(t):
        return pltpu.make_async_remote_copy(
            src_ref=bufs(t)[2],
            dst_ref=results(t),
            send_sem=sib_send.at[t],
            recv_sem=sib_recv.at[t],
            device_id=sibling,
            device_id_type=MESH_ID,
        )

    def to_outer(t):
        dn = bufs(t)[2]
        return pltpu.make_async_remote_copy(
            src_ref=dn,
            dst_ref=dn,
            send_sem=out_send.at[t],
            recv_sem=down_recv.at[t],
            device_id=(outer, core, f),
            device_id_type=MESH_ID,
        )

    def keep_result(t):
        return pltpu.make_async_copy(bufs(t)[2], results(t), copy_sem.at[t])

    def go_down(t, at_edge):
        o, _, dn = bufs(t)
        to_outer(t).wait_recv()
        if at_edge:
            if half == 1:
                join(t, dn, source_at_edge(t), dn)
        else:

            @pl.when(center)
            def _():
                join(t, dn, o, dn)

            to_outer(t).start()
        keep_result(t).start()
        if t < items - 1:
            to_sibling(t).start()

    early = min(11 * CUTS, chunks)
    sequence = [*range(early), *range(items - 1, chunks - 1, -1), *range(early, chunks)]

    def run(up, at_edge, lag):
        for i in range(items + lag):
            if i < items:
                up(i)
            if i >= lag:
                go_down(sequence[i - lag], at_edge)

    @pl.when(edge)
    def _():
        run(
            lambda i: up_from_edge(sequence[i], sequence[i - AHEAD] if i >= AHEAD else None),
            True,
            min(7 * CUTS, items),
        )
        for t in sequence[-AHEAD:]:
            send_up(t, source_at_edge(t), half == 1).wait_send()

    if half > 1:

        @pl.when(has_outer)
        def _():
            run(lambda i: up_from_inside(sequence[i]), False, 1)
            for t in range(items):
                send_up(t, bufs(t)[0], False).wait_send()
                to_outer(t).wait_send()

    for n in range(4):
        for d in range(1, members):
            scatter(n, d).wait_send()
    if handed:
        hand().wait()
        handed_here.wait()
    for t in range(items):
        keep_result(t).wait()
        if t < items - 1:
            to_sibling(t).wait()


def sum_all(mats, dense, peaks, early, handed, nz, groups):
    slices = mats[0].shape[0]
    blocks = len(mats) * slices
    chunks = blocks * CUTS
    members = CORES * groups
    items = chunks + 4
    any_space = pl.BlockSpec(memory_space=pl.ANY)
    vmem = pl.BlockSpec(memory_space=pltpu.VMEM)
    pieces = [(a.shape[0] // members, a.shape[1]) for a in dense]
    block = pltpu.VMEM((chunks, BLOCK // CUTS, BLOCK), NARROW)

    def four(lead=()):
        return [pltpu.VMEM((*lead, *p), NARROW) for p in pieces] + [
            pltpu.VMEM((*lead, *peaks.shape), WIDE)
        ]

    dma = pltpu.SemaphoreType.DMA
    extra = [] if handed is None else [early, handed]
    count = handed.shape[0] if extra else 0
    first = early.shape[0] - blocks if extra else 0
    return pl.pallas_call(
        partial(sum_kernel, nz, groups, len(mats), slices, first, count),
        in_specs=[any_space] * (len(mats) + 3) + [vmem] + [any_space] * len(extra),
        out_specs=[any_space] * 4 + [vmem],
        out_shape=[
            sds((first + blocks, CORES, BLOCK, BLOCK), NARROW),
            *[sds((CORES * r, c), NARROW) for r, c in pieces],
            sds(peaks.shape, WIDE),
        ],
        scratch_shapes=[
            block,
            block,
            block,
            *four((members,)),
            *four(),
            *four(),
            *four(),
            *[dma((items,)) for _ in range(8)],
            dma((4, members)),
            dma((4, members)),
            *([pltpu.VMEM(handed.shape, NARROW), dma((3,))] if extra else []),
        ],
        compiler_params=pltpu.CompilerParams(
            vmem_limit_bytes=58 * MIB, collective_id=3, has_side_effects=True
        ),
        input_output_aliases={len(mats) + 4: 0} if extra else {},
        name="sums",
    )(*mats, *dense, peaks, *extra)


SUMMED = 12
LAGS = (2, 4, 6)
BESIDE = 8


def exchange_kernel(nz, groups, mine, *refs):
    pos_ref, moe_ref, cot_ref, prob_ref, win_hbm, wout_hbm, refs = *refs[:6], refs[6:]
    table_out, sum_out, beside_out, rest_out, refs = *refs[:4], refs[4:]
    sent, line_ref, refs = *refs[:2], refs[2:]
    (rows, back, res, sgr, w_in, w_out, own, up, down, made) = refs[:10]
    (d_send, d_recv, r_send, r_recv, w_sem, made_sem, up_send, up_recv, down_recv) = refs[10:19]
    (out_send, sib_send, sib_recv, keep_sem) = refs[19:]
    s = pl.program_id(0)
    z, core, f = lax.axis_index("z"), lax.axis_index("core"), lax.axis_index("fsdp")
    members = CORES * groups
    me = core * groups + f
    parts = FF // BLOCK
    steps = mine * parts
    last = pl.num_programs(0) - 1
    left = z < nz // 2
    inner = jnp.where(left, z + 1, z - 1)
    has_outer = jnp.logical_and(z > 0, z < nz - 1)
    edge = jnp.logical_not(has_outer)
    outer = jnp.where(has_outer, jnp.where(left, z - 1, z + 1), inner)

    def member(d):
        there = lax.rem(me + d, members)
        return there, (z, there // groups, lax.rem(there, groups))

    def rows_to(j, d):
        there, device = member(d)
        return pltpu.make_async_remote_copy(
            src_ref=sent.at[j, there],
            dst_ref=rows.at[j, me],
            send_sem=d_send.at[j, d],
            recv_sem=d_recv.at[j, d],
            device_id=device,
            device_id_type=MESH_ID,
        )

    def rows_here(j):
        return pltpu.make_async_copy(sent.at[j, me], rows.at[j, me], d_recv.at[j, 0])

    def prepare(j, others):
        theirs = [member(d)[0] for d in others]
        make_rows(
            [slot_expert(j * members + there, groups, CORES * mine) for there in theirs],
            [pos_ref[pl.ds(j * members + there, 1), :] for there in theirs],
            moe_ref[...],
            cot_ref[...],
            line_ref,
            [sent.at[j, there] for there in theirs],
        )

    def send_rows(j):
        for d in range(1, members):
            rows_to(j, d).start()
        rows_here(j).start()

    def results_to(j, d):
        there, device = member(d)
        return pltpu.make_async_remote_copy(
            src_ref=back.at[j % 2, there],
            dst_ref=table_out.at[j, me],
            send_sem=r_send.at[j, d],
            recv_sem=r_recv.at[j, d],
            device_id=device,
            device_id_type=MESH_ID,
        )

    def results_here(j):
        return pltpu.make_async_copy(back.at[j % 2, me], table_out.at[j, me], r_recv.at[j, 0])

    def weights(step):
        e = core * mine + step // parts
        c = pl.ds(pl.multiple_of(lax.rem(step, parts) * BLOCK, BLOCK), BLOCK)
        slot = lax.rem(step, 2)
        return (
            pltpu.make_async_copy(win_hbm.at[e, :, c], w_in.at[slot], w_sem.at[0, slot]),
            pltpu.make_async_copy(wout_hbm.at[e, c, :], w_out.at[slot], w_sem.at[1, slot]),
        )

    @pl.when(s == 0)
    def _():
        barrier = pltpu.get_barrier_semaphore()
        pl.semaphore_signal(barrier, inc=1, device_id=(inner, core, f), device_id_type=MESH_ID)

        @pl.when(has_outer)
        def _():
            pl.semaphore_signal(barrier, inc=1, device_id=(outer, core, f), device_id_type=MESH_ID)

        for d in range(1, members):
            pl.semaphore_signal(barrier, inc=1, device_id=member(d)[1], device_id_type=MESH_ID)

        @pl.when(has_outer)
        def _():
            pl.semaphore_wait(barrier, members + 1)

        @pl.when(edge)
        def _():
            pl.semaphore_wait(barrier, members)

        for w in weights(s):
            w.start()
        turn_probs(prob_ref, line_ref)
        for d in range(1, members, 2):
            others = [d, (d + 1) % members]
            prepare(0, others)
            for there in others:
                if there:
                    rows_to(0, there).start()
        rows_here(0).start()
        for j in range(1, mine):
            prepare(j, range(members))

    for j in range(mine):

        @pl.when(s == j * parts)
        def _(j=j):
            for d in range(1, members):
                rows_to(j, d).wait_recv()
            rows_here(j).wait()
            if j == 0:
                send_rows(1)
            if j == 1:
                send_rows(3)

    slot = lax.rem(s, 2)

    def made_to(step, side, near):
        place = 2 * step + side - SUMMED - (0 if near else BESIDE)
        there = lax.rem(step, 2)
        out = beside_out if near else rest_out
        return pltpu.make_async_copy(
            made.at[there, side],
            out.at[jnp.clip(place, 0, out.shape[0] - 1)],
            made_sem.at[there, side],
        )

    def each_made(step, act):
        near = step < (SUMMED + BESIDE) // 2

        @pl.when(near)
        def _():
            for side in range(2):
                act(made_to(step, side, True))

        @pl.when(jnp.logical_not(near))
        def _():
            for side in range(2):
                act(made_to(step, side, False))

    @pl.when(s < steps)
    def _():
        for w in weights(s):
            w.wait()

        @pl.when(s + 1 < steps)
        def _():
            for w in weights(s + 1):
                w.start()

        @pl.when(jnp.logical_and(s >= SUMMED // 2 + 2, s < steps))
        def _():
            each_made(s - 2, lambda copy: copy.wait())

        j = s // parts
        part = lax.rem(s, parts)
        count = members * CAP
        half = members // 2
        halves = []
        for h in range(2):
            side = slice(h * half, (h + 1) * half)
            slots = rows[j, side, 0:CAP, :].reshape(count // 2, D)
            grads = rows[j, side, CAP : 2 * CAP, :].reshape(count // 2, D)
            halves.append(expert_math(slots, grads, w_in[slot], w_out[slot]))
        result, slot_grad = (jnp.concatenate([halves[0][n], halves[1][n]], 0) for n in range(2))
        d_in, d_out = (halves[0][n] + halves[1][n] for n in range(2, 4))

        @pl.when(part == 0)
        def _():
            res[...] = result
            sgr[...] = slot_grad

        @pl.when(part > 0)
        def _():
            res[...] += result
            sgr[...] += slot_grad

        @pl.when(s < SUMMED // 2)
        def _():
            own[2 * s] = d_in.astype(NARROW)
            own[2 * s + 1] = d_out.astype(NARROW)

        @pl.when(s >= SUMMED // 2)
        def _():
            made[slot, 0] = d_in.astype(NARROW)
            made[slot, 1] = d_out.astype(NARROW)

            each_made(s, lambda copy: copy.start())

    @pl.when(s == 1)
    def _():
        send_rows(2)

    for j in range(mine):

        @pl.when(s == (j + 1) * parts - 1)
        def _(j=j):
            if j >= 2:
                for d in range(1, members):
                    results_to(j - 2, d).wait_send()
                results_here(j - 2).wait()
            back[j % 2, :, :, 0:D] = res[...].astype(NARROW).reshape(members, CAP, D)
            back[j % 2, :, :, D : 2 * D] = sgr[...].astype(NARROW).reshape(members, CAP, D)
            for d in range(1, members):
                results_to(j, d).start()
            results_here(j).start()

    def send_up(t, to_center):
        return pltpu.make_async_remote_copy(
            src_ref=own.at[t],
            dst_ref=(down if to_center else up).at[t],
            send_sem=up_send.at[t],
            recv_sem=(down_recv if to_center else up_recv).at[t],
            device_id=(inner, core, f),
            device_id_type=MESH_ID,
        )

    def send_out(t):
        return pltpu.make_async_remote_copy(
            src_ref=down.at[t],
            dst_ref=down.at[t],
            send_sem=out_send.at[t],
            recv_sem=down_recv.at[t],
            device_id=(outer, core, f),
            device_id_type=MESH_ID,
        )

    def to_sibling(t):
        return pltpu.make_async_remote_copy(
            src_ref=down.at[t],
            dst_ref=sum_out.at[t, core],
            send_sem=sib_send.at[t],
            recv_sem=sib_recv.at[t],
            device_id=(z, 1 - core, f),
            device_id_type=MESH_ID,
        )

    def keep_sum(t):
        return pltpu.make_async_copy(down.at[t], sum_out.at[t, core], keep_sem.at[t])

    def at(lag, role):
        t = s - lag
        return pl.when(jnp.logical_and(role, jnp.logical_and(t >= 0, t < SUMMED)))

    def tick(t):
        return jnp.clip(t, 0, SUMMED - 1)

    @at(0, edge)
    def _():
        send_up(tick(s), False).start()

    @at(LAGS[0], has_outer)
    def _():
        t = tick(s - LAGS[0])
        send_up(t, False).wait_recv()
        add_rows(own.at[t], own.at[t], up.at[t], BLOCK, 16)
        send_up(t, True).start()

    @at(LAGS[1], has_outer)
    def _():
        t = tick(s - LAGS[1])
        send_out(t).wait_recv()
        add_rows(down.at[t], own.at[t], down.at[t], BLOCK, 16)
        send_out(t).start()
        keep_sum(t).start()
        to_sibling(t).start()

    @at(LAGS[2], edge)
    def _():
        t = tick(s - LAGS[2])
        send_out(t).wait_recv()
        keep_sum(t).start()
        to_sibling(t).start()

    @pl.when(s == last)
    def _():
        for step in (steps - 2, steps - 1):
            for side in range(2):
                made_to(step, side, False).wait()
        for j in range(mine):
            for d in range(1, members):
                rows_to(j, d).wait_send()
                results_to(j, d).wait_recv()
                if j >= mine - 2:
                    results_to(j, d).wait_send()
            if j >= mine - 2:
                results_here(j).wait()

        for t in range(SUMMED):
            send_up(t, False).wait_send()
            keep_sum(t).wait()
            to_sibling(t).wait()

        @pl.when(has_outer)
        def _():
            for t in range(SUMMED):
                send_out(t).wait_send()


def exchange(pos, moe, cot, prob, win, wout, nz, groups):
    members = CORES * groups
    mine = win.shape[0] // CORES
    steps = mine * (FF // BLOCK)
    rest = 2 * steps - SUMMED - BESIDE
    any_space = pl.BlockSpec(memory_space=pl.ANY)
    dma = pltpu.SemaphoreType.DMA
    block = pltpu.VMEM((SUMMED, BLOCK, BLOCK), NARROW)
    return pl.pallas_call(
        partial(exchange_kernel, nz, groups, mine),
        grid=(max(steps, SUMMED + LAGS[2]),),
        in_specs=[*[whole(a.shape) for a in (pos, moe, cot, prob)], any_space, any_space],
        out_specs=[any_space] * 4,
        out_shape=[
            sds((mine, members, CAP, 2 * D), NARROW),
            sds((2 * steps, CORES, BLOCK, BLOCK), NARROW),
            sds((BESIDE, BLOCK, BLOCK), NARROW),
            sds((rest, BLOCK, BLOCK), NARROW),
        ],
        scratch_shapes=[
            pltpu.VMEM((mine, members, 2 * CAP, D), NARROW),
            pltpu.VMEM((128, moe.shape[0]), WIDE),
            pltpu.VMEM((mine, members, 2 * CAP, D), NARROW),
            pltpu.VMEM((2, members, CAP, 2 * D), NARROW),
            pltpu.VMEM((members * CAP, D), WIDE),
            pltpu.VMEM((members * CAP, D), WIDE),
            pltpu.VMEM((2, D, BLOCK), NARROW),
            pltpu.VMEM((2, BLOCK, D), NARROW),
            block,
            block,
            block,
            pltpu.VMEM((2, 2, BLOCK, BLOCK), NARROW),
            *[dma((mine, members)) for _ in range(4)],
            dma((2, 2)),
            dma((2, 2)),
            *[dma((SUMMED,)) for _ in range(7)],
        ],
        compiler_params=pltpu.CompilerParams(
            vmem_limit_bytes=62 * MIB, collective_id=7, has_side_effects=True
        ),
        name="experts",
    )(pos, moe, cot, prob, win, wout)


def finish_small(refs):
    (wide_ref, deep_ref, out_ref, peak_ref, limit_ref, query_ref, key_ref) = refs[:7]
    (gain_out, q_out, k_out, v_out, o_out, ffn_out, in_out, mlp_out, router_out, cq_out, ck_out) = refs[7:]
    for n, ref in enumerate((q_out, k_out, v_out, o_out)):
        c = slice(n * D, (n + 1) * D)
        ref[0] = wide_ref[:, c].astype(WIDE)
        ref[1] = deep_ref[:, c].astype(WIDE)
    in_out[...] = wide_ref[:, 4 * D : 8 * D].astype(WIDE)
    mlp_out[...] = out_ref[...].astype(WIDE)
    small = deep_ref[:, 4 * D :].astype(WIDE) + wide_ref[:, 8 * D :].astype(WIDE)
    router_out[...] = small[:, :EXPERTS]
    count = small.shape[0]
    if count < 128:
        small = jnp.concatenate([small, jnp.zeros((128 - count, 128), WIDE)], 0)
    turned = jnp.transpose(small)
    gain_out[...] = turned[EXPERTS : EXPERTS + 2, :count]
    ffn_out[...] = turned[EXPERTS + 2 : EXPERTS + 4, :count]
    head = lax.broadcasted_iota(jnp.int32, (HEADS, D), 0)
    feature = lax.broadcasted_iota(jnp.int32, (HEADS, D), 1)
    owns = jnp.logical_and(feature >= head * HEAD, feature < (head + 1) * HEAD)
    for layer in range(2):
        limit = limit_ref[:, layer : layer + 1]
        top = peak_ref[:, layer * 64 : layer * 64 + 1]
        scale = jnp.sqrt(limit / jnp.maximum(top, limit))
        row = jnp.sum(jnp.where(owns, scale, 0.0), 0, keepdims=True)
        cq_out[layer] = query_ref[layer] * row
        ck_out[layer] = key_ref[layer] * row


PAIRS = 2


def widen_blocks(blocks_ref, in_ref, out_ref):
    for n in range(PAIRS):
        r = slice(n * BLOCK, (n + 1) * BLOCK)
        in_ref[:, r] = blocks_ref[n, 0].astype(WIDE)
        out_ref[r, :] = blocks_ref[n, 1].astype(WIDE)


def block_specs(mine, first):
    parts = FF // BLOCK // PAIRS
    wide = PAIRS * BLOCK

    def place(c, s):
        return c * mine + (s + first) // parts, (s + first) % parts

    return (
        pl.BlockSpec((PAIRS, 2, None, BLOCK, BLOCK), lambda c, s: (s + first, 0, c, 0, 0)),
        [
            pl.BlockSpec((None, D, wide), lambda c, s: (place(c, s)[0], 0, place(c, s)[1])),
            pl.BlockSpec((None, wide, D), lambda c, s: (*place(c, s), 0)),
        ],
    )


def gradient_shapes(mine):
    return [sds((CORES * mine, D, FF), WIDE), sds((CORES * mine, FF, D), WIDE)]


def widen_early(blocks, count, mine):
    source, places = block_specs(mine, 0)
    return pl.pallas_call(
        widen_blocks,
        grid=(CORES, count // 2 // PAIRS),
        in_specs=[source],
        out_specs=places,
        out_shape=gradient_shapes(mine),
        compiler_params=params(60),
        name="widen_early",
    )(blocks.reshape(-1, 2, CORES, BLOCK, BLOCK))


def finish_kernel(given, blocks_ref, *refs):
    small, (in_ref, out_ref) = refs[given:-2], refs[-2:]

    @pl.when(jnp.logical_and(pl.program_id(0) == 0, pl.program_id(1) == 0))
    def _():
        finish_small(small)

    widen_blocks(blocks_ref, in_ref, out_ref)


def finish(blocks, done, given, mine, small, outs):
    first = done // 2 // PAIRS
    source, places = block_specs(mine, first)
    steps = blocks.shape[0] // 2 // PAIRS - first
    return pl.pallas_call(
        partial(finish_kernel, len(given)),
        grid=(CORES, steps),
        in_specs=[
            source,
            *[pl.BlockSpec(memory_space=pl.ANY)] * len(given),
            *[whole(a.shape) for a in small],
        ],
        out_specs=[whole(o.shape) for o in outs] + places,
        out_shape=[*outs, *gradient_shapes(mine)],
        input_output_aliases={1 + n: len(outs) + n for n in range(len(given))},
        compiler_params=params(60),
        name="finish",
    )(blocks.reshape(-1, 2, CORES, BLOCK, BLOCK), *given, *small)


def forward_kernel(groups, ib, *refs):
    q_ref, k_ref, v_ref, o_ref, small_ref, in_ref, out_ref, refs = *refs[:7], refs[7:]
    token_ref, cot_ref, order_ref, routes_ref, refs = *refs[:4], refs[4:]
    kept, refs = refs[:4], refs[4:]
    gain_ref, router_ref, x_out, cot_out, pos_ref, aux_ref, refs = *refs[:6], refs[6:]
    first_ref, qkv0_ref, mixed0_ref, peak0_ref, mid_ref, refs = *refs[:5], refs[5:]
    second_ref, qkv1_ref, mixed1_ref, peak1_ref, moe_ref, prob_ref, refs = *refs[:6], refs[6:]
    w0, win, wout, w1, small_all, state, wide_ref, line_ref, rows_ref, refs = *refs[:9], refs[9:]
    send, recv, pass_send, pass_recv, copy, rows_sem, kept_sem = refs
    phase, i = pl.program_id(0), pl.program_id(1)
    z, core, f = lax.axis_index("z"), lax.axis_index("core"), lax.axis_index("fsdp")

    def rows(count, owner, side):
        half = count // CORES
        return pl.ds(pl.multiple_of(owner * count + side * half, 16), half)

    def item(n):
        if n < 4 or n >= 7:
            ref = (q_ref, k_ref, v_ref, o_ref)[n % 7]
            full, layer = (w0, 0) if n < 4 else (w1, 1)
            count = ref.shape[1]
            cols = pl.ds(n % 7 * D, D)
            return (
                lambda side: ref.at[layer, rows(count, 0, side), :],
                lambda owner, side: full.at[rows(count, owner, side), cols],
            )
        ref, full = ((small_ref, small_all), (in_ref, win), (out_ref, wout))[n - 4]
        count = ref.shape[0]
        return (
            lambda side: ref.at[rows(count, 0, side), :],
            lambda owner, side: full.at[rows(count, owner, side), :],
        )

    def fetch(n, d):
        source, place = item(n)
        return pltpu.make_async_remote_copy(
            src_ref=source(core),
            dst_ref=place(f, core),
            send_sem=send.at[n, d],
            recv_sem=recv.at[n, d],
            device_id=(z, core, lax.rem(f + d, groups)),
            device_id_type=MESH_ID,
        )

    def hand_on(n, d):
        _, place = item(n)
        there = place(lax.rem(f + groups - d, groups), core)
        return pltpu.make_async_remote_copy(
            src_ref=there,
            dst_ref=there,
            send_sem=pass_send.at[n, d],
            recv_sem=pass_recv.at[n, d],
            device_id=(z, 1 - core, f),
            device_id_type=MESH_ID,
        )

    def keep(n, side):
        source, place = item(n)
        return pltpu.make_async_copy(source(side), place(f, side), copy.at[n, side])

    sets = ((0, 1, 2, 3, 4), (5, 6), (7, 8, 9, 10))

    def begin(stage):
        for n in sets[stage]:
            for d in range(1, groups):
                fetch(n, d).start()
            for side in range(CORES):
                keep(n, side).start()

    def arrive(stage):
        for n in sets[stage]:
            for d in range(1, groups):
                fetch(n, d).wait_recv()
                hand_on(n, d).start()

    def complete(stage):
        for n in sets[stage]:
            for side in range(CORES):
                keep(n, side).wait()
            for d in range(1, groups):
                fetch(n, d).wait_send()
                hand_on(n, d).wait()

    def keepers():
        return [
            pltpu.make_async_copy(ref, out, kept_sem.at[n])
            for n, (ref, out) in enumerate(zip((w0, win, wout, w1), kept))
        ]

    start = i == 0

    @pl.when(jnp.logical_and(phase == 0, start))
    def _():
        barrier = pltpu.get_barrier_semaphore()
        for d in range(1, groups):
            there = (z, core, lax.rem(f + d, groups))
            pl.semaphore_signal(barrier, inc=1, device_id=there, device_id_type=MESH_ID)
        pl.semaphore_signal(barrier, inc=1, device_id=(z, 1 - core, f), device_id_type=MESH_ID)
        pl.semaphore_wait(barrier, groups)
        begin(0)
        begin(1)
        loads = [
            pltpu.make_async_copy(ref, rows_ref.at[n], rows_sem.at[n])
            for n, ref in enumerate((token_ref, cot_ref))
        ]
        for load in loads:
            load.start()
        for n, out in enumerate((x_out, cot_out)):
            loads[n].wait()
            pad_images(rows_ref.at[n], wide_ref, out)
        arrive(0)
        find_places(order_ref, routes_ref, pos_ref, aux_ref, line_ref)
        complete(0)
        lane = lax.broadcasted_iota(jnp.int32, (1, 128), 1)
        small = small_all[...].astype(WIDE)
        router_ref[...] = jnp.where(lane < EXPERTS, small, 0.0).astype(NARROW)
        gain_ref[...] = jnp.transpose(small)[EXPERTS : EXPERTS + 8, :]

    @pl.when(jnp.logical_and(phase == 1, start))
    def _():
        arrive(1)
        begin(2)
        complete(1)

    @pl.when(jnp.logical_and(phase == 2, start))
    def _():
        arrive(2)
        complete(2)
        for k in keepers():
            k.start()

    images = pl.ds(i * ib, ib)

    @pl.when(phase == 0)
    def _():
        x = x_out[images].astype(WIDE).reshape(ib * SP, D)
        y = attn_fwd_body(x, gain_ref[0:1, :], w0, qkv0_ref, mixed0_ref, peak0_ref, ib)
        y = y.reshape(ib, SP, D)
        first_ref[...] = y
        state[images] = y

    @pl.when(phase == 1)
    def _():
        x = state[images].reshape(ib * SP, D)
        unit, _ = norm_parts(x)
        normed = (unit * gain_ref[2:3, :]).astype(NARROW)
        acc = x
        for n in range(FF // 512):
            c = slice(n * 512, (n + 1) * 512)
            pre = nn(normed, win[:, c])
            cdf, _ = normal_parts(pre)
            acc = acc + nn((pre * cdf).astype(NARROW), wout[c, :])
        y = acc.reshape(ib, SP, D)
        mid_ref[...] = y
        state[images] = y

    @pl.when(phase == 2)
    def _():
        x = state[images].reshape(ib * SP, D)
        y = attn_fwd_body(x, gain_ref[1:2, :], w1, qkv1_ref, mixed1_ref, peak1_ref, ib)
        second_ref[...] = y.reshape(ib, SP, D)
        unit, _ = norm_parts(y)
        moe = (unit * gain_ref[3:4, :]).astype(NARROW)
        moe_ref[...] = moe.reshape(ib, SP, D)
        lane = lax.broadcasted_iota(jnp.int32, (1, 128), 1)
        logits = jnp.where(lane < EXPERTS, nn(moe, router_ref[...]), LOWEST)
        e = jnp.exp(logits - jnp.max(logits, -1, keepdims=True))
        prob_ref[...] = (e / jnp.sum(e, -1, keepdims=True)).reshape(ib, SP, 128)

    @pl.when(jnp.logical_and(phase == 2, i == pl.num_programs(1) - 1))
    def _():
        for k in keepers():
            k.wait()


def forward(weights, tokens, cotangent, routes_rows, groups, held, ib):
    any_space = pl.BlockSpec(memory_space=pl.ANY)
    vmem = pl.BlockSpec(memory_space=pltpu.VMEM)
    dma = pltpu.SemaphoreType.DMA
    images = tokens.shape[0] // SEQ
    padded, pairs = images * SP, images // ib
    slots = np.arange(EXPERTS, dtype=np.int32)[:, None]
    order = np.broadcast_to(slot_expert(slots, groups, held), (EXPERTS, 128)).astype(np.int32)

    def of_phase(n, *tail):
        def place(phase, i):
            return (jnp.where(phase == n, i, jnp.where(phase < n, 0, pairs - 1)), *[0] * len(tail))

        return pl.BlockSpec((ib, *tail), place)

    tails = (
        (0, WIDE, SP, D),
        (0, NARROW, SP, 3 * D),
        (0, NARROW, SP, D),
        (0, WIDE, HEADS, 128),
        (1, WIDE, SP, D),
        (2, WIDE, SP, D),
        (2, NARROW, SP, 3 * D),
        (2, NARROW, SP, D),
        (2, WIDE, HEADS, 128),
        (2, NARROW, SP, D),
        (2, WIDE, SP, 128),
    )
    matrices = [(D, 4 * D), (D, FF), (FF, D), (D, 4 * D)]
    return pl.pallas_call(
        partial(forward_kernel, groups, ib),
        grid=(3, pairs),
        in_specs=[any_space] * 9 + [vmem] * 2,
        out_specs=[any_space] * 4
        + [vmem] * 6
        + [of_phase(n, *tail) for n, _, *tail in tails],
        out_shape=[
            *[sds(m, NARROW) for m in matrices],
            sds((8, D), WIDE),
            sds((D, 128), NARROW),
            sds((images, SP, D), NARROW),
            sds((images, SP, D), NARROW),
            sds((EXPERTS, padded), WIDE),
            sds((padded, 128), WIDE),
            *[sds((images, *tail), dtype) for _, dtype, *tail in tails],
        ],
        scratch_shapes=[
            *[pltpu.VMEM(m, NARROW) for m in matrices],
            pltpu.VMEM((D, 128), NARROW),
            pltpu.VMEM((images, SP, D), WIDE),
            pltpu.VMEM((-(-(tokens.shape[0] + SP) // 16) * 16, D), WIDE),
            pltpu.VMEM((128, padded), WIDE),
            pltpu.VMEM((2, *tokens.shape), NARROW),
            *[dma((11, groups)) for _ in range(4)],
            dma((11, CORES)),
            dma((2,)),
            dma((4,)),
        ],
        compiler_params=pltpu.CompilerParams(
            vmem_limit_bytes=60 * MIB, collective_id=5, has_side_effects=True
        ),
        name="forward",
    )(*weights, tokens, cotangent, jnp.asarray(order), routes_rows)


def local(
    tokens,
    cotangent,
    routes,
    attn_norm,
    query_w,
    key_w,
    value_w,
    output_w,
    ffn_norm,
    mlp_in,
    mlp_out,
    router_w,
    expert_in,
    expert_out,
    updated_query,
    updated_key,
    clip_threshold,
):
    images = tokens.shape[0] // SEQ
    ib = 2
    groups = lax.axis_size("fsdp")
    core = lax.axis_index("core")
    held = expert_in.shape[0]
    mine = held // CORES
    owners = CORES * groups

    small = jnp.concatenate(
        [
            router_w,
            jnp.transpose(attn_norm),
            jnp.transpose(ffn_norm),
            jnp.zeros((router_w.shape[0], 128 - EXPERTS - 4), NARROW),
        ],
        1,
    )
    routes_rows = jnp.pad(
        jnp.transpose(routes).reshape(2, images, SEQ),
        ((0, 6), (0, 0), (0, SP - SEQ)),
        constant_values=-1,
    ).reshape(8, -1)
    w0, win, wout, w1, gains, wr, x, cot, pos, aux, *states = forward(
        (query_w, key_w, value_w, output_w, small, mlp_in, mlp_out),
        tokens,
        cotangent,
        routes_rows,
        groups,
        held,
        ib,
    )
    first, qkv0, mixed0, peak0, mid, second, qkv1, mixed1, peak1, moe, prob = states
    aux = aux.reshape(images, SP, 128)

    routed = (pos, moe.reshape(-1, D), cot.reshape(-1, D), prob.reshape(-1, 128))
    nz = lax.axis_size("z")
    early = own = None
    if nz == 4 and owners == 8 and mine == 4:
        tables, early, own, late = exchange(*routed, expert_in, expert_out, nz, groups)
        own = lax.psum(own, "z")
    else:
        sent = dispatch(*routed, groups, held).reshape(mine, owners, 2 * CAP, D)
        tables, blocks = [], []
        for j in range(mine):
            rows = lax.all_to_all(
                sent[j], ("core", "fsdp"), split_axis=0, concat_axis=0, tiled=True
            )
            pick = (core * mine + j).astype(jnp.int32).reshape(1)
            back, d_in, d_out = expert(pick, rows, expert_in, expert_out)
            tables.append(
                lax.all_to_all(back, ("core", "fsdp"), split_axis=0, concat_axis=0, tiled=True)
            )
            blocks.append(jnp.stack([d_in, d_out], 1).reshape(-1, BLOCK, BLOCK))
        tables = jnp.stack(tables)
        late = jnp.concatenate(blocks)

    y, mid_grad, dw1 = moe_bwd(
        gains, w1, wr, mid, second, cot, prob, aux, qkv1, mixed1, tables, images, ib
    )
    x_grad, dw0, d_wout = dense_bwd(
        gains, w0, win, wout, x, first, mid_grad, qkv0, mixed0, images, ib
    )
    lane = jnp.arange(128)[None, :]
    peaks = jnp.where(lane < 64, jnp.max(peak0, 0), jnp.max(peak1, 0))
    given = []
    if early is not None:
        (early, _, _) = lax.optimization_barrier((early, dw0, d_wout))
        given = widen_early(early, SUMMED, mine)
        (late, *given) = lax.optimization_barrier((late, *given))
    blocks, t1, t0, t_wout, maxima = sum_all(
        [late], [dw1, dw0, d_wout], peaks, early, own, nz, groups
    )
    small_outs = [
        sds(attn_norm.shape, WIDE),
        *[sds(query_w.shape, WIDE)] * 4,
        sds(ffn_norm.shape, WIDE),
        sds(mlp_in.shape, WIDE),
        sds(mlp_out.shape, WIDE),
        sds(router_w.shape, WIDE),
        sds(updated_query.shape, WIDE),
        sds(updated_key.shape, WIDE),
    ]
    *grads, clipped_query, clipped_key, expert_in_grad, expert_out_grad = finish(
        blocks,
        SUMMED if given else 0,
        given,
        mine,
        [t0, t1, t_wout, maxima, jnp.transpose(clip_threshold), updated_query, updated_key],
        small_outs,
    )
    return (y, x_grad, *grads, expert_in_grad, expert_out_grad, clipped_query, clipped_key)


def solution(mesh):
    replicas, groups = mesh.shape["replica"], mesh.shape["fsdp"]
    inner = Mesh(
        mesh.devices.reshape(replicas // CORES, CORES, groups), ("z", "core", "fsdp")
    )
    split = P(("z", "core", "fsdp"), None)
    second = P(None, "fsdp", None)
    in_specs = (
        split,
        split,
        split,
        P(None, "fsdp"),
        second,
        second,
        second,
        second,
        P(None, "fsdp"),
        P("fsdp", None),
        P("fsdp", None),
        P("fsdp", None),
        P("fsdp", None, None),
        P("fsdp", None, None),
        second,
        second,
        P(),
    )
    out_specs = (
        split,
        split,
        P(None, "fsdp"),
        second,
        second,
        second,
        second,
        P(None, "fsdp"),
        P("fsdp", None),
        P("fsdp", None),
        P("fsdp", None),
        P("fsdp", None, None),
        P("fsdp", None, None),
        second,
        second,
    )
    return jax.shard_map(local, mesh=inner, in_specs=in_specs, out_specs=out_specs, check_vma=False)
```

```python
from functools import partial

import jax
import jax.numpy as jnp
import numpy as np
from jax import lax
from jax.experimental import pallas as pl
from jax.experimental.pallas import tpu as pltpu
from jax.sharding import Mesh
from jax.sharding import PartitionSpec as P

D = 512
HEADS = 8
HEAD = 64
FF = 2048
SEQ = 197
SP = 208
CAP = 128
EXPERTS = 32
EPSILON = 1e-06
SCALE = HEAD ** (-0.5)
LOWEST = -1e30
NARROW = jnp.bfloat16
WIDE = jnp.float32
CORES = 2
MIB = 1 << 20


def nn(a, b):
    return lax.dot_general(a, b, (((1,), (0,)), ((), ())), preferred_element_type=WIDE)


def nt(a, b):
    return lax.dot_general(a, b, (((1,), (1,)), ((), ())), preferred_element_type=WIDE)


def tn(a, b):
    return lax.dot_general(a, b, (((0,), (0,)), ((), ())), preferred_element_type=WIDE)


def norm_parts(values):
    centred = values - jnp.mean(values, -1, keepdims=True)
    inverse = lax.rsqrt(jnp.mean(centred * centred, -1, keepdims=True) + EPSILON)
    return centred * inverse, inverse


def norm_backward(incoming, unit, inverse, gain):
    gain_grad = jnp.sum(incoming * unit, 0, keepdims=True)
    scaled = incoming * gain
    centred = (
        scaled
        - jnp.mean(scaled, -1, keepdims=True)
        - unit * jnp.mean(scaled * unit, -1, keepdims=True)
    )
    return inverse * centred, gain_grad


def normal_parts(x):
    z = jnp.abs(x)
    t = 1.0 / (1.0 + (0.3275911 * 0.7071067811865476) * z)
    bell = jnp.exp(-0.5 * (x * x))
    poly = t * (
        0.5 * 0.254829592
        + t
        * (
            0.5 * -0.284496736
            + t * (0.5 * 1.421413741 + t * (0.5 * -1.453152027 + t * (0.5 * 1.061405429)))
        )
    )
    tail = poly * bell
    return jnp.where(x >= 0, 1.0 - tail, tail), bell


INV_ROOT = 0.3989422804014327


def head_masks(dtype):
    lane = lax.broadcasted_iota(jnp.int32, (1, 2 * HEAD), 1)
    low = (lane < HEAD).astype(dtype)
    return (low, (1 - low.astype(WIDE)).astype(dtype))


def attn_fwd_body(x, gain, w_ref, qkv_ref, mixed_ref, peak_ref, ib):
    unit, _ = norm_parts(x)
    normed = (unit * gain).astype(NARROW)
    q = (nn(normed, w_ref[:, 0:D]).astype(NARROW).astype(WIDE) * SCALE).astype(NARROW)
    k = nn(normed, w_ref[:, D : 2 * D]).astype(NARROW)
    v = nn(normed, w_ref[:, 2 * D : 3 * D]).astype(NARROW)
    masks = head_masks(NARROW)
    cols = lax.broadcasted_iota(jnp.int32, (SP, SP), 1)
    rows = lax.broadcasted_iota(jnp.int32, (SP, 1), 0)
    head_row = lax.broadcasted_iota(jnp.int32, (HEADS, 128), 0)
    mixed_all = []
    for i in range(ib):
        peaks = jnp.full((HEADS, 128), LOWEST, WIDE)
        r = slice(i * SP, (i + 1) * SP)
        pairs = []
        for pair in range(HEADS // 2):
            c = slice(pair * 2 * HEAD, (pair + 1) * 2 * HEAD)
            qp, kp, vp = q[r, c], k[r, c], v[r, c]
            acc = None
            for half in range(2):
                s = nt(qp * masks[half], kp)
                s = jnp.where(cols < SEQ, s, LOWEST)
                top = jnp.max(s, -1, keepdims=True)
                e = jnp.exp(s - top)
                p = (e * (1.0 / jnp.sum(e, -1, keepdims=True))).astype(NARROW)
                part = nn(p, vp * masks[half])
                acc = part if acc is None else acc + part
                peak = jnp.max(jnp.where(rows < SEQ, top, LOWEST), 0, keepdims=True)
                peaks = jnp.where(head_row == pair * 2 + half, peak, peaks)
            pairs.append(acc.astype(NARROW))
        mixed_all.append(jnp.concatenate(pairs, 1))
        peak_ref[i] = peaks
    mixed = jnp.concatenate(mixed_all, 0) if ib > 1 else mixed_all[0]
    qkv_ref[...] = jnp.concatenate([q, k, v], 1).reshape(ib, SP, 3 * D)
    mixed_ref[...] = mixed.reshape(ib, SP, D)
    return x + nn(mixed, w_ref[:, 3 * D : 4 * D])


def whole(shape):
    return pl.BlockSpec(
        shape, lambda *_: (0,) * len(shape), pipeline_mode=pl.Buffered(buffer_count=1)
    )


def per_image(ib, *tail):
    return pl.BlockSpec((ib, *tail), lambda i, *_: (i,) + (0,) * len(tail))


def sds(shape, dtype):
    return jax.ShapeDtypeStruct(shape, dtype)


def cost(flops, moved):
    return pl.CostEstimate(flops=int(flops), bytes_accessed=int(moved), transcendentals=0)


def params(mib):
    return pltpu.CompilerParams(vmem_limit_bytes=mib * MIB)


def find_places(order_ref, routes_ref, pos_ref, aux_ref, line_ref):
    tokens = routes_ref.shape[1]
    order = order_ref[:, 0:1]
    chunk = 128
    strict = (
        lax.broadcasted_iota(jnp.int32, (chunk, chunk), 0)
        < lax.broadcasted_iota(jnp.int32, (chunk, chunk), 1)
    ).astype(NARROW)
    slot_row = lax.broadcasted_iota(jnp.int32, (EXPERTS, 1), 0).astype(WIDE) * CAP
    base = jnp.zeros((EXPERTS, 1), WIDE)
    pos_ref[...] = jnp.full(pos_ref.shape, -1.0, WIDE)
    line_ref[...] = jnp.zeros(line_ref.shape, WIDE)
    for k in range(2):
        for c in range(tokens // chunk):
            s = slice(c * chunk, (c + 1) * chunk)
            hit = (order == routes_ref[k : k + 1, s]).astype(WIDE)
            place = base + nn(hit.astype(NARROW), strict)
            base = base + jnp.sum(hit, -1, keepdims=True)
            pos_ref[:, s] = jnp.where(hit > 0, place, pos_ref[:, s])
            slot = jnp.where(place < CAP, slot_row + place, 2.0 * EXPERTS * CAP)
            found = jnp.sum(hit * slot, 0, keepdims=True)
            real = jnp.sum(hit, 0, keepdims=True)
            line_ref[k : k + 1, s] = jnp.where(real > 0, found, 2.0 * EXPERTS * CAP)
            line_ref[2 + k : 3 + k, s] = routes_ref[k : k + 1, s].astype(WIDE)
    for c in range(tokens // chunk):
        s = slice(c * chunk, (c + 1) * chunk)
        aux_ref[s, :] = jnp.transpose(line_ref[:, s])


def pad_images(ref, wide_ref, out_ref):
    tokens = ref.shape[0]
    wide_ref[0:tokens, :] = ref[...].astype(WIDE)
    rows = lax.broadcasted_iota(jnp.int32, (SP, 1), 0)
    for i in range(tokens // SEQ):
        image = wide_ref[i * SEQ : i * SEQ + SP, :]
        out_ref[i] = jnp.where(rows < SEQ, image, 0.0).astype(NARROW)


GROUP = 8


def slot_expert(index, groups, held):
    owners, mine = CORES * groups, held // CORES
    owner = index % owners
    return (owner % groups) * held + (owner // groups) * mine + index // owners


def turn_probs(prob_ref, line_ref):
    for c in range(prob_ref.shape[0] // 128):
        s = slice(c * 128, (c + 1) * 128)
        line_ref[:, s] = jnp.transpose(prob_ref[s, :])


def make_rows(experts, places, moe, cot, line_ref, outs):
    slot = lax.broadcasted_iota(jnp.int32, (CAP, 1), 0).astype(WIDE)
    hot, gates = [], []
    for expert, place in zip(experts, places):
        mine = place == slot
        hot.append(mine.astype(WIDE).astype(NARROW))
        gate_row = line_ref[pl.ds(expert, 1), :]
        gates.append(jnp.sum(jnp.where(mine, gate_row, 0.0), -1, keepdims=True))
    hot = jnp.concatenate(hot, 0)
    rows = nn(hot, moe).astype(NARROW)
    grads = nn(hot, cot)
    for g, (gate, out) in enumerate(zip(gates, outs)):
        s = slice(g * CAP, (g + 1) * CAP)
        out[0:CAP, :] = rows[s]
        out[CAP : 2 * CAP, :] = (gate * grads[s]).astype(NARROW)


def dispatch_kernel(groups, held, pos_ref, moe_ref, cot_ref, prob_ref, out_ref, line_ref):
    step = pl.program_id(0)

    @pl.when(step == 0)
    def _():
        turn_probs(prob_ref, line_ref)

    make_rows(
        [slot_expert(step * GROUP + g, groups, held) for g in range(GROUP)],
        [pos_ref[g : g + 1, :] for g in range(GROUP)],
        moe_ref[...],
        cot_ref[...],
        line_ref,
        [out_ref.at[g] for g in range(GROUP)],
    )


def dispatch(pos, moe, cot, prob, groups, held):
    tokens = moe.shape[0]
    return pl.pallas_call(
        partial(dispatch_kernel, groups, held),
        grid=(EXPERTS // GROUP,),
        in_specs=[
            pl.BlockSpec((GROUP, tokens), lambda i: (i, 0)),
            whole(moe.shape),
            whole(cot.shape),
            whole(prob.shape),
        ],
        out_specs=pl.BlockSpec((GROUP, 2 * CAP, D), lambda i: (i, 0, 0)),
        out_shape=sds((EXPERTS, 2 * CAP, D), NARROW),
        scratch_shapes=[pltpu.VMEM((128, tokens), WIDE)],
        compiler_params=params(60),
        name="dispatch",
    )(pos, moe, cot, prob)


def expert_math(slots, grads, win, wout):
    pre = nn(slots, win)
    hidden_grad = nt(grads, wout)
    cdf, bell = normal_parts(pre)
    hidden = (pre * cdf).astype(NARROW)
    pre_grad = ((cdf + pre * (bell * INV_ROOT)) * hidden_grad).astype(NARROW)
    return nn(hidden, wout), nt(pre_grad, win), tn(slots, pre_grad), tn(hidden, grads)


def expert_kernel(pick, rows_ref, win_ref, wout_ref, back_ref, din_ref, dout_ref, res, sgr):
    f = pl.program_id(0)
    senders = rows_ref.shape[0]
    part = min(senders, 8)
    count = part * CAP
    win, wout = win_ref[...], wout_ref[...]
    d_in = d_out = None
    for first in range(0, senders, part):
        slots = rows_ref[first : first + part, 0:CAP, :].reshape(count, D)
        grads = rows_ref[first : first + part, CAP : 2 * CAP, :].reshape(count, D)
        r = slice(first * CAP, (first + part) * CAP)
        result, slot_grad, in_part, out_part = expert_math(slots, grads, win, wout)
        d_in = in_part if d_in is None else d_in + in_part
        d_out = out_part if d_out is None else d_out + out_part

        @pl.when(f == 0)
        def _(r=r, result=result, slot_grad=slot_grad):
            res[r, :] = result
            sgr[r, :] = slot_grad

        @pl.when(f > 0)
        def _(r=r, result=result, slot_grad=slot_grad):
            res[r, :] += result
            sgr[r, :] += slot_grad

    din_ref[...] = d_in.astype(NARROW)
    dout_ref[...] = d_out.astype(NARROW)

    @pl.when(f == pl.num_programs(0) - 1)
    def _():
        back_ref[:, :, 0:D] = res[...].astype(NARROW).reshape(senders, CAP, D)
        back_ref[:, :, D : 2 * D] = sgr[...].astype(NARROW).reshape(senders, CAP, D)


def expert(pick, rows, win, wout):
    senders = rows.shape[0]
    wide = 512
    return pl.pallas_call(
        expert_kernel,
        grid_spec=pltpu.PrefetchScalarGridSpec(
            num_scalar_prefetch=1,
            grid=(FF // wide,),
            in_specs=[
                whole(rows.shape),
                pl.BlockSpec((None, D, wide), lambda f, p: (p[0], 0, f)),
                pl.BlockSpec((None, wide, D), lambda f, p: (p[0], f, 0)),
            ],
            out_specs=[
                whole((senders, CAP, 2 * D)),
                pl.BlockSpec((None, D, wide), lambda f, p: (f, 0, 0)),
                pl.BlockSpec((None, wide, D), lambda f, p: (f, 0, 0)),
            ],
            scratch_shapes=[
                pltpu.VMEM((senders * CAP, D), WIDE),
                pltpu.VMEM((senders * CAP, D), WIDE),
            ],
        ),
        out_shape=[
            sds((senders, CAP, 2 * D), NARROW),
            sds((FF // wide, D, wide), NARROW),
            sds((FF // wide, wide, D), NARROW),
        ],
        compiler_params=params(60),
        cost_estimate=cost(5e9, 1),
        name="one_expert",
    )(pick, rows, win, wout)


def attn_bwd_body(x, incoming, gain, qkv_ref, mixed_ref, w_ref, dw_ref, ib):
    unit, inverse = norm_parts(x)
    normed = (unit * gain).astype(NARROW)
    out_grad = incoming.astype(NARROW)
    mixed = mixed_ref[...].reshape(ib * SP, D)
    dw_ref[:, 3 * D : 4 * D] += tn(mixed, out_grad)
    mixed_grad = nt(out_grad, w_ref[:, 3 * D : 4 * D]).astype(NARROW)
    masks = head_masks(NARROW)
    rows = lax.broadcasted_iota(jnp.int32, (SP, SP), 0)
    dq_all, dk_all, dv_all = [], [], []
    for i in range(ib):
        r = slice(i * SP, (i + 1) * SP)
        dqs, dks, dvs = [], [], []
        for pair in range(HEADS // 2):
            qp = qkv_ref[i, :, pair * 128 : (pair + 1) * 128]
            kp = qkv_ref[i, :, D + pair * 128 : D + (pair + 1) * 128]
            vp = qkv_ref[i, :, 2 * D + pair * 128 : 2 * D + (pair + 1) * 128]
            mp = mixed_grad[r, pair * 128 : (pair + 1) * 128]
            dq = dk = dv = None
            for half in range(2):
                qm, mm, km = qp * masks[half], mp * masks[half], kp * masks[half]
                s = jnp.where(rows < SEQ, nt(kp, qm), LOWEST)
                e = jnp.exp(s - jnp.max(s, 0, keepdims=True))
                soft = e * (1.0 / jnp.sum(e, 0, keepdims=True))
                pg = nt(vp, mm)
                delta = jnp.sum(soft * pg, 0, keepdims=True)
                sg = (soft * (pg - delta)).astype(NARROW)
                v_part = nn(soft.astype(NARROW), mm)
                k_part = nn(sg, qm)
                q_part = tn(sg, km)
                dq = q_part if dq is None else dq + q_part
                dk = k_part if dk is None else dk + k_part
                dv = v_part if dv is None else dv + v_part
            dqs.append((dq * SCALE).astype(NARROW))
            dks.append(dk.astype(NARROW))
            dvs.append(dv.astype(NARROW))
        dq_all.append(jnp.concatenate(dqs, 1))
        dk_all.append(jnp.concatenate(dks, 1))
        dv_all.append(jnp.concatenate(dvs, 1))
    dqkv = jnp.concatenate(
        [
            jnp.concatenate(a, 0) if ib > 1 else a[0]
            for a in (dq_all, dk_all, dv_all)
        ],
        1,
    )
    dw_ref[:, 0 : 3 * D] += tn(normed, dqkv)
    normed_grad = nt(dqkv, w_ref[:, 0 : 3 * D])
    input_grad, gain_grad = norm_backward(normed_grad, unit, inverse, gain)
    return incoming + input_grad, gain_grad


def gain_columns(dg_ref):
    tall = jnp.concatenate(
        [jnp.zeros((EXPERTS, D), WIDE), dg_ref[...], jnp.zeros((128 - EXPERTS - 8, D), WIDE)], 0
    )
    return jnp.transpose(tall)


def put_rows(ref, step, ib, value):
    for image in range(ref.shape[0] // SEQ):

        @pl.when(step == image // ib)
        def _(image=image):
            first = image % ib * SP
            ref[image * SEQ : (image + 1) * SEQ, :] = value[first : first + SEQ]


def moe_bwd_kernel(
    ib,
    g_ref,
    w_ref,
    wr_ref,
    mid_ref,
    second_ref,
    cot_ref,
    prob_ref,
    aux_ref,
    qkv_ref,
    mixed_ref,
    table_ref,
    y_ref,
    grad_ref,
    dw_out,
    dr_ref,
    dg_ref,
    dw_ref,
):
    step = pl.program_id(0)

    @pl.when(step == 0)
    def _():
        dw_ref[...] = jnp.zeros(dw_ref.shape, WIDE)
        dr_ref[...] = jnp.zeros(dr_ref.shape, WIDE)
        dg_ref[...] = jnp.zeros(dg_ref.shape, WIDE)

    second = second_ref[...].reshape(ib * SP, D)
    upstream = cot_ref[...].astype(WIDE).reshape(ib * SP, D)
    prob = prob_ref[...].reshape(ib * SP, 128)
    aux = aux_ref[...].reshape(ib * SP, 128)
    first_pick = second_pick = back = None
    for j in range(table_ref.shape[0]):
        count = table_ref.shape[1] * CAP
        slot = lax.broadcasted_iota(jnp.int32, (1, count), 1).astype(WIDE) + float(j * count)
        hot_one = (aux[:, 0:1] == slot).astype(WIDE).astype(NARROW)
        hot_two = (aux[:, 1:2] == slot).astype(WIDE).astype(NARROW)
        rows = table_ref[j].reshape(count, 2 * D)
        one = nn(hot_one, rows[:, 0:D])
        two = nn(hot_two, rows[:, 0:D])
        both = nn(hot_one + hot_two, rows[:, D : 2 * D])
        first_pick = one if first_pick is None else first_pick + one
        second_pick = two if second_pick is None else second_pick + two
        back = both if back is None else back + both
    lane = lax.broadcasted_iota(jnp.int32, (1, 128), 1)
    first_hit = (aux[:, 2:3] == lane.astype(WIDE)).astype(WIDE)
    second_hit = (aux[:, 3:4] == lane.astype(WIDE)).astype(WIDE)
    gate_one = jnp.sum(prob * first_hit, -1, keepdims=True)
    gate_two = jnp.sum(prob * second_hit, -1, keepdims=True)
    put_rows(y_ref, step, ib, second + (gate_one * first_pick + gate_two * second_pick))
    gate_one_grad = jnp.sum(upstream * first_pick, -1, keepdims=True)
    gate_two_grad = jnp.sum(upstream * second_pick, -1, keepdims=True)
    prob_grad = gate_one_grad * first_hit + gate_two_grad * second_hit
    logit_grad = (prob * (prob_grad - jnp.sum(prob * prob_grad, -1, keepdims=True))).astype(NARROW)
    unit, inverse = norm_parts(second)
    gain = g_ref[3:4, :]
    moe = (unit * gain).astype(NARROW)
    dr_ref[...] += tn(moe, logit_grad)
    normed_grad = back + nt(logit_grad, wr_ref[...])
    moe_grad, gain_grad = norm_backward(normed_grad, unit, inverse, gain)
    dg_ref[3:4, :] += gain_grad
    mid = mid_ref[...].reshape(ib * SP, D)
    grad, gain_grad = attn_bwd_body(
        mid, upstream + moe_grad, g_ref[1:2, :], qkv_ref, mixed_ref, w_ref, dw_ref, ib
    )
    dg_ref[1:2, :] += gain_grad
    grad_ref[...] = grad.reshape(ib, SP, D)

    @pl.when(step == pl.num_programs(0) - 1)
    def _():
        dw_out[:, : 4 * D] = dw_ref[...].astype(NARROW)
        dw_out[:, 4 * D :] = (dr_ref[...] + gain_columns(dg_ref)).astype(NARROW)


def moe_bwd(gains, w1, wr, mid, second, cot, prob, aux, qkv, mixed, tables, images, ib):
    return pl.pallas_call(
        partial(moe_bwd_kernel, ib),
        grid=(images // ib,),
        in_specs=[
            whole(gains.shape),
            whole(w1.shape),
            whole(wr.shape),
            per_image(ib, SP, D),
            per_image(ib, SP, D),
            per_image(ib, SP, D),
            per_image(ib, SP, 128),
            per_image(ib, SP, 128),
            per_image(ib, SP, 3 * D),
            per_image(ib, SP, D),
            whole(tables.shape),
        ],
        out_specs=[
            whole((images * SEQ, D)),
            per_image(ib, SP, D),
            whole((D, 4 * D + 128)),
        ],
        out_shape=[
            sds((images * SEQ, D), WIDE),
            sds((images, SP, D), WIDE),
            sds((D, 4 * D + 128), NARROW),
        ],
        scratch_shapes=[
            pltpu.VMEM((D, 128), WIDE),
            pltpu.VMEM((8, D), WIDE),
            pltpu.VMEM((D, 4 * D), WIDE),
        ],
        compiler_params=params(60),
        cost_estimate=cost(1e6, 1),
        name="expert_block_backward",
    )(gains, w1, wr, mid, second, cot, prob, aux, qkv, mixed, tables)


def dense_bwd_kernel(
    ib,
    g_ref,
    w_ref,
    win_ref,
    wout_ref,
    x_ref,
    first_ref,
    grad_ref,
    qkv_ref,
    mixed_ref,
    out_ref,
    dw_out,
    dout_out,
    dg_ref,
    dw_ref,
    din_ref,
    dout_ref,
):
    step = pl.program_id(0)

    @pl.when(step == 0)
    def _():
        dw_ref[...] = jnp.zeros(dw_ref.shape, WIDE)
        din_ref[...] = jnp.zeros(din_ref.shape, WIDE)
        dout_ref[...] = jnp.zeros(dout_ref.shape, WIDE)
        dg_ref[...] = jnp.zeros(dg_ref.shape, WIDE)

    incoming = grad_ref[...].reshape(ib * SP, D)
    first = first_ref[...].reshape(ib * SP, D)
    unit, inverse = norm_parts(first)
    gain = g_ref[2:3, :]
    normed = (unit * gain).astype(NARROW)
    out_grad = incoming.astype(NARROW)
    y_grad = None
    for f in range(FF // 512):
        c = slice(f * 512, (f + 1) * 512)
        win, wout = win_ref[:, c], wout_ref[c, :]
        pre = nn(normed, win)
        hidden_grad = nt(out_grad, wout)
        cdf, bell = normal_parts(pre)
        hidden = (pre * cdf).astype(NARROW)
        pre_grad = ((cdf + pre * (bell * INV_ROOT)) * hidden_grad).astype(NARROW)
        dout_ref[c, :] += tn(hidden, out_grad)
        din_ref[:, c] += tn(normed, pre_grad)
        part = nt(pre_grad, win)
        y_grad = part if y_grad is None else y_grad + part
    ffn_grad, gain_grad = norm_backward(y_grad, unit, inverse, gain)
    dg_ref[2:3, :] += gain_grad
    x = x_ref[...].astype(WIDE).reshape(ib * SP, D)
    grad, gain_grad = attn_bwd_body(
        x, incoming + ffn_grad, g_ref[0:1, :], qkv_ref, mixed_ref, w_ref, dw_ref, ib
    )
    dg_ref[0:1, :] += gain_grad
    put_rows(out_ref, step, ib, grad)

    @pl.when(step == pl.num_programs(0) - 1)
    def _():
        dw_out[:, : 4 * D] = dw_ref[...].astype(NARROW)
        dw_out[:, 4 * D : 8 * D] = din_ref[...].astype(NARROW)
        dw_out[:, 8 * D :] = gain_columns(dg_ref).astype(NARROW)
        dout_out[...] = dout_ref[...].astype(NARROW)


def dense_bwd(gains, w0, win, wout, x, first, grad, qkv, mixed, images, ib):
    return pl.pallas_call(
        partial(dense_bwd_kernel, ib),
        grid=(images // ib,),
        in_specs=[
            whole(gains.shape),
            whole(w0.shape),
            whole(win.shape),
            whole(wout.shape),
            per_image(ib, SP, D),
            per_image(ib, SP, D),
            per_image(ib, SP, D),
            per_image(ib, SP, 3 * D),
            per_image(ib, SP, D),
        ],
        out_specs=[
            whole((images * SEQ, D)),
            whole((D, 8 * D + 128)),
            whole((FF, D)),
        ],
        out_shape=[
            sds((images * SEQ, D), WIDE),
            sds((D, 8 * D + 128), NARROW),
            sds((FF, D), NARROW),
        ],
        scratch_shapes=[
            pltpu.VMEM((8, D), WIDE),
            pltpu.VMEM((D, 4 * D), WIDE),
            pltpu.VMEM((D, FF), WIDE),
            pltpu.VMEM((FF, D), WIDE),
        ],
        compiler_params=params(60),
        cost_estimate=cost(1e6, 1),
        name="dense_block_backward",
    )(gains, w0, win, wout, x, first, grad, qkv, mixed)


BLOCK = 512
CUTS = 2
AHEAD = 3
MESH_ID = pl.DeviceIdType.MESH


def add_rows(out, one, two, rows, step):
    @pl.loop(0, rows // step)
    def _(i):
        r = pl.ds(pl.multiple_of(i * step, step), step)
        out[r, :] = (one[r, :].astype(WIDE) + two[r, :].astype(WIDE)).astype(out.dtype)


def sum_kernel(nz, groups, mats, slices, first, handed, *refs):
    exp_refs, refs = refs[:mats], refs[mats:]
    dense_refs, peak_ref, refs = refs[:3], refs[3], refs[4:]
    if handed:
        _, hand_ref, refs = refs[0], refs[1], refs[2:]
    exp_out, dense_outs, peak_out, refs = refs[0], refs[1:4], refs[4], refs[5:]
    if handed:
        hand_buf, hand_sem, refs = refs[-2], refs[-1], refs[:-2]
    own, up, down, refs = refs[0], refs[1], refs[2], refs[3:]
    land, refs = refs[:4], refs[4:]
    dense_own, refs = refs[:4], refs[4:]
    dense_up, refs = refs[:4], refs[4:]
    dense_down, refs = refs[:4], refs[4:]
    (own_sem, up_send, up_recv, down_recv, out_send, sib_send, sib_recv, copy_sem, rs_send, rs_recv) = refs

    z, core, f = lax.axis_index("z"), lax.axis_index("core"), lax.axis_index("fsdp")
    half = nz // 2
    left = z < half
    inner = jnp.where(left, z + 1, z - 1)
    outer = jnp.where(left, z - 1, z + 1)
    has_outer = jnp.logical_and(z > 0, z < nz - 1)
    edge = jnp.logical_not(has_outer)
    center = jnp.logical_or(z == half - 1, z == half)
    away = jnp.logical_not(center)
    outer = jnp.where(has_outer, outer, inner)
    sibling = (z, 1 - core, f)
    members = CORES * groups
    me = core * groups + f

    barrier = pltpu.get_barrier_semaphore()
    pl.semaphore_signal(barrier, inc=1, device_id=(inner, core, f), device_id_type=MESH_ID)

    @pl.when(has_outer)
    def _():
        pl.semaphore_signal(barrier, inc=1, device_id=(outer, core, f), device_id_type=MESH_ID)

    for d in range(1, members):
        there = lax.rem(me + d, members)
        pl.semaphore_signal(
            barrier,
            inc=1,
            device_id=(z, there // groups, lax.rem(there, groups)),
            device_id_type=MESH_ID,
        )

    if handed:
        arrived = pltpu.make_async_copy(hand_ref, hand_buf, hand_sem.at[2])
        arrived.start()

    @pl.when(has_outer)
    def _():
        pl.semaphore_wait(barrier, members + 1)

    @pl.when(edge)
    def _():
        pl.semaphore_wait(barrier, members)

    chunks = mats * slices * CUTS
    items = chunks + 4

    def cut_rows(t):
        return pl.ds(t % CUTS * (BLOCK // CUTS), BLOCK // CUTS)

    def piece(n, ref, there):
        if n == 3:
            return ref
        rows = ref.shape[0] // members
        place = (lax.rem(there, groups) * CORES + there // groups) * rows
        return ref.at[pl.ds(pl.multiple_of(place, 16), rows), :]

    def scatter(n, d):
        there = lax.rem(me + d, members)
        source = dense_refs[n] if n < 3 else peak_ref
        return pltpu.make_async_remote_copy(
            src_ref=piece(n, source, there),
            dst_ref=land[n].at[d],
            send_sem=rs_send.at[n, d],
            recv_sem=rs_recv.at[n, d],
            device_id=(z, there // groups, lax.rem(there, groups)),
            device_id_type=MESH_ID,
        )

    def hand():
        return pltpu.make_async_remote_copy(
            src_ref=hand_buf,
            dst_ref=exp_out.at[pl.ds(first - handed, handed), core],
            send_sem=hand_sem.at[0],
            recv_sem=hand_sem.at[1],
            device_id=sibling,
            device_id_type=MESH_ID,
        )

    if handed:
        arrived.wait()
        handed_here = pltpu.make_async_copy(
            hand_buf, exp_out.at[pl.ds(first - handed, handed), core], hand_sem.at[2]
        )
        handed_here.start()
        hand().start()
    for n in (3, 1, 0, 2):
        for d in range(1, members):
            scatter(n, d).start()
    keep = [
        pltpu.make_async_copy(
            piece(n, dense_refs[n] if n < 3 else peak_ref, me), land[n].at[0], rs_recv.at[n, 0]
        )
        for n in range(4)
    ]
    for k in keep:
        k.start()

    def source_at_edge(t):
        if t >= chunks:
            return dense_own[t - chunks]
        return exp_refs[t // CUTS // slices].at[t // CUTS % slices, cut_rows(t), :]

    def load(t):
        return pltpu.make_async_copy(source_at_edge(t), own.at[t], own_sem.at[t])

    @pl.when(has_outer)
    def _():
        for t in range(chunks):
            load(t).start()

    def bufs(t):
        if t < chunks:
            return own.at[t], up.at[t], down.at[t]
        n = t - chunks
        return dense_own[n], dense_up[n], dense_down[n]

    def send_up(t, source, to_center):
        _, u, dn = bufs(t)
        return pltpu.make_async_remote_copy(
            src_ref=source,
            dst_ref=dn if to_center else u,
            send_sem=up_send.at[t],
            recv_sem=(down_recv if to_center else up_recv).at[t],
            device_id=(inner, core, f),
            device_id_type=MESH_ID,
        )

    def join(t, out, one, two):
        if t == items - 1:
            out[...] = jnp.maximum(one[...], two[...])
        else:
            add_rows(out, one, two, out.shape[0], 16)

    def reduce_own(n):
        for d in range(members):
            if d == 0:
                keep[n].wait()
            else:
                scatter(n, d).wait_recv()
        if n == 3:
            best = land[n][0]
            for d in range(1, members):
                best = jnp.maximum(best, land[n][d])
            dense_own[n][...] = best
            return

        @pl.loop(0, dense_own[n].shape[0] // 16)
        def _(i):
            r = pl.ds(pl.multiple_of(i * 16, 16), 16)
            total = land[n][0, r, :].astype(WIDE)
            for d in range(1, members):
                total = total + land[n][d, r, :].astype(WIDE)
            dense_own[n][r, :] = total.astype(NARROW)

    def up_from_edge(t, before):
        if before is not None:
            send_up(before, source_at_edge(before), half == 1).wait_send()
        if t >= chunks:
            reduce_own(t - chunks)
        send_up(t, source_at_edge(t), half == 1).start()

    def up_from_inside(t):
        o, u, _ = bufs(t)
        if t >= chunks:
            reduce_own(t - chunks)
        else:
            load(t).wait()
        send_up(t, u, False).wait_recv()
        join(t, o, o, u)

        @pl.when(center)
        def _():
            send_up(t, o, True).start()

        if half > 2:

            @pl.when(away)
            def _():
                send_up(t, o, False).start()

    def results(t):
        if t < chunks:
            return exp_out.at[first + t // CUTS, core, cut_rows(t), :]
        n = t - chunks
        if n == 3:
            return peak_out
        ref = dense_outs[n]
        rows = ref.shape[0] // CORES
        return ref.at[pl.ds(pl.multiple_of(core * rows, 16), rows), :]

    def to_sibling(t):
        return pltpu.make_async_remote_copy(
            src_ref=bufs(t)[2],
            dst_ref=results(t),
            send_sem=sib_send.at[t],
            recv_sem=sib_recv.at[t],
            device_id=sibling,
            device_id_type=MESH_ID,
        )

    def to_outer(t):
        dn = bufs(t)[2]
        return pltpu.make_async_remote_copy(
            src_ref=dn,
            dst_ref=dn,
            send_sem=out_send.at[t],
            recv_sem=down_recv.at[t],
            device_id=(outer, core, f),
            device_id_type=MESH_ID,
        )

    def keep_result(t):
        return pltpu.make_async_copy(bufs(t)[2], results(t), copy_sem.at[t])

    def go_down(t, at_edge):
        o, _, dn = bufs(t)
        to_outer(t).wait_recv()
        if at_edge:
            if half == 1:
                join(t, dn, source_at_edge(t), dn)
        else:

            @pl.when(center)
            def _():
                join(t, dn, o, dn)

            to_outer(t).start()
        keep_result(t).start()
        if t < items - 1:
            to_sibling(t).start()

    early = min(11 * CUTS, chunks)
    sequence = [*range(early), *range(items - 1, chunks - 1, -1), *range(early, chunks)]

    def run(up, at_edge, lag):
        for i in range(items + lag):
            if i < items:
                up(i)
            if i >= lag:
                go_down(sequence[i - lag], at_edge)

    @pl.when(edge)
    def _():
        run(
            lambda i: up_from_edge(sequence[i], sequence[i - AHEAD] if i >= AHEAD else None),
            True,
            min(7 * CUTS, items),
        )
        for t in sequence[-AHEAD:]:
            send_up(t, source_at_edge(t), half == 1).wait_send()

    if half > 1:

        @pl.when(has_outer)
        def _():
            run(lambda i: up_from_inside(sequence[i]), False, 1)
            for t in range(items):
                send_up(t, bufs(t)[0], False).wait_send()
                to_outer(t).wait_send()

    for n in range(4):
        for d in range(1, members):
            scatter(n, d).wait_send()
    if handed:
        hand().wait()
        handed_here.wait()
    for t in range(items):
        keep_result(t).wait()
        if t < items - 1:
            to_sibling(t).wait()


def sum_all(mats, dense, peaks, early, handed, nz, groups):
    slices = mats[0].shape[0]
    blocks = len(mats) * slices
    chunks = blocks * CUTS
    members = CORES * groups
    items = chunks + 4
    any_space = pl.BlockSpec(memory_space=pl.ANY)
    vmem = pl.BlockSpec(memory_space=pltpu.VMEM)
    pieces = [(a.shape[0] // members, a.shape[1]) for a in dense]
    block = pltpu.VMEM((chunks, BLOCK // CUTS, BLOCK), NARROW)

    def four(lead=()):
        return [pltpu.VMEM((*lead, *p), NARROW) for p in pieces] + [
            pltpu.VMEM((*lead, *peaks.shape), WIDE)
        ]

    dma = pltpu.SemaphoreType.DMA
    extra = [] if handed is None else [early, handed]
    count = handed.shape[0] if extra else 0
    first = early.shape[0] - blocks if extra else 0
    return pl.pallas_call(
        partial(sum_kernel, nz, groups, len(mats), slices, first, count),
        in_specs=[any_space] * (len(mats) + 3) + [vmem] + [any_space] * len(extra),
        out_specs=[any_space] * 4 + [vmem],
        out_shape=[
            sds((first + blocks, CORES, BLOCK, BLOCK), NARROW),
            *[sds((CORES * r, c), NARROW) for r, c in pieces],
            sds(peaks.shape, WIDE),
        ],
        scratch_shapes=[
            block,
            block,
            block,
            *four((members,)),
            *four(),
            *four(),
            *four(),
            *[dma((items,)) for _ in range(8)],
            dma((4, members)),
            dma((4, members)),
            *([pltpu.VMEM(handed.shape, NARROW), dma((3,))] if extra else []),
        ],
        compiler_params=pltpu.CompilerParams(
            vmem_limit_bytes=58 * MIB, collective_id=3, has_side_effects=True
        ),
        input_output_aliases={len(mats) + 4: 0} if extra else {},
        name="sums",
    )(*mats, *dense, peaks, *extra)


SUMMED = 12
LAGS = (2, 4, 6)
BESIDE = 8


def exchange_kernel(nz, groups, mine, *refs):
    pos_ref, moe_ref, cot_ref, prob_ref, win_hbm, wout_hbm, refs = *refs[:6], refs[6:]
    table_out, sum_out, beside_out, rest_out, refs = *refs[:4], refs[4:]
    sent, line_ref, refs = *refs[:2], refs[2:]
    (rows, back, res, sgr, w_in, w_out, own, up, down, made) = refs[:10]
    (d_send, d_recv, r_send, r_recv, w_sem, made_sem, up_send, up_recv, down_recv) = refs[10:19]
    (out_send, sib_send, sib_recv, keep_sem) = refs[19:]
    s = pl.program_id(0)
    z, core, f = lax.axis_index("z"), lax.axis_index("core"), lax.axis_index("fsdp")
    members = CORES * groups
    me = core * groups + f
    parts = FF // BLOCK
    steps = mine * parts
    last = pl.num_programs(0) - 1
    left = z < nz // 2
    inner = jnp.where(left, z + 1, z - 1)
    has_outer = jnp.logical_and(z > 0, z < nz - 1)
    edge = jnp.logical_not(has_outer)
    outer = jnp.where(has_outer, jnp.where(left, z - 1, z + 1), inner)

    def member(d):
        there = lax.rem(me + d, members)
        return there, (z, there // groups, lax.rem(there, groups))

    def rows_to(j, d):
        there, device = member(d)
        return pltpu.make_async_remote_copy(
            src_ref=sent.at[j, there],
            dst_ref=rows.at[j, me],
            send_sem=d_send.at[j, d],
            recv_sem=d_recv.at[j, d],
            device_id=device,
            device_id_type=MESH_ID,
        )

    def rows_here(j):
        return pltpu.make_async_copy(sent.at[j, me], rows.at[j, me], d_recv.at[j, 0])

    def prepare(j, others):
        theirs = [member(d)[0] for d in others]
        make_rows(
            [slot_expert(j * members + there, groups, CORES * mine) for there in theirs],
            [pos_ref[pl.ds(j * members + there, 1), :] for there in theirs],
            moe_ref[...],
            cot_ref[...],
            line_ref,
            [sent.at[j, there] for there in theirs],
        )

    def send_rows(j):
        for d in range(1, members):
            rows_to(j, d).start()
        rows_here(j).start()

    def results_to(j, d):
        there, device = member(d)
        return pltpu.make_async_remote_copy(
            src_ref=back.at[j % 2, there],
            dst_ref=table_out.at[j, me],
            send_sem=r_send.at[j, d],
            recv_sem=r_recv.at[j, d],
            device_id=device,
            device_id_type=MESH_ID,
        )

    def results_here(j):
        return pltpu.make_async_copy(back.at[j % 2, me], table_out.at[j, me], r_recv.at[j, 0])

    def weights(step):
        e = core * mine + step // parts
        c = pl.ds(pl.multiple_of(lax.rem(step, parts) * BLOCK, BLOCK), BLOCK)
        slot = lax.rem(step, 2)
        return (
            pltpu.make_async_copy(win_hbm.at[e, :, c], w_in.at[slot], w_sem.at[0, slot]),
            pltpu.make_async_copy(wout_hbm.at[e, c, :], w_out.at[slot], w_sem.at[1, slot]),
        )

    @pl.when(s == 0)
    def _():
        barrier = pltpu.get_barrier_semaphore()
        pl.semaphore_signal(barrier, inc=1, device_id=(inner, core, f), device_id_type=MESH_ID)

        @pl.when(has_outer)
        def _():
            pl.semaphore_signal(barrier, inc=1, device_id=(outer, core, f), device_id_type=MESH_ID)

        for d in range(1, members):
            pl.semaphore_signal(barrier, inc=1, device_id=member(d)[1], device_id_type=MESH_ID)

        for w in weights(s):
            w.start()
        turn_probs(prob_ref, line_ref)
        prepare(0, [1, 2])

        @pl.when(has_outer)
        def _():
            pl.semaphore_wait(barrier, members + 1)

        @pl.when(edge)
        def _():
            pl.semaphore_wait(barrier, members)

        for d in range(1, members, 2):
            others = [d, (d + 1) % members]
            if d > 1:
                prepare(0, others)
            for there in others:
                if there:
                    rows_to(0, there).start()
        rows_here(0).start()
        for j in range(1, mine):
            prepare(j, range(members))

    for j in range(mine):

        @pl.when(s == j * parts)
        def _(j=j):
            for d in range(1, members):
                rows_to(j, d).wait_recv()
            rows_here(j).wait()
            if j == 0:
                send_rows(1)
            if j == 1:
                send_rows(3)

    slot = lax.rem(s, 2)

    def made_to(step, side, near):
        place = 2 * step + side - SUMMED - (0 if near else BESIDE)
        there = lax.rem(step, 2)
        out = beside_out if near else rest_out
        return pltpu.make_async_copy(
            made.at[there, side],
            out.at[jnp.clip(place, 0, out.shape[0] - 1)],
            made_sem.at[there, side],
        )

    def each_made(step, act):
        near = step < (SUMMED + BESIDE) // 2

        @pl.when(near)
        def _():
            for side in range(2):
                act(made_to(step, side, True))

        @pl.when(jnp.logical_not(near))
        def _():
            for side in range(2):
                act(made_to(step, side, False))

    @pl.when(s < steps)
    def _():
        for w in weights(s):
            w.wait()

        @pl.when(s + 1 < steps)
        def _():
            for w in weights(s + 1):
                w.start()

        @pl.when(jnp.logical_and(s >= SUMMED // 2 + 2, s < steps))
        def _():
            each_made(s - 2, lambda copy: copy.wait())

        j = s // parts
        part = lax.rem(s, parts)
        count = members * CAP
        half = members // 2
        halves = []
        for h in range(2):
            side = slice(h * half, (h + 1) * half)
            slots = rows[j, side, 0:CAP, :].reshape(count // 2, D)
            grads = rows[j, side, CAP : 2 * CAP, :].reshape(count // 2, D)
            halves.append(expert_math(slots, grads, w_in[slot], w_out[slot]))
        result, slot_grad = (jnp.concatenate([halves[0][n], halves[1][n]], 0) for n in range(2))
        d_in, d_out = (halves[0][n] + halves[1][n] for n in range(2, 4))

        @pl.when(part == 0)
        def _():
            res[...] = result
            sgr[...] = slot_grad

        @pl.when(part > 0)
        def _():
            res[...] += result
            sgr[...] += slot_grad

        @pl.when(s < SUMMED // 2)
        def _():
            own[2 * s] = d_in.astype(NARROW)
            own[2 * s + 1] = d_out.astype(NARROW)

        @pl.when(s >= SUMMED // 2)
        def _():
            made[slot, 0] = d_in.astype(NARROW)
            made[slot, 1] = d_out.astype(NARROW)

            each_made(s, lambda copy: copy.start())

    @pl.when(s == 1)
    def _():
        send_rows(2)

    for j in range(mine):

        @pl.when(s == (j + 1) * parts - 1)
        def _(j=j):
            if j >= 2:
                for d in range(1, members):
                    results_to(j - 2, d).wait_send()
                results_here(j - 2).wait()
            back[j % 2, :, :, 0:D] = res[...].astype(NARROW).reshape(members, CAP, D)
            back[j % 2, :, :, D : 2 * D] = sgr[...].astype(NARROW).reshape(members, CAP, D)
            for d in range(1, members):
                results_to(j, d).start()
            results_here(j).start()

    def send_up(t, to_center):
        return pltpu.make_async_remote_copy(
            src_ref=own.at[t],
            dst_ref=(down if to_center else up).at[t],
            send_sem=up_send.at[t],
            recv_sem=(down_recv if to_center else up_recv).at[t],
            device_id=(inner, core, f),
            device_id_type=MESH_ID,
        )

    def send_out(t):
        return pltpu.make_async_remote_copy(
            src_ref=down.at[t],
            dst_ref=down.at[t],
            send_sem=out_send.at[t],
            recv_sem=down_recv.at[t],
            device_id=(outer, core, f),
            device_id_type=MESH_ID,
        )

    def to_sibling(t):
        return pltpu.make_async_remote_copy(
            src_ref=down.at[t],
            dst_ref=sum_out.at[t, core],
            send_sem=sib_send.at[t],
            recv_sem=sib_recv.at[t],
            device_id=(z, 1 - core, f),
            device_id_type=MESH_ID,
        )

    def keep_sum(t):
        return pltpu.make_async_copy(down.at[t], sum_out.at[t, core], keep_sem.at[t])

    def at(lag, role):
        t = s - lag
        return pl.when(jnp.logical_and(role, jnp.logical_and(t >= 0, t < SUMMED)))

    def tick(t):
        return jnp.clip(t, 0, SUMMED - 1)

    @at(0, edge)
    def _():
        send_up(tick(s), False).start()

    @at(LAGS[0], has_outer)
    def _():
        t = tick(s - LAGS[0])
        send_up(t, False).wait_recv()
        add_rows(own.at[t], own.at[t], up.at[t], BLOCK, 16)
        send_up(t, True).start()

    @at(LAGS[1], has_outer)
    def _():
        t = tick(s - LAGS[1])
        send_out(t).wait_recv()
        add_rows(down.at[t], own.at[t], down.at[t], BLOCK, 16)
        send_out(t).start()
        keep_sum(t).start()
        to_sibling(t).start()

    @at(LAGS[2], edge)
    def _():
        t = tick(s - LAGS[2])
        send_out(t).wait_recv()
        keep_sum(t).start()
        to_sibling(t).start()

    @pl.when(s == last)
    def _():
        for step in (steps - 2, steps - 1):
            for side in range(2):
                made_to(step, side, False).wait()
        for j in range(mine):
            for d in range(1, members):
                rows_to(j, d).wait_send()
                results_to(j, d).wait_recv()
                if j >= mine - 2:
                    results_to(j, d).wait_send()
            if j >= mine - 2:
                results_here(j).wait()

        for t in range(SUMMED):
            send_up(t, False).wait_send()
            keep_sum(t).wait()
            to_sibling(t).wait()

        @pl.when(has_outer)
        def _():
            for t in range(SUMMED):
                send_out(t).wait_send()


def exchange(pos, moe, cot, prob, win, wout, nz, groups):
    members = CORES * groups
    mine = win.shape[0] // CORES
    steps = mine * (FF // BLOCK)
    rest = 2 * steps - SUMMED - BESIDE
    any_space = pl.BlockSpec(memory_space=pl.ANY)
    dma = pltpu.SemaphoreType.DMA
    block = pltpu.VMEM((SUMMED, BLOCK, BLOCK), NARROW)
    return pl.pallas_call(
        partial(exchange_kernel, nz, groups, mine),
        grid=(max(steps, SUMMED + LAGS[2]),),
        in_specs=[*[whole(a.shape) for a in (pos, moe, cot, prob)], any_space, any_space],
        out_specs=[any_space] * 4,
        out_shape=[
            sds((mine, members, CAP, 2 * D), NARROW),
            sds((2 * steps, CORES, BLOCK, BLOCK), NARROW),
            sds((BESIDE, BLOCK, BLOCK), NARROW),
            sds((rest, BLOCK, BLOCK), NARROW),
        ],
        scratch_shapes=[
            pltpu.VMEM((mine, members, 2 * CAP, D), NARROW),
            pltpu.VMEM((128, moe.shape[0]), WIDE),
            pltpu.VMEM((mine, members, 2 * CAP, D), NARROW),
            pltpu.VMEM((2, members, CAP, 2 * D), NARROW),
            pltpu.VMEM((members * CAP, D), WIDE),
            pltpu.VMEM((members * CAP, D), WIDE),
            pltpu.VMEM((2, D, BLOCK), NARROW),
            pltpu.VMEM((2, BLOCK, D), NARROW),
            block,
            block,
            block,
            pltpu.VMEM((2, 2, BLOCK, BLOCK), NARROW),
            *[dma((mine, members)) for _ in range(4)],
            dma((2, 2)),
            dma((2, 2)),
            *[dma((SUMMED,)) for _ in range(7)],
        ],
        compiler_params=pltpu.CompilerParams(
            vmem_limit_bytes=62 * MIB, collective_id=7, has_side_effects=True
        ),
        name="experts",
    )(pos, moe, cot, prob, win, wout)


def finish_small(refs):
    (wide_ref, deep_ref, out_ref, peak_ref, limit_ref, query_ref, key_ref) = refs[:7]
    (gain_out, q_out, k_out, v_out, o_out, ffn_out, in_out, mlp_out, router_out, cq_out, ck_out) = refs[7:]
    for n, ref in enumerate((q_out, k_out, v_out, o_out)):
        c = slice(n * D, (n + 1) * D)
        ref[0] = wide_ref[:, c].astype(WIDE)
        ref[1] = deep_ref[:, c].astype(WIDE)
    in_out[...] = wide_ref[:, 4 * D : 8 * D].astype(WIDE)
    mlp_out[...] = out_ref[...].astype(WIDE)
    small = deep_ref[:, 4 * D :].astype(WIDE) + wide_ref[:, 8 * D :].astype(WIDE)
    router_out[...] = small[:, :EXPERTS]
    count = small.shape[0]
    if count < 128:
        small = jnp.concatenate([small, jnp.zeros((128 - count, 128), WIDE)], 0)
    turned = jnp.transpose(small)
    gain_out[...] = turned[EXPERTS : EXPERTS + 2, :count]
    ffn_out[...] = turned[EXPERTS + 2 : EXPERTS + 4, :count]
    head = lax.broadcasted_iota(jnp.int32, (HEADS, D), 0)
    feature = lax.broadcasted_iota(jnp.int32, (HEADS, D), 1)
    owns = jnp.logical_and(feature >= head * HEAD, feature < (head + 1) * HEAD)
    for layer in range(2):
        limit = limit_ref[:, layer : layer + 1]
        top = peak_ref[:, layer * 64 : layer * 64 + 1]
        scale = jnp.sqrt(limit / jnp.maximum(top, limit))
        row = jnp.sum(jnp.where(owns, scale, 0.0), 0, keepdims=True)
        cq_out[layer] = query_ref[layer] * row
        ck_out[layer] = key_ref[layer] * row


PAIRS = 2


def widen_blocks(blocks_ref, in_ref, out_ref):
    for n in range(PAIRS):
        r = slice(n * BLOCK, (n + 1) * BLOCK)
        in_ref[:, r] = blocks_ref[n, 0].astype(WIDE)
        out_ref[r, :] = blocks_ref[n, 1].astype(WIDE)


def block_specs(mine, first):
    parts = FF // BLOCK // PAIRS
    wide = PAIRS * BLOCK

    def place(c, s):
        return c * mine + (s + first) // parts, (s + first) % parts

    return (
        pl.BlockSpec((PAIRS, 2, None, BLOCK, BLOCK), lambda c, s: (s + first, 0, c, 0, 0)),
        [
            pl.BlockSpec((None, D, wide), lambda c, s: (place(c, s)[0], 0, place(c, s)[1])),
            pl.BlockSpec((None, wide, D), lambda c, s: (*place(c, s), 0)),
        ],
    )


def gradient_shapes(mine):
    return [sds((CORES * mine, D, FF), WIDE), sds((CORES * mine, FF, D), WIDE)]


def widen_early(blocks, count, mine):
    source, places = block_specs(mine, 0)
    return pl.pallas_call(
        widen_blocks,
        grid=(CORES, count // 2 // PAIRS),
        in_specs=[source],
        out_specs=places,
        out_shape=gradient_shapes(mine),
        compiler_params=params(60),
        name="widen_early",
    )(blocks.reshape(-1, 2, CORES, BLOCK, BLOCK))


def finish_kernel(given, blocks_ref, *refs):
    small, (in_ref, out_ref) = refs[given:-2], refs[-2:]

    @pl.when(jnp.logical_and(pl.program_id(0) == 0, pl.program_id(1) == 0))
    def _():
        finish_small(small)

    widen_blocks(blocks_ref, in_ref, out_ref)


def finish(blocks, done, given, mine, small, outs):
    first = done // 2 // PAIRS
    source, places = block_specs(mine, first)
    steps = blocks.shape[0] // 2 // PAIRS - first
    return pl.pallas_call(
        partial(finish_kernel, len(given)),
        grid=(CORES, steps),
        in_specs=[
            source,
            *[pl.BlockSpec(memory_space=pl.ANY)] * len(given),
            *[whole(a.shape) for a in small],
        ],
        out_specs=[whole(o.shape) for o in outs] + places,
        out_shape=[*outs, *gradient_shapes(mine)],
        input_output_aliases={1 + n: len(outs) + n for n in range(len(given))},
        compiler_params=params(60),
        name="finish",
    )(blocks.reshape(-1, 2, CORES, BLOCK, BLOCK), *given, *small)


def forward_kernel(groups, ib, *refs):
    q_ref, k_ref, v_ref, o_ref, small_ref, in_ref, out_ref, refs = *refs[:7], refs[7:]
    token_ref, cot_ref, order_ref, routes_ref, refs = *refs[:4], refs[4:]
    kept, refs = refs[:4], refs[4:]
    gain_ref, router_ref, x_out, cot_out, pos_ref, aux_ref, refs = *refs[:6], refs[6:]
    first_ref, qkv0_ref, mixed0_ref, peak0_ref, mid_ref, refs = *refs[:5], refs[5:]
    second_ref, qkv1_ref, mixed1_ref, peak1_ref, moe_ref, prob_ref, refs = *refs[:6], refs[6:]
    w0, win, wout, w1, small_all, state, wide_ref, line_ref, rows_ref, refs = *refs[:9], refs[9:]
    send, recv, pass_send, pass_recv, copy, rows_sem, kept_sem = refs
    phase, i = pl.program_id(0), pl.program_id(1)
    z, core, f = lax.axis_index("z"), lax.axis_index("core"), lax.axis_index("fsdp")

    def rows(count, owner, side):
        half = count // CORES
        return pl.ds(pl.multiple_of(owner * count + side * half, 16), half)

    def item(n):
        if n < 4 or n >= 7:
            ref = (q_ref, k_ref, v_ref, o_ref)[n % 7]
            full, layer = (w0, 0) if n < 4 else (w1, 1)
            count = ref.shape[1]
            cols = pl.ds(n % 7 * D, D)
            return (
                lambda side: ref.at[layer, rows(count, 0, side), :],
                lambda owner, side: full.at[rows(count, owner, side), cols],
            )
        ref, full = ((small_ref, small_all), (in_ref, win), (out_ref, wout))[n - 4]
        count = ref.shape[0]
        return (
            lambda side: ref.at[rows(count, 0, side), :],
            lambda owner, side: full.at[rows(count, owner, side), :],
        )

    def fetch(n, d):
        source, place = item(n)
        return pltpu.make_async_remote_copy(
            src_ref=source(core),
            dst_ref=place(f, core),
            send_sem=send.at[n, d],
            recv_sem=recv.at[n, d],
            device_id=(z, core, lax.rem(f + d, groups)),
            device_id_type=MESH_ID,
        )

    def hand_on(n, d):
        _, place = item(n)
        there = place(lax.rem(f + groups - d, groups), core)
        return pltpu.make_async_remote_copy(
            src_ref=there,
            dst_ref=there,
            send_sem=pass_send.at[n, d],
            recv_sem=pass_recv.at[n, d],
            device_id=(z, 1 - core, f),
            device_id_type=MESH_ID,
        )

    def keep(n, side):
        source, place = item(n)
        return pltpu.make_async_copy(source(side), place(f, side), copy.at[n, side])

    sets = ((0, 1, 2, 3, 4), (5, 6), (7, 8, 9, 10))

    def begin(stage):
        for n in sets[stage]:
            for d in range(1, groups):
                fetch(n, d).start()
            for side in range(CORES):
                keep(n, side).start()

    def arrive(stage):
        for n in sets[stage]:
            for d in range(1, groups):
                fetch(n, d).wait_recv()
                hand_on(n, d).start()

    def complete(stage):
        for n in sets[stage]:
            for side in range(CORES):
                keep(n, side).wait()
            for d in range(1, groups):
                fetch(n, d).wait_send()
                hand_on(n, d).wait()

    def keepers():
        return [
            pltpu.make_async_copy(ref, out, kept_sem.at[n])
            for n, (ref, out) in enumerate(zip((w0, win, wout, w1), kept))
        ]

    start = i == 0

    @pl.when(jnp.logical_and(phase == 0, start))
    def _():
        barrier = pltpu.get_barrier_semaphore()
        for d in range(1, groups):
            there = (z, core, lax.rem(f + d, groups))
            pl.semaphore_signal(barrier, inc=1, device_id=there, device_id_type=MESH_ID)
        pl.semaphore_signal(barrier, inc=1, device_id=(z, 1 - core, f), device_id_type=MESH_ID)
        pl.semaphore_wait(barrier, groups)
        begin(0)
        begin(1)
        loads = [
            pltpu.make_async_copy(ref, rows_ref.at[n], rows_sem.at[n])
            for n, ref in enumerate((token_ref, cot_ref))
        ]
        for load in loads:
            load.start()
        for n, out in enumerate((x_out, cot_out)):
            loads[n].wait()
            pad_images(rows_ref.at[n], wide_ref, out)
        arrive(0)
        find_places(order_ref, routes_ref, pos_ref, aux_ref, line_ref)
        complete(0)
        lane = lax.broadcasted_iota(jnp.int32, (1, 128), 1)
        small = small_all[...].astype(WIDE)
        router_ref[...] = jnp.where(lane < EXPERTS, small, 0.0).astype(NARROW)
        gain_ref[...] = jnp.transpose(small)[EXPERTS : EXPERTS + 8, :]

    @pl.when(jnp.logical_and(phase == 1, start))
    def _():
        arrive(1)
        begin(2)
        complete(1)

    @pl.when(jnp.logical_and(phase == 2, start))
    def _():
        arrive(2)
        complete(2)
        for k in keepers():
            k.start()

    images = pl.ds(i * ib, ib)

    @pl.when(phase == 0)
    def _():
        x = x_out[images].astype(WIDE).reshape(ib * SP, D)
        y = attn_fwd_body(x, gain_ref[0:1, :], w0, qkv0_ref, mixed0_ref, peak0_ref, ib)
        y = y.reshape(ib, SP, D)
        first_ref[...] = y
        state[images] = y

    @pl.when(phase == 1)
    def _():
        x = state[images].reshape(ib * SP, D)
        unit, _ = norm_parts(x)
        normed = (unit * gain_ref[2:3, :]).astype(NARROW)
        acc = x
        for n in range(FF // 512):
            c = slice(n * 512, (n + 1) * 512)
            pre = nn(normed, win[:, c])
            cdf, _ = normal_parts(pre)
            acc = acc + nn((pre * cdf).astype(NARROW), wout[c, :])
        y = acc.reshape(ib, SP, D)
        mid_ref[...] = y
        state[images] = y

    @pl.when(phase == 2)
    def _():
        x = state[images].reshape(ib * SP, D)
        y = attn_fwd_body(x, gain_ref[1:2, :], w1, qkv1_ref, mixed1_ref, peak1_ref, ib)
        second_ref[...] = y.reshape(ib, SP, D)
        unit, _ = norm_parts(y)
        moe = (unit * gain_ref[3:4, :]).astype(NARROW)
        moe_ref[...] = moe.reshape(ib, SP, D)
        lane = lax.broadcasted_iota(jnp.int32, (1, 128), 1)
        logits = jnp.where(lane < EXPERTS, nn(moe, router_ref[...]), LOWEST)
        e = jnp.exp(logits - jnp.max(logits, -1, keepdims=True))
        prob_ref[...] = (e / jnp.sum(e, -1, keepdims=True)).reshape(ib, SP, 128)

    @pl.when(jnp.logical_and(phase == 2, i == pl.num_programs(1) - 1))
    def _():
        for k in keepers():
            k.wait()


def forward(weights, tokens, cotangent, routes_rows, groups, held, ib):
    any_space = pl.BlockSpec(memory_space=pl.ANY)
    vmem = pl.BlockSpec(memory_space=pltpu.VMEM)
    dma = pltpu.SemaphoreType.DMA
    images = tokens.shape[0] // SEQ
    padded, pairs = images * SP, images // ib
    slots = np.arange(EXPERTS, dtype=np.int32)[:, None]
    order = np.broadcast_to(slot_expert(slots, groups, held), (EXPERTS, 128)).astype(np.int32)

    def of_phase(n, *tail):
        def place(phase, i):
            return (jnp.where(phase == n, i, jnp.where(phase < n, 0, pairs - 1)), *[0] * len(tail))

        return pl.BlockSpec((ib, *tail), place)

    tails = (
        (0, WIDE, SP, D),
        (0, NARROW, SP, 3 * D),
        (0, NARROW, SP, D),
        (0, WIDE, HEADS, 128),
        (1, WIDE, SP, D),
        (2, WIDE, SP, D),
        (2, NARROW, SP, 3 * D),
        (2, NARROW, SP, D),
        (2, WIDE, HEADS, 128),
        (2, NARROW, SP, D),
        (2, WIDE, SP, 128),
    )
    matrices = [(D, 4 * D), (D, FF), (FF, D), (D, 4 * D)]
    return pl.pallas_call(
        partial(forward_kernel, groups, ib),
        grid=(3, pairs),
        in_specs=[any_space] * 9 + [vmem] * 2,
        out_specs=[any_space] * 4
        + [vmem] * 6
        + [of_phase(n, *tail) for n, _, *tail in tails],
        out_shape=[
            *[sds(m, NARROW) for m in matrices],
            sds((8, D), WIDE),
            sds((D, 128), NARROW),
            sds((images, SP, D), NARROW),
            sds((images, SP, D), NARROW),
            sds((EXPERTS, padded), WIDE),
            sds((padded, 128), WIDE),
            *[sds((images, *tail), dtype) for _, dtype, *tail in tails],
        ],
        scratch_shapes=[
            *[pltpu.VMEM(m, NARROW) for m in matrices],
            pltpu.VMEM((D, 128), NARROW),
            pltpu.VMEM((images, SP, D), WIDE),
            pltpu.VMEM((-(-(tokens.shape[0] + SP) // 16) * 16, D), WIDE),
            pltpu.VMEM((128, padded), WIDE),
            pltpu.VMEM((2, *tokens.shape), NARROW),
            *[dma((11, groups)) for _ in range(4)],
            dma((11, CORES)),
            dma((2,)),
            dma((4,)),
        ],
        compiler_params=pltpu.CompilerParams(
            vmem_limit_bytes=60 * MIB, collective_id=5, has_side_effects=True
        ),
        name="forward",
    )(*weights, tokens, cotangent, jnp.asarray(order), routes_rows)


def local(
    tokens,
    cotangent,
    routes,
    attn_norm,
    query_w,
    key_w,
    value_w,
    output_w,
    ffn_norm,
    mlp_in,
    mlp_out,
    router_w,
    expert_in,
    expert_out,
    updated_query,
    updated_key,
    clip_threshold,
):
    images = tokens.shape[0] // SEQ
    ib = 2
    groups = lax.axis_size("fsdp")
    core = lax.axis_index("core")
    held = expert_in.shape[0]
    mine = held // CORES
    owners = CORES * groups

    small = jnp.concatenate(
        [
            router_w,
            jnp.transpose(attn_norm),
            jnp.transpose(ffn_norm),
            jnp.zeros((router_w.shape[0], 128 - EXPERTS - 4), NARROW),
        ],
        1,
    )
    routes_rows = jnp.pad(
        jnp.transpose(routes).reshape(2, images, SEQ),
        ((0, 6), (0, 0), (0, SP - SEQ)),
        constant_values=-1,
    ).reshape(8, -1)
    w0, win, wout, w1, gains, wr, x, cot, pos, aux, *states = forward(
        (query_w, key_w, value_w, output_w, small, mlp_in, mlp_out),
        tokens,
        cotangent,
        routes_rows,
        groups,
        held,
        ib,
    )
    first, qkv0, mixed0, peak0, mid, second, qkv1, mixed1, peak1, moe, prob = states
    aux = aux.reshape(images, SP, 128)

    routed = (pos, moe.reshape(-1, D), cot.reshape(-1, D), prob.reshape(-1, 128))
    nz = lax.axis_size("z")
    early = own = None
    if nz == 4 and owners == 8 and mine == 4:
        tables, early, own, late = exchange(*routed, expert_in, expert_out, nz, groups)
        own = lax.psum(own, "z")
    else:
        sent = dispatch(*routed, groups, held).reshape(mine, owners, 2 * CAP, D)
        tables, blocks = [], []
        for j in range(mine):
            rows = lax.all_to_all(
                sent[j], ("core", "fsdp"), split_axis=0, concat_axis=0, tiled=True
            )
            pick = (core * mine + j).astype(jnp.int32).reshape(1)
            back, d_in, d_out = expert(pick, rows, expert_in, expert_out)
            tables.append(
                lax.all_to_all(back, ("core", "fsdp"), split_axis=0, concat_axis=0, tiled=True)
            )
            blocks.append(jnp.stack([d_in, d_out], 1).reshape(-1, BLOCK, BLOCK))
        tables = jnp.stack(tables)
        late = jnp.concatenate(blocks)

    y, mid_grad, dw1 = moe_bwd(
        gains, w1, wr, mid, second, cot, prob, aux, qkv1, mixed1, tables, images, ib
    )
    x_grad, dw0, d_wout = dense_bwd(
        gains, w0, win, wout, x, first, mid_grad, qkv0, mixed0, images, ib
    )
    lane = jnp.arange(128)[None, :]
    peaks = jnp.where(lane < 64, jnp.max(peak0, 0), jnp.max(peak1, 0))
    given = []
    if early is not None:
        (early, _, _) = lax.optimization_barrier((early, dw0, d_wout))
        given = widen_early(early, SUMMED, mine)
        (late, *given) = lax.optimization_barrier((late, *given))
    blocks, t1, t0, t_wout, maxima = sum_all(
        [late], [dw1, dw0, d_wout], peaks, early, own, nz, groups
    )
    small_outs = [
        sds(attn_norm.shape, WIDE),
        *[sds(query_w.shape, WIDE)] * 4,
        sds(ffn_norm.shape, WIDE),
        sds(mlp_in.shape, WIDE),
        sds(mlp_out.shape, WIDE),
        sds(router_w.shape, WIDE),
        sds(updated_query.shape, WIDE),
        sds(updated_key.shape, WIDE),
    ]
    *grads, clipped_query, clipped_key, expert_in_grad, expert_out_grad = finish(
        blocks,
        SUMMED if given else 0,
        given,
        mine,
        [t0, t1, t_wout, maxima, jnp.transpose(clip_threshold), updated_query, updated_key],
        small_outs,
    )
    return (y, x_grad, *grads, expert_in_grad, expert_out_grad, clipped_query, clipped_key)


def solution(mesh):
    replicas, groups = mesh.shape["replica"], mesh.shape["fsdp"]
    inner = Mesh(
        mesh.devices.reshape(replicas // CORES, CORES, groups), ("z", "core", "fsdp")
    )
    split = P(("z", "core", "fsdp"), None)
    second = P(None, "fsdp", None)
    in_specs = (
        split,
        split,
        split,
        P(None, "fsdp"),
        second,
        second,
        second,
        second,
        P(None, "fsdp"),
        P("fsdp", None),
        P("fsdp", None),
        P("fsdp", None),
        P("fsdp", None, None),
        P("fsdp", None, None),
        second,
        second,
        P(),
    )
    out_specs = (
        split,
        split,
        P(None, "fsdp"),
        second,
        second,
        second,
        second,
        P(None, "fsdp"),
        P("fsdp", None),
        P("fsdp", None),
        P("fsdp", None),
        P("fsdp", None, None),
        P("fsdp", None, None),
        second,
        second,
    )
    return jax.shard_map(local, mesh=inner, in_specs=in_specs, out_specs=out_specs, check_vma=False)
```
